32 devices in a mesh: ctx: 16 (over z, x, core), tp: 2 (over y).
Axes of the slice: x: 2, y: 2, z: 4, core: 2. Of those that a mesh axis runs over, the one named last changes fastest.
Arguments:
- layer_input: bfloat16 [2048, 2560], P('ctx'), may hold values from -6 to 6
- first_gain: bfloat16 [2560], P('ctx'), may hold values from 0.5 to 1.5
- query_down: bfloat16 [2560, 768], P('ctx'), may hold values from -0.125 to 0.125
- query_gain: bfloat16 [768], P('ctx'), may hold values from 0.5 to 1.5
- query_up: bfloat16 [768, 3840], P('ctx', 'tp'), may hold values from -0.21875 to 0.21875
- latent_down: bfloat16 [2560, 288], P('ctx'), may hold values from -0.125 to 0.125
- latent_gain: bfloat16 [256], P('ctx'), may hold values from 0.5 to 1.5
- latent_up: bfloat16 [256, 5120], P('ctx', 'tp'), may hold values from -0.375 to 0.375
- out_weight: bfloat16 [2560, 2560], P('tp', 'ctx'), may hold values from -12 to 12
- second_gain: bfloat16 [2560], P('ctx'), may hold values from 0.5 to 1.5
- gate_weight: bfloat16 [2560, 6400], P('ctx', 'tp'), may hold values from -0.125 to 0.125
- up_weight: bfloat16 [2560, 6400], P('ctx', 'tp'), may hold values from -0.125 to 0.125
- down_weight: bfloat16 [6400, 2560], P('tp', 'ctx'), may hold values from -0.4375 to 0.4375
- out_grad: bfloat16 [2048, 2560], P('ctx'), may hold values from -6 to 6
Outputs:
- layer_output: bfloat16 [2048, 2560], P('ctx')
- input_grad: float32 [2048, 2560], P('ctx')
- first_gain_grad: float32 [2560], P('ctx')
- query_down_grad: float32 [2560, 768], P('ctx')
- query_gain_grad: float32 [768], P('ctx')
- query_up_grad: float32 [768, 3840], P('ctx', 'tp')
- latent_down_grad: float32 [2560, 288], P('ctx')
- latent_gain_grad: float32 [256], P('ctx')
- latent_up_grad: float32 [256, 5120], P('ctx', 'tp')
- out_weight_grad: float32 [2560, 2560], P('tp', 'ctx')
- second_gain_grad: float32 [2560], P('ctx')
- gate_weight_grad: float32 [2560, 6400], P('ctx', 'tp')
- up_weight_grad: float32 [2560, 6400], P('ctx', 'tp')
- down_weight_grad: float32 [6400, 2560], P('tp', 'ctx')
The draws below stay inside these ranges and needn't reach their ends.
All inputs are finite; a program needn't handle non-finite values.
Results may differ from the reference program's by a relative error of at most 0.03.
Values may be sent and summed in bfloat16 or wider, within the bound.
A program may use at most 320 MiB of HBM per device.

```python
import math
import jax
import jax.numpy as jnp
from jax import lax

D = 2560
H = 40
QR = 768
KVR = 256
NOPE = 64
ROPE = 32
VH = 64
FF = 6400
TOK_DEV = 128
TOKENS = 2048
N_CTX = 16


def level_of(own_key, extent, pieces, least, largest):
    level = 1.0
    for position, parts in pieces:
        heights = jax.random.uniform(jax.random.fold_in(jax.random.fold_in(own_key, 6), position), (parts,), jnp.float32, least / len(pieces), largest / len(pieces))
        level = level * jnp.repeat(jnp.exp(heights), extent[position] // parts).reshape((-1,) + (1,) * (len(extent) - 1 - position))
    return level


def bell_draw(rng, shape, width, reach, shards=(), held_as=jnp.bfloat16):
    values = width * jax.random.normal(rng, shape, jnp.float32)
    if shards:
        values = values * level_of(rng, shape, shards, -0.22, 0.18)
    return jnp.clip(values, -reach, reach).astype(held_as)


def setup_inputs(seed: int = 0) -> dict:
    seeds = jax.random.split(jax.random.key(seed), 15)
    return {
        "layer_input": bell_draw(seeds[0], (TOKENS, D), 1.0, 6.0, ((0, 16),)),
        "first_gain": jnp.clip(1.0 + 0.1 * jax.random.normal(seeds[1], (D,), jnp.float32), 0.5, 1.5).astype(jnp.bfloat16),
        "query_down": bell_draw(seeds[2], (D, QR), D ** -0.5, 0.125, ((0, 16),)),
        "query_gain": jnp.clip(1.0 + 0.1 * jax.random.normal(seeds[3], (QR,), jnp.float32), 0.5, 1.5).astype(jnp.bfloat16),
        "query_up": bell_draw(seeds[4], (QR, H * (NOPE + ROPE)), QR ** -0.5, 0.21875, ((0, 16), (1, 2))),
        "latent_down": bell_draw(seeds[5], (D, KVR + ROPE), D ** -0.5, 0.125, ((0, 16),)),
        "latent_gain": jnp.clip(1.0 + 0.1 * jax.random.normal(seeds[6], (KVR,), jnp.float32), 0.5, 1.5).astype(jnp.bfloat16),
        "latent_up": bell_draw(seeds[7], (KVR, H * (NOPE + VH)), KVR ** -0.5, 0.375, ((0, 16), (1, 2))),
        "out_weight": bell_draw(seeds[8], (H * VH, D), 2.0, 12.0, ((0, 2), (1, 16))),
        "second_gain": jnp.clip(1.0 + 0.1 * jax.random.normal(seeds[9], (D,), jnp.float32), 0.5, 1.5).astype(jnp.bfloat16),
        "gate_weight": bell_draw(seeds[10], (D, FF), D ** -0.5, 0.125, ((0, 16), (1, 2))),
        "up_weight": bell_draw(seeds[11], (D, FF), D ** -0.5, 0.125, ((0, 16), (1, 2))),
        "down_weight": bell_draw(seeds[12], (FF, D), (FF // 32) ** -0.5, 0.4375, ((0, 2), (1, 16))),
        "out_grad": bell_draw(seeds[13], (TOKENS, D), 1.0, 6.0, ((0, 16),)),
    }


@jax.custom_vjp
def low(v):
    return lax.optimization_barrier(v.astype(jnp.bfloat16)).astype(jnp.float32)

@jax.custom_vjp
def low_back(v):
    return v

def low_keep(v):
    return (low(v), None)

def low_pass(kept, grad):
    return (grad,)

def back_keep(v):
    return (v, None)

def back_low(kept, grad):
    return (low(grad),)
low.defvjp(low_keep, low_pass)
low_back.defvjp(back_keep, back_low)
eps_norm = 1e-06
residual_scale = 1.4 / math.sqrt(62.0)
rope_base = 10000.0

def matmul(left_side, right_side):
    return jnp.dot(left_side, right_side, precision=lax.Precision.HIGHEST, preferred_element_type=jnp.float32)

def rms_norm(values, scale_gain):
    factor = lax.rsqrt(lax.optimization_barrier(jnp.mean(values * values, axis=-1, keepdims=True)) + eps_norm)
    return values * factor * scale_gain

def rotate(values, cosine, sine_table):
    half_width = values.shape[-1] // 2
    first_half = values[..., :half_width]
    second_half = values[..., half_width:]
    return jnp.concatenate([first_half * cosine - second_half * sine_table, second_half * cosine + first_half * sine_table], axis=-1)

def rope_tables(count_rows):
    positions = jnp.arange(count_rows, dtype=jnp.float32)[:, None]
    frequency = rope_base ** (-jnp.arange(ROPE // 2, dtype=jnp.float32) / (ROPE // 2))
    angles = positions * frequency[None, :]
    return (jnp.cos(angles), jnp.sin(angles))

def layer(inputs_wide, first_gain, query_down, query_gain, query_up, latent_down, latent_gain, latent_up, out_weight, second_gain, gate_weight, up_weight, down_weight):
    cosine, sine_table = rope_tables(TOKENS)
    normed = low(rms_norm(inputs_wide, first_gain))
    query_latent = low_back(matmul(normed, query_down))
    query_normed = low(rms_norm(query_latent, query_gain))
    queries_raw = low_back(matmul(query_normed, query_up)).reshape(TOKENS, H, NOPE + ROPE)
    queries = low(jnp.concatenate([queries_raw[..., :NOPE], rotate(queries_raw[..., NOPE:], cosine[:, None, :], sine_table[:, None, :])], axis=-1))
    compressed = low_back(matmul(normed, latent_down))
    latent = low(rms_norm(compressed[:, :KVR], latent_gain))
    key_rope = low(rotate(compressed[:, KVR:], cosine, sine_table))
    expanded_all = low(matmul(latent, latent_up))
    key_positions = jnp.arange(TOKENS, dtype=jnp.int32)

    def attend(block_args):
        query_block, start_row = block_args
        expanded = low_back(expanded_all).reshape(TOKENS, H, NOPE + VH)
        nope_part = jnp.einsum('qhd,khd->hqk', query_block[..., :NOPE], expanded[..., :NOPE], precision=lax.Precision.HIGHEST)
        rope_part = jnp.einsum('qhd,kd->hqk', query_block[..., NOPE:], key_rope, precision=lax.Precision.HIGHEST)
        scores = low_back((nope_part + rope_part) * (NOPE + ROPE) ** (-0.5))
        query_positions = start_row + jnp.arange(TOK_DEV, dtype=jnp.int32)
        allowed = key_positions[None, :] <= query_positions[:, None]
        scores = jnp.where(allowed[None], scores, -1e+30)
        running_top = lax.optimization_barrier(jnp.max(scores, axis=-1, keepdims=True))
        weights = jnp.exp(scores - running_top)
        probs = low(weights / lax.optimization_barrier(jnp.sum(weights, axis=-1, keepdims=True)))
        return jnp.einsum('hqk,khd->qhd', probs, expanded[..., NOPE:], precision=lax.Precision.HIGHEST)
    query_blocks = queries.reshape(N_CTX, TOK_DEV, H, NOPE + ROPE)
    block_starts = jnp.arange(N_CTX, dtype=jnp.int32) * TOK_DEV
    attended = lax.map(jax.checkpoint(attend), (query_blocks, block_starts)).reshape(TOKENS, H * VH)
    attended = low(low_back(attended))
    branch = low_back(matmul(attended, out_weight))
    middle = inputs_wide + residual_scale * branch
    normed_second = low(rms_norm(middle, second_gain))
    gate_values = low_back(matmul(normed_second, gate_weight))
    up_values = low_back(matmul(normed_second, up_weight))
    hidden = low(jax.nn.silu(gate_values) * up_values)
    ffn_sum = low_back(matmul(hidden, down_weight))
    return middle + residual_scale * ffn_sum

def reference(layer_input, first_gain, query_down, query_gain, query_up, latent_down, latent_gain, latent_up, out_weight, second_gain, gate_weight, up_weight, down_weight, out_grad):
    wide_args = [item.astype(jnp.float32) for item in (layer_input, first_gain, query_down, query_gain, query_up, latent_down, latent_gain, latent_up, out_weight, second_gain, gate_weight, up_weight, down_weight)]
    result, pullback = jax.vjp(layer, *wide_args)
    grads = pullback(out_grad.astype(jnp.float32))
    return (result.astype(jnp.bfloat16), grads[0], grads[1], grads[2], grads[3], grads[4], grads[5], grads[6], grads[7], grads[8], grads[9], grads[10], grads[11], grads[12])
```

```python
import math

import jax
import jax.numpy as jnp
from jax import lax
from jax.sharding import PartitionSpec as P

H = 40
KVR = 256
NOPE = 64
ROPE = 32
VH = 64
HEAD_GROUPS = 8
FF_GROUPS = 16

eps_norm = 1e-06
residual_scale = 1.4 / math.sqrt(62.0)
score_scale = (NOPE + ROPE) ** (-0.5)
rope_base = 10000.0
BF = jnp.bfloat16
F32 = jnp.float32


def matmul(left_side, right_side):
    return jnp.dot(left_side, right_side, preferred_element_type=F32)


def matmul_nt(left_side, right_side):
    return lax.dot_general(
        left_side, right_side, (((1,), (1,)), ((), ())), preferred_element_type=F32
    )


def matmul_tn(left_side, right_side):
    return lax.dot_general(
        left_side, right_side, (((0,), (0,)), ((), ())), preferred_element_type=F32
    )


def rms_norm(values, scale_gain):
    factor = lax.rsqrt(jnp.mean(values * values, axis=-1, keepdims=True) + eps_norm)
    return values * factor * scale_gain


def norm_back(values, scale_gain, upstream):
    factor = lax.rsqrt(jnp.mean(values * values, axis=-1, keepdims=True) + eps_norm)
    scaled = upstream * scale_gain
    inner_sum = jnp.mean(scaled * values, axis=-1, keepdims=True)
    grad_values = factor * scaled - values * factor * factor * factor * inner_sum
    grad_gain = jnp.sum(upstream * values * factor, axis=0)
    return (grad_values, grad_gain)


def rotate(values, cosine, sine_table):
    half_width = values.shape[-1] // 2
    first_half = values[..., :half_width]
    second_half = values[..., half_width:]
    return jnp.concatenate(
        [
            first_half * cosine - second_half * sine_table,
            second_half * cosine + first_half * sine_table,
        ],
        axis=-1,
    )


def rope_tables(positions):
    frequency = rope_base ** (-jnp.arange(ROPE // 2, dtype=F32) / (ROPE // 2))
    angles = positions.astype(F32)[:, None] * frequency[None, :]
    return (jnp.cos(angles), jnp.sin(angles))


def member_groups(n_ctx, count):
    size = n_ctx // count
    return [[f * size + j for f in range(count)] for j in range(size)]


def gather_over(values, count):
    return lax.all_gather(
        values,
        "ctx",
        axis=0,
        tiled=True,
        axis_index_groups=member_groups(lax.axis_size("ctx"), count),
    )


def scatter_over(values, count):
    return lax.psum_scatter(
        values,
        "ctx",
        scatter_dimension=0,
        tiled=True,
        axis_index_groups=member_groups(lax.axis_size("ctx"), count),
    )


def swap_tp(values):
    return lax.ppermute(values, "tp", [(0, 1), (1, 0)])


def shards(
    layer_input,
    first_gain,
    query_down,
    query_gain,
    query_up,
    latent_down,
    latent_gain,
    latent_up,
    out_weight,
    second_gain,
    gate_weight,
    up_weight,
    down_weight,
    out_grad,
):
    n_ctx = lax.axis_size("ctx")
    n_tp = lax.axis_size("tp")
    c = lax.axis_index("ctx")
    t = lax.axis_index("tp")
    dim = layer_input.shape[1]
    ctx_rows = layer_input.shape[0]
    rows = ctx_rows // n_tp
    qr = query_down.shape[1]
    down_width = qr + KVR + ROPE
    heads = H // HEAD_GROUPS
    size_a = n_ctx // HEAD_GROUPS
    f_a, j_a = c // size_a, c % size_a
    size_f = n_ctx // FF_GROUPS
    ff_cols = gate_weight.shape[1] // FF_GROUPS

    gains = jnp.concatenate([first_gain, query_gain, latent_gain, second_gain])
    widths = [first_gain.shape[0], query_gain.shape[0], latent_gain.shape[0], second_gain.shape[0]]
    gains = lax.all_gather(gains, "ctx", axis=0).astype(F32)
    starts = [0, widths[0], widths[0] + widths[1], widths[0] + widths[1] + widths[2]]
    gain_first, gain_query, gain_latent, gain_second = [
        gains[:, s : s + w].reshape(-1) for s, w in zip(starts, widths)
    ]
    down_shard = jnp.concatenate([query_down, latent_down], axis=1)
    down_full = lax.all_gather(down_shard, "ctx", axis=0, tiled=True)

    def own_heads(mine):
        return jnp.where(f_a // (HEAD_GROUPS // n_tp) == t, mine, swap_tp(mine))

    local_f = f_a % (HEAD_GROUPS // n_tp)
    q_width = heads * (NOPE + ROPE)
    kv_width = heads * (NOPE + VH)
    o_width = heads * VH
    up_all = lax.all_gather(query_up, "ctx", axis=0, tiled=True)
    q_up = own_heads(lax.dynamic_slice_in_dim(up_all, local_f * q_width, q_width, 1))
    lat_all = lax.all_gather(latent_up, "ctx", axis=0, tiled=True)
    l_up = own_heads(lax.dynamic_slice_in_dim(lat_all, local_f * kv_width, kv_width, 1))
    out_all = lax.all_gather(out_weight, "ctx", axis=1, tiled=True)
    w_out = own_heads(lax.dynamic_slice_in_dim(out_all, local_f * o_width, o_width, 0))

    def to_units(shard):
        pieces = shard.reshape(shard.shape[0], FF_GROUPS, ff_cols)
        pieces = lax.all_to_all(
            jnp.transpose(pieces, (1, 0, 2)),
            "ctx",
            0,
            0,
            axis_index_groups=member_groups(n_ctx, FF_GROUPS),
            tiled=True,
        )
        if size_f > 1:
            pieces = lax.all_gather(
                pieces,
                "ctx",
                axis=1,
                tiled=False,
                axis_index_groups=[
                    [f * size_f + j for j in range(size_f)] for f in range(FF_GROUPS)
                ],
            )
        return pieces.reshape(dim, ff_cols)

    def from_units(grads):
        pieces = grads.reshape(FF_GROUPS, dim // FF_GROUPS, ff_cols)
        if size_f > 1:
            pieces = lax.psum_scatter(
                pieces.astype(F32),
                "ctx",
                scatter_dimension=1,
                tiled=True,
                axis_index_groups=[
                    [f * size_f + j for j in range(size_f)] for f in range(FF_GROUPS)
                ],
            ).astype(BF)
        pieces = lax.all_to_all(
            pieces,
            "ctx",
            0,
            0,
            axis_index_groups=member_groups(n_ctx, FF_GROUPS),
            tiled=True,
        )
        return jnp.transpose(pieces, (1, 0, 2)).reshape(dim // n_ctx, FF_GROUPS * ff_cols)

    gate_own, up_own, down_own = (
        to_units(gate_weight),
        to_units(up_weight),
        to_units(down_weight.T),
    )
    w_gate = jnp.concatenate([gate_own, swap_tp(gate_own)], axis=1)
    w_up = jnp.concatenate([up_own, swap_tp(up_own)], axis=1)
    w_down_t = jnp.concatenate([down_own, swap_tp(down_own)], axis=1)

    x = lax.dynamic_slice_in_dim(layer_input, t * rows, rows, 0).astype(F32)
    out_grad_rows = lax.dynamic_slice_in_dim(out_grad, t * rows, rows, 0).astype(F32)
    positions = c * ctx_rows + t * rows + jnp.arange(rows, dtype=jnp.int32)
    cosine, sine_table = rope_tables(positions)

    grad_ffn = (residual_scale * out_grad_rows).astype(BF)
    grad_ffn_all = gather_over(grad_ffn, FF_GROUPS)

    normed = rms_norm(x, gain_first).astype(BF)
    both = matmul(normed, down_full)
    query_latent, compressed = both[:, :qr], both[:, qr:]
    query_normed = rms_norm(query_latent, gain_query).astype(BF)
    latent = rms_norm(compressed[:, :KVR], gain_latent).astype(BF)
    key_rope = rotate(compressed[:, KVR:], cosine, sine_table).astype(BF)
    lat_rope = lax.all_gather(
        jnp.concatenate([latent, key_rope], axis=1), ("ctx", "tp"), axis=0, tiled=True
    )
    latent_all, rope_all = lat_rope[:, :KVR], lat_rope[:, KVR:]
    qn_all = gather_over(query_normed, HEAD_GROUPS)
    q_rows = qn_all.shape[0]
    keys = latent_all.shape[0]

    q_positions = (
        (jnp.arange(HEAD_GROUPS, dtype=jnp.int32)[:, None] * size_a + j_a) * ctx_rows
        + t * rows
        + jnp.arange(rows, dtype=jnp.int32)[None, :]
    ).reshape(-1)
    q_cos, q_sin = rope_tables(q_positions)
    queries_raw = matmul(qn_all, q_up).reshape(q_rows, heads, NOPE + ROPE)
    queries = jnp.concatenate(
        [
            queries_raw[..., :NOPE],
            rotate(queries_raw[..., NOPE:], q_cos[:, None, :], q_sin[:, None, :]),
        ],
        axis=-1,
    ).astype(BF)
    expanded = matmul(latent_all, l_up).astype(BF)
    allowed = jnp.arange(keys, dtype=jnp.int32)[None, :] <= q_positions[:, None]

    def head_keys(h):
        part = expanded[:, h * (NOPE + VH) : (h + 1) * (NOPE + VH)]
        return jnp.concatenate([part[:, :NOPE], rope_all], axis=1), part[:, NOPE:]

    outs, logs = [], []
    for h in range(heads):
        k, v = head_keys(h)
        scores = jnp.where(allowed, matmul_nt(queries[:, h], k) * score_scale, -1e30)
        top = jnp.max(scores, axis=-1, keepdims=True)
        weights = jnp.exp(scores - top)
        total = jnp.sum(weights, axis=-1, keepdims=True)
        outs.append(matmul(weights.astype(BF), v) / total)
        logs.append(top + jnp.log(total))
    attended_wide = jnp.concatenate(outs, axis=1)
    attended = attended_wide.astype(BF)

    branch = scatter_over(matmul(attended, w_out).astype(BF), HEAD_GROUPS).astype(F32)
    middle = x + residual_scale * branch
    normed_second = rms_norm(middle, gain_second).astype(BF)
    ns_all = gather_over(normed_second, FF_GROUPS)
    gate_values = matmul(ns_all, w_gate)
    up_values = matmul(ns_all, w_up)
    sigmoid_gate = jax.nn.sigmoid(gate_values)
    hidden = (gate_values * sigmoid_gate * up_values).astype(BF)
    ffn_sum = scatter_over(matmul_nt(hidden, w_down_t).astype(BF), FF_GROUPS).astype(F32)
    out_half = (middle + residual_scale * ffn_sum).astype(BF)
    layer_output = lax.all_gather(out_half, "tp", axis=0, tiled=True)

    grad_hidden = matmul(grad_ffn_all, w_down_t)
    grad_gate = (
        grad_hidden * up_values * sigmoid_gate * (1.0 + gate_values * (1.0 - sigmoid_gate))
    ).astype(BF)
    grad_up = (grad_hidden * gate_values * sigmoid_gate).astype(BF)
    grad_second = scatter_over(
        (matmul_nt(grad_gate, w_gate) + matmul_nt(grad_up, w_up)).astype(BF), FF_GROUPS
    ).astype(F32)

    def unit_grads(left, right):
        whole = matmul_tn(left, right)
        mine, other = whole[:, :ff_cols], whole[:, ff_cols:]
        mine = mine + swap_tp(other.astype(BF)).astype(F32)
        return from_units(mine.astype(BF)).astype(F32)

    gate_weight_grad = unit_grads(ns_all, grad_gate)
    up_weight_grad = unit_grads(ns_all, grad_up)
    down_weight_grad = unit_grads(grad_ffn_all, hidden).T

    grad_middle_part, second_gain_part = norm_back(middle, gain_second, grad_second)
    grad_middle = out_grad_rows + grad_middle_part

    grad_branch = (residual_scale * grad_middle).astype(BF)
    gb_all = gather_over(grad_branch, HEAD_GROUPS)
    out_part = matmul_tn(attended, gb_all)
    grad_attended = matmul_nt(gb_all, w_out).astype(BF)

    grad_q_rows, grad_kv, grad_rope = [], [], jnp.zeros((keys, ROPE), F32)
    for h in range(heads):
        k, v = head_keys(h)
        q, ga = queries[:, h], grad_attended[:, h * VH : (h + 1) * VH]
        row_inner = jnp.sum(
            ga.astype(F32) * attended_wide[:, h * VH : (h + 1) * VH], axis=-1, keepdims=True
        )
        scores = jnp.where(allowed, matmul_nt(q, k) * score_scale, -1e30)
        probs = jnp.exp(scores - logs[h])
        grad_probs = matmul_nt(ga, v)
        grad_scores = (probs * (grad_probs - row_inner)).astype(BF)
        gq = matmul(grad_scores, k) * score_scale
        grad_q_rows += [gq[:, :NOPE], rotate(gq[:, NOPE:], q_cos, -q_sin)]
        gk = matmul_tn(grad_scores, q) * score_scale
        grad_kv += [gk[:, :NOPE], matmul_tn(probs.astype(BF), ga)]
        grad_rope = grad_rope + gk[:, NOPE:]
    grad_q_rows = jnp.concatenate(grad_q_rows, axis=1).astype(BF)
    grad_expanded = jnp.concatenate(grad_kv, axis=1).astype(BF)
    grad_lat_rope = jnp.concatenate([matmul_nt(grad_expanded, l_up), grad_rope], axis=1)
    l_up_part = matmul_tn(latent_all, grad_expanded)
    q_up_part = matmul_tn(qn_all, grad_q_rows)

    grad_query_normed = scatter_over(matmul_nt(grad_q_rows, q_up).astype(BF), HEAD_GROUPS)
    own_lat_rope = lax.psum_scatter(
        grad_lat_rope.astype(BF), ("ctx", "tp"), scatter_dimension=0, tiled=True
    ).astype(F32)
    grad_query_latent, query_gain_part = norm_back(
        query_latent, gain_query, grad_query_normed.astype(F32)
    )
    grad_latent_rows, latent_gain_part = norm_back(
        compressed[:, :KVR], gain_latent, own_lat_rope[:, :KVR]
    )
    grad_both = jnp.concatenate(
        [grad_query_latent, grad_latent_rows, rotate(own_lat_rope[:, KVR:], cosine, -sine_table)],
        axis=1,
    ).astype(BF)
    down_part = matmul_tn(normed, grad_both)
    grad_normed = matmul_nt(grad_both, down_full)
    grad_input_part, first_gain_part = norm_back(x, gain_first, grad_normed)
    input_grad = lax.all_gather(grad_middle + grad_input_part, "tp", axis=0, tiled=True)

    down_grads = lax.psum(
        lax.psum_scatter(down_part.astype(BF), "ctx", scatter_dimension=0, tiled=True), "tp"
    ).astype(F32)

    def head_grads(part, axis):
        part = part.astype(BF)
        width = part.shape[axis]
        shape = list(part.shape)
        shape[axis] = width * (HEAD_GROUPS // n_tp)
        wide = lax.dynamic_update_slice_in_dim(
            jnp.zeros(shape, BF), part, local_f * width, axis
        )
        here = f_a // (HEAD_GROUPS // n_tp) == t
        mine = jnp.where(here, wide, 0)
        other = swap_tp(jnp.where(here, 0, wide))
        return lax.psum_scatter(
            mine + other, "ctx", scatter_dimension=1 - axis, tiled=True
        ).astype(F32)

    query_up_grad = head_grads(q_up_part, 1)
    latent_up_grad = head_grads(l_up_part, 1)
    out_weight_grad = head_grads(out_part, 0)

    gain_parts = jnp.concatenate(
        [
            p.reshape(n_ctx, -1)
            for p in (first_gain_part, query_gain_part, latent_gain_part, second_gain_part)
        ],
        axis=1,
    )
    gain_grads = lax.psum(
        lax.psum_scatter(gain_parts, "ctx", scatter_dimension=0, tiled=True), "tp"
    ).reshape(-1)
    first_gain_grad, query_gain_grad, latent_gain_grad, second_gain_grad = [
        gain_grads[s : s + w] for s, w in zip(starts, widths)
    ]
    return (
        layer_output,
        input_grad,
        first_gain_grad,
        down_grads[:, :qr],
        query_gain_grad,
        query_up_grad,
        down_grads[:, qr:],
        latent_gain_grad,
        latent_up_grad,
        out_weight_grad,
        second_gain_grad,
        gate_weight_grad,
        up_weight_grad,
        down_weight_grad,
    )


def solution(mesh):
    return jax.shard_map(
        shards,
        mesh=mesh,
        in_specs=(
            P("ctx", None),
            P("ctx"),
            P("ctx", None),
            P("ctx"),
            P("ctx", "tp"),
            P("ctx", None),
            P("ctx"),
            P("ctx", "tp"),
            P("tp", "ctx"),
            P("ctx"),
            P("ctx", "tp"),
            P("ctx", "tp"),
            P("tp", "ctx"),
            P("ctx", None),
        ),
        out_specs=(
            P("ctx", None),
            P("ctx", None),
            P("ctx"),
            P("ctx", None),
            P("ctx"),
            P("ctx", "tp"),
            P("ctx", None),
            P("ctx"),
            P("ctx", "tp"),
            P("tp", "ctx"),
            P("ctx"),
            P("ctx", "tp"),
            P("ctx", "tp"),
            P("tp", "ctx"),
        ),
        check_vma=False,
    )
```

```python
import math

import jax
import jax.numpy as jnp
from jax import lax
from jax.experimental import pallas as pl
from jax.experimental.pallas import tpu as pltpu
from jax.sharding import PartitionSpec as P

BF = jnp.bfloat16
F32 = jnp.float32

H = 40
KVR = 256
NOPE = 64
ROPE = 32
VH = 64

eps_norm = 1e-06
residual_scale = 1.4 / math.sqrt(62.0)
score_scale = (NOPE + ROPE) ** (-0.5)
rope_base = 10000.0


def matmul(left_side, right_side):
    return jnp.dot(left_side, right_side, preferred_element_type=F32)


def matmul_nt(left_side, right_side):
    return lax.dot_general(
        left_side, right_side, (((1,), (1,)), ((), ())), preferred_element_type=F32
    )


def matmul_tn(left_side, right_side):
    return lax.dot_general(
        left_side, right_side, (((0,), (0,)), ((), ())), preferred_element_type=F32
    )


def rms_norm(values, scale_gain):
    factor = lax.rsqrt(jnp.mean(values * values, axis=-1, keepdims=True) + eps_norm)
    return values * factor * scale_gain


def norm_back(values, scale_gain, upstream):
    factor = lax.rsqrt(jnp.mean(values * values, axis=-1, keepdims=True) + eps_norm)
    scaled = upstream * scale_gain
    inner_sum = jnp.mean(scaled * values, axis=-1, keepdims=True)
    grad_values = factor * scaled - values * factor * factor * factor * inner_sum
    grad_gain = jnp.sum(upstream * values * factor, axis=0)
    return (grad_values, grad_gain)


def rotate(values, cosine, sine_table):
    half_width = values.shape[-1] // 2
    first_half = values[..., :half_width]
    second_half = values[..., half_width:]
    return jnp.concatenate(
        [
            first_half * cosine - second_half * sine_table,
            second_half * cosine + first_half * sine_table,
        ],
        axis=-1,
    )


def rope_tables(positions):
    frequency = rope_base ** (-jnp.arange(ROPE // 2, dtype=F32) / (ROPE // 2))
    angles = positions.astype(F32)[:, None] * frequency[None, :]
    return (jnp.cos(angles), jnp.sin(angles))


MESH = pl.DeviceIdType.MESH
OFFSETS = (0, -1, 1, -2, 2, -3, 3)


class Place:
    def __init__(self, n_ctx):
        c = lax.axis_index("ctx")
        self.members = n_ctx // 16
        self.c = c
        self.t = lax.axis_index("tp")
        self.m = lax.rem(c, self.members)
        g = c // self.members
        self.g = g
        self.a, self.b, self.d = g // 4, lax.rem(g // 2, 2), lax.rem(g, 2)

    def at(self, a=None, b=None, d=None):
        a = self.a if a is None else a
        b = self.b if b is None else b
        d = self.d if d is None else d
        return (((a * 2 + b) * 2 + d) * self.members + self.m, self.t)

    def up(self):
        return self.at(a=self.a + 1)

    def down(self):
        return self.at(a=self.a - 1)

    def across(self):
        return self.at(b=1 - self.b)

    def core(self):
        return self.at(d=1 - self.d)

    def other(self):
        return (self.c, 1 - self.t)

    def valid(self, o):
        return None if o == 0 else (self.a + o >= 0 if o < 0 else self.a + o <= 3)


def both_of(p, q):
    if p is None:
        return q
    return p if q is None else p & q


def when(p, body):
    if p is None:
        body()
    else:
        pl.when(p)(body)


class Net:
    def __init__(self, place, sems):
        self.place, self.sems, self.count, self.pending = place, sems, 0, []

    def sem(self):
        self.count += 1
        return self.sems.at[self.count - 1]

    def send(self, src, dst, recv, to, cond=None):
        mine = self.sem()

        def copy():
            return pltpu.make_async_remote_copy(
                src(), dst(), mine, recv, device_id=to(), device_id_type=MESH
            )

        when(cond, lambda: copy().start())
        self.pending.append((cond, lambda: copy().wait_send()))

    def recv(self, dst, sem, cond=None):
        def wait():
            ref = dst()
            pltpu.make_async_remote_copy(
                ref, ref, sem, sem, device_id=self.place.other(), device_id_type=MESH
            ).wait_recv()

        when(cond, wait)

    def finish(self):
        for cond, wait in self.pending:
            when(cond, wait)


def greet(place, line=False, across=False, core=False, other=False, everyone=0):
    barrier = pltpu.get_barrier_semaphore()

    def tell(device):
        pl.semaphore_signal(barrier, inc=1, device_id=device, device_id_type=MESH)

    count = 0
    if everyone:
        for k in range(1, everyone):
            tell((lax.rem(place.c + k * place.members, everyone * place.members), place.t))
        count = count + everyone - 1
    else:
        if line:
            pl.when(place.a < 3)(lambda: tell(place.up()))
            pl.when(place.a > 0)(lambda: tell(place.down()))
            count = count + (place.a < 3).astype(jnp.int32) + (place.a > 0).astype(jnp.int32)
        if across:
            tell(place.across())
            count = count + 1
        if core:
            tell(place.core())
            count = count + 1
    if other:
        tell(place.other())
        count = count + 1
    pl.semaphore_wait(barrier, count)


def gather_steps(net, src, out, width):
    p = net.place
    cores = width == 16

    def slot(o, b, d):
        g = (p.a + o) * 2 + b
        return out.at[g * 2 + d] if cores else out.at[g]

    z_sem = {o: net.sem() for o in OFFSETS if o}
    x_sem = {o: net.sem() for o in OFFSETS}
    c_sem = {(s, o): net.sem() for s in (0, 1) for o in OFFSETS} if cores else {}
    own_sem = net.sem()
    keep = pltpu.make_async_copy(src, slot(0, p.b, p.d), own_sem)
    keep.start()

    def forward(o):
        ok = p.valid(o)
        here = lambda: slot(o, p.b, p.d)
        origin = (lambda: src) if o == 0 else here
        if o <= 0 and o > -3:
            net.send(origin, here, z_sem[o - 1], p.up, both_of(ok, p.a < 3))
        if o >= 0 and o < 3:
            net.send(origin, here, z_sem[o + 1], p.down, both_of(ok, p.a > 0))
        net.send(origin, here, x_sem[o], p.across, ok)
        if cores:
            net.send(origin, here, c_sem[0, o], p.core, ok)

    def from_line(o):
        net.recv(lambda: slot(o, p.b, p.d), z_sem[o], p.valid(o))
        forward(o)

    def from_across(o):
        there = lambda: slot(o, 1 - p.b, p.d)
        net.recv(there, x_sem[o], p.valid(o))
        if cores:
            net.send(there, there, c_sem[1, o], p.core, p.valid(o))

    forward(0)
    yield
    for near in (1, 2, 3):
        from_line(-near)
        from_line(near)
        yield
        if near == 1:
            from_across(0)
        else:
            from_across(1 - near)
            from_across(near - 1)
        yield
    from_across(-3)
    from_across(3)
    yield
    if cores:
        for o in OFFSETS:
            net.recv(lambda: slot(o, p.b, 1 - p.d), c_sem[0, o], p.valid(o))
            net.recv(lambda: slot(o, 1 - p.b, 1 - p.d), c_sem[1, o], p.valid(o))
    keep.wait()


def add_into(out, terms, rows):
    step = 16 if rows % 16 == 0 else rows

    def body(i):
        part = pl.ds(pl.multiple_of(i * step, step), step)
        total = terms[0][part].astype(F32)
        for term in terms[1:]:
            total = total + term[part].astype(F32)
        out[part] = total.astype(out.dtype)

    pl.loop(0, rows // step)(body)


def reduce_steps(net, parts, out, near_core, near_x, line_in, line_out, rows, width):
    p = net.place
    cores = width == 16
    order = (-3, 3, -2, 2, -1, 1, 0)
    if cores:
        c_sem = {(b, o): net.sem() for b in (0, 1) for o in order}
        for o in order:
            for side in (1, 0):
                def src(o=o, side=side):
                    b = 1 - p.b if side else p.b
                    return parts.at[((p.a + o) * 2 + b) * 2 + 1 - p.d]

                def dst(o=o, side=side):
                    b = 1 - p.b if side else p.b
                    return near_core.at[(p.a + o) * 2 + b]

                net.send(src, dst, c_sem[side, o], p.core, p.valid(o))
        yield
    x_sem = {o: net.sem() for o in order}
    up_sem = {o: net.sem() for o in (0, 1, 2)}
    down_sem = {o: net.sem() for o in (0, 1, 2)}

    def mine(o, b):
        g = (p.a + o) * 2 + b
        return near_core.at[g] if cores else parts.at[g]

    for o in order:
        if cores:
            def join(o=o):
                g = (p.a + o) * 2 + 1 - p.b
                add_into(near_core.at[g], [near_core.at[g], parts.at[g * 2 + p.d]], rows)

            net.recv(lambda: near_core.at[(p.a + o) * 2 + 1 - p.b], c_sem[1, o], p.valid(o))
            when(p.valid(o), join)
        net.send(
            lambda o=o: mine(o, 1 - p.b),
            lambda o=o: near_x.at[p.a + o],
            x_sem[o],
            p.across,
            p.valid(o),
        )
    yield
    for o in order:
        ok = p.valid(o)
        if cores:
            net.recv(lambda: near_core.at[(p.a + o) * 2 + p.b], c_sem[0, o], ok)

        def terms(o=o):
            g = (p.a + o) * 2 + p.b
            own = [near_core.at[g], parts.at[g * 2 + p.d]] if cores else [parts.at[g]]
            return own + [near_x.at[p.a + o]]

        net.recv(lambda: near_x.at[p.a + o], x_sem[o], ok)
        if o == 0:
            below, above = line_in.at[0, 0], line_in.at[1, 0]
            net.recv(lambda: below, up_sem[0], p.a > 0)
            net.recv(lambda: above, down_sem[0], p.a < 3)
            inner = (p.a > 0) & (p.a < 3)
            pl.when(inner)(lambda: add_into(out, terms() + [below, above], rows))
            pl.when(p.a == 0)(lambda: add_into(out, terms() + [above], rows))
            pl.when(p.a == 3)(lambda: add_into(out, terms() + [below], rows))
            continue
        far = abs(o)
        way = 0 if o > 0 else 1
        stage = line_out.at[way, far - 1]
        sems = up_sem if o > 0 else down_sem
        first = p.a == 0 if o > 0 else p.a == 3
        if far < 3:
            came = line_in.at[way, far]
            later = ok & ~first
            net.recv(lambda: came, sems[far], later)
            pl.when(later)(lambda: add_into(stage, terms() + [came], rows))
            pl.when(ok & first)(lambda: add_into(stage, terms(), rows))
        else:
            pl.when(ok)(lambda: add_into(stage, terms(), rows))
        net.send(
            lambda stage=stage: stage,
            lambda far=far, way=way: line_in.at[way, far - 1],
            sems[far - 1],
            p.up if o > 0 else p.down,
            ok,
        )
        yield


def swap_steps(net, src, dst):
    sem = net.sem()
    net.send(lambda: src, lambda: dst, sem, net.place.other)
    yield
    net.recv(lambda: dst, sem)


def run_together(*tasks):
    tasks = list(tasks)
    while tasks:
        for task in list(tasks):
            try:
                next(task)
            except StopIteration:
                tasks.remove(task)


ANY = pl.BlockSpec(memory_space=pl.ANY)
VMEM = pl.BlockSpec(memory_space=pltpu.VMEM)


def comm_call(name, number, body, ins, in_specs, outs, out_specs, scratch, sems):
    return pl.pallas_call(
        body,
        out_shape=outs,
        in_specs=in_specs,
        out_specs=out_specs,
        scratch_shapes=list(scratch) + [pltpu.SemaphoreType.DMA((sems,))],
        compiler_params=pltpu.CompilerParams(
            collective_id=number, has_side_effects=True, vmem_limit_bytes=56 << 20
        ),
        name=name,
    )(*ins)


def shape(dims, dtype=BF):
    return jax.ShapeDtypeStruct(tuple(dims), dtype)


def reduce_scratch(rows, cols, width):
    near_core = [pltpu.VMEM((8, rows, cols), BF)] if width == 16 else []
    return near_core + [
        pltpu.VMEM((4, rows, cols), BF),
        pltpu.VMEM((2, 3, rows, cols), BF),
        pltpu.VMEM((2, 3, rows, cols), BF),
    ]


def gather_blocks(name, number, items, widths, n_ctx):
    k = len(items)

    def body(*refs):
        ins, outs, sems = refs[:k], refs[k : 2 * k], refs[-1]
        place = Place(n_ctx)
        greet(place, line=True, across=True, core=16 in widths)
        net = Net(place, sems)
        run_together(*[gather_steps(net, i, o, w) for i, o, w in zip(ins, outs, widths)])
        net.finish()

    outs = comm_call(
        name,
        number,
        body,
        items,
        [ANY] * k,
        [shape((w,) + i.shape, i.dtype) for i, w in zip(items, widths)],
        [ANY] * k,
        [],
        64 * k,
    )
    return [o.reshape((-1,) + o.shape[2:]) for o in outs]


def reduce_blocks(name, number, items, widths, n_ctx):
    k = len(items)
    blocks = [i.reshape(w, i.shape[0] // w, i.shape[1]) for i, w in zip(items, widths)]

    def body(*refs):
        ins, outs, rest = refs[:k], refs[k : 2 * k], list(refs[2 * k :])
        place = Place(n_ctx)
        greet(place, line=True, across=True, core=16 in widths)
        net = Net(place, rest.pop())
        tasks = []
        for i, o, w in zip(ins, outs, widths):
            near_core = rest.pop(0) if w == 16 else None
            near_x, line_in, line_out = rest.pop(0), rest.pop(0), rest.pop(0)
            tasks.append(
                reduce_steps(net, i, o, near_core, near_x, line_in, line_out, o.shape[0], w)
            )
        run_together(*tasks)
        net.finish()

    scratch = []
    for i, w in zip(blocks, widths):
        scratch += reduce_scratch(i.shape[1], i.shape[2], w)
    return comm_call(
        name,
        number,
        body,
        blocks,
        [VMEM] * k,
        [shape(i.shape[1:], F32) for i in blocks],
        [VMEM] * k,
        scratch,
        64 * k,
    )


def weights_in(number, ff, at, block, n_ctx):
    def body(ff_ref, at_ref, block_ref, own, oth, heads, blocks, ff_sems, at_sems, sems):
        place = Place(n_ctx)
        p = place
        greet(p, everyone=16, other=True)
        net = Net(p, sems)

        def device(g):
            return (g * p.members + p.m, p.t)

        keep_own = pltpu.make_async_copy(ff_ref.at[p.g], own.at[p.g], net.sem())
        keep_own.start()
        owner = p.b == p.t
        f = p.a * 2 + p.b

        def units():
            for k in range(1, 16):
                net.send(
                    lambda k=k: ff_ref.at[p.g ^ k],
                    lambda: own.at[p.g],
                    ff_sems.at[0, k],
                    lambda k=k: device(p.g ^ k),
                )
            net.send(lambda: ff_ref.at[p.g], lambda: oth.at[p.g], ff_sems.at[1, 0], p.other)
            yield
            for k in range(1, 16):
                there = lambda k=k: own.at[p.g ^ k]
                net.recv(there, ff_sems.at[0, k])
                net.send(there, lambda k=k: oth.at[p.g ^ k], ff_sems.at[1, k], p.other)
                yield
            for k in range(16):
                net.recv(lambda k=k: oth.at[p.g ^ k], ff_sems.at[1, k])

        def attention():
            keep = pltpu.make_async_copy(at_ref.at[p.a], heads.at[p.g], net.sem())
            pl.when(owner)(lambda: keep.start())
            for s in range(4):
                net.send(
                    lambda s=s: at_ref.at[s],
                    lambda: heads.at[p.g],
                    at_sems.at[0, f],
                    lambda s=s: p.at(a=s, b=p.t),
                    ~(owner & (p.a == s)),
                )
            pl.when(owner)(lambda: keep.wait())
            yield
            for q in range(8):
                mine = lambda q=q: heads.at[q * 2 + p.d]
                net.recv(mine, at_sems.at[0, q], owner & (f != q))
                net.send(mine, mine, at_sems.at[1, q], p.other, owner)
                net.recv(mine, at_sems.at[1, q], ~owner)
                net.send(mine, mine, at_sems.at[2, q], p.core)
                yield
            for q in range(8):
                net.recv(lambda q=q: heads.at[q * 2 + 1 - p.d], at_sems.at[2, q])

        run_together(attention(), units(), gather_steps(net, block_ref, blocks, 16))
        keep_own.wait()
        net.finish()

    outs = [
        shape(ff.shape),
        shape(ff.shape),
        shape((16,) + at.shape[1:]),
        shape((16,) + block.shape),
    ]
    return comm_call(
        "weights_in",
        number,
        body,
        [ff, at, block],
        [ANY] * 3,
        outs,
        [ANY] * 4,
        [pltpu.SemaphoreType.DMA((2, 16)), pltpu.SemaphoreType.DMA((3, 8))],
        160,
    )


def grads_out(number, ff_own, ff_oth, at, parts, n_ctx):
    def body(
        own, oth, at_ref, parts_ref,
        ff_out, at_out, sum_out,
        ff_near, ff_sum, at_core, at_tp, near_core, near_x, line_in, line_out,
        ff_sems, at_sems, sems,
    ):
        place = Place(n_ctx)
        p = place
        greet(p, everyone=16, other=True)
        net = Net(p, sems)
        owner = p.b == p.t
        f = p.a * 2 + p.b
        rows, at_rows = ff_own.shape[1], at.shape[1]

        def device(g):
            return (g * p.members + p.m, p.t)

        def units():
            order = list(range(1, 16)) + [0]
            for k in order:
                there = lambda k=k: oth.at[p.g ^ k]
                net.send(there, lambda k=k: ff_near.at[p.g ^ k], ff_sems.at[0, k], p.other)
            yield
            for k in order:
                g = p.g ^ k
                net.recv(lambda: ff_near.at[g], ff_sems.at[0, k])
                add_into(ff_sum.at[g], [own.at[g], ff_near.at[g]], rows)
                if k:
                    net.send(
                        lambda g=g: ff_sum.at[g],
                        lambda: ff_out.at[p.g],
                        ff_sems.at[1, k],
                        lambda g=g: device(g),
                    )
                else:
                    keep = pltpu.make_async_copy(ff_sum.at[g], ff_out.at[g], net.sem())
                    keep.start()
                yield
            for k in range(1, 16):
                net.recv(lambda k=k: ff_out.at[p.g ^ k], ff_sems.at[1, k])
            keep.wait()

        def attention():
            for q in range(8):
                net.send(
                    lambda q=q: at_ref.at[q * 2 + 1 - p.d],
                    lambda q=q: at_core.at[q],
                    at_sems.at[0, q],
                    p.core,
                )
            yield
            for q in range(8):
                near = at_core.at[q]
                net.recv(lambda: near, at_sems.at[0, q])
                add_into(near, [near, at_ref.at[q * 2 + p.d]], at_rows)
                net.send(
                    lambda near=near: near,
                    lambda q=q: at_tp.at[q],
                    at_sems.at[1, q],
                    p.other,
                    ~owner,
                )
                yield
            keep = pltpu.make_async_copy(at_core.at[f], at_out.at[p.a], net.sem())
            for q in range(8):
                near, tp = at_core.at[q], at_tp.at[q]
                net.recv(lambda: tp, at_sems.at[1, q], owner)
                pl.when(owner)(lambda: add_into(near, [near, tp], at_rows))
                net.send(
                    lambda near=near: near,
                    lambda: at_out.at[p.a],
                    at_sems.at[2, p.a],
                    lambda q=q: p.at(a=q // 2, b=q % 2),
                    owner & (f != q),
                )
                pl.when(owner & (f == q))(lambda: keep.start())
                yield
            for s in range(4):
                net.recv(lambda s=s: at_out.at[s], at_sems.at[2, s], ~(owner & (p.a == s)))
            pl.when(owner)(lambda: keep.wait())

        run_together(
            attention(),
            reduce_steps(
                net, parts_ref, sum_out, near_core, near_x, line_in, line_out, sum_out.shape[0], 16
            ),
            units(),
        )
        net.finish()

    outs = [
        shape(ff_own.shape),
        shape((4,) + at.shape[1:]),
        shape(parts.shape[1:], F32),
    ]
    scratch = [
        pltpu.VMEM(ff_own.shape, BF),
        pltpu.VMEM(ff_own.shape, BF),
        pltpu.VMEM((8,) + at.shape[1:], BF),
        pltpu.VMEM((8,) + at.shape[1:], BF),
    ]
    scratch += reduce_scratch(parts.shape[1], parts.shape[2], 16)
    scratch += [pltpu.SemaphoreType.DMA((2, 16)), pltpu.SemaphoreType.DMA((3, 8))]
    return comm_call(
        "grads_out",
        number,
        body,
        [ff_own, ff_oth, at, parts],
        [VMEM, ANY, VMEM, VMEM],
        outs,
        [ANY, ANY, VMEM],
        scratch,
        160,
    )


def gather_latent(number, pair_block, query_block, column_blocks, n_ctx):
    def body(pair_ref, query_ref, col_ref, pair, pairs, queries, cols, col_sems, sems):
        place = Place(n_ctx)
        p = place
        greet(p, everyone=16, other=True)
        net = Net(p, sems)

        def columns():
            keep = pltpu.make_async_copy(col_ref.at[p.g], cols.at[p.g], net.sem())
            keep.start()
            for k in range(1, 16):
                net.send(
                    lambda k=k: col_ref.at[p.g ^ k],
                    lambda: cols.at[p.g],
                    col_sems.at[k],
                    lambda k=k: ((p.g ^ k) * p.members + p.m, p.t),
                )
            yield
            yield
            yield
            for k in range(1, 16):
                net.recv(lambda k=k: cols.at[p.g ^ k], col_sems.at[k])
            keep.wait()

        def latents():
            sem = net.sem()
            keep = pltpu.make_async_copy(pair_ref, pair.at[p.t], net.sem())
            keep.start()
            net.send(lambda: pair_ref, lambda: pair.at[p.t], sem, p.other)
            yield
            net.recv(lambda: pair.at[1 - p.t], sem)
            keep.wait()
            yield from gather_steps(net, pair, pairs, 16)

        run_together(latents(), gather_steps(net, query_ref, queries, 8), columns())
        net.finish()

    pair_shape = (2,) + pair_block.shape
    return comm_call(
        "gather_latent",
        number,
        body,
        [pair_block, query_block, column_blocks],
        [ANY] * 3,
        [
            shape(pair_shape),
            shape((16,) + pair_shape),
            shape((8,) + query_block.shape),
            shape(column_blocks.shape),
        ],
        [ANY] * 4,
        [pltpu.SemaphoreType.DMA((16,))],
        180,
    )[1:]


def reduce_latent(number, pairs, queries, n_ctx):
    def body(pairs_ref, queries_ref, pair_out, query_out, tp_in, *rest):
        place = Place(n_ctx)
        p = place
        greet(p, line=True, across=True, core=True, other=True)
        rest = list(rest)
        net = Net(p, rest.pop())
        rows = pair_out.shape[0]

        def latents():
            sems = [net.sem() for _ in range(16)]
            for g in range(16):
                net.send(
                    lambda g=g: pairs_ref.at[g, 1 - p.t], lambda g=g: tp_in.at[g], sems[g], p.other
                )
            yield
            for g in range(16):
                net.recv(lambda g=g: tp_in.at[g], sems[g])
                add_into(tp_in.at[g], [tp_in.at[g], pairs_ref.at[g, p.t]], rows)
            yield from reduce_steps(net, tp_in, pair_out, *rest[:4], rows, 16)

        run_together(
            latents(),
            reduce_steps(net, queries_ref, query_out, None, *rest[4:7], query_out.shape[0], 8),
        )
        net.finish()

    rows, cols = pairs.shape[2:]
    scratch = [pltpu.VMEM((16, rows, cols), BF)]
    scratch += reduce_scratch(rows, cols, 16)
    scratch += reduce_scratch(queries.shape[1], queries.shape[2], 8)
    return comm_call(
        "reduce_latent",
        number,
        body,
        [pairs, queries],
        [VMEM] * 2,
        [shape((rows, cols), F32), shape(queries.shape[1:], F32)],
        [VMEM] * 2,
        scratch,
        180,
    )


def finish_blocks(number, swaps, gain_blocks, n_ctx):
    k = len(swaps)

    def body(*refs):
        ins, gains = refs[:k], refs[k]
        outs, gains_out = refs[k + 1 : 2 * k + 1], refs[2 * k + 1]
        rest = list(refs[2 * k + 2 :])
        net_sems = rest.pop()
        tp_in = rest.pop(0)
        place = Place(n_ctx)
        greet(place, line=True, across=True, core=True, other=True)
        net = Net(place, net_sems)

        def sums():
            sem = net.sem()
            net.send(lambda: gains, lambda: tp_in, sem, place.other)
            yield
            net.recv(lambda: tp_in, sem)
            pl.loop(0, 16)(
                lambda g: add_into(tp_in.at[g], [tp_in.at[g], gains.at[g]], gains.shape[1])
            )
            yield from reduce_steps(net, tp_in, gains_out, *rest, gains_out.shape[0], 16)

        run_together(sums(), *[swap_steps(net, i, o) for i, o in zip(ins, outs)])
        net.finish()

    scratch = [pltpu.VMEM(gain_blocks.shape, BF)]
    scratch += reduce_scratch(gain_blocks.shape[1], gain_blocks.shape[2], 16)
    return comm_call(
        "finish_blocks",
        number,
        body,
        list(swaps) + [gain_blocks],
        [ANY] * k + [VMEM],
        [shape(s.shape, s.dtype) for s in swaps] + [shape(gain_blocks.shape[1:], F32)],
        [ANY] * k + [VMEM],
        scratch,
        100,
    )


def shards(
    layer_input,
    first_gain,
    query_down,
    query_gain,
    query_up,
    latent_down,
    latent_gain,
    latent_up,
    out_weight,
    second_gain,
    gate_weight,
    up_weight,
    down_weight,
    out_grad,
):
    n_ctx = lax.axis_size("ctx")
    n_tp = lax.axis_size("tp")
    members = n_ctx // 16
    c = lax.axis_index("ctx")
    t = lax.axis_index("tp")
    g = c // members
    b = lax.rem(g // 2, 2)
    d = lax.rem(g, 2)
    member = lax.rem(c, members)
    ctx_rows, dim = layer_input.shape
    rows = ctx_rows // n_tp
    shard_rows = query_down.shape[0]
    qr = query_down.shape[1]
    heads = H // 8
    units = gate_weight.shape[1] // 16
    member_lists = [[k * members + m for m in range(members)] for k in range(16)]

    def widen(blocks):
        if members == 1:
            return blocks[:, None]
        return lax.all_gather(blocks, "ctx", axis=1, axis_index_groups=member_lists)

    def narrow(blocks):
        if members == 1:
            return blocks[:, 0]
        return lax.psum_scatter(
            blocks.astype(F32), "ctx", scatter_dimension=1, axis_index_groups=member_lists
        ).astype(BF)

    widths = [first_gain.shape[0], query_gain.shape[0], latent_gain.shape[0], second_gain.shape[0]]
    starts = [0, widths[0], widths[0] + widths[1], widths[0] + widths[1] + widths[2]]
    gains = jnp.concatenate([first_gain, query_gain, latent_gain, second_gain]).astype(F32)
    gains = jnp.broadcast_to(gains[None], (8, gains.shape[0]))
    down_shard = jnp.concatenate([query_down, latent_down], axis=1)
    down_full, gains = gather_blocks("gather_entry", 1, [down_shard, gains], [16, 16], n_ctx)
    down_full = widen(down_full.reshape(16, shard_rows, -1)).reshape(dim, -1)
    gains = widen(gains.reshape(16, 8, -1)[:, 0]).reshape(n_ctx, -1)
    gain_first, gain_query, gain_latent, gain_second = [
        gains[:, s : s + w].reshape(-1) for s, w in zip(starts, widths)
    ]

    def unit_pieces(shard):
        return jnp.transpose(shard.reshape(shard_rows, 16, units), (1, 0, 2))

    wide = 640
    ff = jnp.concatenate(
        [
            unit_pieces(gate_weight),
            unit_pieces(up_weight),
            unit_pieces(down_weight.T),
            jnp.zeros((16, shard_rows, wide - 3 * units), BF),
        ],
        axis=2,
    )
    q_rows_w, l_rows_w, o_rows_w = query_up.shape[0], latent_up.shape[0], shard_rows // 2
    q_width, o_width = heads * (NOPE + ROPE), heads * VH
    at = jnp.concatenate(
        [
            jnp.pad(
                jnp.transpose(query_up.reshape(q_rows_w, 4, q_width), (1, 0, 2)),
                ((0, 0), (0, 0), (0, wide - q_width)),
            ),
            jnp.transpose(latent_up.reshape(l_rows_w, 4, wide), (1, 0, 2)),
            jnp.transpose(out_weight.reshape(4, o_width, shard_rows), (0, 2, 1)).reshape(
                4, o_rows_w, wide
            ),
        ],
        axis=1,
    )

    x = lax.dynamic_slice_in_dim(layer_input, t * rows, rows, 0).astype(F32)
    out_grad_rows = lax.dynamic_slice_in_dim(out_grad, t * rows, rows, 0).astype(F32)
    positions = c * ctx_rows + t * rows + jnp.arange(rows, dtype=jnp.int32)
    cosine, sine_table = rope_tables(positions)
    grad_ffn = (residual_scale * out_grad_rows).astype(BF)

    ff_own, ff_oth, at_all, gf_all = weights_in(2, ff, at, grad_ffn, n_ctx)
    gf_all = gf_all.reshape(-1, dim)
    w_own = widen(ff_own).reshape(dim, wide)
    w_oth = widen(ff_oth).reshape(dim, wide)

    def third(k):
        return jnp.concatenate(
            [w[:, k * units : (k + 1) * units] for w in (w_own, w_oth)], axis=1
        )

    w_gate, w_up, w_down_t = third(0), third(1), third(2)
    at_all = widen(at_all).reshape(n_ctx, -1, wide)
    q_up = at_all[:, :q_rows_w, :q_width].reshape(qr, q_width)
    l_up = at_all[:, q_rows_w : q_rows_w + l_rows_w].reshape(KVR, wide)
    w_out_t = at_all[:, q_rows_w + l_rows_w :].reshape(dim, o_width)

    normed = rms_norm(x, gain_first).astype(BF)
    both = matmul(normed, down_full)
    query_latent, compressed = both[:, :qr], both[:, qr:]
    query_normed = rms_norm(query_latent, gain_query).astype(BF)
    latent = rms_norm(compressed[:, :KVR], gain_latent).astype(BF)
    key_rope = rotate(compressed[:, KVR:], cosine, sine_table).astype(BF)
    pair_block = jnp.concatenate(
        [latent, key_rope, jnp.zeros((rows, 384 - KVR - ROPE), BF)], axis=1
    )
    normed_columns = jnp.transpose(
        normed.reshape(rows, 16, dim // 16), (1, 0, 2)
    )
    pairs, qn_all, token_columns = gather_latent(
        3, pair_block, query_normed, normed_columns, n_ctx
    )
    lat_rope = widen(pairs).reshape(-1, 384)
    latent_all, rope_all = lat_rope[:, :KVR], lat_rope[:, KVR : KVR + ROPE]
    qn_all = qn_all.reshape(-1, qr)
    q_rows = qn_all.shape[0]
    keys = latent_all.shape[0]

    q_positions = (
        ((jnp.arange(8, dtype=jnp.int32)[:, None] * 2 + d) * members + member) * ctx_rows
        + t * rows
        + jnp.arange(rows, dtype=jnp.int32)[None, :]
    ).reshape(-1)
    q_cos, q_sin = rope_tables(q_positions)
    queries_raw = matmul(qn_all, q_up).reshape(q_rows, heads, NOPE + ROPE)
    queries = jnp.concatenate(
        [
            queries_raw[..., :NOPE],
            rotate(queries_raw[..., NOPE:], q_cos[:, None, :], q_sin[:, None, :]),
        ],
        axis=-1,
    ).astype(BF)
    expanded = matmul(latent_all, l_up).astype(BF)
    allowed = jnp.arange(keys, dtype=jnp.int32)[None, :] <= q_positions[:, None]

    def head_keys(h):
        part = expanded[:, h * (NOPE + VH) : (h + 1) * (NOPE + VH)]
        return jnp.concatenate([part[:, :NOPE], rope_all], axis=1), part[:, NOPE:]

    outs, logs = [], []
    for h in range(heads):
        k, v = head_keys(h)
        scores = jnp.where(allowed, matmul_nt(queries[:, h], k) * score_scale, -1e30)
        top = jnp.max(scores, axis=-1, keepdims=True)
        weights = jnp.exp(scores - top)
        total = jnp.sum(weights, axis=-1, keepdims=True)
        outs.append(matmul(weights.astype(BF), v) / total)
        logs.append(top + jnp.log(total))
    attended_wide = jnp.concatenate(outs, axis=1)
    attended = attended_wide.astype(BF)

    (branch,) = reduce_blocks(
        "reduce_branch", 4, [matmul_nt(attended, w_out_t).astype(BF)], [8], n_ctx
    )
    middle = x + residual_scale * branch
    normed_second = rms_norm(middle, gain_second).astype(BF)
    (ns_all,) = gather_blocks("gather_second", 5, [normed_second], [16], n_ctx)
    gate_values = matmul(ns_all, w_gate)
    up_values = matmul(ns_all, w_up)
    sigmoid_gate = jax.nn.sigmoid(gate_values)
    hidden = (gate_values * sigmoid_gate * up_values).astype(BF)
    ffn_part = matmul_nt(hidden, w_down_t).astype(BF)

    grad_hidden = matmul(gf_all, w_down_t)
    grad_gate = (
        grad_hidden * up_values * sigmoid_gate * (1.0 + gate_values * (1.0 - sigmoid_gate))
    ).astype(BF)
    grad_up = (grad_hidden * gate_values * sigmoid_gate).astype(BF)
    (grad_second,) = reduce_blocks(
        "reduce_second",
        6,
        [(matmul_nt(grad_gate, w_gate) + matmul_nt(grad_up, w_up)).astype(BF)],
        [16],
        n_ctx,
    )

    ff_grads = [
        matmul_tn(ns_all, grad_gate).astype(BF),
        matmul_tn(ns_all, grad_up).astype(BF),
        matmul_tn(gf_all, hidden).astype(BF),
        jnp.zeros((dim, 2 * (wide - 3 * units)), BF),
    ]

    def half_grads(k):
        whole = jnp.concatenate(
            [p[:, : p.shape[1] // 2] if k == 0 else p[:, p.shape[1] // 2 :] for p in ff_grads],
            axis=1,
        )
        return narrow(whole.reshape(16, members, shard_rows, wide))

    grads_own, grads_oth = half_grads(0), half_grads(1)

    grad_middle_part, second_gain_part = norm_back(middle, gain_second, grad_second)
    grad_middle = out_grad_rows + grad_middle_part

    grad_branch = (residual_scale * grad_middle).astype(BF)
    (gb_all,) = gather_blocks("gather_branch", 7, [grad_branch], [8], n_ctx)
    out_part = matmul_tn(gb_all, attended).astype(BF)
    grad_attended = matmul(gb_all, w_out_t).astype(BF)

    grad_q_rows, grad_kv, grad_rope = [], [], jnp.zeros((keys, ROPE), F32)
    for h in range(heads):
        k, v = head_keys(h)
        q, ga = queries[:, h], grad_attended[:, h * VH : (h + 1) * VH]
        row_inner = jnp.sum(
            ga.astype(F32) * attended_wide[:, h * VH : (h + 1) * VH], axis=-1, keepdims=True
        )
        scores = jnp.where(allowed, matmul_nt(q, k) * score_scale, -1e30)
        probs = jnp.exp(scores - logs[h])
        grad_probs = matmul_nt(ga, v)
        grad_scores = (probs * (grad_probs - row_inner)).astype(BF)
        gq = matmul(grad_scores, k) * score_scale
        grad_q_rows += [gq[:, :NOPE], rotate(gq[:, NOPE:], q_cos, -q_sin)]
        gk = matmul_tn(grad_scores, q) * score_scale
        grad_kv += [gk[:, :NOPE], matmul_tn(probs.astype(BF), ga)]
        grad_rope = grad_rope + gk[:, NOPE:]
    grad_q_rows = jnp.concatenate(grad_q_rows, axis=1).astype(BF)
    grad_expanded = jnp.concatenate(grad_kv, axis=1).astype(BF)
    grad_lat_rope = jnp.concatenate(
        [
            matmul_nt(grad_expanded, l_up),
            grad_rope,
            jnp.zeros((keys, 384 - KVR - ROPE), F32),
        ],
        axis=1,
    ).astype(BF)
    l_up_part = matmul_tn(latent_all, grad_expanded).astype(BF)
    q_up_part = matmul_tn(qn_all, grad_q_rows).astype(BF)
    gqn_part = matmul_nt(grad_q_rows, q_up).astype(BF)

    own_lat_rope, grad_query_normed = reduce_latent(
        8,
        narrow(grad_lat_rope.reshape(16, members, 2, rows, 384)),
        gqn_part.reshape(8, rows, qr),
        n_ctx,
    )
    grad_query_latent, query_gain_part = norm_back(query_latent, gain_query, grad_query_normed)
    grad_latent_rows, latent_gain_part = norm_back(
        compressed[:, :KVR], gain_latent, own_lat_rope[:, :KVR]
    )
    grad_both = jnp.concatenate(
        [
            grad_query_latent,
            grad_latent_rows,
            rotate(own_lat_rope[:, KVR : KVR + ROPE], cosine, -sine_table),
        ],
        axis=1,
    ).astype(BF)
    if members == 1:
        (both_all,) = gather_blocks("gather_both", 9, [grad_both], [16], n_ctx)
        down_part = matmul_tn(token_columns.reshape(16 * rows, shard_rows), both_all).astype(BF)
    else:
        down_part = lax.psum_scatter(
            matmul_tn(normed, grad_both).astype(BF), "ctx", scatter_dimension=0, tiled=True
        )
    grad_normed = matmul_nt(grad_both, down_full)
    grad_input_part, first_gain_part = norm_back(x, gain_first, grad_normed)
    input_half = (grad_middle + grad_input_part).astype(BF)

    at_part = jnp.concatenate(
        [
            jnp.pad(q_up_part, ((0, 0), (0, wide - q_width))).reshape(n_ctx, q_rows_w, wide),
            l_up_part.reshape(n_ctx, l_rows_w, wide),
            out_part.reshape(n_ctx, o_rows_w, wide),
        ],
        axis=1,
    )
    at_part = narrow(at_part.reshape(16, members, -1, wide))
    ff_sums, at_sums, ffn_sum = grads_out(
        10, grads_own, grads_oth, at_part, ffn_part.reshape(16, rows, dim), n_ctx
    )
    out_half = (middle + residual_scale * ffn_sum).astype(BF)

    gain_parts = jnp.concatenate(
        [
            p.reshape(n_ctx, -1)
            for p in (first_gain_part, query_gain_part, latent_gain_part, second_gain_part)
        ],
        axis=1,
    )
    gain_parts = narrow(gain_parts.reshape(16, members, -1)).astype(BF)
    gain_blocks = jnp.pad(gain_parts[:, None], ((0, 0), (0, 15), (0, 0)))
    out_other, input_other, down_other, gain_sums = finish_blocks(
        11, [out_half, input_half, down_part], gain_blocks, n_ctx
    )

    def in_order(mine, other):
        return jnp.where(
            t == 0, jnp.concatenate([mine, other]), jnp.concatenate([other, mine])
        )

    layer_output = in_order(out_half, out_other)
    input_grad = in_order(input_half, input_other).astype(F32)
    down_grads = down_part.astype(F32) + down_other.astype(F32)
    gain_grads = gain_sums[0]
    first_gain_grad, query_gain_grad, latent_gain_grad, second_gain_grad = [
        gain_grads[s : s + w] for s, w in zip(starts, widths)
    ]

    def unit_grads(k):
        part = ff_sums[:, :, k * units : (k + 1) * units]
        return jnp.transpose(part, (1, 0, 2)).reshape(shard_rows, 16 * units).astype(F32)

    query_up_grad = jnp.transpose(at_sums[:, :q_rows_w, :q_width], (1, 0, 2)).reshape(
        q_rows_w, 4 * q_width
    )
    latent_up_grad = jnp.transpose(at_sums[:, q_rows_w : q_rows_w + l_rows_w], (1, 0, 2)).reshape(
        l_rows_w, 4 * wide
    )
    out_weight_grad = jnp.transpose(
        at_sums[:, q_rows_w + l_rows_w :].reshape(4, shard_rows, o_width), (0, 2, 1)
    ).reshape(4 * o_width, shard_rows)
    return (
        layer_output,
        input_grad,
        first_gain_grad,
        down_grads[:, :qr],
        query_gain_grad,
        query_up_grad.astype(F32),
        down_grads[:, qr:],
        latent_gain_grad,
        latent_up_grad.astype(F32),
        out_weight_grad.astype(F32),
        second_gain_grad,
        unit_grads(0),
        unit_grads(1),
        unit_grads(2).T,
    )


def solution(mesh):
    return jax.shard_map(
        shards,
        mesh=mesh,
        in_specs=(
            P("ctx", None),
            P("ctx"),
            P("ctx", None),
            P("ctx"),
            P("ctx", "tp"),
            P("ctx", None),
            P("ctx"),
            P("ctx", "tp"),
            P("tp", "ctx"),
            P("ctx"),
            P("ctx", "tp"),
            P("ctx", "tp"),
            P("tp", "ctx"),
            P("ctx", None),
        ),
        out_specs=(
            P("ctx", None),
            P("ctx", None),
            P("ctx"),
            P("ctx", None),
            P("ctx"),
            P("ctx", "tp"),
            P("ctx", None),
            P("ctx"),
            P("ctx", "tp"),
            P("tp", "ctx"),
            P("ctx"),
            P("ctx", "tp"),
            P("ctx", "tp"),
            P("tp", "ctx"),
        ),
        check_vma=False,
    )
```

```python
import math

import jax
import jax.numpy as jnp
from jax import lax
from jax.experimental import pallas as pl
from jax.experimental.pallas import tpu as pltpu
from jax.sharding import PartitionSpec as P

BF = jnp.bfloat16
F32 = jnp.float32

H = 40
KVR = 256
NOPE = 64
ROPE = 32
VH = 64

eps_norm = 1e-06
residual_scale = 1.4 / math.sqrt(62.0)
score_scale = (NOPE + ROPE) ** (-0.5)
rope_base = 10000.0


def matmul(left_side, right_side):
    return jnp.dot(left_side, right_side, preferred_element_type=F32)


def matmul_nt(left_side, right_side):
    return lax.dot_general(
        left_side, right_side, (((1,), (1,)), ((), ())), preferred_element_type=F32
    )


def matmul_tn(left_side, right_side):
    return lax.dot_general(
        left_side, right_side, (((0,), (0,)), ((), ())), preferred_element_type=F32
    )


def rms_norm(values, scale_gain):
    factor = lax.rsqrt(jnp.mean(values * values, axis=-1, keepdims=True) + eps_norm)
    return values * factor * scale_gain


def norm_back(values, scale_gain, upstream):
    factor = lax.rsqrt(jnp.mean(values * values, axis=-1, keepdims=True) + eps_norm)
    scaled = upstream * scale_gain
    inner_sum = jnp.mean(scaled * values, axis=-1, keepdims=True)
    grad_values = factor * scaled - values * factor * factor * factor * inner_sum
    grad_gain = jnp.sum(upstream * values * factor, axis=0)
    return (grad_values, grad_gain)


def rotate(values, cosine, sine_table):
    half_width = values.shape[-1] // 2
    first_half = values[..., :half_width]
    second_half = values[..., half_width:]
    return jnp.concatenate(
        [
            first_half * cosine - second_half * sine_table,
            second_half * cosine + first_half * sine_table,
        ],
        axis=-1,
    )


def rope_tables(positions):
    frequency = rope_base ** (-jnp.arange(ROPE // 2, dtype=F32) / (ROPE // 2))
    angles = positions.astype(F32)[:, None] * frequency[None, :]
    return (jnp.cos(angles), jnp.sin(angles))


MESH = pl.DeviceIdType.MESH
OFFSETS = (0, -1, 1, -2, 2, -3, 3)


class Place:
    def __init__(self, n_ctx):
        c = lax.axis_index("ctx")
        self.members = n_ctx // 16
        self.c = c
        self.t = lax.axis_index("tp")
        self.m = lax.rem(c, self.members)
        g = c // self.members
        self.g = g
        self.a, self.b, self.d = g // 4, lax.rem(g // 2, 2), lax.rem(g, 2)

    def at(self, a=None, b=None, d=None):
        a = self.a if a is None else a
        b = self.b if b is None else b
        d = self.d if d is None else d
        return (((a * 2 + b) * 2 + d) * self.members + self.m, self.t)

    def up(self):
        return self.at(a=self.a + 1)

    def down(self):
        return self.at(a=self.a - 1)

    def across(self):
        return self.at(b=1 - self.b)

    def core(self):
        return self.at(d=1 - self.d)

    def other(self):
        return (self.c, 1 - self.t)

    def valid(self, o):
        return None if o == 0 else (self.a + o >= 0 if o < 0 else self.a + o <= 3)


def both_of(p, q):
    if p is None:
        return q
    return p if q is None else p & q


def when(p, body):
    if p is None:
        body()
    else:
        pl.when(p)(body)


class Net:
    def __init__(self, place, sems):
        self.place, self.sems, self.count, self.pending = place, sems, 0, []

    def sem(self):
        self.count += 1
        return self.sems.at[self.count - 1]

    def send(self, src, dst, recv, to, cond=None):
        mine = self.sem()

        def copy():
            return pltpu.make_async_remote_copy(
                src(), dst(), mine, recv, device_id=to(), device_id_type=MESH
            )

        when(cond, lambda: copy().start())
        self.pending.append((cond, lambda: copy().wait_send()))

    def recv(self, dst, sem, cond=None):
        def wait():
            ref = dst()
            pltpu.make_async_remote_copy(
                ref, ref, sem, sem, device_id=self.place.other(), device_id_type=MESH
            ).wait_recv()

        when(cond, wait)

    def finish(self):
        for cond, wait in self.pending:
            when(cond, wait)


def greet(place, line=False, across=False, core=False, other=False, everyone=0):
    barrier = pltpu.get_barrier_semaphore()

    def tell(device):
        pl.semaphore_signal(barrier, inc=1, device_id=device, device_id_type=MESH)

    count = 0
    if everyone:
        for k in range(1, everyone):
            tell((lax.rem(place.c + k * place.members, everyone * place.members), place.t))
        count = count + everyone - 1
    else:
        if line:
            pl.when(place.a < 3)(lambda: tell(place.up()))
            pl.when(place.a > 0)(lambda: tell(place.down()))
            count = count + (place.a < 3).astype(jnp.int32) + (place.a > 0).astype(jnp.int32)
        if across:
            tell(place.across())
            count = count + 1
        if core:
            tell(place.core())
            count = count + 1
    if other:
        tell(place.other())
        count = count + 1
    pl.semaphore_wait(barrier, count)


def gather_steps(net, src, out, width):
    p = net.place
    cores = width == 16

    def slot(o, b, d):
        return out.at[((p.a + o) * 2 + b) * 2 + d] if cores else out.at[(p.a + o) * 2 + d]

    z_sem = {o: net.sem() for o in OFFSETS if o}
    x_sem = {o: net.sem() for o in OFFSETS} if cores else {}
    c_sem = {(s, o): net.sem() for s in ((0, 1) if cores else (0,)) for o in OFFSETS}
    own_sem = net.sem()
    keep = pltpu.make_async_copy(src, slot(0, p.b, p.d), own_sem)
    keep.start()

    def forward(o):
        ok = p.valid(o)
        here = lambda: slot(o, p.b, p.d)
        origin = (lambda: src) if o == 0 else here
        if o <= 0 and o > -3:
            net.send(origin, here, z_sem[o - 1], p.up, both_of(ok, p.a < 3))
        if o >= 0 and o < 3:
            net.send(origin, here, z_sem[o + 1], p.down, both_of(ok, p.a > 0))
        if cores:
            net.send(origin, here, x_sem[o], p.across, ok)
        net.send(origin, here, c_sem[0, o], p.core, ok)

    def from_line(o):
        net.recv(lambda: slot(o, p.b, p.d), z_sem[o], p.valid(o))
        forward(o)

    def from_across(o):
        if cores:
            there = lambda: slot(o, 1 - p.b, p.d)
            net.recv(there, x_sem[o], p.valid(o))
            net.send(there, there, c_sem[1, o], p.core, p.valid(o))

    forward(0)
    yield
    for near in (1, 2, 3):
        from_line(-near)
        from_line(near)
        yield
        if near == 1:
            from_across(0)
        else:
            from_across(1 - near)
            from_across(near - 1)
        yield
    from_across(-3)
    from_across(3)
    yield
    for o in OFFSETS:
        net.recv(lambda: slot(o, p.b, 1 - p.d), c_sem[0, o], p.valid(o))
        if cores:
            net.recv(lambda: slot(o, 1 - p.b, 1 - p.d), c_sem[1, o], p.valid(o))
    keep.wait()


def add_into(out, terms, rows):
    step = 16 if rows % 16 == 0 else rows

    def body(i):
        part = pl.ds(pl.multiple_of(i * step, step), step)
        total = terms[0][part].astype(F32)
        for term in terms[1:]:
            total = total + term[part].astype(F32)
        out[part] = total.astype(out.dtype)

    pl.loop(0, rows // step)(body)


def reduce_steps(net, parts, out, near_core, near_x, line_in, line_out, rows, width):
    p = net.place
    cores = width == 16
    order = (-3, 3, -2, 2, -1, 1, 0)
    if cores:
        c_sem = {(b, o): net.sem() for b in (0, 1) for o in order}
        for o in order:
            for side in (1, 0):
                def src(o=o, side=side):
                    b = 1 - p.b if side else p.b
                    return parts.at[((p.a + o) * 2 + b) * 2 + 1 - p.d]

                def dst(o=o, side=side):
                    b = 1 - p.b if side else p.b
                    return near_core.at[(p.a + o) * 2 + b]

                net.send(src, dst, c_sem[side, o], p.core, p.valid(o))
        yield
    x_sem = {o: net.sem() for o in order}
    up_sem = {o: net.sem() for o in (0, 1, 2)}
    down_sem = {o: net.sem() for o in (0, 1, 2)}

    pair = p.b if cores else p.d

    def mine(o, b):
        g = (p.a + o) * 2 + b
        return near_core.at[g] if cores else parts.at[g]

    for o in order:
        if cores:
            def join(o=o):
                g = (p.a + o) * 2 + 1 - p.b
                add_into(near_core.at[g], [near_core.at[g], parts.at[g * 2 + p.d]], rows)

            net.recv(lambda: near_core.at[(p.a + o) * 2 + 1 - p.b], c_sem[1, o], p.valid(o))
            when(p.valid(o), join)
        net.send(
            lambda o=o: mine(o, 1 - pair),
            lambda o=o: near_x.at[p.a + o],
            x_sem[o],
            p.across if cores else p.core,
            p.valid(o),
        )
    yield
    for o in order:
        ok = p.valid(o)
        if cores:
            net.recv(lambda: near_core.at[(p.a + o) * 2 + p.b], c_sem[0, o], ok)

        def terms(o=o):
            g = (p.a + o) * 2 + pair
            own = [near_core.at[g], parts.at[g * 2 + p.d]] if cores else [parts.at[g]]
            return own + [near_x.at[p.a + o]]

        net.recv(lambda: near_x.at[p.a + o], x_sem[o], ok)
        if o == 0:
            below, above = line_in.at[0, 0], line_in.at[1, 0]
            net.recv(lambda: below, up_sem[0], p.a > 0)
            net.recv(lambda: above, down_sem[0], p.a < 3)
            inner = (p.a > 0) & (p.a < 3)
            pl.when(inner)(lambda: add_into(out, terms() + [below, above], rows))
            pl.when(p.a == 0)(lambda: add_into(out, terms() + [above], rows))
            pl.when(p.a == 3)(lambda: add_into(out, terms() + [below], rows))
            continue
        far = abs(o)
        way = 0 if o > 0 else 1
        stage = line_out.at[way, far - 1]
        sems = up_sem if o > 0 else down_sem
        first = p.a == 0 if o > 0 else p.a == 3
        if far < 3:
            came = line_in.at[way, far]
            later = ok & ~first
            net.recv(lambda: came, sems[far], later)
            pl.when(later)(lambda: add_into(stage, terms() + [came], rows))
            pl.when(ok & first)(lambda: add_into(stage, terms(), rows))
        else:
            pl.when(ok)(lambda: add_into(stage, terms(), rows))
        net.send(
            lambda stage=stage: stage,
            lambda far=far, way=way: line_in.at[way, far - 1],
            sems[far - 1],
            p.up if o > 0 else p.down,
            ok,
        )
        yield


def swap_steps(net, src, dst):
    sem = net.sem()
    net.send(lambda: src, lambda: dst, sem, net.place.other)
    yield
    net.recv(lambda: dst, sem)


def run_together(*tasks):
    tasks = list(tasks)
    while tasks:
        for task in list(tasks):
            try:
                next(task)
            except StopIteration:
                tasks.remove(task)


ANY = pl.BlockSpec(memory_space=pl.ANY)
VMEM = pl.BlockSpec(memory_space=pltpu.VMEM)


def comm_call(name, number, body, ins, in_specs, outs, out_specs, scratch, sems):
    return pl.pallas_call(
        body,
        out_shape=outs,
        in_specs=in_specs,
        out_specs=out_specs,
        scratch_shapes=list(scratch) + [pltpu.SemaphoreType.DMA((sems,))],
        compiler_params=pltpu.CompilerParams(
            collective_id=number, has_side_effects=True, vmem_limit_bytes=56 << 20
        ),
        name=name,
    )(*ins)


def shape(dims, dtype=BF):
    return jax.ShapeDtypeStruct(tuple(dims), dtype)


def reduce_scratch(rows, cols, width):
    near_core = [pltpu.VMEM((8, rows, cols), BF)] if width == 16 else []
    return near_core + [
        pltpu.VMEM((4, rows, cols), BF),
        pltpu.VMEM((2, 3, rows, cols), BF),
        pltpu.VMEM((2, 3, rows, cols), BF),
    ]


def gather_blocks(name, number, items, widths, n_ctx):
    k = len(items)

    def body(*refs):
        ins, outs, sems = refs[:k], refs[k : 2 * k], refs[-1]
        place = Place(n_ctx)
        greet(place, line=True, across=16 in widths, core=True)
        net = Net(place, sems)
        run_together(*[gather_steps(net, i, o, w) for i, o, w in zip(ins, outs, widths)])
        net.finish()

    outs = comm_call(
        name,
        number,
        body,
        items,
        [ANY] * k,
        [shape((w,) + i.shape, i.dtype) for i, w in zip(items, widths)],
        [ANY] * k,
        [],
        64 * k,
    )
    return [o.reshape((-1,) + o.shape[2:]) for o in outs]


def reduce_blocks(name, number, items, widths, n_ctx):
    k = len(items)
    blocks = [i.reshape(w, i.shape[0] // w, i.shape[1]) for i, w in zip(items, widths)]

    def body(*refs):
        ins, outs, rest = refs[:k], refs[k : 2 * k], list(refs[2 * k :])
        place = Place(n_ctx)
        greet(place, line=True, across=16 in widths, core=True)
        net = Net(place, rest.pop())
        tasks = []
        for i, o, w in zip(ins, outs, widths):
            near_core = rest.pop(0) if w == 16 else None
            near_x, line_in, line_out = rest.pop(0), rest.pop(0), rest.pop(0)
            tasks.append(
                reduce_steps(net, i, o, near_core, near_x, line_in, line_out, o.shape[0], w)
            )
        run_together(*tasks)
        net.finish()

    scratch = []
    for i, w in zip(blocks, widths):
        scratch += reduce_scratch(i.shape[1], i.shape[2], w)
    return comm_call(
        name,
        number,
        body,
        blocks,
        [VMEM] * k,
        [shape(i.shape[1:], F32) for i in blocks],
        [VMEM] * k,
        scratch,
        64 * k,
    )


def weights_in(number, down, gains, at, n_ctx):
    def body(down_ref, gains_ref, at_ref, downs, gain_blocks, heads, at_sems, tp_sems, sems):
        p = Place(n_ctx)
        greet(p, everyone=16, other=True)
        net = Net(p, sems)
        owner = p.d == p.t
        f = p.a * 2 + p.d

        def attention():
            keep = pltpu.make_async_copy(at_ref.at[p.a], heads.at[p.g], net.sem())
            pl.when(owner)(lambda: keep.start())
            for s in range(4):
                net.send(
                    lambda s=s: at_ref.at[s],
                    lambda: heads.at[p.g],
                    at_sems.at[0, f],
                    lambda s=s: p.at(a=s, d=p.t),
                    ~(owner & (p.a == s)),
                )
            pl.when(owner)(lambda: keep.wait())
            yield
            yield
            for q in range(8):
                mine = lambda q=q: heads.at[(q // 2 * 2 + p.b) * 2 + q % 2]
                net.recv(mine, at_sems.at[0, q], owner & (f != q))
                net.send(mine, mine, at_sems.at[1, q], p.across, owner)
                net.send(mine, mine, tp_sems.at[0, q], p.other, owner)
                if q % 2:
                    yield
            for q in range(8):
                theirs = lambda q=q: heads.at[(q // 2 * 2 + 1 - p.b) * 2 + q % 2]
                net.recv(theirs, at_sems.at[1, q], owner)
                net.send(theirs, theirs, tp_sems.at[1, q], p.other, owner)
                if q % 2:
                    yield
            for q in range(8):
                for side in (0, 1):
                    b = 1 - p.b if side else p.b
                    net.recv(
                        lambda: heads.at[(q // 2 * 2 + b) * 2 + q % 2], tp_sems.at[side, q], ~owner
                    )

        run_together(
            gather_steps(net, gains_ref, gain_blocks, 16),
            gather_steps(net, down_ref, downs, 16),
            attention(),
        )
        net.finish()

    outs = [
        shape((16,) + down.shape),
        shape((16,) + gains.shape, gains.dtype),
        shape((16,) + at.shape[1:]),
    ]
    return comm_call(
        "weights_in",
        number,
        body,
        [down, gains, at],
        [ANY] * 3,
        outs,
        [ANY] * 3,
        [pltpu.SemaphoreType.DMA((2, 8)), pltpu.SemaphoreType.DMA((2, 8))],
        180,
    )


def head_grads_steps(net, at_ref, at_out, at_x, at_tp, x_sems, rows):
    p = net.place
    owner = p.d == p.t
    f = p.a * 2 + p.d
    for q in range(8):
        net.send(
            lambda q=q: at_ref.at[(q // 2 * 2 + 1 - p.b) * 2 + q % 2],
            lambda q=q: at_x.at[q],
            x_sems.at[0, q],
            p.across,
        )
    yield
    for q in range(8):
        near = at_x.at[q]
        net.recv(lambda: near, x_sems.at[0, q])
        add_into(near, [near, at_ref.at[(q // 2 * 2 + p.b) * 2 + q % 2]], rows)
        net.send(
            lambda near=near: near, lambda q=q: at_tp.at[q], x_sems.at[1, q], p.other, ~owner
        )
        yield
    keep = pltpu.make_async_copy(at_x.at[f], at_out.at[p.a], net.sem())
    for q in range(8):
        near, tp = at_x.at[q], at_tp.at[q]
        net.recv(lambda: tp, x_sems.at[1, q], owner)
        pl.when(owner)(lambda: add_into(near, [near, tp], rows))
        net.send(
            lambda near=near: near,
            lambda: at_out.at[p.a],
            x_sems.at[2, p.a],
            lambda q=q: p.at(a=q // 2, d=q % 2),
            owner & (f != q),
        )
        pl.when(owner & (f == q))(lambda: keep.start())
        yield
    for s in range(4):
        net.recv(lambda s=s: at_out.at[s], x_sems.at[2, s], ~(owner & (p.a == s)))
    pl.when(owner)(lambda: keep.wait())


def local_call(name, body, grid, ins, in_specs, outs, out_specs, members):
    g = (lax.axis_index("ctx") // members).astype(jnp.int32).reshape(1)
    return pl.pallas_call(
        body,
        out_shape=outs,
        grid_spec=pltpu.PrefetchScalarGridSpec(
            num_scalar_prefetch=1, grid=grid, in_specs=in_specs, out_specs=out_specs
        ),
        compiler_params=pltpu.CompilerParams(vmem_limit_bytes=56 << 20),
        name=name,
    )(g, *ins)


def pack(gate, up, down, wide, members):
    rows = gate.shape[0]
    units = gate.shape[1] // 16

    def body(g_ref, gate_ref, up_ref, down_ref, *rest):
        outs, hold, down_t = rest[:4], rest[4], rest[5]
        down_t[...] = down_ref[...].astype(F32).T.astype(BF)
        for n in range(16):
            cut = slice(n * units, (n + 1) * units)
            for k, part in enumerate((gate_ref, up_ref, down_t)):
                hold[n, :, k * units : (k + 1) * units] = part[:, cut]
            hold[n, :, 3 * units :] = jnp.zeros((rows, wide - 3 * units), BF)
        for i in range(16):
            outs[i // 4][i % 4] = hold[g_ref[0] ^ i]

    def whole(*dims):
        return pl.BlockSpec(dims, lambda i, g: (0,) * len(dims))

    g = (lax.axis_index("ctx") // members).astype(jnp.int32).reshape(1)
    return pl.pallas_call(
        body,
        out_shape=[shape((4, rows, wide))] * 4,
        grid_spec=pltpu.PrefetchScalarGridSpec(
            num_scalar_prefetch=1,
            grid=(1,),
            in_specs=[whole(*gate.shape), whole(*up.shape), whole(*down.shape)],
            out_specs=[whole(4, rows, wide)] * 4,
            scratch_shapes=[
                pltpu.VMEM((16, rows, wide), BF),
                pltpu.VMEM((rows, 16 * units), BF),
            ],
        ),
        compiler_params=pltpu.CompilerParams(vmem_limit_bytes=56 << 20),
        name="pack",
    )(g, gate, up, down)


def arrange(own, oth, units, members):
    def body(g_ref, own_ref, oth_ref, *outs):
        for k, out in enumerate(outs):
            cut = slice(k * units, (k + 1) * units)
            out[0, :, :units] = own_ref[0, :, cut]
            out[0, :, units:] = oth_ref[0, :, cut]

    rows, cols = own.shape[1:]
    spec = pl.BlockSpec((1, rows, cols), lambda i, g: (i, 0, 0))
    return local_call(
        "arrange",
        body,
        (16,),
        [own, oth],
        [spec] * 2,
        [shape((16, rows, 2 * units))] * 3,
        [pl.BlockSpec((1, rows, 2 * units), lambda i, g: (g[0] ^ i, 0, 0))] * 3,
        members,
    )


def collect(parts, wide, members):
    rows, both = parts[0].shape[1:]
    units = both // 2

    def body(g_ref, *refs):
        for half, out in enumerate(refs[3:]):
            for k, part in enumerate(refs[:3]):
                out[0, :, k * units : (k + 1) * units] = part[
                    0, :, half * units : (half + 1) * units
                ]
            out[0, :, 3 * units :] = jnp.zeros((rows, wide - 3 * units), BF)

    return local_call(
        "collect",
        body,
        (16,),
        parts,
        [pl.BlockSpec((1, rows, both), lambda i, g: (g[0] ^ i, 0, 0))] * 3,
        [shape((16, rows, wide))] * 2,
        [pl.BlockSpec((1, rows, wide), lambda i, g: (i, 0, 0))] * 2,
        members,
    )


def spread(blocks, units, members):
    rows = blocks.shape[1]

    def body(g_ref, src, gate, up, down):
        for k in range(16):
            part = src[g_ref[0] ^ k].astype(F32)
            cut = slice(k * units, (k + 1) * units)
            gate[:, cut] = part[:, :units]
            up[:, cut] = part[:, units : 2 * units]
            down[cut, :] = part[:, 2 * units : 3 * units].T

    return local_call(
        "spread",
        body,
        (1,),
        [blocks],
        [pl.BlockSpec(blocks.shape, lambda i, g: (0, 0, 0))],
        [
            shape((rows, 16 * units), F32),
            shape((rows, 16 * units), F32),
            shape((16 * units, rows), F32),
        ],
        [
            pl.BlockSpec((rows, 16 * units), lambda i, g: (0, 0)),
            pl.BlockSpec((rows, 16 * units), lambda i, g: (0, 0)),
            pl.BlockSpec((16 * units, rows), lambda i, g: (0, 0)),
        ],
        members,
    )


def gather_latent(number, pair_block, query_block, column_blocks, n_ctx):
    def body(pair_ref, query_ref, col_ref, pair, pairs, queries, cols, col_sems, sems):
        place = Place(n_ctx)
        p = place
        greet(p, everyone=16, other=True)
        net = Net(p, sems)

        def columns():
            keep = pltpu.make_async_copy(col_ref.at[p.g], cols.at[p.g], net.sem())
            keep.start()
            for k in range(1, 16):
                net.send(
                    lambda k=k: col_ref.at[p.g ^ k],
                    lambda: cols.at[p.g],
                    col_sems.at[k],
                    lambda k=k: ((p.g ^ k) * p.members + p.m, p.t),
                )
            yield
            yield
            yield
            for k in range(1, 16):
                net.recv(lambda k=k: cols.at[p.g ^ k], col_sems.at[k])
            keep.wait()

        def latents():
            sem = net.sem()
            keep = pltpu.make_async_copy(pair_ref, pair.at[p.t], net.sem())
            keep.start()
            net.send(lambda: pair_ref, lambda: pair.at[p.t], sem, p.other)
            yield
            net.recv(lambda: pair.at[1 - p.t], sem)
            keep.wait()
            yield from gather_steps(net, pair, pairs, 16)

        run_together(latents(), gather_steps(net, query_ref, queries, 8), columns())
        net.finish()

    pair_shape = (2,) + pair_block.shape
    return comm_call(
        "gather_latent",
        number,
        body,
        [pair_block, query_block, column_blocks],
        [ANY] * 3,
        [
            shape(pair_shape),
            shape((16,) + pair_shape),
            shape((8,) + query_block.shape),
            shape(column_blocks.shape),
        ],
        [ANY] * 4,
        [pltpu.SemaphoreType.DMA((16,))],
        180,
    )[1:]


def reduce_latent(number, pairs, queries, at, n_ctx):
    def body(
        pairs_ref, queries_ref, at_ref, pair_out, query_out, at_out,
        at_x, at_tp, x_sems, tp_in, *rest,
    ):
        place = Place(n_ctx)
        p = place
        greet(p, everyone=16, other=True)
        rest = list(rest)
        net = Net(p, rest.pop())
        rows = pair_out.shape[0]

        def latents():
            sems = [net.sem() for _ in range(16)]
            for g in range(16):
                net.send(
                    lambda g=g: pairs_ref.at[g, 1 - p.t], lambda g=g: tp_in.at[g], sems[g], p.other
                )
            yield
            for g in range(16):
                net.recv(lambda g=g: tp_in.at[g], sems[g])
                add_into(tp_in.at[g], [tp_in.at[g], pairs_ref.at[g, p.t]], rows)
            yield from reduce_steps(net, tp_in, pair_out, *rest[:4], rows, 16)

        run_together(
            latents(),
            reduce_steps(net, queries_ref, query_out, None, *rest[4:7], query_out.shape[0], 8),
            head_grads_steps(net, at_ref, at_out, at_x, at_tp, x_sems, at.shape[1]),
        )
        net.finish()

    rows, cols = pairs.shape[2:]
    scratch = [
        pltpu.VMEM((8,) + at.shape[1:], BF),
        pltpu.VMEM((8,) + at.shape[1:], BF),
        pltpu.SemaphoreType.DMA((3, 8)),
        pltpu.VMEM((16, rows, cols), BF),
    ]
    scratch += reduce_scratch(rows, cols, 16)
    scratch += reduce_scratch(queries.shape[1], queries.shape[2], 8)
    return comm_call(
        "reduce_latent",
        number,
        body,
        [pairs, queries, at],
        [VMEM] * 3,
        [shape((rows, cols), F32), shape(queries.shape[1:], F32), shape((4,) + at.shape[1:])],
        [VMEM] * 2 + [ANY],
        scratch,
        220,
    )


def finish_blocks(number, block, swaps, gain_blocks, n_ctx):
    k = len(swaps)

    def body(*refs):
        block_ref, ins, gains = refs[0], refs[1 : k + 1], refs[k + 1]
        blocks, outs, gains_out = refs[k + 2], refs[k + 3 : 2 * k + 3], refs[2 * k + 3]
        rest = list(refs[2 * k + 4 :])
        net_sems = rest.pop()
        tp_in = rest.pop(0)
        place = Place(n_ctx)
        greet(place, line=True, across=True, core=True, other=True)
        net = Net(place, net_sems)

        def sums():
            sem = net.sem()
            net.send(lambda: gains, lambda: tp_in, sem, place.other)
            yield
            net.recv(lambda: tp_in, sem)
            pl.loop(0, 16)(
                lambda g: add_into(tp_in.at[g], [tp_in.at[g], gains.at[g]], gains.shape[1])
            )
            yield from reduce_steps(net, tp_in, gains_out, *rest, gains_out.shape[0], 16)

        run_together(
            gather_steps(net, block_ref, blocks, 16),
            sums(),
            *[swap_steps(net, i, o) for i, o in zip(ins, outs)],
        )
        net.finish()

    scratch = [pltpu.VMEM(gain_blocks.shape, BF)]
    scratch += reduce_scratch(gain_blocks.shape[1], gain_blocks.shape[2], 16)
    return comm_call(
        "finish_blocks",
        number,
        body,
        [block] + list(swaps) + [gain_blocks],
        [ANY] * (k + 1) + [VMEM],
        [shape((16,) + block.shape)]
        + [shape(s.shape, s.dtype) for s in swaps]
        + [shape(gain_blocks.shape[1:], F32)],
        [ANY] * (k + 1) + [VMEM],
        scratch,
        160,
    )


def turn(values, table, back=False):
    near = pltpu.roll(values, 16, 1) * table[:, 256:384]
    far = pltpu.roll(values, 112, 1) * table[:, 128:256]
    turned = near + far
    return values * table[:, :128] + (-turned if back else turned)


def by_rows(rows, step, body):
    pl.loop(0, rows // step)(lambda i: body(pl.ds(pl.multiple_of(i * step, step), step)))


def lanes_of(h):
    return pl.ds(pl.multiple_of(h * 128, 128), 128)


def key_tile(expanded, ropes):
    lane = lax.broadcasted_iota(jnp.int32, expanded.shape, 1)
    return jnp.where(lane < NOPE, expanded, ropes)


def attend(qn, q_up, pairs, l_up, w_out_t, table, q_pos):
    rows, keys, heads = qn.shape[0], pairs.shape[0], q_up.shape[1] // 128
    span, block = keys // 4, rows // 4
    dim = w_out_t.shape[0]

    def body(
        qn_ref, q_up_ref, pairs_ref, l_up_ref, w_ref, table_ref, pos_ref,
        branch_ref, q_ref, o_ref, lse_ref, att_ref,
        e_ref, top_ref, sum_ref, acc_ref,
    ):
        by_rows(
            keys,
            256,
            lambda r: e_ref.__setitem__(
                r, matmul(pairs_ref[r, :KVR], l_up_ref[...]).astype(BF)
            ),
        )

        def head(h):
            lanes = lanes_of(h)
            raw = matmul(qn_ref[...], q_up_ref[:, lanes])
            q_ref[:, lanes] = turn(raw, table_ref[...]).astype(BF)
            top_ref[...] = jnp.full(top_ref.shape, -1e30, F32)
            sum_ref[...] = jnp.zeros(sum_ref.shape, F32)
            acc_ref[...] = jnp.zeros(acc_ref.shape, F32)
            for kb in range(4):
                part, cols = slice(kb * block, rows), slice(kb * span, (kb + 1) * span)
                values = e_ref[cols, lanes]
                key = key_tile(values, pairs_ref[cols, KVR:])
                scores = matmul_nt(q_ref[part, lanes], key) * score_scale
                index = lax.broadcasted_iota(jnp.int32, scores.shape, 1) + kb * span
                scores = jnp.where(index <= pos_ref[part, :1], scores, -1e30)
                old = top_ref[part, :1]
                top = jnp.maximum(old, jnp.max(scores, axis=1, keepdims=True))
                weights = jnp.exp(scores - top)
                decay = jnp.exp(old - top)
                total = sum_ref[part, :1] * decay + jnp.sum(weights, axis=1, keepdims=True)
                acc_ref[part] = acc_ref[part] * decay + matmul(weights.astype(BF), values)
                top_ref[part] = jnp.broadcast_to(top, acc_ref[part].shape)
                sum_ref[part] = jnp.broadcast_to(total, acc_ref[part].shape)
            lane = lax.broadcasted_iota(jnp.int32, acc_ref.shape, 1)
            o_ref[:, lanes] = jnp.where(lane < NOPE, 0.0, acc_ref[...] / sum_ref[...])
            lse_ref[:, lanes] = top_ref[...] + jnp.log(sum_ref[...])

        pl.loop(0, heads)(head)
        for h in range(heads):
            att_ref[:, h * VH : (h + 1) * VH] = o_ref[
                :, h * 128 + NOPE : (h + 1) * 128
            ].astype(BF)
        for i in range(dim // 512):
            cut = slice(i * 512, (i + 1) * 512)
            branch_ref[:, cut] = matmul_nt(att_ref[...], w_ref[cut]).astype(BF)

    wide = heads * 128
    return pl.pallas_call(
        body,
        out_shape=[
            shape((rows, dim)),
            shape((rows, wide)),
            shape((rows, wide), F32),
            shape((rows, wide), F32),
            shape((rows, heads * VH)),
        ],
        in_specs=[VMEM] * 7,
        out_specs=[VMEM] * 5,
        scratch_shapes=[pltpu.VMEM((keys, wide), BF)] + [pltpu.VMEM((rows, 128), F32)] * 3,
        compiler_params=pltpu.CompilerParams(vmem_limit_bytes=60 << 20),
        cost_estimate=pl.CostEstimate(
            flops=20_000_000_000, bytes_accessed=20 << 20, transcendentals=0
        ),
        name="attend",
    )(qn, q_up, pairs, l_up, w_out_t, table, q_pos)


def attend_back(gb, qn, q_up, pairs, l_up, w_out_t, table, q_pos, q, o, lse, att):
    rows, keys, heads = qn.shape[0], pairs.shape[0], q_up.shape[1] // 128
    span, block = keys // 4, rows // 4
    dim, wide = gb.shape[1], heads * 128

    def body(
        gb_ref, qn_ref, q_up_ref, pairs_ref, l_up_ref, w_ref, table_ref, pos_ref,
        q_ref, o_ref, lse_ref, att_ref,
        gp_ref, gqn_ref, gq_up_ref, gl_up_ref, gw_ref,
        e_ref, rope_ref, go_ref, gq_ref, dq_ref, inner_ref,
    ):
        def expand(r):
            e_ref[r] = matmul(pairs_ref[r, :KVR], l_up_ref[...]).astype(BF)
            rope_ref[r] = jnp.zeros((256, 128), F32)

        by_rows(keys, 256, expand)
        ga = matmul(gb_ref[...], w_ref[...]).astype(BF)
        for h in range(heads):
            go_ref[:, h * 128 : h * 128 + NOPE] = jnp.zeros((rows, NOPE), BF)
            go_ref[:, h * 128 + NOPE : (h + 1) * 128] = ga[:, h * VH : (h + 1) * VH]
        for i in range(dim // 512):
            cut = slice(i * 512, (i + 1) * 512)
            gw_ref[cut] = matmul_tn(gb_ref[:, cut], att_ref[...]).astype(BF)

        def head(h):
            lanes = lanes_of(h)
            dq_ref[...] = jnp.zeros(dq_ref.shape, F32)
            inner = jnp.sum(
                go_ref[:, lanes].astype(F32) * o_ref[:, lanes], axis=1, keepdims=True
            )
            inner_ref[...] = jnp.broadcast_to(inner, inner_ref.shape)
            for kb in range(4):
                part, cols = slice(kb * block, rows), slice(kb * span, (kb + 1) * span)
                values = e_ref[cols, lanes]
                key = key_tile(values, pairs_ref[cols, KVR:])
                queries, grads = q_ref[part, lanes], go_ref[part, lanes]
                scores = matmul_nt(queries, key) * score_scale
                index = lax.broadcasted_iota(jnp.int32, scores.shape, 1) + kb * span
                probs = jnp.where(
                    index <= pos_ref[part, :1],
                    jnp.exp(scores - lse_ref[part, lanes][:, :1]),
                    0.0,
                )
                grad_probs = matmul_nt(grads, values)
                grad_scores = (probs * (grad_probs - inner_ref[part, :1])).astype(BF)
                dq_ref[part] += matmul(grad_scores, key)
                grad_key = matmul_tn(grad_scores, queries) * score_scale
                grad_value = matmul_tn(probs.astype(BF), grads)
                lane = lax.broadcasted_iota(jnp.int32, grad_key.shape, 1)
                e_ref[cols, lanes] = jnp.where(lane < NOPE, grad_key, grad_value).astype(BF)
                rope_ref[cols] += jnp.where(lane < NOPE, 0.0, grad_key)
            gq_ref[:, lanes] = turn(dq_ref[...] * score_scale, table_ref[...], True).astype(BF)

        pl.loop(0, heads)(head)

        def latents(r):
            gp_ref[r, :KVR] = matmul_nt(e_ref[r], l_up_ref[...]).astype(BF)
            gp_ref[r, KVR:] = rope_ref[r].astype(BF)

        by_rows(keys, 256, latents)
        gl_up_ref[...] = matmul_tn(pairs_ref[:, :KVR], e_ref[...]).astype(BF)
        gq_up_ref[...] = matmul_tn(qn_ref[...], gq_ref[...]).astype(BF)
        gqn_ref[...] = matmul_nt(gq_ref[...], q_up_ref[...]).astype(BF)

    return pl.pallas_call(
        body,
        out_shape=[
            shape(pairs.shape),
            shape(qn.shape),
            shape(q_up.shape),
            shape(l_up.shape),
            shape(w_out_t.shape),
        ],
        in_specs=[VMEM] * 12,
        out_specs=[VMEM] * 5,
        scratch_shapes=[
            pltpu.VMEM((keys, wide), BF),
            pltpu.VMEM((keys, 128), F32),
            pltpu.VMEM((rows, wide), BF),
            pltpu.VMEM((rows, wide), BF),
            pltpu.VMEM((rows, 128), F32),
            pltpu.VMEM((rows, 128), F32),
        ],
        compiler_params=pltpu.CompilerParams(vmem_limit_bytes=60 << 20),
        cost_estimate=pl.CostEstimate(
            flops=40_000_000_000, bytes_accessed=30 << 20, transcendentals=0
        ),
        name="attend_back",
    )(gb, qn, q_up, pairs, l_up, w_out_t, table, q_pos, q, o, lse, att)


def shards(
    layer_input,
    first_gain,
    query_down,
    query_gain,
    query_up,
    latent_down,
    latent_gain,
    latent_up,
    out_weight,
    second_gain,
    gate_weight,
    up_weight,
    down_weight,
    out_grad,
):
    n_ctx = lax.axis_size("ctx")
    n_tp = lax.axis_size("tp")
    members = n_ctx // 16
    c = lax.axis_index("ctx")
    t = lax.axis_index("tp")
    g = c // members
    b = lax.rem(g // 2, 2)
    d = lax.rem(g, 2)
    member = lax.rem(c, members)
    ctx_rows, dim = layer_input.shape
    rows = ctx_rows // n_tp
    shard_rows = query_down.shape[0]
    qr = query_down.shape[1]
    heads = H // 8
    units = gate_weight.shape[1] // 16
    plane_lists = [[k * members + m for k in range(16)] for m in range(members)]
    member_lists = [[k * members + m for m in range(members)] for k in range(16)]

    def widen(blocks):
        if members == 1:
            return blocks[:, None]
        return lax.all_gather(blocks, "ctx", axis=1, axis_index_groups=member_lists)

    def narrow(blocks):
        if members == 1:
            return blocks[:, 0]
        return lax.psum_scatter(
            blocks.astype(F32), "ctx", scatter_dimension=1, axis_index_groups=member_lists
        ).astype(BF)

    def gather_over(block):
        return lax.all_gather(
            block, "ctx", axis=0, tiled=True, axis_index_groups=plane_lists if members > 1 else None
        )

    def scatter_over(part):
        return lax.psum_scatter(
            part,
            "ctx",
            scatter_dimension=0,
            tiled=True,
            axis_index_groups=plane_lists if members > 1 else None,
        )

    widths = [first_gain.shape[0], query_gain.shape[0], latent_gain.shape[0], second_gain.shape[0]]
    starts = [0, widths[0], widths[0] + widths[1], widths[0] + widths[1] + widths[2]]
    gains = jnp.concatenate([first_gain, query_gain, latent_gain, second_gain]).astype(F32)
    gains = jnp.broadcast_to(gains[None], (8, gains.shape[0]))
    down_shard = jnp.concatenate([query_down, latent_down], axis=1)

    def trade(block, k):
        return lax.ppermute(
            block, "ctx", [(i, (i // members ^ k) * members + i % members) for i in range(n_ctx)]
        )

    def swap_tp(block):
        return lax.ppermute(block, "tp", [(0, 1), (1, 0)])

    wide = 640
    ff = pack(gate_weight, up_weight, down_weight, wide, members)
    near = [ff[0]] + [trade(ff[j], 4 * j) for j in (1, 2, 3)]
    q_rows_w, l_rows_w, o_rows_w = query_up.shape[0], latent_up.shape[0], shard_rows // 2
    q_width, o_width = heads * (NOPE + ROPE), heads * VH
    q_tiles = jnp.pad(
        query_up.reshape(q_rows_w, 4, heads, NOPE + ROPE),
        ((0, 0), (0, 0), (0, 0), (0, 128 - NOPE - ROPE)),
    ).reshape(q_rows_w, 4, wide)
    out_tiles = jnp.transpose(
        out_weight.reshape(4, o_width, 2, o_rows_w), (0, 3, 2, 1)
    ).reshape(4, o_rows_w, wide)
    at = jnp.concatenate(
        [
            jnp.transpose(q_tiles, (1, 0, 2)),
            jnp.transpose(latent_up.reshape(l_rows_w, 4, wide), (1, 0, 2)),
            out_tiles,
        ],
        axis=1,
    )

    x = lax.dynamic_slice_in_dim(layer_input, t * rows, rows, 0).astype(F32)
    out_grad_rows = lax.dynamic_slice_in_dim(out_grad, t * rows, rows, 0).astype(F32)
    positions = c * ctx_rows + t * rows + jnp.arange(rows, dtype=jnp.int32)
    cosine, sine_table = rope_tables(positions)
    grad_ffn = (residual_scale * out_grad_rows).astype(BF)

    down_full, gains, at_all = weights_in(1, down_shard, gains, at, n_ctx)
    down_full, near = lax.optimization_barrier((down_full, near))
    own = [jnp.stack([r[0] for r in near])]
    own += [trade(jnp.stack([r[k] for r in near]), k) for k in (1, 2, 3)]
    down_full = widen(down_full).reshape(dim, -1)
    gains = widen(gains[:, 0]).reshape(n_ctx, -1)
    gain_first, gain_query, gain_latent, gain_second = [
        gains[:, s : s + w].reshape(-1) for s, w in zip(starts, widths)
    ]
    at_all = widen(at_all).reshape(n_ctx, -1, wide)
    q_up = at_all[:, :q_rows_w].reshape(qr, wide)
    l_up = at_all[:, q_rows_w : q_rows_w + l_rows_w].reshape(KVR, wide)
    w_out_t = jnp.transpose(
        at_all[:, q_rows_w + l_rows_w :].reshape(n_ctx, o_rows_w, 2, o_width), (0, 2, 1, 3)
    ).reshape(dim, o_width)

    normed = rms_norm(x, gain_first).astype(BF)
    both = matmul(normed, down_full)
    query_latent, compressed = both[:, :qr], both[:, qr:]
    query_normed = rms_norm(query_latent, gain_query).astype(BF)
    latent = rms_norm(compressed[:, :KVR], gain_latent).astype(BF)
    key_rope = rotate(compressed[:, KVR:], cosine, sine_table).astype(BF)
    pair_block = jnp.concatenate(
        [latent, jnp.zeros((rows, NOPE), BF), key_rope, jnp.zeros((rows, ROPE), BF)], axis=1
    )
    normed_columns = jnp.transpose(
        normed.reshape(rows, 16, dim // 16), (1, 0, 2)
    )
    pairs, qn_all, token_columns = gather_latent(
        3, pair_block, query_normed, normed_columns, n_ctx
    )
    own, pairs, grad_ffn = lax.optimization_barrier((own, pairs, grad_ffn))
    gf_all = gather_over(grad_ffn)
    oth = [swap_tp(r) for r in own]
    lat_rope = widen(pairs).reshape(-1, 384)
    qn_all = qn_all.reshape(-1, qr)

    block = jnp.arange(8, dtype=jnp.int32)
    block_ctx = ((block // 2 * 2 + b) * 2 + block % 2) * members + member
    q_positions = (
        block_ctx[:, None] * ctx_rows + t * rows + jnp.arange(rows, dtype=jnp.int32)[None, :]
    ).reshape(-1)
    q_cos, q_sin = rope_tables(q_positions)
    none, half = jnp.zeros((q_positions.shape[0], NOPE), F32), jnp.zeros_like(q_cos)
    table = jnp.concatenate(
        [none + 1, q_cos, q_cos, half, half]
        + [none, -q_sin, half, half, half]
        + [none, half, q_sin, half, half],
        axis=1,
    )
    q_pos = jnp.broadcast_to(q_positions[:, None], (q_positions.shape[0], 128))
    branch_part, queries, attended_wide, log_total, attended = attend(
        qn_all, q_up, lat_rope, l_up, w_out_t, table, q_pos
    )

    (branch,) = reduce_blocks("reduce_branch", 4, [branch_part], [8], n_ctx)
    middle = x + residual_scale * branch
    normed_second = rms_norm(middle, gain_second).astype(BF)
    (ns_all,) = gather_blocks("gather_second", 5, [normed_second], [16], n_ctx)
    ns_all, oth = lax.optimization_barrier((ns_all, oth))
    w_gate, w_up, w_down_t = [
        widen(w).reshape(dim, 2 * units)
        for w in arrange(
            jnp.stack(own, axis=1).reshape(16, shard_rows, wide),
            jnp.stack(oth, axis=1).reshape(16, shard_rows, wide),
            units,
            members,
        )
    ]
    gate_values = matmul(ns_all, w_gate)
    up_values = matmul(ns_all, w_up)
    sigmoid_gate = jax.nn.sigmoid(gate_values)
    hidden = (gate_values * sigmoid_gate * up_values).astype(BF)
    ffn_part = matmul_nt(hidden, w_down_t).astype(BF)

    grad_hidden = matmul(gf_all, w_down_t)
    grad_gate = (
        grad_hidden * up_values * sigmoid_gate * (1.0 + gate_values * (1.0 - sigmoid_gate))
    ).astype(BF)
    grad_up = (grad_hidden * gate_values * sigmoid_gate).astype(BF)
    (grad_second,) = reduce_blocks(
        "reduce_second",
        6,
        [(matmul_nt(grad_gate, w_gate) + matmul_nt(grad_up, w_up)).astype(BF)],
        [16],
        n_ctx,
    )

    ff_grads = [
        narrow(matmul_tn(left, right).astype(BF).reshape(16, members, shard_rows, 2 * units))
        for left, right in ((ns_all, grad_gate), (ns_all, grad_up), (gf_all, hidden))
    ]
    grads_own, grads_oth = collect(ff_grads, wide, members)
    grads_oth = swap_tp(grads_oth)

    grad_middle_part, second_gain_part = norm_back(middle, gain_second, grad_second)
    grad_middle = out_grad_rows + grad_middle_part

    grad_branch = (residual_scale * grad_middle).astype(BF)
    (gb_all,) = gather_blocks("gather_branch", 7, [grad_branch], [8], n_ctx)
    gb_all, grads_oth, ffn_part = lax.optimization_barrier((gb_all, grads_oth, ffn_part))
    ffn_sum = scatter_over(ffn_part).astype(F32)
    out_half = (middle + residual_scale * ffn_sum).astype(BF)
    ff_back = (grads_own.astype(F32) + grads_oth.astype(F32)).astype(BF)
    ff_back = ff_back.reshape(4, 4, shard_rows, wide)
    back = [ff_back[0]] + [trade(ff_back[j], 4 * j) for j in (1, 2, 3)]
    grad_lat_rope, gqn_part, q_up_part, l_up_part, out_part = attend_back(
        gb_all, qn_all, q_up, lat_rope, l_up, w_out_t, table, q_pos,
        queries, attended_wide, log_total, attended,
    )

    at_part = jnp.concatenate(
        [
            q_up_part.reshape(n_ctx, q_rows_w, wide),
            l_up_part.reshape(n_ctx, l_rows_w, wide),
            jnp.transpose(
                out_part.reshape(n_ctx, 2, o_rows_w, o_width), (0, 2, 1, 3)
            ).reshape(n_ctx, o_rows_w, wide),
        ],
        axis=1,
    )
    at_part = narrow(at_part.reshape(16, members, -1, wide))

    own_lat_rope, grad_query_normed, at_sums = reduce_latent(
        8,
        narrow(grad_lat_rope.reshape(16, members, 2, rows, 384)),
        gqn_part.reshape(8, rows, qr),
        at_part,
        n_ctx,
    )
    own_lat_rope, back = lax.optimization_barrier((own_lat_rope, back))
    sums = [jnp.stack([r[0] for r in back])]
    sums += [trade(jnp.stack([r[k] for r in back]), k) for k in (1, 2, 3)]
    grad_query_latent, query_gain_part = norm_back(query_latent, gain_query, grad_query_normed)
    grad_latent_rows, latent_gain_part = norm_back(
        compressed[:, :KVR], gain_latent, own_lat_rope[:, :KVR]
    )
    grad_both = jnp.concatenate(
        [
            grad_query_latent,
            grad_latent_rows,
            rotate(own_lat_rope[:, KVR + NOPE : KVR + NOPE + ROPE], cosine, -sine_table),
        ],
        axis=1,
    ).astype(BF)
    grad_normed = matmul_nt(grad_both, down_full)
    grad_input_part, first_gain_part = norm_back(x, gain_first, grad_normed)
    input_half = (grad_middle + grad_input_part).astype(BF)
    gain_parts = jnp.concatenate(
        [
            p.reshape(n_ctx, -1)
            for p in (first_gain_part, query_gain_part, latent_gain_part, second_gain_part)
        ],
        axis=1,
    )
    gain_parts = narrow(gain_parts.reshape(16, members, -1)).astype(BF)
    gain_blocks = jnp.pad(gain_parts[:, None], ((0, 0), (0, 15), (0, 0)))
    both_all, out_other, input_other, gain_sums = finish_blocks(
        9, grad_both, [out_half, input_half], gain_blocks, n_ctx
    )
    both_all, sums = lax.optimization_barrier((both_all, sums))
    ff_sums = jnp.stack(sums, axis=1).reshape(16, shard_rows, wide)
    if members == 1:
        down_part = matmul_tn(
            token_columns.reshape(16 * rows, shard_rows), both_all.reshape(16 * rows, -1)
        ).astype(BF)
    else:
        down_part = lax.psum_scatter(
            matmul_tn(normed, grad_both).astype(BF), "ctx", scatter_dimension=0, tiled=True
        )

    down_other = swap_tp(down_part)

    def in_order(mine, other):
        return jnp.where(
            t == 0, jnp.concatenate([mine, other]), jnp.concatenate([other, mine])
        )

    layer_output = in_order(out_half, out_other)
    input_grad = in_order(input_half, input_other).astype(F32)
    down_grads = down_part.astype(F32) + down_other.astype(F32)
    gain_grads = gain_sums[0]
    first_gain_grad, query_gain_grad, latent_gain_grad, second_gain_grad = [
        gain_grads[s : s + w] for s, w in zip(starts, widths)
    ]

    gate_weight_grad, up_weight_grad, down_weight_grad = spread(ff_sums, units, members)
    query_up_grad = jnp.transpose(
        at_sums[:, :q_rows_w].reshape(4, q_rows_w, heads, 128)[..., : NOPE + ROPE], (1, 0, 2, 3)
    ).reshape(q_rows_w, 4 * q_width)
    latent_up_grad = jnp.transpose(at_sums[:, q_rows_w : q_rows_w + l_rows_w], (1, 0, 2)).reshape(
        l_rows_w, 4 * wide
    )
    out_weight_grad = jnp.transpose(
        at_sums[:, q_rows_w + l_rows_w :].reshape(4, o_rows_w, 2, o_width), (0, 3, 2, 1)
    ).reshape(4 * o_width, shard_rows)
    return (
        layer_output,
        input_grad,
        first_gain_grad,
        down_grads[:, :qr],
        query_gain_grad,
        query_up_grad.astype(F32),
        down_grads[:, qr:],
        latent_gain_grad,
        latent_up_grad.astype(F32),
        out_weight_grad.astype(F32),
        second_gain_grad,
        gate_weight_grad,
        up_weight_grad,
        down_weight_grad,
    )


def solution(mesh):
    return jax.shard_map(
        shards,
        mesh=mesh,
        in_specs=(
            P("ctx", None),
            P("ctx"),
            P("ctx", None),
            P("ctx"),
            P("ctx", "tp"),
            P("ctx", None),
            P("ctx"),
            P("ctx", "tp"),
            P("tp", "ctx"),
            P("ctx"),
            P("ctx", "tp"),
            P("ctx", "tp"),
            P("tp", "ctx"),
            P("ctx", None),
        ),
        out_specs=(
            P("ctx", None),
            P("ctx", None),
            P("ctx"),
            P("ctx", None),
            P("ctx"),
            P("ctx", "tp"),
            P("ctx", None),
            P("ctx"),
            P("ctx", "tp"),
            P("tp", "ctx"),
            P("ctx"),
            P("ctx", "tp"),
            P("ctx", "tp"),
            P("tp", "ctx"),
        ),
        check_vma=False,
    )
```

```python
import math

import jax
import jax.numpy as jnp
from jax import lax
from jax.experimental import pallas as pl
from jax.experimental.pallas import tpu as pltpu
from jax.sharding import PartitionSpec as P

BF = jnp.bfloat16
F32 = jnp.float32

H = 40
KVR = 256
NOPE = 64
ROPE = 32
VH = 64

eps_norm = 1e-06
residual_scale = 1.4 / math.sqrt(62.0)
score_scale = (NOPE + ROPE) ** (-0.5)
rope_base = 10000.0


def matmul(left_side, right_side):
    return jnp.dot(left_side, right_side, preferred_element_type=F32)


def matmul_nt(left_side, right_side):
    return lax.dot_general(
        left_side, right_side, (((1,), (1,)), ((), ())), preferred_element_type=F32
    )


def matmul_tn(left_side, right_side):
    return lax.dot_general(
        left_side, right_side, (((0,), (0,)), ((), ())), preferred_element_type=F32
    )


def rms_norm(values, scale_gain):
    factor = lax.rsqrt(jnp.mean(values * values, axis=-1, keepdims=True) + eps_norm)
    return values * factor * scale_gain


def norm_back(values, scale_gain, upstream):
    factor = lax.rsqrt(jnp.mean(values * values, axis=-1, keepdims=True) + eps_norm)
    scaled = upstream * scale_gain
    inner_sum = jnp.mean(scaled * values, axis=-1, keepdims=True)
    grad_values = factor * scaled - values * factor * factor * factor * inner_sum
    grad_gain = jnp.sum(upstream * values * factor, axis=0)
    return (grad_values, grad_gain)


def rotate(values, cosine, sine_table):
    half_width = values.shape[-1] // 2
    first_half = values[..., :half_width]
    second_half = values[..., half_width:]
    return jnp.concatenate(
        [
            first_half * cosine - second_half * sine_table,
            second_half * cosine + first_half * sine_table,
        ],
        axis=-1,
    )


def rope_tables(positions):
    frequency = rope_base ** (-jnp.arange(ROPE // 2, dtype=F32) / (ROPE // 2))
    angles = positions.astype(F32)[:, None] * frequency[None, :]
    return (jnp.cos(angles), jnp.sin(angles))


MESH = pl.DeviceIdType.MESH
OFFSETS = (0, -1, 1, -2, 2, -3, 3)


class Place:
    def __init__(self, n_ctx):
        c = lax.axis_index("ctx")
        self.members = n_ctx // 16
        self.c = c
        self.t = lax.axis_index("tp")
        self.m = lax.rem(c, self.members)
        g = c // self.members
        self.g = g
        self.a, self.b, self.d = g // 4, lax.rem(g // 2, 2), lax.rem(g, 2)

    def at(self, a=None, b=None, d=None):
        a = self.a if a is None else a
        b = self.b if b is None else b
        d = self.d if d is None else d
        return (((a * 2 + b) * 2 + d) * self.members + self.m, self.t)

    def up(self):
        return self.at(a=self.a + 1)

    def down(self):
        return self.at(a=self.a - 1)

    def across(self):
        return self.at(b=1 - self.b)

    def core(self):
        return self.at(d=1 - self.d)

    def other(self):
        return (self.c, 1 - self.t)

    def valid(self, o):
        return None if o == 0 else (self.a + o >= 0 if o < 0 else self.a + o <= 3)


def both_of(p, q):
    if p is None:
        return q
    return p if q is None else p & q


def when(p, body):
    if p is None:
        body()
    else:
        pl.when(p)(body)


class Net:
    def __init__(self, place, sems):
        self.place, self.sems, self.count, self.pending = place, sems, 0, []

    def sem(self):
        self.count += 1
        return self.sems.at[self.count - 1]

    def send(self, src, dst, recv, to, cond=None):
        mine = self.sem()

        def copy():
            return pltpu.make_async_remote_copy(
                src(), dst(), mine, recv, device_id=to(), device_id_type=MESH
            )

        when(cond, lambda: copy().start())
        self.pending.append((cond, lambda: copy().wait_send()))

    def recv(self, dst, sem, cond=None):
        def wait():
            ref = dst()
            pltpu.make_async_remote_copy(
                ref, ref, sem, sem, device_id=self.place.other(), device_id_type=MESH
            ).wait_recv()

        when(cond, wait)

    def finish(self):
        for cond, wait in self.pending:
            when(cond, wait)


def greet(place, line=False, across=False, core=False, other=False, everyone=0):
    barrier = pltpu.get_barrier_semaphore()

    def tell(device):
        pl.semaphore_signal(barrier, inc=1, device_id=device, device_id_type=MESH)

    count = 0
    if everyone:
        for k in range(1, everyone):
            tell((lax.rem(place.c + k * place.members, everyone * place.members), place.t))
        count = count + everyone - 1
    else:
        if line:
            pl.when(place.a < 3)(lambda: tell(place.up()))
            pl.when(place.a > 0)(lambda: tell(place.down()))
            count = count + (place.a < 3).astype(jnp.int32) + (place.a > 0).astype(jnp.int32)
        if across:
            tell(place.across())
            count = count + 1
        if core:
            tell(place.core())
            count = count + 1
    if other:
        tell(place.other())
        count = count + 1
    pl.semaphore_wait(barrier, count)


def trade_away(place, src, out, sems, first):
    barrier = pltpu.get_barrier_semaphore()
    count = src.shape[0]
    devices = [
        ((place.g ^ (first + k)) * place.members + place.m, place.t) for k in range(count)
    ]
    for device in devices:
        pl.semaphore_signal(barrier, inc=1, device_id=device, device_id_type=MESH)
    pl.semaphore_wait(barrier, count)
    copies = [
        pltpu.make_async_remote_copy(
            src.at[k],
            out.at[k],
            sems.at[0, k],
            sems.at[1, k],
            device_id=devices[k],
            device_id_type=MESH,
        )
        for k in range(count)
    ]
    for copy in copies:
        copy.start()
    return copies


def gather_steps(net, src, out, width):
    p = net.place
    cores = width == 16

    def slot(o, b, d):
        return out.at[((p.a + o) * 2 + b) * 2 + d] if cores else out.at[(p.a + o) * 2 + d]

    z_sem = {o: net.sem() for o in OFFSETS if o}
    x_sem = {o: net.sem() for o in OFFSETS} if cores else {}
    c_sem = {(s, o): net.sem() for s in ((0, 1) if cores else (0,)) for o in OFFSETS}
    own_sem = net.sem()
    keep = pltpu.make_async_copy(src, slot(0, p.b, p.d), own_sem)
    keep.start()

    def forward(o):
        ok = p.valid(o)
        here = lambda: slot(o, p.b, p.d)
        origin = (lambda: src) if o == 0 else here
        if o <= 0 and o > -3:
            net.send(origin, here, z_sem[o - 1], p.up, both_of(ok, p.a < 3))
        if o >= 0 and o < 3:
            net.send(origin, here, z_sem[o + 1], p.down, both_of(ok, p.a > 0))
        if cores:
            net.send(origin, here, x_sem[o], p.across, ok)
        net.send(origin, here, c_sem[0, o], p.core, ok)

    def from_line(o):
        net.recv(lambda: slot(o, p.b, p.d), z_sem[o], p.valid(o))
        forward(o)

    def from_across(o):
        if cores:
            there = lambda: slot(o, 1 - p.b, p.d)
            net.recv(there, x_sem[o], p.valid(o))
            net.send(there, there, c_sem[1, o], p.core, p.valid(o))

    forward(0)
    yield
    for near in (1, 2, 3):
        from_line(-near)
        from_line(near)
        yield
        if near == 1:
            from_across(0)
        else:
            from_across(1 - near)
            from_across(near - 1)
        yield
    from_across(-3)
    from_across(3)
    yield
    for o in OFFSETS:
        net.recv(lambda: slot(o, p.b, 1 - p.d), c_sem[0, o], p.valid(o))
        if cores:
            net.recv(lambda: slot(o, 1 - p.b, 1 - p.d), c_sem[1, o], p.valid(o))
    keep.wait()


def add_into(out, terms, rows):
    step = 16 if rows % 16 == 0 else rows

    def body(i):
        part = pl.ds(pl.multiple_of(i * step, step), step)
        total = terms[0][part].astype(F32)
        for term in terms[1:]:
            total = total + term[part].astype(F32)
        out[part] = total.astype(out.dtype)

    pl.loop(0, rows // step)(body)


def reduce_steps(net, parts, out, near_core, near_x, line_in, line_out, rows, width):
    p = net.place
    cores = width == 16
    order = (-3, 3, -2, 2, -1, 1, 0)
    if cores:
        c_sem = {(b, o): net.sem() for b in (0, 1) for o in order}
        for o in order:
            for side in (1, 0):
                def src(o=o, side=side):
                    b = 1 - p.b if side else p.b
                    return parts.at[((p.a + o) * 2 + b) * 2 + 1 - p.d]

                def dst(o=o, side=side):
                    b = 1 - p.b if side else p.b
                    return near_core.at[(p.a + o) * 2 + b]

                net.send(src, dst, c_sem[side, o], p.core, p.valid(o))
        yield
    x_sem = {o: net.sem() for o in order}
    up_sem = {o: net.sem() for o in (0, 1, 2)}
    down_sem = {o: net.sem() for o in (0, 1, 2)}

    pair = p.b if cores else p.d

    def mine(o, b):
        g = (p.a + o) * 2 + b
        return near_core.at[g] if cores else parts.at[g]

    for o in order:
        if cores:
            def join(o=o):
                g = (p.a + o) * 2 + 1 - p.b
                add_into(near_core.at[g], [near_core.at[g], parts.at[g * 2 + p.d]], rows)

            net.recv(lambda: near_core.at[(p.a + o) * 2 + 1 - p.b], c_sem[1, o], p.valid(o))
            when(p.valid(o), join)
        net.send(
            lambda o=o: mine(o, 1 - pair),
            lambda o=o: near_x.at[p.a + o],
            x_sem[o],
            p.across if cores else p.core,
            p.valid(o),
        )
    yield
    for o in order:
        ok = p.valid(o)
        if cores:
            net.recv(lambda: near_core.at[(p.a + o) * 2 + p.b], c_sem[0, o], ok)

        def terms(o=o):
            g = (p.a + o) * 2 + pair
            own = [near_core.at[g], parts.at[g * 2 + p.d]] if cores else [parts.at[g]]
            return own + [near_x.at[p.a + o]]

        net.recv(lambda: near_x.at[p.a + o], x_sem[o], ok)
        if o == 0:
            below, above = line_in.at[0, 0], line_in.at[1, 0]
            net.recv(lambda: below, up_sem[0], p.a > 0)
            net.recv(lambda: above, down_sem[0], p.a < 3)
            inner = (p.a > 0) & (p.a < 3)
            pl.when(inner)(lambda: add_into(out, terms() + [below, above], rows))
            pl.when(p.a == 0)(lambda: add_into(out, terms() + [above], rows))
            pl.when(p.a == 3)(lambda: add_into(out, terms() + [below], rows))
            continue
        far = abs(o)
        way = 0 if o > 0 else 1
        stage = line_out.at[way, far - 1]
        sems = up_sem if o > 0 else down_sem
        first = p.a == 0 if o > 0 else p.a == 3
        if far < 3:
            came = line_in.at[way, far]
            later = ok & ~first
            net.recv(lambda: came, sems[far], later)
            pl.when(later)(lambda: add_into(stage, terms() + [came], rows))
            pl.when(ok & first)(lambda: add_into(stage, terms(), rows))
        else:
            pl.when(ok)(lambda: add_into(stage, terms(), rows))
        net.send(
            lambda stage=stage: stage,
            lambda far=far, way=way: line_in.at[way, far - 1],
            sems[far - 1],
            p.up if o > 0 else p.down,
            ok,
        )
        yield


def swap_steps(net, src, dst):
    sem = net.sem()
    net.send(lambda: src, lambda: dst, sem, net.place.other)
    yield
    net.recv(lambda: dst, sem)


def run_together(*tasks):
    tasks = list(tasks)
    while tasks:
        for task in list(tasks):
            try:
                next(task)
            except StopIteration:
                tasks.remove(task)


ANY = pl.BlockSpec(memory_space=pl.ANY)
VMEM = pl.BlockSpec(memory_space=pltpu.VMEM)


def comm_call(name, number, body, ins, in_specs, outs, out_specs, scratch, sems):
    return pl.pallas_call(
        body,
        out_shape=outs,
        in_specs=in_specs,
        out_specs=out_specs,
        scratch_shapes=list(scratch) + [pltpu.SemaphoreType.DMA((sems,))],
        compiler_params=pltpu.CompilerParams(
            collective_id=number, has_side_effects=True, vmem_limit_bytes=56 << 20
        ),
        name=name,
    )(*ins)


def shape(dims, dtype=BF):
    return jax.ShapeDtypeStruct(tuple(dims), dtype)


def reduce_scratch(rows, cols, width):
    near_core = [pltpu.VMEM((8, rows, cols), BF)] if width == 16 else []
    return near_core + [
        pltpu.VMEM((4, rows, cols), BF),
        pltpu.VMEM((2, 3, rows, cols), BF),
        pltpu.VMEM((2, 3, rows, cols), BF),
    ]


def gather_blocks(name, number, items, widths, n_ctx):
    k = len(items)

    def body(*refs):
        ins, outs, sems = refs[:k], refs[k : 2 * k], refs[-1]
        place = Place(n_ctx)
        greet(place, line=True, across=16 in widths, core=True)
        net = Net(place, sems)
        run_together(*[gather_steps(net, i, o, w) for i, o, w in zip(ins, outs, widths)])
        net.finish()

    outs = comm_call(
        name,
        number,
        body,
        items,
        [ANY] * k,
        [shape((w,) + i.shape, i.dtype) for i, w in zip(items, widths)],
        [ANY] * k,
        [],
        64 * k,
    )
    return [o.reshape((-1,) + o.shape[2:]) for o in outs]


def reduce_blocks(name, number, items, widths, n_ctx):
    k = len(items)
    blocks = [i.reshape(w, i.shape[0] // w, i.shape[1]) for i, w in zip(items, widths)]

    def body(*refs):
        ins, outs, rest = refs[:k], refs[k : 2 * k], list(refs[2 * k :])
        place = Place(n_ctx)
        greet(place, line=True, across=16 in widths, core=True)
        net = Net(place, rest.pop())
        tasks = []
        for i, o, w in zip(ins, outs, widths):
            near_core = rest.pop(0) if w == 16 else None
            near_x, line_in, line_out = rest.pop(0), rest.pop(0), rest.pop(0)
            tasks.append(
                reduce_steps(net, i, o, near_core, near_x, line_in, line_out, o.shape[0], w)
            )
        run_together(*tasks)
        net.finish()

    scratch = []
    for i, w in zip(blocks, widths):
        scratch += reduce_scratch(i.shape[1], i.shape[2], w)
    return comm_call(
        name,
        number,
        body,
        blocks,
        [VMEM] * k,
        [shape(i.shape[1:], F32) for i in blocks],
        [VMEM] * k,
        scratch,
        64 * k,
    )


def trade_steps(net, src, out, sems, onward=None):
    p = net.place

    def device(i):
        return ((p.g ^ i) * p.members + p.m, p.t)

    keep = pltpu.make_async_copy(src.at[0], out.at[0], net.sem())
    keep.start()
    if onward is not None:
        net.send(lambda: src.at[0], lambda: onward.at[0], sems.at[1, 0], p.other)
    yield
    for i in (4, 5, 6, 7, 2, 3, 1):
        net.send(lambda i=i: src.at[i], lambda i=i: out.at[i], sems.at[0, i], lambda i=i: device(i))
        yield
    for i in (1, 2, 3, 4, 5, 6, 7):
        here = lambda i=i: out.at[i]
        net.recv(here, sems.at[0, i])
        if onward is not None and i < 4:
            net.send(here, lambda i=i: onward.at[i], sems.at[1, i], p.other)
        yield
    if onward is not None:
        for i in range(4):
            net.recv(lambda i=i: onward.at[i], sems.at[1, i])
    keep.wait()


def weights_in(number, down, gains, at, ff, n_ctx):
    def body(
        down_ref, gains_ref, at_ref, ff_ref,
        downs, gain_blocks, heads, near, other_near,
        at_sems, tp_sems, ff_sems, sems,
    ):
        p = Place(n_ctx)
        greet(p, everyone=16, other=True)
        net = Net(p, sems)
        owner = p.d == p.t
        f = p.a * 2 + p.d

        def attention():
            keep = pltpu.make_async_copy(at_ref.at[p.a], heads.at[p.g], net.sem())
            pl.when(owner)(lambda: keep.start())
            for s in range(4):
                net.send(
                    lambda s=s: at_ref.at[s],
                    lambda: heads.at[p.g],
                    at_sems.at[0, f],
                    lambda s=s: p.at(a=s, d=p.t),
                    ~(owner & (p.a == s)),
                )
            pl.when(owner)(lambda: keep.wait())
            yield
            yield
            for q in range(8):
                mine = lambda q=q: heads.at[(q // 2 * 2 + p.b) * 2 + q % 2]
                net.recv(mine, at_sems.at[0, q], owner & (f != q))
                net.send(mine, mine, at_sems.at[1, q], p.across, owner)
                net.send(mine, mine, tp_sems.at[0, q], p.other, owner)
                if q % 2:
                    yield
            for q in range(8):
                theirs = lambda q=q: heads.at[(q // 2 * 2 + 1 - p.b) * 2 + q % 2]
                net.recv(theirs, at_sems.at[1, q], owner)
                net.send(theirs, theirs, tp_sems.at[1, q], p.other, owner)
                if q % 2:
                    yield
            for q in range(8):
                for side in (0, 1):
                    b = 1 - p.b if side else p.b
                    net.recv(
                        lambda: heads.at[(q // 2 * 2 + b) * 2 + q % 2], tp_sems.at[side, q], ~owner
                    )

        run_together(
            gather_steps(net, gains_ref, gain_blocks, 16),
            gather_steps(net, down_ref, downs, 16),
            attention(),
            trade_steps(net, ff_ref, near, ff_sems, other_near),
        )
        net.finish()

    outs = [
        shape((16,) + down.shape),
        shape((16,) + gains.shape, gains.dtype),
        shape((16,) + at.shape[1:]),
        shape((8,) + ff.shape[1:]),
        shape((4,) + ff.shape[1:]),
    ]
    return comm_call(
        "weights_in",
        number,
        body,
        [down, gains, at, ff],
        [ANY] * 4,
        outs,
        [ANY] * 5,
        [pltpu.SemaphoreType.DMA((2, 8))] * 3,
        200,
    )


def head_grads_steps(net, at_ref, at_out, at_x, at_tp, x_sems, rows):
    p = net.place
    owner = p.d == p.t
    f = p.a * 2 + p.d
    for q in range(8):
        net.send(
            lambda q=q: at_ref.at[(q // 2 * 2 + 1 - p.b) * 2 + q % 2],
            lambda q=q: at_x.at[q],
            x_sems.at[0, q],
            p.across,
        )
    yield
    for q in range(8):
        near = at_x.at[q]
        net.recv(lambda: near, x_sems.at[0, q])
        add_into(near, [near, at_ref.at[(q // 2 * 2 + p.b) * 2 + q % 2]], rows)
        net.send(
            lambda near=near: near, lambda q=q: at_tp.at[q], x_sems.at[1, q], p.other, ~owner
        )
        yield
    keep = pltpu.make_async_copy(at_x.at[f], at_out.at[p.a], net.sem())
    for q in range(8):
        near, tp = at_x.at[q], at_tp.at[q]
        net.recv(lambda: tp, x_sems.at[1, q], owner)
        pl.when(owner)(lambda: add_into(near, [near, tp], rows))
        net.send(
            lambda near=near: near,
            lambda: at_out.at[p.a],
            x_sems.at[2, p.a],
            lambda q=q: p.at(a=q // 2, d=q % 2),
            owner & (f != q),
        )
        pl.when(owner & (f == q))(lambda: keep.start())
        yield
    for s in range(4):
        net.recv(lambda s=s: at_out.at[s], x_sems.at[2, s], ~(owner & (p.a == s)))
    pl.when(owner)(lambda: keep.wait())


def plain_call(name, body, ins, outs, scratch, members):
    def whole(array):
        return pl.BlockSpec(array.shape, lambda i, g: (0,) * len(array.shape))

    g = (lax.axis_index("ctx") // members).astype(jnp.int32).reshape(1)
    return pl.pallas_call(
        body,
        out_shape=outs,
        grid_spec=pltpu.PrefetchScalarGridSpec(
            num_scalar_prefetch=1,
            grid=(1,),
            in_specs=[whole(i) for i in ins],
            out_specs=[whole(o) for o in outs],
            scratch_shapes=scratch,
        ),
        compiler_params=pltpu.CompilerParams(vmem_limit_bytes=62 << 20),
        cost_estimate=pl.CostEstimate(
            flops=1_000_000_000, bytes_accessed=20 << 20, transcendentals=0
        ),
        name=name,
    )(g, *ins)


def pack(gate, up, down_t, wide, members):
    rows = gate.shape[0]
    units = gate.shape[1] // 16

    def body(g_ref, gate_ref, up_ref, down_ref, out):
        for n in range(16):
            cut = slice(n * units, (n + 1) * units)
            i = g_ref[0] ^ n
            for k, part in enumerate((gate_ref, up_ref, down_ref)):
                out[i, :, k * units : (k + 1) * units] = part[:, cut]
            out[i, :, 3 * units :] = jnp.zeros((rows, wide - 3 * units), BF)

    return plain_call(
        "pack", body, [gate, up, down_t], [shape((16, rows, wide))], [], members
    )[0]


def feed_forward(ns, gf, own, oth, units, members):
    tokens, dim = ns.shape
    rows, wide = own[0].shape[1:]
    lanes = 256
    both = 2 * lanes
    places = [[(a, k) for a, w in enumerate(side) for k in range(w.shape[0])] for side in (own, oth)]

    def body(g_ref, ns_ref, gf_ref, *refs):
        own_refs, oth_refs = refs[: len(own)], refs[len(own) : len(own) + len(oth)]
        out_ref, gs_ref, gown_ref, goth_ref = refs[len(own) + len(oth) :][:4]
        wgu_ref, wd_ref, hidden_ref, ggu_ref = refs[-4:]
        g = g_ref[0]
        for i in range(16):
            cut = pl.ds(pl.multiple_of((g ^ i) * rows, rows), rows)
            for half, side in enumerate((own_refs, oth_refs)):
                a, k = places[half][i]
                block = side[a][k]
                pad = jnp.zeros((rows, lanes - units), BF)
                for k in range(3):
                    part = jnp.concatenate([block[:, k * units : (k + 1) * units], pad], axis=1)
                    into = wgu_ref if k < 2 else wd_ref
                    at = (both * k if k < 2 else 0) + half * lanes
                    into[cut, at : at + lanes] = part

        def forth(i):
            r = pl.ds(pl.multiple_of(i * 256, 256), 256)
            gate_up = matmul(ns_ref[r], wgu_ref[...])
            gate, up = gate_up[:, :both], gate_up[:, both:]
            grad_hidden = matmul(gf_ref[r], wd_ref[...])
            sigmoid_gate = 1.0 / (1.0 + jnp.exp(-gate))
            silu = gate * sigmoid_gate
            hidden_ref[r] = (silu * up).astype(BF)
            ggu_ref[r, :both] = (
                grad_hidden * up * sigmoid_gate * (1.0 + gate * (1.0 - sigmoid_gate))
            ).astype(BF)
            ggu_ref[r, both:] = (grad_hidden * silu).astype(BF)
            gs_ref[r] = matmul_nt(ggu_ref[r], wgu_ref[...]).astype(BF)
            out_ref[r] = matmul_nt(hidden_ref[r], wd_ref[...]).astype(BF)

        pl.loop(0, tokens // 256)(forth)

        span = dim // 4

        def give(q, k, grads):
            for jj in range(4):
                for half, out in enumerate((gown_ref, goth_ref)):
                    out[g ^ (4 * q + jj), :, k * units : (k + 1) * units] = grads[
                        jj * rows : (jj + 1) * rows, half * lanes : half * lanes + units
                    ].astype(BF)

        for q in range(4):
            cut = slice(q * span, (q + 1) * span)
            grads = matmul_tn(ns_ref[:, cut], ggu_ref[...])
            give(q, 0, grads[:, :both])
            give(q, 1, grads[:, both:])
            give(q, 2, matmul_tn(gf_ref[:, cut], hidden_ref[...]))
        for out in (gown_ref, goth_ref):
            out[:, :, 3 * units :] = jnp.zeros((16, rows, wide - 3 * units), BF)

    return plain_call(
        "feed_forward",
        body,
        [ns, gf, *own, *oth],
        [shape((tokens, dim))] * 2 + [shape((16, rows, wide))] * 2,
        [
            pltpu.VMEM((dim, 2 * both), BF),
            pltpu.VMEM((dim, both), BF),
            pltpu.VMEM((tokens, both), BF),
            pltpu.VMEM((tokens, 2 * both), BF),
        ],
        members,
    )


def spread(parts, units, members):
    rows, cols = parts[0].shape[1:]
    places = [(a, k) for a, w in enumerate(parts) for k in range(w.shape[0])]

    def body(g_ref, *refs):
        hold = refs[-1]
        for i, (a, k) in enumerate(places):
            hold[g_ref[0] ^ i] = refs[a][k].astype(F32)
        for n in range(16):
            for k, out in enumerate(refs[len(parts) : len(parts) + 3]):
                out[:, n * units : (n + 1) * units] = hold[n, :, k * units : (k + 1) * units]

    return plain_call(
        "spread",
        body,
        list(parts),
        [shape((rows, 16 * units), F32)] * 3,
        [pltpu.VMEM((16, rows, cols), F32)],
        members,
    )


def gather_latent(number, pair_block, query_block, column_blocks, n_ctx):
    def body(pair_ref, query_ref, col_ref, pair, pairs, queries, cols, col_sems, sems):
        place = Place(n_ctx)
        p = place
        greet(p, everyone=16, other=True)
        net = Net(p, sems)

        def columns():
            keep = pltpu.make_async_copy(col_ref.at[p.g], cols.at[p.g], net.sem())
            keep.start()
            for k in range(1, 16):
                net.send(
                    lambda k=k: col_ref.at[p.g ^ k],
                    lambda: cols.at[p.g],
                    col_sems.at[k],
                    lambda k=k: ((p.g ^ k) * p.members + p.m, p.t),
                )
            yield
            yield
            yield
            for k in range(1, 16):
                net.recv(lambda k=k: cols.at[p.g ^ k], col_sems.at[k])
            keep.wait()

        def latents():
            sem = net.sem()
            keep = pltpu.make_async_copy(pair_ref, pair.at[p.t], net.sem())
            keep.start()
            net.send(lambda: pair_ref, lambda: pair.at[p.t], sem, p.other)
            yield
            net.recv(lambda: pair.at[1 - p.t], sem)
            keep.wait()
            yield from gather_steps(net, pair, pairs, 16)

        run_together(latents(), gather_steps(net, query_ref, queries, 8), columns())
        net.finish()

    pair_shape = (2,) + pair_block.shape
    return comm_call(
        "gather_latent",
        number,
        body,
        [pair_block, query_block, column_blocks],
        [ANY] * 3,
        [
            shape(pair_shape),
            shape((16,) + pair_shape),
            shape((8,) + query_block.shape),
            shape(column_blocks.shape),
        ],
        [ANY] * 4,
        [pltpu.SemaphoreType.DMA((16,))],
        180,
    )[1:]


def reduce_latent(number, pairs, queries, at, n_ctx):
    def body(
        pairs_ref, queries_ref, at_ref, pair_out, query_out, at_out,
        at_x, at_tp, x_sems, tp_in, *rest,
    ):
        place = Place(n_ctx)
        p = place
        greet(p, everyone=16, other=True)
        rest = list(rest)
        net = Net(p, rest.pop())
        rows = pair_out.shape[0]

        def latents():
            sems = [net.sem() for _ in range(16)]
            for g in range(16):
                net.send(
                    lambda g=g: pairs_ref.at[g, 1 - p.t], lambda g=g: tp_in.at[g], sems[g], p.other
                )
            yield
            for g in range(16):
                net.recv(lambda g=g: tp_in.at[g], sems[g])
                add_into(tp_in.at[g], [tp_in.at[g], pairs_ref.at[g, p.t]], rows)
            yield from reduce_steps(net, tp_in, pair_out, *rest[:4], rows, 16)

        run_together(
            latents(),
            reduce_steps(net, queries_ref, query_out, None, *rest[4:7], query_out.shape[0], 8),
            head_grads_steps(net, at_ref, at_out, at_x, at_tp, x_sems, at.shape[1]),
        )
        net.finish()

    rows, cols = pairs.shape[2:]
    scratch = [
        pltpu.VMEM((8,) + at.shape[1:], BF),
        pltpu.VMEM((8,) + at.shape[1:], BF),
        pltpu.SemaphoreType.DMA((3, 8)),
        pltpu.VMEM((16, rows, cols), BF),
    ]
    scratch += reduce_scratch(rows, cols, 16)
    scratch += reduce_scratch(queries.shape[1], queries.shape[2], 8)
    return comm_call(
        "reduce_latent",
        number,
        body,
        [pairs, queries, at],
        [VMEM] * 3,
        [shape((rows, cols), F32), shape(queries.shape[1:], F32), shape((4,) + at.shape[1:])],
        [VMEM] * 2 + [ANY],
        scratch,
        220,
    )


def finish_blocks(number, block, swaps, gain_blocks, ff, n_ctx):
    k = len(swaps)

    def body(*refs):
        ff_ref, block_ref, ins, gains = refs[0], refs[1], refs[2 : k + 2], refs[k + 2]
        ff_out, blocks, outs = refs[k + 3], refs[k + 4], refs[k + 5 : 2 * k + 5]
        gains_out = refs[2 * k + 5]
        rest = list(refs[2 * k + 6 :])
        ff_sems = rest.pop(0)
        net_sems = rest.pop()
        tp_in = rest.pop(0)
        place = Place(n_ctx)
        greet(place, everyone=16, other=True)
        net = Net(place, net_sems)

        def sums():
            sem = net.sem()
            net.send(lambda: gains, lambda: tp_in, sem, place.other)
            yield
            net.recv(lambda: tp_in, sem)
            pl.loop(0, 16)(
                lambda g: add_into(tp_in.at[g], [tp_in.at[g], gains.at[g]], gains.shape[1])
            )
            yield from reduce_steps(net, tp_in, gains_out, *rest, gains_out.shape[0], 16)

        run_together(
            gather_steps(net, block_ref, blocks, 16),
            sums(),
            *[swap_steps(net, i, o) for i, o in zip(ins, outs)],
            trade_steps(net, ff_ref, ff_out, ff_sems),
        )
        net.finish()

    scratch = [pltpu.SemaphoreType.DMA((2, 8)), pltpu.VMEM(gain_blocks.shape, BF)]
    scratch += reduce_scratch(gain_blocks.shape[1], gain_blocks.shape[2], 16)
    return comm_call(
        "finish_blocks",
        number,
        body,
        [ff, block] + list(swaps) + [gain_blocks],
        [ANY] * (k + 2) + [VMEM],
        [shape(ff.shape), shape((16,) + block.shape)]
        + [shape(s.shape, s.dtype) for s in swaps]
        + [shape(gain_blocks.shape[1:], F32)],
        [ANY] * (k + 2) + [VMEM],
        scratch,
        180,
    )


def norm_factor(values):
    return lax.rsqrt(jnp.mean(values * values, axis=-1, keepdims=True) + eps_norm)


def branch_and_norm(number, parts, x, gain, gf, n_ctx):
    rows, dim = x.shape
    parts = parts.reshape(8, rows, dim)

    def body(
        parts_ref, x_ref, gain_ref, gf_ref,
        middle, norms, gfs,
        branch, normed, near, line_in, line_out, sems,
    ):
        place = Place(n_ctx)
        greet(place, line=True, across=True, core=True)
        net = Net(place, sems)

        def second():
            yield from reduce_steps(
                net, parts_ref, branch, None, near, line_in, line_out, rows, 8
            )

            def norm(r):
                values = x_ref[r] + residual_scale * branch[r]
                middle[r] = values
                normed[r] = (values * norm_factor(values) * gain_ref[...]).astype(BF)

            by_rows(rows, 16, norm)
            yield from gather_steps(net, normed, norms, 16)

        run_together(second(), gather_steps(net, gf_ref, gfs, 16))
        net.finish()

    return comm_call(
        "branch_and_norm",
        number,
        body,
        [parts, x, gain, gf],
        [VMEM] * 3 + [ANY],
        [shape((rows, dim), F32), shape((16, rows, dim)), shape((16, rows, dim))],
        [VMEM, ANY, ANY],
        [pltpu.VMEM((rows, dim), F32), pltpu.VMEM((rows, dim), BF)]
        + reduce_scratch(rows, dim, 8),
        220,
    )


def norm_and_branch_back(number, parts, middle, out_grad, gain, n_ctx):
    rows, dim = middle.shape
    parts = parts.reshape(16, rows, dim)

    def body(
        parts_ref, middle_ref, out_grad_ref, gain_ref,
        grad_middle, gain_part, branches,
        upstream, branch, near_core, near, line_in, line_out, sems,
    ):
        place = Place(n_ctx)
        greet(place, line=True, across=True, core=True)
        net = Net(place, sems)
        run_together(
            reduce_steps(
                net, parts_ref, upstream, near_core, near, line_in, line_out, rows, 16
            )
        )
        gain_part[...] = jnp.zeros((8, dim), F32)

        def back(r):
            values, grads = middle_ref[r], upstream[r]
            factor = norm_factor(values)
            scaled = grads * gain_ref[...]
            inner = jnp.mean(scaled * values, axis=-1, keepdims=True)
            total = out_grad_ref[r] + (
                factor * scaled - values * factor * factor * factor * inner
            )
            grad_middle[r] = total
            branch[r] = (residual_scale * total).astype(BF)
            share = grads * values * factor
            gain_part[...] += share[:8] + share[8:]

        by_rows(rows, 16, back)
        run_together(gather_steps(net, branch, branches, 8))
        net.finish()

    return comm_call(
        "norm_and_branch_back",
        number,
        body,
        [parts, middle, out_grad, gain],
        [VMEM] * 4,
        [shape((rows, dim), F32), shape((8, dim), F32), shape((8, rows, dim))],
        [VMEM, VMEM, ANY],
        [pltpu.VMEM((rows, dim), F32), pltpu.VMEM((rows, dim), BF)]
        + reduce_scratch(rows, dim, 16),
        180,
    )


def turn(values, table, back=False):
    near = pltpu.roll(values, 16, 1) * table[:, 256:384]
    far = pltpu.roll(values, 112, 1) * table[:, 128:256]
    turned = near + far
    return values * table[:, :128] + (-turned if back else turned)


def by_rows(rows, step, body):
    pl.loop(0, rows // step)(lambda i: body(pl.ds(pl.multiple_of(i * step, step), step)))


def lanes_of(h):
    return pl.ds(pl.multiple_of(h * 128, 128), 128)


def key_tile(expanded, ropes):
    lane = lax.broadcasted_iota(jnp.int32, expanded.shape, 1)
    return jnp.where(lane < NOPE, expanded, ropes)


def attend(number, qn, q_up, pairs, l_up, w_out_t, table, q_pos, ff, n_ctx):
    rows, keys, heads = qn.shape[0], pairs.shape[0], q_up.shape[1] // 128
    span, block = keys // 4, rows // 4
    dim = w_out_t.shape[0]

    def body(
        qn_ref, q_up_ref, pairs_ref, l_up_ref, w_ref, table_ref, pos_ref, ff_ref,
        branch_ref, q_ref, o_ref, lse_ref, att_ref, far_ref,
        e_ref, top_ref, sum_ref, acc_ref, sems,
    ):
        copies = trade_away(Place(n_ctx), ff_ref, far_ref, sems, 12)
        by_rows(
            keys,
            256,
            lambda r: e_ref.__setitem__(
                r, matmul(pairs_ref[r, :KVR], l_up_ref[...]).astype(BF)
            ),
        )

        def head(h):
            lanes = lanes_of(h)
            raw = matmul(qn_ref[...], q_up_ref[:, lanes])
            q_ref[:, lanes] = turn(raw, table_ref[...]).astype(BF)
            top_ref[...] = jnp.full(top_ref.shape, -1e30, F32)
            sum_ref[...] = jnp.zeros(sum_ref.shape, F32)
            acc_ref[...] = jnp.zeros(acc_ref.shape, F32)
            for kb in range(4):
                part, cols = slice(kb * block, rows), slice(kb * span, (kb + 1) * span)
                values = e_ref[cols, lanes]
                key = key_tile(values, pairs_ref[cols, KVR:])
                scores = matmul_nt(q_ref[part, lanes], key) * score_scale
                index = lax.broadcasted_iota(jnp.int32, scores.shape, 1) + kb * span
                scores = jnp.where(index <= pos_ref[part, :1], scores, -1e30)
                old = top_ref[part, :1]
                top = jnp.maximum(old, jnp.max(scores, axis=1, keepdims=True))
                weights = jnp.exp(scores - top)
                decay = jnp.exp(old - top)
                total = sum_ref[part, :1] * decay + jnp.sum(weights, axis=1, keepdims=True)
                acc_ref[part] = acc_ref[part] * decay + matmul(weights.astype(BF), values)
                top_ref[part] = jnp.broadcast_to(top, acc_ref[part].shape)
                sum_ref[part] = jnp.broadcast_to(total, acc_ref[part].shape)
            lane = lax.broadcasted_iota(jnp.int32, acc_ref.shape, 1)
            o_ref[:, lanes] = jnp.where(lane < NOPE, 0.0, acc_ref[...] / sum_ref[...])
            lse_ref[:, lanes] = top_ref[...] + jnp.log(sum_ref[...])

        pl.loop(0, heads)(head)
        for h in range(heads):
            att_ref[:, h * VH : (h + 1) * VH] = o_ref[
                :, h * 128 + NOPE : (h + 1) * 128
            ].astype(BF)
        for i in range(dim // 512):
            cut = slice(i * 512, (i + 1) * 512)
            branch_ref[:, cut] = matmul_nt(att_ref[...], w_ref[cut]).astype(BF)
        for copy in copies:
            copy.wait()

    wide = heads * 128
    return pl.pallas_call(
        body,
        out_shape=[
            shape((rows, dim)),
            shape((rows, wide)),
            shape((rows, wide), F32),
            shape((rows, wide), F32),
            shape((rows, heads * VH)),
            shape(ff.shape),
        ],
        in_specs=[VMEM] * 7 + [ANY],
        out_specs=[VMEM] * 5 + [ANY],
        scratch_shapes=[pltpu.VMEM((keys, wide), BF)]
        + [pltpu.VMEM((rows, 128), F32)] * 3
        + [pltpu.SemaphoreType.DMA((2, ff.shape[0]))],
        compiler_params=pltpu.CompilerParams(
            collective_id=number, has_side_effects=True, vmem_limit_bytes=60 << 20
        ),
        cost_estimate=pl.CostEstimate(
            flops=20_000_000_000, bytes_accessed=20 << 20, transcendentals=0
        ),
        name="attend",
    )(qn, q_up, pairs, l_up, w_out_t, table, q_pos, ff)


def attend_back(
    number, gb, qn, q_up, pairs, l_up, w_out_t, table, q_pos, q, o, lse, att, ff, n_ctx
):
    rows, keys, heads = qn.shape[0], pairs.shape[0], q_up.shape[1] // 128
    span, block = keys // 4, rows // 4
    dim, wide = gb.shape[1], heads * 128

    def body(
        gb_ref, qn_ref, q_up_ref, pairs_ref, l_up_ref, w_ref, table_ref, pos_ref,
        q_ref, o_ref, lse_ref, att_ref, ff_ref,
        gp_ref, gqn_ref, gq_up_ref, gl_up_ref, gw_ref, far_ref,
        e_ref, rope_ref, go_ref, gq_ref, dq_ref, inner_ref, sems,
    ):
        copies = trade_away(Place(n_ctx), ff_ref, far_ref, sems, 12)

        def expand(r):
            e_ref[r] = matmul(pairs_ref[r, :KVR], l_up_ref[...]).astype(BF)
            rope_ref[r] = jnp.zeros((256, 128), F32)

        by_rows(keys, 256, expand)
        ga = matmul(gb_ref[...], w_ref[...]).astype(BF)
        for h in range(heads):
            go_ref[:, h * 128 : h * 128 + NOPE] = jnp.zeros((rows, NOPE), BF)
            go_ref[:, h * 128 + NOPE : (h + 1) * 128] = ga[:, h * VH : (h + 1) * VH]
        for i in range(dim // 512):
            cut = slice(i * 512, (i + 1) * 512)
            gw_ref[cut] = matmul_tn(gb_ref[:, cut], att_ref[...]).astype(BF)

        def head(h):
            lanes = lanes_of(h)
            dq_ref[...] = jnp.zeros(dq_ref.shape, F32)
            inner = jnp.sum(
                go_ref[:, lanes].astype(F32) * o_ref[:, lanes], axis=1, keepdims=True
            )
            inner_ref[...] = jnp.broadcast_to(inner, inner_ref.shape)
            for kb in range(4):
                part, cols = slice(kb * block, rows), slice(kb * span, (kb + 1) * span)
                values = e_ref[cols, lanes]
                key = key_tile(values, pairs_ref[cols, KVR:])
                queries, grads = q_ref[part, lanes], go_ref[part, lanes]
                scores = matmul_nt(queries, key) * score_scale
                index = lax.broadcasted_iota(jnp.int32, scores.shape, 1) + kb * span
                probs = jnp.where(
                    index <= pos_ref[part, :1],
                    jnp.exp(scores - lse_ref[part, lanes][:, :1]),
                    0.0,
                )
                grad_probs = matmul_nt(grads, values)
                grad_scores = (probs * (grad_probs - inner_ref[part, :1])).astype(BF)
                dq_ref[part] += matmul(grad_scores, key)
                grad_key = matmul_tn(grad_scores, queries) * score_scale
                grad_value = matmul_tn(probs.astype(BF), grads)
                lane = lax.broadcasted_iota(jnp.int32, grad_key.shape, 1)
                e_ref[cols, lanes] = jnp.where(lane < NOPE, grad_key, grad_value).astype(BF)
                rope_ref[cols] += jnp.where(lane < NOPE, 0.0, grad_key)
            gq_ref[:, lanes] = turn(dq_ref[...] * score_scale, table_ref[...], True).astype(BF)

        pl.loop(0, heads)(head)

        def latents(r):
            gp_ref[r, :KVR] = matmul_nt(e_ref[r], l_up_ref[...]).astype(BF)
            gp_ref[r, KVR:] = rope_ref[r].astype(BF)

        by_rows(keys, 256, latents)
        gl_up_ref[...] = matmul_tn(pairs_ref[:, :KVR], e_ref[...]).astype(BF)
        gq_up_ref[...] = matmul_tn(qn_ref[...], gq_ref[...]).astype(BF)
        gqn_ref[...] = matmul_nt(gq_ref[...], q_up_ref[...]).astype(BF)
        for copy in copies:
            copy.wait()

    return pl.pallas_call(
        body,
        out_shape=[
            shape(pairs.shape),
            shape(qn.shape),
            shape(q_up.shape),
            shape(l_up.shape),
            shape(w_out_t.shape),
            shape(ff.shape),
        ],
        in_specs=[VMEM] * 12 + [ANY],
        out_specs=[VMEM] * 5 + [ANY],
        scratch_shapes=[
            pltpu.VMEM((keys, wide), BF),
            pltpu.VMEM((keys, 128), F32),
            pltpu.VMEM((rows, wide), BF),
            pltpu.VMEM((rows, wide), BF),
            pltpu.VMEM((rows, 128), F32),
            pltpu.VMEM((rows, 128), F32),
            pltpu.SemaphoreType.DMA((2, ff.shape[0])),
        ],
        compiler_params=pltpu.CompilerParams(
            collective_id=number, has_side_effects=True, vmem_limit_bytes=60 << 20
        ),
        cost_estimate=pl.CostEstimate(
            flops=40_000_000_000, bytes_accessed=30 << 20, transcendentals=0
        ),
        name="attend_back",
    )(gb, qn, q_up, pairs, l_up, w_out_t, table, q_pos, q, o, lse, att, ff)


def shards(
    layer_input,
    first_gain,
    query_down,
    query_gain,
    query_up,
    latent_down,
    latent_gain,
    latent_up,
    out_weight,
    second_gain,
    gate_weight,
    up_weight,
    down_weight,
    out_grad,
):
    n_ctx = lax.axis_size("ctx")
    n_tp = lax.axis_size("tp")
    members = n_ctx // 16
    c = lax.axis_index("ctx")
    t = lax.axis_index("tp")
    g = c // members
    b = lax.rem(g // 2, 2)
    d = lax.rem(g, 2)
    member = lax.rem(c, members)
    ctx_rows, dim = layer_input.shape
    rows = ctx_rows // n_tp
    shard_rows = query_down.shape[0]
    qr = query_down.shape[1]
    heads = H // 8
    units = gate_weight.shape[1] // 16
    plane_lists = [[k * members + m for k in range(16)] for m in range(members)]
    member_lists = [[k * members + m for m in range(members)] for k in range(16)]

    def widen(blocks):
        if members == 1:
            return blocks[:, None]
        return lax.all_gather(blocks, "ctx", axis=1, axis_index_groups=member_lists)

    def narrow(blocks):
        if members == 1:
            return blocks[:, 0]
        return lax.psum_scatter(
            blocks.astype(F32), "ctx", scatter_dimension=1, axis_index_groups=member_lists
        ).astype(BF)

    def gather_over(block):
        return lax.all_gather(
            block, "ctx", axis=0, tiled=True, axis_index_groups=plane_lists if members > 1 else None
        )

    def scatter_over(part):
        return lax.psum_scatter(
            part,
            "ctx",
            scatter_dimension=0,
            tiled=True,
            axis_index_groups=plane_lists if members > 1 else None,
        )

    widths = [first_gain.shape[0], query_gain.shape[0], latent_gain.shape[0], second_gain.shape[0]]
    starts = [0, widths[0], widths[0] + widths[1], widths[0] + widths[1] + widths[2]]
    gains = jnp.concatenate([first_gain, query_gain, latent_gain, second_gain]).astype(F32)
    gains = jnp.broadcast_to(gains[None], (8, gains.shape[0]))
    down_shard = jnp.concatenate([query_down, latent_down], axis=1)

    def trade(block, k):
        return lax.ppermute(
            block, "ctx", [(i, (i // members ^ k) * members + i % members) for i in range(n_ctx)]
        )

    def swap_tp(block):
        return lax.ppermute(block, "tp", [(0, 1), (1, 0)])

    wide = 640
    ff = pack(gate_weight, up_weight, down_weight.T, wide, members)
    q_rows_w, l_rows_w, o_rows_w = query_up.shape[0], latent_up.shape[0], shard_rows // 2
    q_width, o_width = heads * (NOPE + ROPE), heads * VH
    q_tiles = jnp.pad(
        query_up.reshape(q_rows_w, 4, heads, NOPE + ROPE),
        ((0, 0), (0, 0), (0, 0), (0, 128 - NOPE - ROPE)),
    ).reshape(q_rows_w, 4, wide)
    out_tiles = jnp.transpose(
        out_weight.reshape(4, o_width, 2, o_rows_w), (0, 3, 2, 1)
    ).reshape(4, o_rows_w, wide)
    at = jnp.concatenate(
        [
            jnp.transpose(q_tiles, (1, 0, 2)),
            jnp.transpose(latent_up.reshape(l_rows_w, 4, wide), (1, 0, 2)),
            out_tiles,
        ],
        axis=1,
    )

    x = lax.dynamic_slice_in_dim(layer_input, t * rows, rows, 0).astype(F32)
    out_grad_rows = lax.dynamic_slice_in_dim(out_grad, t * rows, rows, 0).astype(F32)
    positions = c * ctx_rows + t * rows + jnp.arange(rows, dtype=jnp.int32)
    cosine, sine_table = rope_tables(positions)
    grad_ffn = (residual_scale * out_grad_rows).astype(BF)

    down_full, gains, at_all, own_near, oth_near = weights_in(
        1, down_shard, gains, at, ff, n_ctx
    )
    own_near, ff = lax.optimization_barrier((own_near, ff))
    own_mid = [trade(ff[i : i + 1], i) for i in (8, 9, 10, 11)]
    oth_next = swap_tp(own_near[4:])
    down_full = widen(down_full).reshape(dim, -1)
    gains = widen(gains[:, 0]).reshape(n_ctx, -1)
    gain_first, gain_query, gain_latent, gain_second = [
        gains[:, s : s + w].reshape(-1) for s, w in zip(starts, widths)
    ]
    at_all = widen(at_all).reshape(n_ctx, -1, wide)
    q_up = at_all[:, :q_rows_w].reshape(qr, wide)
    l_up = at_all[:, q_rows_w : q_rows_w + l_rows_w].reshape(KVR, wide)
    w_out_t = jnp.transpose(
        at_all[:, q_rows_w + l_rows_w :].reshape(n_ctx, o_rows_w, 2, o_width), (0, 2, 1, 3)
    ).reshape(dim, o_width)

    normed = rms_norm(x, gain_first).astype(BF)
    both = matmul(normed, down_full)
    query_latent, compressed = both[:, :qr], both[:, qr:]
    query_normed = rms_norm(query_latent, gain_query).astype(BF)
    latent = rms_norm(compressed[:, :KVR], gain_latent).astype(BF)
    key_rope = rotate(compressed[:, KVR:], cosine, sine_table).astype(BF)
    pair_block = jnp.concatenate(
        [latent, jnp.zeros((rows, NOPE), BF), key_rope, jnp.zeros((rows, ROPE), BF)], axis=1
    )
    normed_columns = jnp.transpose(
        normed.reshape(rows, 16, dim // 16), (1, 0, 2)
    )
    pairs, qn_all, token_columns = gather_latent(
        3, pair_block, query_normed, normed_columns, n_ctx
    )
    pairs, own_mid, ff = lax.optimization_barrier((pairs, own_mid, ff))
    own_mid = jnp.concatenate(own_mid)
    oth_mid = swap_tp(own_mid)
    lat_rope = widen(pairs).reshape(-1, 384)
    qn_all = qn_all.reshape(-1, qr)

    block = jnp.arange(8, dtype=jnp.int32)
    block_ctx = ((block // 2 * 2 + b) * 2 + block % 2) * members + member
    q_positions = (
        block_ctx[:, None] * ctx_rows + t * rows + jnp.arange(rows, dtype=jnp.int32)[None, :]
    ).reshape(-1)
    q_cos, q_sin = rope_tables(q_positions)
    none, half = jnp.zeros((q_positions.shape[0], NOPE), F32), jnp.zeros_like(q_cos)
    table = jnp.concatenate(
        [none + 1, q_cos, q_cos, half, half]
        + [none, -q_sin, half, half, half]
        + [none, half, q_sin, half, half],
        axis=1,
    )
    q_pos = jnp.broadcast_to(q_positions[:, None], (q_positions.shape[0], 128))
    branch_part, queries, attended_wide, log_total, attended, own_far = attend(
        5, qn_all, q_up, lat_rope, l_up, w_out_t, table, q_pos, ff[12:], n_ctx
    )

    middle, ns_all, gf_all = branch_and_norm(
        4, branch_part, x, gain_second[None], grad_ffn, n_ctx
    )
    ns_all, gf_all = ns_all.reshape(-1, dim), gf_all.reshape(-1, dim)
    oth_far = swap_tp(own_far)
    own = [own_near, own_mid, own_far]
    oth = [oth_near, oth_next, oth_mid, oth_far]
    ns_all, oth = lax.optimization_barrier((ns_all, oth))
    if members > 1:
        own, oth = [
            [widen(jnp.concatenate(w)).reshape(16, dim // 16, wide)] for w in (own, oth)
        ]
    ffn_part, second_part, grads_own, grads_oth = feed_forward(
        ns_all, gf_all, own, oth, units, members
    )
    grads_own = narrow(grads_own.reshape(16, members, shard_rows, wide))
    grads_oth = narrow(grads_oth.reshape(16, members, shard_rows, wide))
    gots = [swap_tp(grads_oth[12:]), swap_tp(grads_oth[8:12]), swap_tp(grads_oth[:8])]
    grad_middle, second_gain_part, gb_all = norm_and_branch_back(
        6, second_part, middle, out_grad_rows, gain_second[None], n_ctx
    )
    second_gain_part = jnp.sum(second_gain_part, axis=0)
    gb_all = gb_all.reshape(-1, dim)
    gb_all, gots, ffn_part = lax.optimization_barrier((gb_all, gots, ffn_part))
    back_far, back_mid, back_near = [
        (mine.astype(F32) + got.astype(F32)).astype(BF)
        for mine, got in zip((grads_own[12:], grads_own[8:12], grads_own[:8]), gots)
    ]
    ffn_sum = scatter_over(ffn_part).astype(F32)
    out_half = (middle + residual_scale * ffn_sum).astype(BF)
    grad_lat_rope, gqn_part, q_up_part, l_up_part, out_part, sums_far = attend_back(
        7, gb_all, qn_all, q_up, lat_rope, l_up, w_out_t, table, q_pos,
        queries, attended_wide, log_total, attended, back_far, n_ctx,
    )

    at_part = jnp.concatenate(
        [
            q_up_part.reshape(n_ctx, q_rows_w, wide),
            l_up_part.reshape(n_ctx, l_rows_w, wide),
            jnp.transpose(
                out_part.reshape(n_ctx, 2, o_rows_w, o_width), (0, 2, 1, 3)
            ).reshape(n_ctx, o_rows_w, wide),
        ],
        axis=1,
    )
    at_part = narrow(at_part.reshape(16, members, -1, wide))

    own_lat_rope, grad_query_normed, at_sums = reduce_latent(
        8,
        narrow(grad_lat_rope.reshape(16, members, 2, rows, 384)),
        gqn_part.reshape(8, rows, qr),
        at_part,
        n_ctx,
    )
    own_lat_rope, back_mid = lax.optimization_barrier((own_lat_rope, back_mid))
    sums_mid = [trade(back_mid[i : i + 1], 8 + i) for i in range(4)]
    grad_query_latent, query_gain_part = norm_back(query_latent, gain_query, grad_query_normed)
    grad_latent_rows, latent_gain_part = norm_back(
        compressed[:, :KVR], gain_latent, own_lat_rope[:, :KVR]
    )
    grad_both = jnp.concatenate(
        [
            grad_query_latent,
            grad_latent_rows,
            rotate(own_lat_rope[:, KVR + NOPE : KVR + NOPE + ROPE], cosine, -sine_table),
        ],
        axis=1,
    ).astype(BF)
    grad_normed = matmul_nt(grad_both, down_full)
    grad_input_part, first_gain_part = norm_back(x, gain_first, grad_normed)
    input_half = (grad_middle + grad_input_part).astype(BF)
    gain_parts = jnp.concatenate(
        [
            p.reshape(n_ctx, -1)
            for p in (first_gain_part, query_gain_part, latent_gain_part, second_gain_part)
        ],
        axis=1,
    )
    gain_parts = narrow(gain_parts.reshape(16, members, -1)).astype(BF)
    gain_blocks = jnp.pad(gain_parts[:, None], ((0, 0), (0, 15), (0, 0)))
    sums_near, both_all, out_other, input_other, gain_sums = finish_blocks(
        9, grad_both, [out_half, input_half], gain_blocks, back_near, n_ctx
    )
    both_all, sums_mid = lax.optimization_barrier((both_all, sums_mid))
    sums = [sums_near, *sums_mid, sums_far]
    if members == 1:
        down_part = matmul_tn(
            token_columns.reshape(16 * rows, shard_rows), both_all.reshape(16 * rows, -1)
        ).astype(BF)
    else:
        down_part = lax.psum_scatter(
            matmul_tn(normed, grad_both).astype(BF), "ctx", scatter_dimension=0, tiled=True
        )

    down_other = swap_tp(down_part)

    def in_order(mine, other):
        return jnp.where(
            t == 0, jnp.concatenate([mine, other]), jnp.concatenate([other, mine])
        )

    layer_output = in_order(out_half, out_other)
    input_grad = in_order(input_half, input_other).astype(F32)
    down_grads = down_part.astype(F32) + down_other.astype(F32)
    gain_grads = gain_sums[0]
    first_gain_grad, query_gain_grad, latent_gain_grad, second_gain_grad = [
        gain_grads[s : s + w] for s, w in zip(starts, widths)
    ]

    gate_weight_grad, up_weight_grad, down_grad_t = spread(sums, units, members)
    query_up_grad = jnp.transpose(
        at_sums[:, :q_rows_w].reshape(4, q_rows_w, heads, 128)[..., : NOPE + ROPE], (1, 0, 2, 3)
    ).reshape(q_rows_w, 4 * q_width)
    latent_up_grad = jnp.transpose(at_sums[:, q_rows_w : q_rows_w + l_rows_w], (1, 0, 2)).reshape(
        l_rows_w, 4 * wide
    )
    out_weight_grad = jnp.transpose(
        at_sums[:, q_rows_w + l_rows_w :].reshape(4, o_rows_w, 2, o_width), (0, 3, 2, 1)
    ).reshape(4 * o_width, shard_rows)
    return (
        layer_output,
        input_grad,
        first_gain_grad,
        down_grads[:, :qr],
        query_gain_grad,
        query_up_grad.astype(F32),
        down_grads[:, qr:],
        latent_gain_grad,
        latent_up_grad.astype(F32),
        out_weight_grad.astype(F32),
        second_gain_grad,
        gate_weight_grad,
        up_weight_grad,
        down_grad_t.T,
    )


def solution(mesh):
    return jax.shard_map(
        shards,
        mesh=mesh,
        in_specs=(
            P("ctx", None),
            P("ctx"),
            P("ctx", None),
            P("ctx"),
            P("ctx", "tp"),
            P("ctx", None),
            P("ctx"),
            P("ctx", "tp"),
            P("tp", "ctx"),
            P("ctx"),
            P("ctx", "tp"),
            P("ctx", "tp"),
            P("tp", "ctx"),
            P("ctx", None),
        ),
        out_specs=(
            P("ctx", None),
            P("ctx", None),
            P("ctx"),
            P("ctx", None),
            P("ctx"),
            P("ctx", "tp"),
            P("ctx", None),
            P("ctx"),
            P("ctx", "tp"),
            P("tp", "ctx"),
            P("ctx"),
            P("ctx", "tp"),
            P("ctx", "tp"),
            P("tp", "ctx"),
        ),
        check_vma=False,
    )
```

```python
import math

import jax
import jax.numpy as jnp
from jax import lax
from jax.experimental import pallas as pl
from jax.experimental.pallas import tpu as pltpu
from jax.sharding import PartitionSpec as P

BF = jnp.bfloat16
F32 = jnp.float32

H = 40
KVR = 256
NOPE = 64
ROPE = 32
VH = 64

eps_norm = 1e-06
residual_scale = 1.4 / math.sqrt(62.0)
score_scale = (NOPE + ROPE) ** (-0.5)
rope_base = 10000.0


def matmul(left_side, right_side):
    return jnp.dot(left_side, right_side, preferred_element_type=F32)


def matmul_nt(left_side, right_side):
    return lax.dot_general(
        left_side, right_side, (((1,), (1,)), ((), ())), preferred_element_type=F32
    )


def matmul_tn(left_side, right_side):
    return lax.dot_general(
        left_side, right_side, (((0,), (0,)), ((), ())), preferred_element_type=F32
    )


def rms_norm(values, scale_gain):
    factor = lax.rsqrt(jnp.mean(values * values, axis=-1, keepdims=True) + eps_norm)
    return values * factor * scale_gain


def norm_back(values, scale_gain, upstream):
    factor = lax.rsqrt(jnp.mean(values * values, axis=-1, keepdims=True) + eps_norm)
    scaled = upstream * scale_gain
    inner_sum = jnp.mean(scaled * values, axis=-1, keepdims=True)
    grad_values = factor * scaled - values * factor * factor * factor * inner_sum
    grad_gain = jnp.sum(upstream * values * factor, axis=0)
    return (grad_values, grad_gain)


def rotate(values, cosine, sine_table):
    half_width = values.shape[-1] // 2
    first_half = values[..., :half_width]
    second_half = values[..., half_width:]
    return jnp.concatenate(
        [
            first_half * cosine - second_half * sine_table,
            second_half * cosine + first_half * sine_table,
        ],
        axis=-1,
    )


def rope_tables(positions):
    frequency = rope_base ** (-jnp.arange(ROPE // 2, dtype=F32) / (ROPE // 2))
    angles = positions.astype(F32)[:, None] * frequency[None, :]
    return (jnp.cos(angles), jnp.sin(angles))


MESH = pl.DeviceIdType.MESH
OFFSETS = (0, -1, 1, -2, 2, -3, 3)


TRADED_FIRST, TRADED_NEXT, TRADED_LAST = (8, 9, 12, 4, 5, 2, 3, 1), (10, 11, 6, 7), (13, 14, 15)


class Place:
    def __init__(self, n_ctx):
        c = lax.axis_index("ctx")
        self.members = n_ctx // 16
        self.c = c
        self.t = lax.axis_index("tp")
        self.m = lax.rem(c, self.members)
        g = c // self.members
        self.g = g
        self.a, self.b, self.d = g // 4, lax.rem(g // 2, 2), lax.rem(g, 2)

    def at(self, a=None, b=None, d=None):
        a = self.a if a is None else a
        b = self.b if b is None else b
        d = self.d if d is None else d
        return (((a * 2 + b) * 2 + d) * self.members + self.m, self.t)

    def up(self):
        return self.at(a=self.a + 1)

    def down(self):
        return self.at(a=self.a - 1)

    def across(self):
        return self.at(b=1 - self.b)

    def core(self):
        return self.at(d=1 - self.d)

    def other(self):
        return (self.c, 1 - self.t)

    def valid(self, o):
        return None if o == 0 else (self.a + o >= 0 if o < 0 else self.a + o <= 3)


def both_of(p, q):
    if p is None:
        return q
    return p if q is None else p & q


def when(p, body):
    if p is None:
        body()
    else:
        pl.when(p)(body)


class Net:
    def __init__(self, place, sems):
        self.place, self.sems, self.count, self.pending = place, sems, 0, []

    def sem(self):
        self.count += 1
        return self.sems.at[self.count - 1]

    def send(self, src, dst, recv, to, cond=None):
        mine = self.sem()

        def copy():
            return pltpu.make_async_remote_copy(
                src(), dst(), mine, recv, device_id=to(), device_id_type=MESH
            )

        when(cond, lambda: copy().start())
        self.pending.append((cond, lambda: copy().wait_send()))

    def recv(self, dst, sem, cond=None):
        def wait():
            ref = dst()
            pltpu.make_async_remote_copy(
                ref, ref, sem, sem, device_id=self.place.other(), device_id_type=MESH
            ).wait_recv()

        when(cond, wait)

    def finish(self):
        for cond, wait in self.pending:
            when(cond, wait)


def greet(place, line=False, across=False, core=False, other=False, everyone=0):
    barrier = pltpu.get_barrier_semaphore()

    def tell(device):
        pl.semaphore_signal(barrier, inc=1, device_id=device, device_id_type=MESH)

    count = 0
    if everyone:
        for k in range(1, everyone):
            tell((lax.rem(place.c + k * place.members, everyone * place.members), place.t))
        count = count + everyone - 1
    else:
        if line:
            pl.when(place.a < 3)(lambda: tell(place.up()))
            pl.when(place.a > 0)(lambda: tell(place.down()))
            count = count + (place.a < 3).astype(jnp.int32) + (place.a > 0).astype(jnp.int32)
        if across:
            tell(place.across())
            count = count + 1
        if core:
            tell(place.core())
            count = count + 1
    if other:
        tell(place.other())
        count = count + 1
    pl.semaphore_wait(barrier, count)


def trade_away(place, src, out, sems):
    barrier = pltpu.get_barrier_semaphore()
    count = len(TRADED_LAST)
    devices = [((place.g ^ i) * place.members + place.m, place.t) for i in TRADED_LAST]
    for device in devices:
        pl.semaphore_signal(barrier, inc=1, device_id=device, device_id_type=MESH)
    pl.semaphore_wait(barrier, count)
    copies = [
        pltpu.make_async_remote_copy(
            src.at[k],
            out.at[k],
            sems.at[0, k],
            sems.at[1, k],
            device_id=devices[k],
            device_id_type=MESH,
        )
        for k in range(count)
    ]
    for copy in copies:
        copy.start()
    return copies


def gather_steps(net, src, out, width, start, pace):
    p = net.place
    cores = width == 16

    def slot(o, b, d):
        return out.at[((p.a + o) * 2 + b) * 2 + d] if cores else out.at[(p.a + o) * 2 + d]

    z_sem = {o: net.sem() for o in OFFSETS if o}
    x_sem = {o: net.sem() for o in OFFSETS} if cores else {}
    c_sem = {(s, o): net.sem() for s in ((0, 1) if cores else (0,)) for o in OFFSETS}
    own_sem = net.sem()
    keep = pltpu.make_async_copy(src, slot(0, p.b, p.d), own_sem)
    keep.start()

    def forward(o):
        ok = p.valid(o)
        here = lambda: slot(o, p.b, p.d)
        origin = (lambda: src) if o == 0 else here
        if o <= 0 and o > -3:
            net.send(origin, here, z_sem[o - 1], p.up, both_of(ok, p.a < 3))
        if o >= 0 and o < 3:
            net.send(origin, here, z_sem[o + 1], p.down, both_of(ok, p.a > 0))
        if cores:
            net.send(origin, here, x_sem[o], p.across, ok)
        net.send(origin, here, c_sem[0, o], p.core, ok)

    def from_line(o):
        net.recv(lambda: slot(o, p.b, p.d), z_sem[o], p.valid(o))
        forward(o)

    def from_across(o):
        if cores:
            there = lambda: slot(o, 1 - p.b, p.d)
            net.recv(there, x_sem[o], p.valid(o))
            net.send(there, there, c_sem[1, o], p.core, p.valid(o))

    forward(0)
    for near in (1, 2, 3):
        yield start + near * (pace + 2)
        from_line(-near)
        from_line(near)
        yield start + near * (pace + 2) + 0.5
        if near == 1:
            from_across(0)
        else:
            from_across(1 - near)
            from_across(near - 1)
    yield start + 4 * (pace + 2)
    from_across(-3)
    from_across(3)
    yield start + 4 * (pace + 2) + 2
    for o in OFFSETS:
        net.recv(lambda: slot(o, p.b, 1 - p.d), c_sem[0, o], p.valid(o))
        if cores:
            net.recv(lambda: slot(o, 1 - p.b, 1 - p.d), c_sem[1, o], p.valid(o))
    keep.wait()


def add_into(out, terms, rows):
    step = 16 if rows % 16 == 0 else rows

    def body(i):
        part = pl.ds(pl.multiple_of(i * step, step), step)
        total = terms[0][part].astype(F32)
        for term in terms[1:]:
            total = total + term[part].astype(F32)
        out[part] = total.astype(out.dtype)

    pl.loop(0, rows // step)(body)


def reduce_steps(
    net, parts, out, near_core, near_x, line_in, line_out, rows, width, start, pace
):
    p = net.place
    cores = width == 16
    order = (-3, 3, -2, 2, -1, 1, 0)
    if cores:
        c_sem = {(b, o): net.sem() for b in (0, 1) for o in order}
        for o in order:
            for side in (1, 0):
                def src(o=o, side=side):
                    b = 1 - p.b if side else p.b
                    return parts.at[((p.a + o) * 2 + b) * 2 + 1 - p.d]

                def dst(o=o, side=side):
                    b = 1 - p.b if side else p.b
                    return near_core.at[(p.a + o) * 2 + b]

                net.send(src, dst, c_sem[side, o], p.core, p.valid(o))
        yield min(start, 1.0)
    x_sem = {o: net.sem() for o in order}
    up_sem = {o: net.sem() for o in (0, 1, 2)}
    down_sem = {o: net.sem() for o in (0, 1, 2)}

    pair = p.b if cores else p.d

    def mine(o, b):
        g = (p.a + o) * 2 + b
        return near_core.at[g] if cores else parts.at[g]

    for o in order:
        if cores:
            def join(o=o):
                g = (p.a + o) * 2 + 1 - p.b
                add_into(near_core.at[g], [near_core.at[g], parts.at[g * 2 + p.d]], rows)

            net.recv(lambda: near_core.at[(p.a + o) * 2 + 1 - p.b], c_sem[1, o], p.valid(o))
            when(p.valid(o), join)
        net.send(
            lambda o=o: mine(o, 1 - pair),
            lambda o=o: near_x.at[p.a + o],
            x_sem[o],
            p.across if cores else p.core,
            p.valid(o),
        )
    for number, o in enumerate(order):
        yield start + 3 + (number // 2 + 1) * (pace + 0.5)
        ok = p.valid(o)
        if cores:
            net.recv(lambda: near_core.at[(p.a + o) * 2 + p.b], c_sem[0, o], ok)

        def terms(o=o):
            g = (p.a + o) * 2 + pair
            own = [near_core.at[g], parts.at[g * 2 + p.d]] if cores else [parts.at[g]]
            return own + [near_x.at[p.a + o]]

        net.recv(lambda: near_x.at[p.a + o], x_sem[o], ok)
        if o == 0:
            below, above = line_in.at[0, 0], line_in.at[1, 0]
            net.recv(lambda: below, up_sem[0], p.a > 0)
            net.recv(lambda: above, down_sem[0], p.a < 3)
            inner = (p.a > 0) & (p.a < 3)
            pl.when(inner)(lambda: add_into(out, terms() + [below, above], rows))
            pl.when(p.a == 0)(lambda: add_into(out, terms() + [above], rows))
            pl.when(p.a == 3)(lambda: add_into(out, terms() + [below], rows))
            continue
        far = abs(o)
        way = 0 if o > 0 else 1
        stage = line_out.at[way, far - 1]
        sems = up_sem if o > 0 else down_sem
        first = p.a == 0 if o > 0 else p.a == 3
        if far < 3:
            came = line_in.at[way, far]
            later = ok & ~first
            net.recv(lambda: came, sems[far], later)
            pl.when(later)(lambda: add_into(stage, terms() + [came], rows))
            pl.when(ok & first)(lambda: add_into(stage, terms(), rows))
        else:
            pl.when(ok)(lambda: add_into(stage, terms(), rows))
        net.send(
            lambda stage=stage: stage,
            lambda far=far, way=way: line_in.at[way, far - 1],
            sems[far - 1],
            p.up if o > 0 else p.down,
            ok,
        )


def swap_steps(net, src, dst):
    sem = net.sem()
    net.send(lambda: src, lambda: dst, sem, net.place.other)
    yield 90.0
    net.recv(lambda: dst, sem)


def together(*tasks):
    tasks = [[0.0, number, task] for number, task in enumerate(tasks)]
    while tasks:
        first = min(tasks)
        try:
            first[0] = next(first[2])
        except StopIteration:
            tasks.remove(first)
        if tasks:
            yield min(tasks)[0]


def run_together(*tasks):
    for _ in together(*tasks):
        pass


def after(start, task):
    yield start
    yield from task


ANY = pl.BlockSpec(memory_space=pl.ANY)
VMEM = pl.BlockSpec(memory_space=pltpu.VMEM)


def comm_call(name, number, body, ins, in_specs, outs, out_specs, scratch, sems):
    return pl.pallas_call(
        body,
        out_shape=outs,
        in_specs=in_specs,
        out_specs=out_specs,
        scratch_shapes=list(scratch) + [pltpu.SemaphoreType.DMA((sems,))],
        compiler_params=pltpu.CompilerParams(
            collective_id=number, has_side_effects=True, vmem_limit_bytes=56 << 20
        ),
        name=name,
    )(*ins)


def shape(dims, dtype=BF):
    return jax.ShapeDtypeStruct(tuple(dims), dtype)


def reduce_scratch(rows, cols, width):
    near_core = [pltpu.VMEM((8, rows, cols), BF)] if width == 16 else []
    return near_core + [
        pltpu.VMEM((4, rows, cols), BF),
        pltpu.VMEM((2, 3, rows, cols), BF),
        pltpu.VMEM((2, 3, rows, cols), BF),
    ]


def trade_sends(net, block, out, sems, timed):
    p = net.place
    for i, when_to in timed:
        yield when_to
        net.send(
            lambda i=i: block(i),
            lambda i=i: out(i),
            sems.at[i],
            lambda i=i: ((p.g ^ i) * p.members + p.m, p.t),
        )


def trade_receives(net, out, sems, which):
    for i in which:
        net.recv(lambda i=i: out(i), sems.at[i])


def weights_in(number, down, gains, at, ff, n_ctx):
    def body(
        down_ref, gains_ref, at_ref, ff_ref,
        downs, gain_blocks, heads, near,
        at_sems, ff_sems, sems,
    ):
        p = Place(n_ctx)
        greet(p, everyone=16)
        net = Net(p, sems)
        owner = p.d == p.t
        f = p.a * 2 + p.d

        def attention():
            keep = pltpu.make_async_copy(at_ref.at[p.a], heads.at[f], net.sem())
            pl.when(owner)(lambda: keep.start())
            for s in range(4):
                net.send(
                    lambda s=s: at_ref.at[s],
                    lambda: heads.at[f],
                    at_sems.at[f],
                    lambda s=s: p.at(a=s, d=p.t),
                    ~(owner & (p.a == s)),
                )
            yield 50.0
            pl.when(owner)(lambda: keep.wait())
            for q in range(8):
                net.recv(lambda q=q: heads.at[q], at_sems.at[q], owner & (f != q))

        def trades():
            keep = pltpu.make_async_copy(ff_ref.at[0], near.at[0], net.sem())
            keep.start()
            out = lambda i: near.at[1 + TRADED_FIRST.index(i)]
            timed = ((1, 1), (4, 2), (8, 4), (5, 9), (9, 12), (2, 18), (12, 20), (3, 24))
            yield from trade_sends(net, lambda i: ff_ref.at[i], out, ff_sems, timed)
            yield 60.0
            trade_receives(net, out, ff_sems, TRADED_FIRST)
            keep.wait()

        run_together(
            gather_steps(net, gains_ref, gain_blocks, 16, 0, 3),
            gather_steps(net, down_ref, downs, 16, 0, 8),
            after(1.5, attention()),
            trades(),
        )
        net.finish()

    outs = [
        shape((16,) + down.shape),
        shape((16,) + gains.shape, gains.dtype),
        shape((8,) + at.shape[1:]),
        shape((1 + len(TRADED_FIRST),) + ff.shape[1:]),
    ]
    return comm_call(
        "weights_in",
        number,
        body,
        [down, gains, at, ff],
        [ANY] * 4,
        outs,
        [ANY] * 4,
        [pltpu.SemaphoreType.DMA((8,)), pltpu.SemaphoreType.DMA((16,))],
        200,
    )


def head_grads_steps(net, at_ref, at_out, at_x, at_tp, x_sems, tp_sems, rows, start):
    p = net.place
    owner = p.d == p.t
    f = p.a * 2 + p.d
    place = lambda q, side: (q // 2 * 2 + (1 - p.b if side else p.b)) * 2 + q % 2
    for side in (1, 0):
        for q in range(8):
            net.send(
                lambda q=q, side=side: at_ref.at[place(q, side)],
                lambda q=q, side=side: at_tp.at[side, q],
                tp_sems.at[side, q],
                p.other,
                ~owner,
            )
    for q in range(8):
        yield start + 4 + 2 * (q + 1)
        here = at_tp.at[1, q]
        net.recv(lambda: here, tp_sems.at[1, q], owner)
        pl.when(owner)(lambda: add_into(here, [here, at_ref.at[place(q, 1)]], rows))
        net.send(
            lambda here=here: here, lambda q=q: at_x.at[q], x_sems.at[0, q], p.across, owner
        )
    keep = pltpu.make_async_copy(at_tp.at[0, f], at_out.at[p.a], net.sem())
    for q in range(8):
        yield start + 20 + 2 * (q + 1)
        here, near = at_tp.at[0, q], at_x.at[q]
        net.recv(lambda: here, tp_sems.at[0, q], owner)
        net.recv(lambda: near, x_sems.at[0, q], owner)
        pl.when(owner)(lambda: add_into(here, [here, near, at_ref.at[place(q, 0)]], rows))
        net.send(
            lambda here=here: here,
            lambda: at_out.at[p.a],
            x_sems.at[1, p.a],
            lambda q=q: p.at(a=q // 2, d=q % 2),
            owner & (f != q),
        )
        pl.when(owner & (f == q))(lambda: keep.start())
    yield start + 60
    for s in range(4):
        net.recv(lambda s=s: at_out.at[s], x_sems.at[1, s], ~(owner & (p.a == s)))
    pl.when(owner)(lambda: keep.wait())


def plain_call(name, body, ins, outs, scratch, members):
    def whole(array):
        return pl.BlockSpec(array.shape, lambda i, g: (0,) * len(array.shape))

    g = (lax.axis_index("ctx") // members).astype(jnp.int32).reshape(1)
    return pl.pallas_call(
        body,
        out_shape=outs,
        grid_spec=pltpu.PrefetchScalarGridSpec(
            num_scalar_prefetch=1,
            grid=(1,),
            in_specs=[whole(i) for i in ins],
            out_specs=[whole(o) for o in outs],
            scratch_shapes=scratch,
        ),
        compiler_params=pltpu.CompilerParams(vmem_limit_bytes=62 << 20),
        cost_estimate=pl.CostEstimate(
            flops=1_000_000_000, bytes_accessed=20 << 20, transcendentals=0
        ),
        name=name,
    )(g, *ins)


def pack(gate, up, down_t, wide, members):
    rows = gate.shape[0]
    units = gate.shape[1] // 16

    def body(g_ref, gate_ref, up_ref, down_ref, out):
        for n in range(16):
            cut = slice(n * units, (n + 1) * units)
            i = g_ref[0] ^ n
            for k, part in enumerate((gate_ref, up_ref, down_ref)):
                out[i, :, k * units : (k + 1) * units] = part[:, cut]
            out[i, :, 3 * units :] = jnp.zeros((rows, wide - 3 * units), BF)

    return plain_call(
        "pack", body, [gate, up, down_t], [shape((16, rows, wide))], [], members
    )[0]


def feed_forward(ns, gf, own, oth, order, units, members):
    tokens, dim = ns.shape
    rows, wide = own[0].shape[1:]
    lanes = 256
    both = 2 * lanes
    places = [[(a, k) for a, w in enumerate(side) for k in range(w.shape[0])] for side in (own, oth)]

    def body(g_ref, ns_ref, gf_ref, *refs):
        own_refs, oth_refs = refs[: len(own)], refs[len(own) : len(own) + len(oth)]
        out_ref, gs_ref, gown_ref, goth_ref = refs[len(own) + len(oth) :][:4]
        wgu_ref, wd_ref, hidden_ref, ggu_ref = refs[-4:]
        g = g_ref[0]
        for place, i in enumerate(order):
            cut = pl.ds(pl.multiple_of((g ^ i) * rows, rows), rows)
            for half, side in enumerate((own_refs, oth_refs)):
                a, k = places[half][place]
                block = side[a][k]
                pad = jnp.zeros((rows, lanes - units), BF)
                for k in range(3):
                    part = jnp.concatenate([block[:, k * units : (k + 1) * units], pad], axis=1)
                    into = wgu_ref if k < 2 else wd_ref
                    at = (both * k if k < 2 else 0) + half * lanes
                    into[cut, at : at + lanes] = part

        def forth(i):
            r = pl.ds(pl.multiple_of(i * 256, 256), 256)
            gate_up = matmul(ns_ref[r], wgu_ref[...])
            gate, up = gate_up[:, :both], gate_up[:, both:]
            grad_hidden = matmul(gf_ref[r], wd_ref[...])
            sigmoid_gate = 1.0 / (1.0 + jnp.exp(-gate))
            silu = gate * sigmoid_gate
            hidden_ref[r] = (silu * up).astype(BF)
            ggu_ref[r, :both] = (
                grad_hidden * up * sigmoid_gate * (1.0 + gate * (1.0 - sigmoid_gate))
            ).astype(BF)
            ggu_ref[r, both:] = (grad_hidden * silu).astype(BF)
            gs_ref[r] = matmul_nt(ggu_ref[r], wgu_ref[...]).astype(BF)
            out_ref[r] = matmul_nt(hidden_ref[r], wd_ref[...]).astype(BF)

        pl.loop(0, tokens // 256)(forth)

        span = dim // 4

        def give(q, k, grads):
            for jj in range(4):
                for half, out in enumerate((gown_ref, goth_ref)):
                    out[g ^ (4 * q + jj), :, k * units : (k + 1) * units] = grads[
                        jj * rows : (jj + 1) * rows, half * lanes : half * lanes + units
                    ].astype(BF)

        for q in range(4):
            cut = slice(q * span, (q + 1) * span)
            grads = matmul_tn(ns_ref[:, cut], ggu_ref[...])
            give(q, 0, grads[:, :both])
            give(q, 1, grads[:, both:])
            give(q, 2, matmul_tn(gf_ref[:, cut], hidden_ref[...]))
        for out in (gown_ref, goth_ref):
            out[:, :, 3 * units :] = jnp.zeros((16, rows, wide - 3 * units), BF)

    return plain_call(
        "feed_forward",
        body,
        [ns, gf, *own, *oth],
        [shape((tokens, dim))] * 2 + [shape((16, rows, wide))] * 2,
        [
            pltpu.VMEM((dim, 2 * both), BF),
            pltpu.VMEM((dim, both), BF),
            pltpu.VMEM((tokens, both), BF),
            pltpu.VMEM((tokens, 2 * both), BF),
        ],
        members,
    )


def spread(parts, units, members):
    rows, cols = parts[0].shape[1:]
    places = [(a, k) for a, w in enumerate(parts) for k in range(w.shape[0])]

    def body(g_ref, *refs):
        hold = refs[-1]
        for i, (a, k) in enumerate(places):
            hold[g_ref[0] ^ i] = refs[a][k].astype(F32)
        for n in range(16):
            for k, out in enumerate(refs[len(parts) : len(parts) + 3]):
                out[:, n * units : (n + 1) * units] = hold[n, :, k * units : (k + 1) * units]

    return plain_call(
        "spread",
        body,
        list(parts),
        [shape((rows, 16 * units), F32)] * 3,
        [pltpu.VMEM((16, rows, cols), F32)],
        members,
    )


def project(number, x, down, gains, cosine, sine_table, ff, heads_in, n_ctx):
    rows, dim = x.shape
    wide = down.shape[1]
    qr = wide - KVR - 128
    cols = dim // 16

    def body(
        x_ref, down_ref, g1_ref, gq_ref, gl_ref, cos_ref, sin_ref, ff_ref, heads_ref,
        both, pair, pairs, queries, columns, mid, heads,
        normed, column_blocks, pair_block, query_block,
        col_sems, ff_sems, x_sems, tp_sems, sems,
    ):
        p = Place(n_ctx)
        greet(p, everyone=16, other=True)
        net = Net(p, sems)
        owner = p.d == p.t
        place = lambda q, side: (q // 2 * 2 + (1 - p.b if side else p.b)) * 2 + q % 2
        keep_heads = [net.sem() for _ in range(8)]

        def keep_head(q):
            return pltpu.make_async_copy(heads_ref.at[q], heads.at[place(q, 0)], keep_heads[q])

        def send_head(q, sems_of, to):
            net.send(
                lambda: heads_ref.at[q], lambda: heads.at[place(q, 0)], sems_of.at[q], to, owner
            )

        for q in range(8):
            send_head(q, x_sems, p.across)

        def spread_heads():
            yield 9.5
            for q in range(8):
                pl.when(owner)(lambda: keep_head(q).start())
                send_head(q, tp_sems.at[0], p.other)
            for q in range(8):
                yield 16.0 + 2 * q
                theirs = lambda q=q: heads.at[place(q, 1)]
                net.recv(theirs, x_sems.at[q], owner)
                net.send(theirs, theirs, tp_sems.at[1, q], p.other, owner)
            yield 60.0
            for q in range(8):
                for side in (0, 1):
                    net.recv(lambda: heads.at[place(q, side)], tp_sems.at[side, q], ~owner)
                pl.when(owner)(lambda: keep_head(q).wait())

        out = lambda i: mid.at[TRADED_NEXT.index(i)]
        run_together(trade_sends(net, lambda i: ff_ref.at[i], out, ff_sems, ((10, 0), (6, 0))))
        values = x_ref[...]
        normed[...] = (values * norm_factor(values) * g1_ref[...]).astype(BF)
        both[...] = matmul(normed[...], down_ref[...])
        query, latent = both[:, :qr], both[:, qr : qr + KVR]
        query_block[...] = (query * norm_factor(query) * gq_ref[...]).astype(BF)
        pair_block[:, :KVR] = (latent * norm_factor(latent) * gl_ref[...]).astype(BF)
        pair_block[:, KVR:] = turn(both[:, qr + KVR :], cos_ref[...], sin_ref[...]).astype(BF)

        def send_columns():
            for n in range(16):
                column_blocks[n] = normed[:, n * cols : (n + 1) * cols]
            keep = pltpu.make_async_copy(column_blocks.at[p.g], columns.at[p.g], net.sem())
            keep.start()
            for k in range(1, 16):
                if k % 4 == 1:
                    yield 13.0 + k
                net.send(
                    lambda k=k: column_blocks.at[p.g ^ k],
                    lambda: columns.at[p.g],
                    col_sems.at[k],
                    lambda k=k: ((p.g ^ k) * p.members + p.m, p.t),
                )
            yield 50.0
            for k in range(1, 16):
                net.recv(lambda k=k: columns.at[p.g ^ k], col_sems.at[k])
            keep.wait()

        def latents():
            sem = net.sem()
            keep = pltpu.make_async_copy(pair_block, pair.at[p.t], net.sem())
            keep.start()
            net.send(lambda: pair_block, lambda: pair.at[p.t], sem, p.other)
            yield 11.0
            net.recv(lambda: pair.at[1 - p.t], sem)
            keep.wait()
            yield from gather_steps(net, pair, pairs, 16, 12, 2.2)

        run_together(
            latents(),
            gather_steps(net, query_block, queries, 8, 9, 2.2),
            after(9.0, send_columns()),
            spread_heads(),
            trade_sends(net, lambda i: ff_ref.at[i], out, ff_sems, ((7, 20), (11, 22))),
        )
        trade_receives(net, out, ff_sems, TRADED_NEXT)
        net.finish()

    return comm_call(
        "project",
        number,
        body,
        [x, down, *gains, cosine, sine_table, ff, heads_in],
        [VMEM] * 7 + [ANY] * 2,
        [
            shape((rows, wide), F32),
            shape((2, rows, KVR + 128)),
            shape((16, 2, rows, KVR + 128)),
            shape((8, rows, qr)),
            shape((16, rows, cols)),
            shape((len(TRADED_NEXT),) + ff.shape[1:]),
            shape((16,) + heads_in.shape[1:]),
        ],
        [VMEM] + [ANY] * 6,
        [
            pltpu.VMEM((rows, dim), BF),
            pltpu.VMEM((16, rows, cols), BF),
            pltpu.VMEM((rows, KVR + 128), BF),
            pltpu.VMEM((rows, qr), BF),
            pltpu.SemaphoreType.DMA((16,)),
            pltpu.SemaphoreType.DMA((16,)),
            pltpu.SemaphoreType.DMA((8,)),
            pltpu.SemaphoreType.DMA((2, 8)),
        ],
        240,
    )


def norm_back_rows(values, gain, upstream):
    factor = norm_factor(values)
    scaled = upstream * gain
    inner = jnp.mean(scaled * values, axis=-1, keepdims=True)
    share = upstream * values * factor
    total = share[:8]
    for i in range(1, share.shape[0] // 8):
        total = total + share[8 * i : 8 * i + 8]
    return factor * scaled - values * factor * factor * factor * inner, total


def wind_up(
    number, pairs, queries, at, both, x, grad_middle, down, gains, second, cosine, sine_table,
    ff_own, ff_got, widths, n_ctx,
):
    rows, dim = x.shape
    wide = down.shape[1]
    qr = wide - KVR - 128
    members = n_ctx // 16
    unit_rows = ff_own.shape[1]
    traded = TRADED_FIRST + TRADED_NEXT

    def body(
        pairs_ref, queries_ref, at_ref, both_ref, x_ref, middle_ref, down_ref,
        g1_ref, gq_ref, gl_ref, second_ref, cos_ref, sin_ref, own_ref, got_ref,
        at_out, ff_out, both_all, input_half, input_other, gains_out,
        ff_sum, at_x, at_tp, tp_in, pair_sum, query_sum, grad_both, gain_blocks, gain_tp,
        *rest,
    ):
        p = Place(n_ctx)
        greet(p, everyone=16, other=True)
        rest = list(rest)
        net = Net(p, rest.pop())
        tp_sems, x_sems, ff_sems, pair_sems = [rest.pop() for _ in range(4)]

        def latents():
            for g in range(16):
                net.send(
                    lambda g=g: pairs_ref.at[g, 1 - p.t],
                    lambda g=g: tp_in.at[g],
                    pair_sems.at[g],
                    p.other,
                )
            for g in range(16):
                yield 3.0 + 1.1 * (g + 1)
                net.recv(lambda g=g: tp_in.at[g], pair_sems.at[g])
                add_into(tp_in.at[g], [tp_in.at[g], pairs_ref.at[g, p.t]], rows)
            yield from reduce_steps(net, tp_in, pair_sum, *rest[:4], rows, 16, 21, 1.1)

        def trades():
            timed = (
                ((8, 1), (2, 2), (4, 3), (3, 6), (9, 10), (5, 12), (12, 19), (6, 22), (1, 23))
                + ((7, 26), (10, 28), (11, 37))
            )
            for i, when_to in timed:
                yield when_to
                add_into(ff_sum.at[i], [got_ref.at[i], own_ref.at[i]], unit_rows)
                yield from trade_sends(
                    net, lambda i: ff_sum.at[i], lambda i: ff_out.at[i], ff_sems, ((i, when_to),)
                )
            add_into(ff_sum.at[0], [got_ref.at[0], own_ref.at[0]], unit_rows)
            keep = pltpu.make_async_copy(ff_sum.at[0], ff_out.at[0], net.sem())
            keep.start()
            yield 95.0
            trade_receives(net, lambda i: ff_out.at[i], ff_sems, traded)
            keep.wait()

        def gain_sums():
            sem = net.sem()
            net.send(lambda: gain_blocks, lambda: gain_tp, sem, p.other)
            yield 52.0
            net.recv(lambda: gain_tp, sem)
            pl.loop(0, 16)(lambda g: add_into(gain_tp.at[g], [gain_tp.at[g], gain_blocks.at[g]], 16))
            yield from reduce_steps(net, gain_tp, gains_out, *rest[7:11], 16, 16, 53, 2)

        def chain():
            yield from together(
                latents(),
                reduce_steps(net, queries_ref, query_sum, None, *rest[4:7], rows, 8, 0, 2.2),
            )
            query_back, query_share = norm_back_rows(
                both_ref[:, :qr], gq_ref[...], query_sum[...]
            )
            grad_both[:, :qr] = query_back.astype(BF)
            latent_back, latent_share = norm_back_rows(
                both_ref[:, qr : qr + KVR], gl_ref[...], pair_sum[:, :KVR]
            )
            grad_both[:, qr : qr + KVR] = latent_back.astype(BF)
            grad_both[:, qr + KVR :] = turn(
                pair_sum[:, KVR:], cos_ref[...], sin_ref[...], True
            ).astype(BF)

            gather = gather_steps(net, grad_both, both_all, 16, 38, 3.3)
            next(gather)
            input_back, input_share = norm_back_rows(
                x_ref[...], g1_ref[...], matmul_nt(grad_both[...], down_ref[...])
            )
            input_half[...] = (middle_ref[...] + input_back).astype(BF)
            swap = swap_steps(net, input_half, input_other)
            next(swap)
            shares = [
                jnp.sum(share, axis=0, keepdims=True)
                for share in (input_share, query_share, latent_share, second_ref[...])
            ]
            for n in range(16):
                parts = []
                for m in range(members):
                    for share, w in zip(shares, widths):
                        at_lane = (n * members + m) * w
                        parts.append(share[:, at_lane : at_lane + w])
                row = jnp.concatenate(parts, axis=1)
                gain_blocks[n] = jnp.broadcast_to(row, gain_blocks.shape[1:]).astype(BF)
            yield from together(gather, gain_sums(), swap)

        run_together(
            chain(),
            after(
                0.5,
                head_grads_steps(
                    net, at_ref, at_out, at_x, at_tp, x_sems, tp_sems, at.shape[1], 17
                ),
            ),
            trades(),
        )
        net.finish()

    lanes = pairs.shape[3]
    gain_lanes = members * sum(widths)
    scratch = [
        pltpu.VMEM((13,) + ff_own.shape[1:], BF),
        pltpu.VMEM((8,) + at.shape[1:], BF),
        pltpu.VMEM((2, 8) + at.shape[1:], BF),
        pltpu.VMEM((16, rows, lanes), BF),
        pltpu.VMEM((rows, lanes), F32),
        pltpu.VMEM((rows, qr), F32),
        pltpu.VMEM((rows, wide), BF),
        pltpu.VMEM((16, 16, gain_lanes), BF),
        pltpu.VMEM((16, 16, gain_lanes), BF),
    ]
    scratch += reduce_scratch(rows, lanes, 16) + reduce_scratch(rows, qr, 8)
    scratch += reduce_scratch(16, gain_lanes, 16)
    scratch += [
        pltpu.SemaphoreType.DMA((16,)),
        pltpu.SemaphoreType.DMA((16,)),
        pltpu.SemaphoreType.DMA((2, 8)),
        pltpu.SemaphoreType.DMA((2, 8)),
    ]
    return comm_call(
        "wind_up",
        number,
        body,
        [pairs, queries, at, both, x, grad_middle, down, *gains, second, cosine, sine_table]
        + [ff_own, ff_got],
        [VMEM] * 15,
        [
            shape((4,) + at.shape[1:]),
            shape((13,) + ff_own.shape[1:]),
            shape((16, rows, wide)),
            shape((rows, dim)),
            shape((rows, dim)),
            shape((16, gain_lanes), F32),
        ],
        [ANY, ANY, ANY, VMEM, ANY, VMEM],
        scratch,
        260,
    )


def norm_factor(values):
    return lax.rsqrt(jnp.mean(values * values, axis=-1, keepdims=True) + eps_norm)


def branch_and_norm(number, parts, x, gain, gf, n_ctx):
    rows, dim = x.shape
    parts = parts.reshape(8, rows, dim)

    def body(
        parts_ref, x_ref, gain_ref, gf_ref,
        middle, norms, gfs,
        branch, normed, near, line_in, line_out, sems,
    ):
        place = Place(n_ctx)
        greet(place, line=True, across=True, core=True)
        net = Net(place, sems)

        def second():
            yield from reduce_steps(
                net, parts_ref, branch, None, near, line_in, line_out, rows, 8, 0, 7
            )

            def norm(r):
                values = x_ref[r] + residual_scale * branch[r]
                middle[r] = values
                normed[r] = (values * norm_factor(values) * gain_ref[...]).astype(BF)

            by_rows(rows, 16, norm)
            yield from gather_steps(net, normed, norms, 16, 32, 7)

        run_together(second(), after(0.5, gather_steps(net, gf_ref, gfs, 16, 0, 11)))
        net.finish()

    return comm_call(
        "branch_and_norm",
        number,
        body,
        [parts, x, gain, gf],
        [VMEM] * 3 + [ANY],
        [shape((rows, dim), F32), shape((16, rows, dim)), shape((16, rows, dim))],
        [VMEM, ANY, ANY],
        [pltpu.VMEM((rows, dim), F32), pltpu.VMEM((rows, dim), BF)]
        + reduce_scratch(rows, dim, 8),
        220,
    )


def norm_and_branch_back(number, parts, ffn_parts, middle, out_grad, gain, n_ctx):
    rows, dim = middle.shape
    parts, ffn_parts = parts.reshape(16, rows, dim), ffn_parts.reshape(16, rows, dim)

    def body(
        parts_ref, ffn_ref, middle_ref, out_grad_ref, gain_ref,
        grad_middle, gain_part, branches, output,
        upstream, branch, ffn_sum, *rest,
    ):
        place = Place(n_ctx)
        greet(place, line=True, across=True, core=True)
        net = Net(place, rest[-1])

        def chain():
            yield from reduce_steps(net, parts_ref, upstream, *rest[:4], rows, 16, 0, 7)
            gain_part[...] = jnp.zeros((8, dim), F32)

            def back(r):
                grads, share = norm_back_rows(middle_ref[r], gain_ref[...], upstream[r])
                total = out_grad_ref[r] + grads
                grad_middle[r] = total
                branch[r] = (residual_scale * total).astype(BF)
                gain_part[...] += share

            by_rows(rows, 16, back)
            yield from gather_steps(net, branch, branches, 8, 38, 7)

        run_together(
            chain(), after(0.5, reduce_steps(net, ffn_ref, ffn_sum, *rest[4:8], rows, 16, 28, 7))
        )
        output[...] = (middle_ref[...] + residual_scale * ffn_sum[...]).astype(BF)
        net.finish()

    return comm_call(
        "norm_and_branch_back",
        number,
        body,
        [parts, ffn_parts, middle, out_grad, gain],
        [VMEM] * 5,
        [
            shape((rows, dim), F32),
            shape((8, dim), F32),
            shape((8, rows, dim)),
            shape((rows, dim)),
        ],
        [VMEM, VMEM, ANY, VMEM],
        [
            pltpu.VMEM((rows, dim), F32),
            pltpu.VMEM((rows, dim), BF),
            pltpu.VMEM((rows, dim), F32),
        ]
        + reduce_scratch(rows, dim, 16) * 2,
        240,
    )


def turn(values, cosine, sine_table, back=False):
    lane = lax.broadcasted_iota(jnp.int32, values.shape, 1)
    near = jnp.where((lane >= 80) & (lane < 96), pltpu.roll(values, 16, 1), 0.0)
    far = jnp.where((lane >= 64) & (lane < 80), pltpu.roll(values, 112, 1), 0.0)
    turned = (near - far) * sine_table
    kept = values * jnp.where(lane < 64, 1.0, jnp.where(lane < 96, cosine, 0.0))
    return kept - turned if back else kept + turned


def unpack_heads(at_ref, q_up_ref, l_up_ref, w_ref, q_rows, l_rows):
    o_rows, width = w_ref.shape[0] // 32, w_ref.shape[1]
    first = q_rows + l_rows
    for n in range(16):
        q_up_ref[n * q_rows : (n + 1) * q_rows] = at_ref[n, :q_rows]
        l_up_ref[n * l_rows : (n + 1) * l_rows] = at_ref[n, q_rows:first]
        for half in (0, 1):
            row = (2 * n + half) * o_rows
            w_ref[row : row + o_rows] = at_ref[n, first:, half * width : (half + 1) * width]


def by_rows(rows, step, body):
    pl.loop(0, rows // step)(lambda i: body(pl.ds(pl.multiple_of(i * step, step), step)))


def lanes_of(h):
    return pl.ds(pl.multiple_of(h * 128, 128), 128)


def key_tile(expanded, ropes):
    lane = lax.broadcasted_iota(jnp.int32, expanded.shape, 1)
    return jnp.where(lane < NOPE, expanded, ropes)


def attend(number, qn, at, pairs, cosine, sine_table, q_pos, ff, width, n_ctx):
    rows, keys, heads = qn.shape[0], pairs.shape[0], at.shape[2] // 128
    span, block = keys // 4, rows // 4
    q_rows, l_rows = qn.shape[1] // 16, KVR // 16
    dim = (at.shape[1] - q_rows - l_rows) * 32

    def body(
        qn_ref, at_ref, pairs_ref, cos_ref, sin_ref, pos_ref, ff_ref,
        branch_ref, q_ref, o_ref, lse_ref, att_ref, q_up_ref, l_up_ref, w_ref, far_ref,
        e_ref, top_ref, sum_ref, acc_ref, sems,
    ):
        copies = trade_away(Place(n_ctx), ff_ref.at[pl.ds(13, 3)], far_ref, sems)
        unpack_heads(at_ref, q_up_ref, l_up_ref, w_ref, q_rows, l_rows)
        by_rows(
            keys,
            256,
            lambda r: e_ref.__setitem__(
                r, matmul(pairs_ref[r, :KVR], l_up_ref[...]).astype(BF)
            ),
        )

        def head(h):
            lanes = lanes_of(h)
            raw = matmul(qn_ref[...], q_up_ref[:, lanes])
            q_ref[:, lanes] = turn(raw, cos_ref[...], sin_ref[...]).astype(BF)
            top_ref[...] = jnp.full(top_ref.shape, -1e30, F32)
            sum_ref[...] = jnp.zeros(sum_ref.shape, F32)
            acc_ref[...] = jnp.zeros(acc_ref.shape, F32)
            for kb in range(4):
                part, cols = slice(kb * block, rows), slice(kb * span, (kb + 1) * span)
                values = e_ref[cols, lanes]
                key = key_tile(values, pairs_ref[cols, KVR:])
                scores = matmul_nt(q_ref[part, lanes], key) * score_scale
                index = lax.broadcasted_iota(jnp.int32, scores.shape, 1) + kb * span
                scores = jnp.where(index <= pos_ref[part, :1], scores, -1e30)
                old = top_ref[part, :1]
                top = jnp.maximum(old, jnp.max(scores, axis=1, keepdims=True))
                weights = jnp.exp(scores - top)
                decay = jnp.exp(old - top)
                total = sum_ref[part, :1] * decay + jnp.sum(weights, axis=1, keepdims=True)
                acc_ref[part] = acc_ref[part] * decay + matmul(weights.astype(BF), values)
                top_ref[part] = jnp.broadcast_to(top, acc_ref[part].shape)
                sum_ref[part] = jnp.broadcast_to(total, acc_ref[part].shape)
            lane = lax.broadcasted_iota(jnp.int32, acc_ref.shape, 1)
            o_ref[:, lanes] = jnp.where(lane < NOPE, 0.0, acc_ref[...] / sum_ref[...])
            lse_ref[:, lanes] = top_ref[...] + jnp.log(sum_ref[...])

        pl.loop(0, heads)(head)
        for h in range(heads):
            att_ref[:, h * VH : (h + 1) * VH] = o_ref[
                :, h * 128 + NOPE : (h + 1) * 128
            ].astype(BF)
        for i in range(dim // 512):
            cut = slice(i * 512, (i + 1) * 512)
            branch_ref[:, cut] = matmul_nt(att_ref[...], w_ref[cut]).astype(BF)
        for copy in copies:
            copy.wait()

    wide = heads * 128
    return pl.pallas_call(
        body,
        out_shape=[
            shape((rows, dim)),
            shape((rows, wide)),
            shape((rows, wide), F32),
            shape((rows, wide), F32),
            shape((rows, heads * VH)),
            shape((qn.shape[1], wide)),
            shape((KVR, wide)),
            shape((dim, width)),
            shape((3,) + ff.shape[1:]),
        ],
        in_specs=[VMEM] * 6 + [ANY],
        out_specs=[VMEM] * 8 + [ANY],
        scratch_shapes=[pltpu.VMEM((keys, wide), BF)]
        + [pltpu.VMEM((rows, 128), F32)] * 3
        + [pltpu.SemaphoreType.DMA((2, 3))],
        compiler_params=pltpu.CompilerParams(
            collective_id=number, has_side_effects=True, vmem_limit_bytes=60 << 20
        ),
        cost_estimate=pl.CostEstimate(
            flops=20_000_000_000, bytes_accessed=20 << 20, transcendentals=0
        ),
        name="attend",
    )(qn, at, pairs, cosine, sine_table, q_pos, ff)


def attend_back(
    number, gb, qn, q_up, pairs, l_up, w_out_t, cosine, sine_table, q_pos, q, o, lse, att,
    ff_own, ff_got, n_ctx,
):
    rows, keys, heads = qn.shape[0], pairs.shape[0], q_up.shape[1] // 128
    span, block = keys // 4, rows // 4
    dim, wide = gb.shape[1], heads * 128
    q_rows, l_rows, o_rows, width = qn.shape[1] // 16, KVR // 16, dim // 32, att.shape[1]
    first = q_rows + l_rows
    unit_rows = ff_own.shape[1]

    def body(
        gb_ref, qn_ref, q_up_ref, pairs_ref, l_up_ref, w_ref, cos_ref, sin_ref, pos_ref,
        q_ref, o_ref, lse_ref, att_ref, own_ref, got_ref,
        gp_ref, gqn_ref, at_ref, far_ref,
        e_ref, rope_ref, go_ref, gq_ref, dq_ref, inner_ref, mine_ref, theirs_ref, sems, load_sems,
    ):
        loads = [
            pltpu.make_async_copy(part.at[pl.ds(13, 3)], hold, load_sems.at[i])
            for i, (part, hold) in enumerate(((own_ref, mine_ref), (got_ref, theirs_ref)))
        ]
        for load in loads:
            load.start()
        for load in loads:
            load.wait()
        for k in range(3):
            add_into(mine_ref.at[k], [mine_ref.at[k], theirs_ref.at[k]], unit_rows)
        copies = trade_away(Place(n_ctx), mine_ref, far_ref, sems)

        def expand(r):
            e_ref[r] = matmul(pairs_ref[r, :KVR], l_up_ref[...]).astype(BF)
            rope_ref[r] = jnp.zeros((256, 128), F32)

        by_rows(keys, 256, expand)
        ga = matmul(gb_ref[...], w_ref[...]).astype(BF)
        for h in range(heads):
            go_ref[:, h * 128 : h * 128 + NOPE] = jnp.zeros((rows, NOPE), BF)
            go_ref[:, h * 128 + NOPE : (h + 1) * 128] = ga[:, h * VH : (h + 1) * VH]
        for i in range(4):
            part = matmul_tn(gb_ref[:, i * dim // 4 : (i + 1) * dim // 4], att_ref[...]).astype(BF)
            for k in range(8):
                half = k % 2
                at_ref[4 * i + k // 2, first:, half * width : (half + 1) * width] = part[
                    k * o_rows : (k + 1) * o_rows
                ]

        def head(h):
            lanes = lanes_of(h)
            dq_ref[...] = jnp.zeros(dq_ref.shape, F32)
            inner = jnp.sum(
                go_ref[:, lanes].astype(F32) * o_ref[:, lanes], axis=1, keepdims=True
            )
            inner_ref[...] = jnp.broadcast_to(inner, inner_ref.shape)
            for kb in range(4):
                part, cols = slice(kb * block, rows), slice(kb * span, (kb + 1) * span)
                values = e_ref[cols, lanes]
                key = key_tile(values, pairs_ref[cols, KVR:])
                queries, grads = q_ref[part, lanes], go_ref[part, lanes]
                scores = matmul_nt(queries, key) * score_scale
                index = lax.broadcasted_iota(jnp.int32, scores.shape, 1) + kb * span
                probs = jnp.where(
                    index <= pos_ref[part, :1],
                    jnp.exp(scores - lse_ref[part, lanes][:, :1]),
                    0.0,
                )
                grad_probs = matmul_nt(grads, values)
                grad_scores = (probs * (grad_probs - inner_ref[part, :1])).astype(BF)
                dq_ref[part] += matmul(grad_scores, key)
                grad_key = matmul_tn(grad_scores, queries) * score_scale
                grad_value = matmul_tn(probs.astype(BF), grads)
                lane = lax.broadcasted_iota(jnp.int32, grad_key.shape, 1)
                e_ref[cols, lanes] = jnp.where(lane < NOPE, grad_key, grad_value).astype(BF)
                rope_ref[cols] += jnp.where(lane < NOPE, 0.0, grad_key)
            gq_ref[:, lanes] = turn(
                dq_ref[...] * score_scale, cos_ref[...], sin_ref[...], True
            ).astype(BF)

        pl.loop(0, heads)(head)

        def latents(r):
            gp_ref[r, :KVR] = matmul_nt(e_ref[r], l_up_ref[...]).astype(BF)
            gp_ref[r, KVR:] = rope_ref[r].astype(BF)

        by_rows(keys, 256, latents)
        gl_up = matmul_tn(pairs_ref[:, :KVR], e_ref[...]).astype(BF)
        gq_up = matmul_tn(qn_ref[...], gq_ref[...]).astype(BF)
        for n in range(16):
            at_ref[n, :q_rows] = gq_up[n * q_rows : (n + 1) * q_rows]
            at_ref[n, q_rows:first] = gl_up[n * l_rows : (n + 1) * l_rows]
        gqn_ref[...] = matmul_nt(gq_ref[...], q_up_ref[...]).astype(BF)
        for copy in copies:
            copy.wait()

    return pl.pallas_call(
        body,
        out_shape=[
            shape(pairs.shape),
            shape(qn.shape),
            shape((16, first + o_rows, wide)),
            shape((3,) + ff_own.shape[1:]),
        ],
        in_specs=[VMEM] * 13 + [ANY] * 2,
        out_specs=[VMEM] * 3 + [ANY],
        scratch_shapes=[
            pltpu.VMEM((keys, wide), BF),
            pltpu.VMEM((keys, 128), F32),
            pltpu.VMEM((rows, wide), BF),
            pltpu.VMEM((rows, wide), BF),
            pltpu.VMEM((rows, 128), F32),
            pltpu.VMEM((rows, 128), F32),
            pltpu.VMEM((3,) + ff_own.shape[1:], BF),
            pltpu.VMEM((3,) + ff_own.shape[1:], BF),
            pltpu.SemaphoreType.DMA((2, 3)),
            pltpu.SemaphoreType.DMA((2,)),
        ],
        compiler_params=pltpu.CompilerParams(
            collective_id=number, has_side_effects=True, vmem_limit_bytes=60 << 20
        ),
        cost_estimate=pl.CostEstimate(
            flops=40_000_000_000, bytes_accessed=30 << 20, transcendentals=0
        ),
        name="attend_back",
    )(gb, qn, q_up, pairs, l_up, w_out_t, cosine, sine_table, q_pos, q, o, lse, att, ff_own, ff_got)


def shards(
    layer_input,
    first_gain,
    query_down,
    query_gain,
    query_up,
    latent_down,
    latent_gain,
    latent_up,
    out_weight,
    second_gain,
    gate_weight,
    up_weight,
    down_weight,
    out_grad,
):
    n_ctx = lax.axis_size("ctx")
    n_tp = lax.axis_size("tp")
    members = n_ctx // 16
    c = lax.axis_index("ctx")
    t = lax.axis_index("tp")
    g = c // members
    b = lax.rem(g // 2, 2)
    d = lax.rem(g, 2)
    member = lax.rem(c, members)
    ctx_rows, dim = layer_input.shape
    rows = ctx_rows // n_tp
    shard_rows = query_down.shape[0]
    qr = query_down.shape[1]
    heads = H // 8
    units = gate_weight.shape[1] // 16
    member_lists = [[k * members + m for m in range(members)] for k in range(16)]

    def widen(blocks):
        if members == 1:
            return blocks[:, None]
        return lax.all_gather(blocks, "ctx", axis=1, axis_index_groups=member_lists)

    def narrow(blocks):
        if members == 1:
            return blocks[:, 0]
        return lax.psum_scatter(
            blocks.astype(F32), "ctx", scatter_dimension=1, axis_index_groups=member_lists
        ).astype(BF)

    widths = [first_gain.shape[0], query_gain.shape[0], latent_gain.shape[0], second_gain.shape[0]]
    starts = [0, widths[0], widths[0] + widths[1], widths[0] + widths[1] + widths[2]]
    gains = jnp.concatenate([first_gain, query_gain, latent_gain, second_gain]).astype(F32)
    gains = jnp.broadcast_to(gains[None], (8, gains.shape[0]))
    down_shard = jnp.concatenate(
        [
            query_down,
            latent_down[:, :KVR],
            jnp.zeros((shard_rows, NOPE), BF),
            latent_down[:, KVR:],
            jnp.zeros((shard_rows, 128 - NOPE - ROPE), BF),
        ],
        axis=1,
    )

    def trade(block, k):
        return lax.ppermute(
            block, "ctx", [(i, (i // members ^ k) * members + i % members) for i in range(n_ctx)]
        )

    def swap_tp(block):
        return lax.ppermute(block, "tp", [(0, 1), (1, 0)])

    wide = 640
    ff = pack(gate_weight, up_weight, down_weight.T, wide, members)
    q_rows_w, l_rows_w, o_rows_w = query_up.shape[0], latent_up.shape[0], shard_rows // 2
    q_width, o_width = heads * (NOPE + ROPE), heads * VH
    q_tiles = jnp.pad(
        query_up.reshape(q_rows_w, 4, heads, NOPE + ROPE),
        ((0, 0), (0, 0), (0, 0), (0, 128 - NOPE - ROPE)),
    ).reshape(q_rows_w, 4, wide)
    out_tiles = jnp.transpose(
        out_weight.reshape(4, o_width, 2, o_rows_w), (0, 3, 2, 1)
    ).reshape(4, o_rows_w, wide)
    at = jnp.concatenate(
        [
            jnp.transpose(q_tiles, (1, 0, 2)),
            jnp.transpose(latent_up.reshape(l_rows_w, 4, wide), (1, 0, 2)),
            out_tiles,
        ],
        axis=1,
    )

    x = lax.dynamic_slice_in_dim(layer_input, t * rows, rows, 0).astype(F32)
    out_grad_rows = lax.dynamic_slice_in_dim(out_grad, t * rows, rows, 0).astype(F32)
    grad_ffn = (residual_scale * out_grad_rows).astype(BF)

    def rope_tiles(positions):
        lane = jnp.arange(128, dtype=jnp.int32) % (ROPE // 2)
        frequency = rope_base ** (-lane.astype(F32) / (ROPE // 2))
        angles = positions.astype(F32)[:, None] * frequency[None, :]
        return jnp.cos(angles), jnp.sin(angles)

    row = jnp.arange(rows, dtype=jnp.int32)
    cosine, sine_table = rope_tiles(c * ctx_rows + t * rows + row)
    block = jnp.arange(8, dtype=jnp.int32)
    block_ctx = ((block // 2 * 2 + b) * 2 + block % 2) * members + member
    q_positions = (block_ctx[:, None] * ctx_rows + t * rows + row[None, :]).reshape(-1)
    q_cos, q_sin = rope_tiles(q_positions)
    q_pos = jnp.broadcast_to(q_positions[:, None], (q_positions.shape[0], 128))

    down_full, gains, at_mine, own_near = weights_in(1, down_shard, gains, at, ff, n_ctx)
    own_near, ff = lax.optimization_barrier((own_near, ff))
    down_full = widen(down_full).reshape(dim, -1)
    gains = widen(gains[:, 0]).reshape(n_ctx, -1)
    gain_first, gain_query, gain_latent, gain_second = [
        gains[:, s : s + w].reshape(1, -1) for s, w in zip(starts, widths)
    ]
    first_gains = (gain_first, gain_query, gain_latent)
    both, _, pairs, qn_all, token_columns, own_mid, at_all = project(
        3, x, down_full, first_gains, cosine, sine_table, ff, at_mine, n_ctx
    )
    own_near, own_mid = lax.optimization_barrier((own_near, own_mid))
    oth_near, oth_mid = swap_tp(own_near), swap_tp(own_mid)
    lat_rope = widen(pairs).reshape(-1, KVR + 128)
    if members > 1:
        at_all = widen(at_all).reshape(n_ctx, -1, wide)
        out_tiles = at_all[:, q_rows_w + l_rows_w :].reshape(n_ctx, o_rows_w, 2, o_width)
        out_tiles = jnp.transpose(out_tiles, (0, 2, 1, 3)).reshape(16, 2, dim // 32, o_width)
        at_all = jnp.concatenate(
            [
                at_all[:, :q_rows_w].reshape(16, -1, wide),
                at_all[:, q_rows_w : q_rows_w + l_rows_w].reshape(16, -1, wide),
                jnp.transpose(out_tiles, (0, 2, 1, 3)).reshape(16, -1, wide),
            ],
            axis=1,
        )
    branch_part, queries, attended_wide, log_total, attended, q_up, l_up, w_out_t, own_far = attend(
        5, qn_all.reshape(-1, qr), at_all, lat_rope, q_cos, q_sin, q_pos, ff, o_width, n_ctx
    )
    qn_all = qn_all.reshape(-1, qr)

    middle, ns_all, gf_all = branch_and_norm(
        4, branch_part, x, gain_second, grad_ffn, n_ctx
    )
    ns_all, gf_all = ns_all.reshape(-1, dim), gf_all.reshape(-1, dim)
    oth_far = swap_tp(own_far)
    own = [own_near, own_mid, own_far]
    oth = [oth_near, oth_mid, oth_far]
    ns_all, oth = lax.optimization_barrier((ns_all, oth))
    if members > 1:
        own, oth = [
            [widen(jnp.concatenate(w)).reshape(16, dim // 16, wide)] for w in (own, oth)
        ]
    order = (0,) + TRADED_FIRST + TRADED_NEXT + TRADED_LAST
    ffn_part, second_part, grads_own, grads_oth = feed_forward(
        ns_all, gf_all, own, oth, order, units, members
    )
    grads_own = narrow(grads_own.reshape(16, members, shard_rows, wide))
    grads_oth = narrow(grads_oth.reshape(16, members, shard_rows, wide))
    grads_got = swap_tp(grads_oth)
    grad_middle, second_gain_part, gb_all, out_half = norm_and_branch_back(
        6, second_part, ffn_part, middle, out_grad_rows, gain_second, n_ctx
    )
    gb_all, grads_got = lax.optimization_barrier((gb_all, grads_got))
    out_other = swap_tp(out_half)
    grad_pairs, gqn_part, at_part, sums_far = attend_back(
        7, gb_all.reshape(-1, dim), qn_all, q_up, lat_rope, l_up, w_out_t, q_cos, q_sin, q_pos,
        queries, attended_wide, log_total, attended, grads_own, grads_got, n_ctx,
    )
    if members > 1:
        q_part = at_part[:, : qr // 16].reshape(n_ctx, q_rows_w, wide)
        l_part = at_part[:, qr // 16 : (qr + KVR) // 16].reshape(n_ctx, l_rows_w, wide)
        o_part = at_part[:, (qr + KVR) // 16 :].reshape(16, dim // 32, 2, o_width)
        o_part = jnp.transpose(o_part, (0, 2, 1, 3)).reshape(n_ctx, 2, o_rows_w, o_width)
        o_part = jnp.transpose(o_part, (0, 2, 1, 3)).reshape(n_ctx, o_rows_w, wide)
        at_part = narrow(
            jnp.concatenate([q_part, l_part, o_part], axis=1).reshape(16, members, -1, wide)
        )
    at_sums, sums, both_all, input_half, input_other, gain_sums = wind_up(
        8,
        narrow(grad_pairs.reshape(16, members, 2, rows, KVR + 128)),
        gqn_part.reshape(8, rows, qr),
        at_part,
        both,
        x,
        grad_middle,
        down_full,
        first_gains,
        second_gain_part,
        cosine,
        sine_table,
        grads_own,
        grads_got,
        widths,
        n_ctx,
    )
    both_all, out_other = lax.optimization_barrier((both_all, out_other))
    down_part = matmul_tn(
        token_columns.reshape(16 * rows, dim // 16), both_all.reshape(16 * rows, -1)
    ).astype(BF)
    if members > 1:
        down_part = lax.psum_scatter(
            down_part.astype(F32), "ctx", axis_index_groups=member_lists, tiled=True
        ).astype(BF)
    down_other = swap_tp(down_part)

    def in_order(mine, other):
        return jnp.where(
            t == 0, jnp.concatenate([mine, other]), jnp.concatenate([other, mine])
        )

    layer_output = in_order(out_half, out_other)
    input_grad = in_order(input_half, input_other).astype(F32)
    down_grads = down_part.astype(F32) + down_other.astype(F32)
    gain_grads = gain_sums[0]
    if members > 1:
        gain_grads = lax.psum_scatter(
            gain_grads.reshape(members, -1), "ctx", axis_index_groups=member_lists
        )
    first_gain_grad, query_gain_grad, latent_gain_grad, second_gain_grad = [
        gain_grads[s : s + w] for s, w in zip(starts, widths)
    ]

    gate_weight_grad, up_weight_grad, down_grad_t = spread([sums, sums_far], units, members)
    query_up_grad = jnp.transpose(
        at_sums[:, :q_rows_w].reshape(4, q_rows_w, heads, 128)[..., : NOPE + ROPE], (1, 0, 2, 3)
    ).reshape(q_rows_w, 4 * q_width)
    latent_up_grad = jnp.transpose(at_sums[:, q_rows_w : q_rows_w + l_rows_w], (1, 0, 2)).reshape(
        l_rows_w, 4 * wide
    )
    out_weight_grad = jnp.transpose(
        at_sums[:, q_rows_w + l_rows_w :].reshape(4, o_rows_w, 2, o_width), (0, 3, 2, 1)
    ).reshape(4 * o_width, shard_rows)
    return (
        layer_output,
        input_grad,
        first_gain_grad,
        down_grads[:, :qr],
        query_gain_grad,
        query_up_grad.astype(F32),
        jnp.concatenate(
            [down_grads[:, qr : qr + KVR], down_grads[:, qr + KVR + NOPE : qr + KVR + NOPE + ROPE]], axis=1
        ),
        latent_gain_grad,
        latent_up_grad.astype(F32),
        out_weight_grad.astype(F32),
        second_gain_grad,
        gate_weight_grad,
        up_weight_grad,
        down_grad_t.T,
    )


def solution(mesh):
    return jax.shard_map(
        shards,
        mesh=mesh,
        in_specs=(
            P("ctx", None),
            P("ctx"),
            P("ctx", None),
            P("ctx"),
            P("ctx", "tp"),
            P("ctx", None),
            P("ctx"),
            P("ctx", "tp"),
            P("tp", "ctx"),
            P("ctx"),
            P("ctx", "tp"),
            P("ctx", "tp"),
            P("tp", "ctx"),
            P("ctx", None),
        ),
        out_specs=(
            P("ctx", None),
            P("ctx", None),
            P("ctx"),
            P("ctx", None),
            P("ctx"),
            P("ctx", "tp"),
            P("ctx", None),
            P("ctx"),
            P("ctx", "tp"),
            P("tp", "ctx"),
            P("ctx"),
            P("ctx", "tp"),
            P("ctx", "tp"),
            P("tp", "ctx"),
        ),
        check_vma=False,
    )
```

```python
import math

import jax
import jax.numpy as jnp
from jax import lax
from jax.experimental import pallas as pl
from jax.experimental.pallas import tpu as pltpu
from jax.sharding import PartitionSpec as P

BF = jnp.bfloat16
F32 = jnp.float32

H = 40
KVR = 256
NOPE = 64
ROPE = 32
VH = 64

eps_norm = 1e-06
residual_scale = 1.4 / math.sqrt(62.0)
score_scale = (NOPE + ROPE) ** (-0.5)
rope_base = 10000.0


def matmul(left_side, right_side):
    return jnp.dot(left_side, right_side, preferred_element_type=F32)


def matmul_nt(left_side, right_side):
    return lax.dot_general(
        left_side, right_side, (((1,), (1,)), ((), ())), preferred_element_type=F32
    )


def matmul_tn(left_side, right_side):
    return lax.dot_general(
        left_side, right_side, (((0,), (0,)), ((), ())), preferred_element_type=F32
    )


def rms_norm(values, scale_gain):
    factor = lax.rsqrt(jnp.mean(values * values, axis=-1, keepdims=True) + eps_norm)
    return values * factor * scale_gain


def norm_back(values, scale_gain, upstream):
    factor = lax.rsqrt(jnp.mean(values * values, axis=-1, keepdims=True) + eps_norm)
    scaled = upstream * scale_gain
    inner_sum = jnp.mean(scaled * values, axis=-1, keepdims=True)
    grad_values = factor * scaled - values * factor * factor * factor * inner_sum
    grad_gain = jnp.sum(upstream * values * factor, axis=0)
    return (grad_values, grad_gain)


def rotate(values, cosine, sine_table):
    half_width = values.shape[-1] // 2
    first_half = values[..., :half_width]
    second_half = values[..., half_width:]
    return jnp.concatenate(
        [
            first_half * cosine - second_half * sine_table,
            second_half * cosine + first_half * sine_table,
        ],
        axis=-1,
    )


def rope_tables(positions):
    frequency = rope_base ** (-jnp.arange(ROPE // 2, dtype=F32) / (ROPE // 2))
    angles = positions.astype(F32)[:, None] * frequency[None, :]
    return (jnp.cos(angles), jnp.sin(angles))


MESH = pl.DeviceIdType.MESH
OFFSETS = (0, -1, 1, -2, 2, -3, 3)


TRADED_FIRST, TRADED_NEXT, TRADED_LAST = (1, 8, 2, 9, 3, 12), (10, 11, 6, 7), (13, 14, 15, 4, 5)
TRADED_BACK = (0,) + TRADED_FIRST + TRADED_NEXT


class Place:
    def __init__(self, n_ctx):
        c = lax.axis_index("ctx")
        self.members = n_ctx // 16
        self.c = c
        self.t = lax.axis_index("tp")
        self.m = lax.rem(c, self.members)
        g = c // self.members
        self.g = g
        self.a, self.b, self.d = g // 4, lax.rem(g // 2, 2), lax.rem(g, 2)

    def at(self, a=None, b=None, d=None):
        a = self.a if a is None else a
        b = self.b if b is None else b
        d = self.d if d is None else d
        return (((a * 2 + b) * 2 + d) * self.members + self.m, self.t)

    def up(self):
        return self.at(a=self.a + 1)

    def down(self):
        return self.at(a=self.a - 1)

    def across(self):
        return self.at(b=1 - self.b)

    def core(self):
        return self.at(d=1 - self.d)

    def other(self):
        return (self.c, 1 - self.t)

    def valid(self, o):
        return None if o == 0 else (self.a + o >= 0 if o < 0 else self.a + o <= 3)


def both_of(p, q):
    if p is None:
        return q
    return p if q is None else p & q


def when(p, body):
    if p is None:
        body()
    else:
        pl.when(p)(body)


class Net:
    def __init__(self, place, sems):
        self.place, self.sems, self.count, self.pending = place, sems, 0, []

    def sem(self):
        self.count += 1
        return self.sems.at[self.count - 1]

    def send(self, src, dst, recv, to, cond=None):
        mine = self.sem()

        def copy():
            return pltpu.make_async_remote_copy(
                src(), dst(), mine, recv, device_id=to(), device_id_type=MESH
            )

        when(cond, lambda: copy().start())
        self.pending.append((cond, lambda: copy().wait_send()))
        return self.pending[-1]

    def sent(self, one):
        self.pending.remove(one)
        when(one[0], one[1])

    def recv(self, dst, sem, cond=None):
        def wait():
            ref = dst()
            pltpu.make_async_remote_copy(
                ref, ref, sem, sem, device_id=self.place.other(), device_id_type=MESH
            ).wait_recv()

        when(cond, wait)

    def finish(self):
        for cond, wait in self.pending:
            when(cond, wait)


def greet(place, line=False, across=False, core=False, other=False, everyone=0):
    barrier = pltpu.get_barrier_semaphore()

    def tell(device):
        pl.semaphore_signal(barrier, inc=1, device_id=device, device_id_type=MESH)

    count = 0
    if everyone:
        for k in range(1, everyone):
            tell((lax.rem(place.c + k * place.members, everyone * place.members), place.t))
        count = count + everyone - 1
    else:
        if line:
            pl.when(place.a < 3)(lambda: tell(place.up()))
            pl.when(place.a > 0)(lambda: tell(place.down()))
            count = count + (place.a < 3).astype(jnp.int32) + (place.a > 0).astype(jnp.int32)
        if across:
            tell(place.across())
            count = count + 1
        if core:
            tell(place.core())
            count = count + 1
    if other:
        tell(place.other())
        count = count + 1
    pl.semaphore_wait(barrier, count)


def trade_away(place, src, out, sems, swap=None):
    barrier = pltpu.get_barrier_semaphore()
    count = len(TRADED_LAST)
    devices = [((place.g ^ i) * place.members + place.m, place.t) for i in TRADED_LAST]
    pairs = [(src.at[k], out.at[k]) for k in range(count)]
    if swap is not None:
        devices.append(place.other())
        pairs.append(swap)
        count += 1
    for device in devices:
        pl.semaphore_signal(barrier, inc=1, device_id=device, device_id_type=MESH)
    pl.semaphore_wait(barrier, count)
    copies = [
        pltpu.make_async_remote_copy(
            *pairs[k],
            sems.at[0, k],
            sems.at[1, k],
            device_id=devices[k],
            device_id_type=MESH,
        )
        for k in range(count)
    ]
    for copy in copies:
        copy.start()
    return copies


def gather_steps(net, src, out, width, start, pace, ready=None):
    p = net.place
    cores = width == 16

    def slot(o, b, d):
        return out.at[((p.a + o) * 2 + b) * 2 + d] if cores else out.at[(p.a + o) * 2 + d]

    z_sem = {o: net.sem() for o in OFFSETS if o}
    x_sem = {o: net.sem() for o in OFFSETS} if cores else {}
    c_sem = {(s, o): net.sem() for s in ((0, 1) if cores else (0,)) for o in OFFSETS}
    own_sem = net.sem()
    keep = pltpu.make_async_copy(src, slot(0, p.b, p.d), own_sem)
    keep.start()

    def forward(o):
        ok = p.valid(o)
        here = lambda: slot(o, p.b, p.d)
        origin = (lambda: src) if o == 0 else here
        if o <= 0 and o > -3:
            net.send(origin, here, z_sem[o - 1], p.up, both_of(ok, p.a < 3))
        if o >= 0 and o < 3:
            net.send(origin, here, z_sem[o + 1], p.down, both_of(ok, p.a > 0))
        if cores:
            net.send(origin, here, x_sem[o], p.across, ok)
        net.send(origin, here, c_sem[0, o], p.core, ok)

    def from_line(o):
        net.recv(lambda: slot(o, p.b, p.d), z_sem[o], p.valid(o))
        forward(o)

    def from_across(o):
        if cores:
            there = lambda: slot(o, 1 - p.b, p.d)
            net.recv(there, x_sem[o], p.valid(o))
            net.send(there, there, c_sem[1, o], p.core, p.valid(o))

    def from_core(o):
        net.recv(lambda: slot(o, p.b, 1 - p.d), c_sem[0, o], p.valid(o))
        if cores:
            net.recv(lambda: slot(o, 1 - p.b, 1 - p.d), c_sem[1, o], p.valid(o))

    forward(0)
    step = pace + 2
    for near in (1, 2, 3, 4):
        yield start + near * step
        if near < 4:
            from_line(-near)
            from_line(near)
            yield start + near * step + 0.5
        around = (0,) if near == 1 else (1 - near, near - 1)
        for o in around:
            from_across(o)
        yield start + near * step + 2
        for o in around:
            from_core(o)
        if near == 1:
            keep.wait()
        if ready is not None:
            ready(near - 1)


def add_into(out, terms, rows):
    step = 16 if rows % 16 == 0 else rows

    def body(i):
        part = pl.ds(pl.multiple_of(i * step, step), step)
        total = terms[0][part].astype(F32)
        for term in terms[1:]:
            total = total + term[part].astype(F32)
        out[part] = total.astype(out.dtype)

    pl.loop(0, rows // step)(body)


def reduce_steps(
    net, parts, out, near_core, near_x, line_in, line_out, rows, width, start, pace, across=False
):
    p = net.place
    cores = width == 16
    order = (-3, 3, -2, 2, -1, 1, 0)
    if cores:
        c_sem = {(b, o): net.sem() for b in (0, 1) for o in order}
        for o in order:
            for side in (1, 0):
                def src(o=o, side=side):
                    b = 1 - p.b if side else p.b
                    return parts.at[((p.a + o) * 2 + b) * 2 + 1 - p.d]

                def dst(o=o, side=side):
                    b = 1 - p.b if side else p.b
                    return near_core.at[(p.a + o) * 2 + b]

                net.send(src, dst, c_sem[side, o], p.core, p.valid(o))
        yield min(start, 1.0)
    x_sem = {o: net.sem() for o in order}
    up_sem = {o: net.sem() for o in (0, 1, 2)}
    down_sem = {o: net.sem() for o in (0, 1, 2)}

    across = across or cores
    pair = p.b if across else p.d

    def mine(o, b):
        g = (p.a + o) * 2 + b
        return near_core.at[g] if cores else parts.at[g]

    for o in order:
        if cores:
            def join(o=o):
                g = (p.a + o) * 2 + 1 - p.b
                add_into(near_core.at[g], [near_core.at[g], parts.at[g * 2 + p.d]], rows)

            net.recv(lambda: near_core.at[(p.a + o) * 2 + 1 - p.b], c_sem[1, o], p.valid(o))
            when(p.valid(o), join)
        net.send(
            lambda o=o: mine(o, 1 - pair),
            lambda o=o: near_x.at[p.a + o],
            x_sem[o],
            p.across if across else p.core,
            p.valid(o),
        )
    for number, o in enumerate(order):
        yield start + 3 + (number // 2 + 1) * (pace + 0.5)
        ok = p.valid(o)
        if cores:
            net.recv(lambda: near_core.at[(p.a + o) * 2 + p.b], c_sem[0, o], ok)

        def terms(o=o):
            g = (p.a + o) * 2 + pair
            own = [near_core.at[g], parts.at[g * 2 + p.d]] if cores else [parts.at[g]]
            return own + [near_x.at[p.a + o]]

        net.recv(lambda: near_x.at[p.a + o], x_sem[o], ok)
        if o == 0:
            below, above = line_in.at[0, 0], line_in.at[1, 0]
            net.recv(lambda: below, up_sem[0], p.a > 0)
            net.recv(lambda: above, down_sem[0], p.a < 3)
            inner = (p.a > 0) & (p.a < 3)
            pl.when(inner)(lambda: add_into(out, terms() + [below, above], rows))
            pl.when(p.a == 0)(lambda: add_into(out, terms() + [above], rows))
            pl.when(p.a == 3)(lambda: add_into(out, terms() + [below], rows))
            continue
        far = abs(o)
        way = 0 if o > 0 else 1
        stage = line_out.at[way, far - 1]
        sems = up_sem if o > 0 else down_sem
        first = p.a == 0 if o > 0 else p.a == 3
        if far < 3:
            came = line_in.at[way, far]
            later = ok & ~first
            net.recv(lambda: came, sems[far], later)
            pl.when(later)(lambda: add_into(stage, terms() + [came], rows))
            pl.when(ok & first)(lambda: add_into(stage, terms(), rows))
        else:
            pl.when(ok)(lambda: add_into(stage, terms(), rows))
        net.send(
            lambda stage=stage: stage,
            lambda far=far, way=way: line_in.at[way, far - 1],
            sems[far - 1],
            p.up if o > 0 else p.down,
            ok,
        )


def swap_steps(net, src, dst):
    sem = net.sem()
    net.send(lambda: src, lambda: dst, sem, net.place.other)
    yield 90.0
    net.recv(lambda: dst, sem)


def together(*tasks):
    tasks = [[0.0, number, task] for number, task in enumerate(tasks)]
    while tasks:
        first = min(tasks)
        try:
            first[0] = next(first[2])
        except StopIteration:
            tasks.remove(first)
        if tasks:
            yield min(tasks)[0]


def run_together(*tasks):
    for _ in together(*tasks):
        pass


def after(start, task):
    yield start
    yield from task


ANY = pl.BlockSpec(memory_space=pl.ANY)
VMEM = pl.BlockSpec(memory_space=pltpu.VMEM)


def comm_call(name, number, body, ins, in_specs, outs, out_specs, scratch, sems):
    return pl.pallas_call(
        body,
        out_shape=outs,
        in_specs=in_specs,
        out_specs=out_specs,
        scratch_shapes=list(scratch) + [pltpu.SemaphoreType.DMA((sems,))],
        compiler_params=pltpu.CompilerParams(
            collective_id=number, has_side_effects=True, vmem_limit_bytes=62 << 20
        ),
        name=name,
    )(*ins)


def shape(dims, dtype=BF):
    return jax.ShapeDtypeStruct(tuple(dims), dtype)


def reduce_scratch(rows, cols, width):
    near_core = [pltpu.VMEM((8, rows, cols), BF)] if width == 16 else []
    return near_core + [
        pltpu.VMEM((4, rows, cols), BF),
        pltpu.VMEM((2, 3, rows, cols), BF),
        pltpu.VMEM((2, 3, rows, cols), BF),
    ]


def trade_sends(net, block, out, sems, timed, ahead=2):
    p = net.place
    going = []
    for i, when_to in timed:
        yield when_to
        if len(going) == ahead:
            net.sent(going.pop(0))
        going.append(
            net.send(
                lambda i=i: block(i),
                lambda i=i: out(i),
                sems.at[i],
                lambda i=i: ((p.g ^ i) * p.members + p.m, p.t),
            )
        )


def trade_receives(net, out, sems, which):
    for i in which:
        net.recv(lambda i=i: out(i), sems.at[i])


def weights_in(number, down, gains, at, ff, n_ctx):
    def body(
        down_ref, gains_ref, at_ref, ff_ref,
        downs, gain_blocks, heads, near,
        at_sems, ff_sems, sems,
    ):
        p = Place(n_ctx)
        greet(p, everyone=16)
        net = Net(p, sems)
        owner = p.d == p.t
        f = p.a * 2 + p.d

        def attention():
            keep = pltpu.make_async_copy(at_ref.at[p.a], heads.at[f], net.sem())
            pl.when(owner)(lambda: keep.start())
            for s in range(4):
                net.send(
                    lambda s=s: at_ref.at[s],
                    lambda: heads.at[f],
                    at_sems.at[f],
                    lambda s=s: p.at(a=s, d=p.t),
                    ~(owner & (p.a == s)),
                )
            yield 50.0
            pl.when(owner)(lambda: keep.wait())
            for q in range(8):
                net.recv(lambda q=q: heads.at[q], at_sems.at[q], owner & (f != q))

        def trades():
            keep = pltpu.make_async_copy(ff_ref.at[0], near.at[0], net.sem())
            keep.start()
            out = lambda i: near.at[1 + TRADED_FIRST.index(i)]
            timed = ((1, 1), (8, 4), (9, 12), (2, 18), (12, 20), (3, 24))
            yield from trade_sends(net, lambda i: ff_ref.at[i], out, ff_sems, timed)
            yield 60.0
            trade_receives(net, out, ff_sems, TRADED_FIRST)
            keep.wait()

        run_together(
            gather_steps(net, gains_ref, gain_blocks, 16, 0, 3),
            gather_steps(net, down_ref, downs, 16, 0, 8),
            after(1.5, attention()),
            trades(),
        )
        net.finish()

    outs = [
        shape((16,) + down.shape),
        shape((16,) + gains.shape, gains.dtype),
        shape((8,) + at.shape[1:]),
        shape((1 + len(TRADED_FIRST),) + ff.shape[1:]),
    ]
    return comm_call(
        "weights_in",
        number,
        body,
        [down, gains, at, ff],
        [ANY] * 4,
        outs,
        [ANY] * 4,
        [pltpu.SemaphoreType.DMA((8,)), pltpu.SemaphoreType.DMA((16,))],
        200,
    )


class RowBlocks:
    def __init__(self, ref, rows):
        self.ref, self.rows, self.at = ref, rows, self

    def __getitem__(self, i):
        return self.ref.at[pl.ds(pl.multiple_of(i * self.rows, self.rows), self.rows)]


def front(
    number, x, query_down, latent_down, gains, gate, up, down_t, query_up, latent_up, out_t,
    cosine, sine_table, widths, n_ctx,
):
    rows, dim = x.shape
    shard, qr = query_down.shape
    wide = qr + KVR + 128
    units = gate.shape[1] // 16
    q_rows, l_rows, o_rows = query_up.shape[0], latent_up.shape[0], shard // 2
    heads, width = H // 8, H // 8 * VH
    lanes = heads * 128
    at_rows = q_rows + l_rows + o_rows

    def body(
        x_ref, qd_ref, ld_ref, gains_ref, gate_ref, up_ref, down_ref, qu_ref, lu_ref, ow_ref,
        cos_ref, sin_ref,
        both, down_out, g1, gq, gl, g2, pairs, queries, columns, first, mid, last,
        other_first, heads_out,
        down_block, downs, gain_blocks, ff, at, normed, column_blocks, pair, query_block,
        heads_mine,
        at_sems, x_sems, tp_sems, keep_sems, col_sems, ff_sems, other_sems, sems,
    ):
        p = Place(n_ctx)
        down_block[:, :qr] = qd_ref[...]
        down_block[:, qr : qr + KVR] = ld_ref[:, :KVR]
        none = jnp.zeros((shard, NOPE), BF)
        down_block[:, qr + KVR :] = jnp.concatenate(
            [none, ld_ref[:, KVR:], none[:, :ROPE]], axis=1
        )
        greet(p, everyone=16, other=True)
        net = Net(p, sems)
        owner = p.d == p.t
        f = p.a * 2 + p.d
        place = lambda q, side: (q // 2 * 2 + (1 - p.b if side else p.b)) * 2 + q % 2
        first_out = lambda i: first.at[1 + TRADED_FIRST.index(i)]
        mid_out = lambda i: mid.at[TRADED_NEXT.index(i)]

        def pack_heads():
            for s in range(4):
                for h in range(heads):
                    cut = (s * heads + h) * (NOPE + ROPE)
                    at[s, :q_rows, h * 128 : h * 128 + NOPE + ROPE] = qu_ref[
                        :, cut : cut + NOPE + ROPE
                    ]
                    at[s, :q_rows, h * 128 + NOPE + ROPE : (h + 1) * 128] = jnp.zeros(
                        (q_rows, 128 - NOPE - ROPE), BF
                    )
                at[s, q_rows : q_rows + l_rows] = lu_ref[:, s * lanes : (s + 1) * lanes]
                for half in (0, 1):
                    at[s, q_rows + l_rows :, half * width : (half + 1) * width] = ow_ref[
                        half * o_rows : (half + 1) * o_rows, s * width : (s + 1) * width
                    ]

        def pack_units():
            for n in range(16):
                cut = slice(n * units, (n + 1) * units)
                i = p.g ^ n
                for k, part in enumerate((gate_ref, up_ref, down_ref)):
                    ff[i, :, k * units : (k + 1) * units] = part[:, cut]
                ff[i, :, 3 * units :] = jnp.zeros((shard, lanes - 3 * units), BF)

        def trades():
            yield 1.0
            pack_units()
            keeps = [pltpu.make_async_copy(ff.at[0], first.at[0], net.sem())]
            keeps += [
                pltpu.make_async_copy(ff.at[i], last.at[k], net.sem())
                for k, i in enumerate(TRADED_LAST)
            ]
            for keep in keeps:
                keep.start()
            block = lambda i: ff.at[i]

            def onward(k, src):
                net.send(src, lambda: other_first.at[k], other_sems.at[k], p.other)

            onward(0, lambda: ff.at[0])
            timed = ((1, 3), (8, 5), (2, 12), (9, 30), (3, 34), (12, 38))
            yield from trade_sends(net, block, first_out, ff_sems, timed)
            timed = [each for each in ((10, 49), (6, 57), (11, 62), (7, 70)) if each[0] in TRADED_NEXT]
            for k, i in enumerate(TRADED_FIRST[:3]):
                yield 42.0 + 3 * k
                trade_receives(net, first_out, ff_sems, (i,))
                onward(1 + k, lambda i=i: first_out(i))
            yield from trade_sends(net, block, mid_out, ff_sems, timed)
            yield 90.0
            trade_receives(net, first_out, ff_sems, TRADED_FIRST[3:])
            trade_receives(net, mid_out, ff_sems, TRADED_NEXT)
            for k in range(4):
                net.recv(lambda k=k: other_first.at[k], other_sems.at[k])
            for keep in keeps:
                keep.wait()

        def attention():
            pack_heads()
            yield 1.0
            keep = pltpu.make_async_copy(at.at[p.a], heads_mine.at[f], net.sem())
            pl.when(owner)(lambda: keep.start())
            for s in range(4):
                net.send(
                    lambda s=s: at.at[s],
                    lambda: heads_mine.at[f],
                    at_sems.at[f],
                    lambda s=s: p.at(a=s, d=p.t),
                    ~(owner & (p.a == s)),
                )

            def keep_head(q):
                return pltpu.make_async_copy(
                    heads_mine.at[q], heads_out.at[place(q, 0)], keep_sems.at[q]
                )

            yield 24.0
            pl.when(owner)(lambda: keep.wait())
            for q in range(8):
                yield 24.0 + q
                net.recv(lambda q=q: heads_mine.at[q], at_sems.at[q], owner & (f != q))
                pl.when(owner)(lambda: keep_head(q).start())
                for sems_of, to in ((x_sems, p.across), (tp_sems.at[0], p.other)):
                    net.send(
                        lambda q=q: heads_mine.at[q],
                        lambda q=q: heads_out.at[place(q, 0)],
                        sems_of.at[q],
                        to,
                        owner,
                    )
            for q in range(8):
                yield 38.0 + 2 * q
                theirs = lambda q=q: heads_out.at[place(q, 1)]
                net.recv(theirs, x_sems.at[q], owner)
                net.send(theirs, theirs, tp_sems.at[1, q], p.other, owner)
            yield 85.0
            for q in range(8):
                for side in (0, 1):
                    net.recv(lambda: heads_out.at[place(q, side)], tp_sems.at[side, q], ~owner)
                pl.when(owner)(lambda: keep_head(q).wait())

        def send_columns():
            for n in range(16):
                column_blocks[n] = normed[:, n * shard : (n + 1) * shard]
            keep = pltpu.make_async_copy(column_blocks.at[p.g], columns.at[p.g], net.sem())
            keep.start()
            for k in range(1, 16):
                if k % 4 == 1:
                    yield 56.0 + k
                net.send(
                    lambda k=k: column_blocks.at[p.g ^ k],
                    lambda: columns.at[p.g],
                    col_sems.at[k],
                    lambda k=k: ((p.g ^ k) * p.members + p.m, p.t),
                )
            yield 88.0
            for k in range(1, 16):
                net.recv(lambda k=k: columns.at[p.g ^ k], col_sems.at[k])
            keep.wait()

        def latents():
            sem = net.sem()
            net.send(lambda: pair.at[p.t], lambda: pair.at[p.t], sem, p.other)
            yield 54.0
            net.recv(lambda: pair.at[1 - p.t], sem)
            yield from gather_steps(net, pair, pairs, 16, 55, 2.2)

        def chain():
            yield from gather_steps(net, down_block, RowBlocks(downs, shard), 16, 0, 8)
            keep = pltpu.make_async_copy(downs, down_out, net.sem())
            keep.start()
            at_lane = 0
            for out, w in zip((g1, gq, gl, g2), widths):
                for n in range(16):
                    out[:, n * w : (n + 1) * w] = gain_blocks[n, :1, at_lane : at_lane + w]
                at_lane += w
            values = x_ref[...]
            normed[...] = (values * norm_factor(values) * g1[...]).astype(BF)
            both[...] = matmul(normed[...], downs[...])
            query, latent = both[:, :qr], both[:, qr : qr + KVR]
            query_block[...] = (query * norm_factor(query) * gq[...]).astype(BF)
            pair[p.t, :, :KVR] = (latent * norm_factor(latent) * gl[...]).astype(BF)
            pair[p.t, :, KVR:] = turn(both[:, qr + KVR :], cos_ref[...], sin_ref[...]).astype(BF)
            yield from together(
                latents(), gather_steps(net, query_block, queries, 8, 51, 2.2), send_columns()
            )
            keep.wait()

        run_together(
            chain(),
            after(0.5, gather_steps(net, gains_ref, gain_blocks, 16, 0.5, 1)),
            trades(),
            attention(),
        )
        net.finish()

    ff_shape = (shard, lanes)
    return comm_call(
        "front",
        number,
        body,
        [x, query_down, latent_down, gains, gate, up, down_t, query_up, latent_up, out_t]
        + [cosine, sine_table],
        [VMEM] * 12,
        [
            shape((rows, wide), F32),
            shape((dim, wide)),
            *[shape((1, 16 * w), F32) for w in widths],
            shape((16, 2, rows, KVR + 128)),
            shape((8, rows, qr)),
            shape((16, rows, shard)),
            shape((1 + len(TRADED_FIRST),) + ff_shape),
            shape((len(TRADED_NEXT),) + ff_shape),
            shape((len(TRADED_LAST),) + ff_shape),
            shape((4,) + ff_shape),
            shape((16, at_rows, lanes)),
        ],
        [VMEM, ANY] + [VMEM] * 4 + [ANY] * 8,
        [
            pltpu.VMEM((shard, wide), BF),
            pltpu.VMEM((dim, wide), BF),
            pltpu.VMEM((16,) + gains.shape, F32),
            pltpu.VMEM((16,) + ff_shape, BF),
            pltpu.VMEM((4, at_rows, lanes), BF),
            pltpu.VMEM((rows, dim), BF),
            pltpu.VMEM((16, rows, shard), BF),
            pltpu.VMEM((2, rows, KVR + 128), BF),
            pltpu.VMEM((rows, qr), BF),
            pltpu.VMEM((8, at_rows, lanes), BF),
            pltpu.SemaphoreType.DMA((8,)),
            pltpu.SemaphoreType.DMA((8,)),
            pltpu.SemaphoreType.DMA((2, 8)),
            pltpu.SemaphoreType.DMA((8,)),
            pltpu.SemaphoreType.DMA((16,)),
            pltpu.SemaphoreType.DMA((16,)),
            pltpu.SemaphoreType.DMA((16,)),
        ],
        300,
    )


def head_grads_steps(net, at_ref, at_out, at_x, at_tp, x_sems, tp_sems, rows, start):
    p = net.place
    owner = p.d == p.t
    f = p.a * 2 + p.d
    place = lambda q, side: (q // 2 * 2 + (1 - p.b if side else p.b)) * 2 + q % 2
    for side in (1, 0):
        for q in range(8):
            net.send(
                lambda q=q, side=side: at_ref.at[place(q, side)],
                lambda q=q, side=side: at_tp.at[side, q],
                tp_sems.at[side, q],
                p.other,
                ~owner,
            )
    for q in range(8):
        yield start + 4 + 2 * (q + 1)
        here = at_tp.at[1, q]
        net.recv(lambda: here, tp_sems.at[1, q], owner)
        pl.when(owner)(lambda: add_into(here, [here, at_ref.at[place(q, 1)]], rows))
        net.send(
            lambda here=here: here, lambda q=q: at_x.at[q], x_sems.at[0, q], p.across, owner
        )
    keep = pltpu.make_async_copy(at_tp.at[0, f], at_out.at[p.a], net.sem())
    for q in range(8):
        yield start + 20 + 2 * (q + 1)
        here, near = at_tp.at[0, q], at_x.at[q]
        net.recv(lambda: here, tp_sems.at[0, q], owner)
        net.recv(lambda: near, x_sems.at[0, q], owner)
        pl.when(owner)(lambda: add_into(here, [here, near, at_ref.at[place(q, 0)]], rows))
        net.send(
            lambda here=here: here,
            lambda: at_out.at[p.a],
            x_sems.at[1, p.a],
            lambda q=q: p.at(a=q // 2, d=q % 2),
            owner & (f != q),
        )
        pl.when(owner & (f == q))(lambda: keep.start())
    yield start + 60
    for s in range(4):
        net.recv(lambda s=s: at_out.at[s], x_sems.at[1, s], ~(owner & (p.a == s)))
    pl.when(owner)(lambda: keep.wait())


def plain_call(name, body, ins, outs, scratch, members):
    def whole(array):
        return pl.BlockSpec(array.shape, lambda i, g: (0,) * len(array.shape))

    g = (lax.axis_index("ctx") // members).astype(jnp.int32).reshape(1)
    return pl.pallas_call(
        body,
        out_shape=outs,
        grid_spec=pltpu.PrefetchScalarGridSpec(
            num_scalar_prefetch=1,
            grid=(1,),
            in_specs=[whole(i) for i in ins],
            out_specs=[whole(o) for o in outs],
            scratch_shapes=scratch,
        ),
        compiler_params=pltpu.CompilerParams(vmem_limit_bytes=62 << 20),
        cost_estimate=pl.CostEstimate(
            flops=1_000_000_000, bytes_accessed=20 << 20, transcendentals=0
        ),
        name=name,
    )(g, *ins)


def pack(gate, up, down_t, wide, members):
    rows = gate.shape[0]
    units = gate.shape[1] // 16

    def body(g_ref, gate_ref, up_ref, down_ref, out):
        for n in range(16):
            cut = slice(n * units, (n + 1) * units)
            i = g_ref[0] ^ n
            for k, part in enumerate((gate_ref, up_ref, down_ref)):
                out[i, :, k * units : (k + 1) * units] = part[:, cut]
            out[i, :, 3 * units :] = jnp.zeros((rows, wide - 3 * units), BF)

    return plain_call(
        "pack", body, [gate, up, down_t], [shape((16, rows, wide))], [], members
    )[0]


def feed_forward(ns, gf, own, oth, order, units, members):
    tokens, dim = ns.shape
    rows, wide = own[0].shape[1:]
    lanes = 256
    both = 2 * lanes
    places = [[(a, k) for a, w in enumerate(side) for k in range(w.shape[0])] for side in (own, oth)]

    def body(g_ref, ns_ref, gf_ref, *refs):
        own_refs, oth_refs = refs[: len(own)], refs[len(own) : len(own) + len(oth)]
        out_ref, gs_ref, gown_ref, goth_ref = refs[len(own) + len(oth) :][:4]
        wgu_ref, wd_ref, hidden_ref, ggu_ref = refs[-4:]
        g = g_ref[0]
        for place, i in enumerate(order):
            cut = pl.ds(pl.multiple_of((g ^ i) * rows, rows), rows)
            for half, side in enumerate((own_refs, oth_refs)):
                a, k = places[half][place]
                block = side[a][k]
                pad = jnp.zeros((rows, lanes - units), BF)
                for k in range(3):
                    part = jnp.concatenate([block[:, k * units : (k + 1) * units], pad], axis=1)
                    into = wgu_ref if k < 2 else wd_ref
                    at = (both * k if k < 2 else 0) + half * lanes
                    into[cut, at : at + lanes] = part

        def forth(i):
            r = pl.ds(pl.multiple_of(i * 256, 256), 256)
            gate_up = matmul(ns_ref[r], wgu_ref[...])
            gate, up = gate_up[:, :both], gate_up[:, both:]
            grad_hidden = matmul(gf_ref[r], wd_ref[...])
            sigmoid_gate = 1.0 / (1.0 + jnp.exp(-gate))
            silu = gate * sigmoid_gate
            hidden_ref[r] = (silu * up).astype(BF)
            ggu_ref[r, :both] = (
                grad_hidden * up * sigmoid_gate * (1.0 + gate * (1.0 - sigmoid_gate))
            ).astype(BF)
            ggu_ref[r, both:] = (grad_hidden * silu).astype(BF)
            gs_ref[r] = matmul_nt(ggu_ref[r], wgu_ref[...]).astype(BF)
            out_ref[r] = matmul_nt(hidden_ref[r], wd_ref[...]).astype(BF)

        pl.loop(0, tokens // 256)(forth)

        span = dim // 4

        def give(q, k, grads):
            for jj in range(4):
                for half, out in enumerate((gown_ref, goth_ref)):
                    out[g ^ (4 * q + jj), :, k * units : (k + 1) * units] = grads[
                        jj * rows : (jj + 1) * rows, half * lanes : half * lanes + units
                    ].astype(BF)

        for q in range(4):
            cut = slice(q * span, (q + 1) * span)
            grads = matmul_tn(ns_ref[:, cut], ggu_ref[...])
            give(q, 0, grads[:, :both])
            give(q, 1, grads[:, both:])
            give(q, 2, matmul_tn(gf_ref[:, cut], hidden_ref[...]))
        for out in (gown_ref, goth_ref):
            out[:, :, 3 * units :] = jnp.zeros((16, rows, wide - 3 * units), BF)

    return plain_call(
        "feed_forward",
        body,
        [ns, gf, *own, *oth],
        [shape((tokens, dim))] * 2 + [shape((16, rows, wide))] * 2,
        [
            pltpu.VMEM((dim, 2 * both), BF),
            pltpu.VMEM((dim, both), BF),
            pltpu.VMEM((tokens, both), BF),
            pltpu.VMEM((tokens, 2 * both), BF),
        ],
        members,
    )


def spread(parts, order, at, down, halves, units, members):
    rows, cols = parts[0].shape[1:]
    places = [(a, k) for a, w in enumerate(parts) for k in range(w.shape[0])]
    n_parts = len(parts)
    heads, width = H // 8, H // 8 * VH
    o_rows = rows // 2
    q_rows, l_rows = 3 * KVR // 16, KVR // 16
    outs = [shape((rows, 16 * units), F32)] * 3
    if members == 1:
        outs += [
            shape((q_rows, 4 * heads * (NOPE + ROPE)), F32),
            shape((l_rows, 4 * cols), F32),
            shape((rows, 4 * width), F32),
            shape((rows, down.shape[1] - KVR - 128), F32),
            shape((rows, KVR + ROPE), F32),
        ]
    own_rows, dim = halves[0].shape
    outs = [shape((2 * own_rows, dim)), shape((2 * own_rows, dim), F32)] + outs
    ins = list(halves) + ([at, down] if members == 1 else []) + list(parts)
    first = len(ins) - n_parts

    def body(g_ref, *refs):
        out_refs = refs[len(ins) : -1]
        t = lax.axis_index("tp")
        for k in range(4):
            start = pl.multiple_of((t if k % 2 == 0 else 1 - t) * own_rows, own_rows)
            out = out_refs[k // 2]
            out[pl.ds(start, own_rows)] = refs[k][...].astype(out.dtype)
        hold = refs[-1]
        for i, (a, k) in zip(order, places):
            hold[g_ref[0] ^ i] = refs[first + a][k].astype(F32)
        rest = out_refs[2:]
        for n in range(16):
            for k, out in enumerate(rest[:3]):
                out[:, n * units : (n + 1) * units] = hold[n, :, k * units : (k + 1) * units]
        if members == 1:
            at_ref, down_ref = refs[4], refs[5]
            qr = down_ref.shape[1] - KVR - 128
            rest[6][...] = down_ref[:, :qr]
            rest[7][:, :KVR] = down_ref[:, qr : qr + KVR]
            rest[7][:, KVR:] = down_ref[:, qr + KVR + NOPE : qr + KVR + NOPE + ROPE]
            for s in range(4):
                part = at_ref[s].astype(F32)
                for h in range(heads):
                    cut = (s * heads + h) * (NOPE + ROPE)
                    rest[3][:, cut : cut + NOPE + ROPE] = part[
                        :q_rows, h * 128 : h * 128 + NOPE + ROPE
                    ]
                rest[4][:, s * cols : (s + 1) * cols] = part[q_rows : q_rows + l_rows]
                for half in (0, 1):
                    rest[5][half * o_rows : (half + 1) * o_rows, s * width : (s + 1) * width] = (
                        part[q_rows + l_rows :, half * width : (half + 1) * width]
                    )

    return plain_call(
        "spread",
        body,
        ins,
        outs,
        [pltpu.VMEM((16, rows, cols), F32)],
        members,
    )


def project(number, x, down, gains, cosine, sine_table, ff, heads_in, n_ctx):
    rows, dim = x.shape
    wide = down.shape[1]
    qr = wide - KVR - 128
    cols = dim // 16

    def body(
        x_ref, down_ref, g1_ref, gq_ref, gl_ref, cos_ref, sin_ref, ff_ref, heads_ref,
        both, pair, pairs, queries, columns, mid, heads,
        normed, column_blocks, pair_block, query_block,
        col_sems, ff_sems, x_sems, tp_sems, sems,
    ):
        p = Place(n_ctx)
        greet(p, everyone=16, other=True)
        net = Net(p, sems)
        owner = p.d == p.t
        place = lambda q, side: (q // 2 * 2 + (1 - p.b if side else p.b)) * 2 + q % 2
        keep_heads = [net.sem() for _ in range(8)]

        def keep_head(q):
            return pltpu.make_async_copy(heads_ref.at[q], heads.at[place(q, 0)], keep_heads[q])

        def send_head(q, sems_of, to):
            net.send(
                lambda: heads_ref.at[q], lambda: heads.at[place(q, 0)], sems_of.at[q], to, owner
            )

        for q in range(8):
            send_head(q, x_sems, p.across)

        def spread_heads():
            yield 9.5
            for q in range(8):
                pl.when(owner)(lambda: keep_head(q).start())
                send_head(q, tp_sems.at[0], p.other)
            for q in range(8):
                yield 16.0 + 2 * q
                theirs = lambda q=q: heads.at[place(q, 1)]
                net.recv(theirs, x_sems.at[q], owner)
                net.send(theirs, theirs, tp_sems.at[1, q], p.other, owner)
            yield 60.0
            for q in range(8):
                for side in (0, 1):
                    net.recv(lambda: heads.at[place(q, side)], tp_sems.at[side, q], ~owner)
                pl.when(owner)(lambda: keep_head(q).wait())

        out = lambda i: mid.at[TRADED_NEXT.index(i)]
        run_together(trade_sends(net, lambda i: ff_ref.at[i], out, ff_sems, [(i, 0) for i in TRADED_NEXT]))
        values = x_ref[...]
        normed[...] = (values * norm_factor(values) * g1_ref[...]).astype(BF)
        both[...] = matmul(normed[...], down_ref[...])
        query, latent = both[:, :qr], both[:, qr : qr + KVR]
        query_block[...] = (query * norm_factor(query) * gq_ref[...]).astype(BF)
        pair_block[:, :KVR] = (latent * norm_factor(latent) * gl_ref[...]).astype(BF)
        pair_block[:, KVR:] = turn(both[:, qr + KVR :], cos_ref[...], sin_ref[...]).astype(BF)

        def send_columns():
            for n in range(16):
                column_blocks[n] = normed[:, n * cols : (n + 1) * cols]
            keep = pltpu.make_async_copy(column_blocks.at[p.g], columns.at[p.g], net.sem())
            keep.start()
            for k in range(1, 16):
                if k % 4 == 1:
                    yield 13.0 + k
                net.send(
                    lambda k=k: column_blocks.at[p.g ^ k],
                    lambda: columns.at[p.g],
                    col_sems.at[k],
                    lambda k=k: ((p.g ^ k) * p.members + p.m, p.t),
                )
            yield 50.0
            for k in range(1, 16):
                net.recv(lambda k=k: columns.at[p.g ^ k], col_sems.at[k])
            keep.wait()

        def latents():
            sem = net.sem()
            keep = pltpu.make_async_copy(pair_block, pair.at[p.t], net.sem())
            keep.start()
            net.send(lambda: pair_block, lambda: pair.at[p.t], sem, p.other)
            yield 11.0
            net.recv(lambda: pair.at[1 - p.t], sem)
            keep.wait()
            yield from gather_steps(net, pair, pairs, 16, 12, 2.2)

        run_together(
            latents(),
            gather_steps(net, query_block, queries, 8, 9, 2.2),
            after(9.0, send_columns()),
            spread_heads(),
        )
        trade_receives(net, out, ff_sems, TRADED_NEXT)
        net.finish()

    return comm_call(
        "project",
        number,
        body,
        [x, down, *gains, cosine, sine_table, ff, heads_in],
        [VMEM] * 7 + [ANY] * 2,
        [
            shape((rows, wide), F32),
            shape((2, rows, KVR + 128)),
            shape((16, 2, rows, KVR + 128)),
            shape((8, rows, qr)),
            shape((16, rows, cols)),
            shape((len(TRADED_NEXT),) + ff.shape[1:]),
            shape((16,) + heads_in.shape[1:]),
        ],
        [VMEM] + [ANY] * 6,
        [
            pltpu.VMEM((rows, dim), BF),
            pltpu.VMEM((16, rows, cols), BF),
            pltpu.VMEM((rows, KVR + 128), BF),
            pltpu.VMEM((rows, qr), BF),
            pltpu.SemaphoreType.DMA((16,)),
            pltpu.SemaphoreType.DMA((16,)),
            pltpu.SemaphoreType.DMA((8,)),
            pltpu.SemaphoreType.DMA((2, 8)),
        ],
        240,
    )


def norm_back_rows(values, gain, upstream):
    factor = norm_factor(values)
    scaled = upstream * gain
    inner = jnp.mean(scaled * values, axis=-1, keepdims=True)
    share = upstream * values * factor
    total = share[:8]
    for i in range(1, share.shape[0] // 8):
        total = total + share[8 * i : 8 * i + 8]
    return factor * scaled - values * factor * factor * factor * inner, total


def wind_up(
    number, pairs, queries, at, both, x, grad_middle, down, gains, second, cosine, sine_table,
    ff_own, ff_got, columns, widths, n_ctx,
):
    rows, dim = x.shape
    wide = down.shape[1]
    qr = wide - KVR - 128
    members = n_ctx // 16
    down_shape = down.shape
    unit_rows = ff_own.shape[1]
    traded = TRADED_FIRST + TRADED_NEXT

    def body(
        pairs_ref, queries_ref, at_ref, both_ref, x_ref, middle_ref, down_hbm,
        g1_ref, gq_ref, gl_ref, second_ref, cos_ref, sin_ref, columns_ref, own_ref, got_ref,
        at_out, ff_out, down_sum, input_half, input_other, gains_out,
        own_hold, ff_sum, at_x, at_tp, core_in, tp_in, pair_sum, query_sum, grad_both, gain_blocks, gain_tp,
        down, both_all, down_part, down_other, *rest,
    ):
        p = Place(n_ctx)
        greet(p, everyone=16, other=True)
        rest = list(rest)
        net = Net(p, rest.pop())
        load_sems, tp_sems, x_sems, ff_sems, pair_sems = [rest.pop() for _ in range(5)]
        load_down = pltpu.make_async_copy(down_hbm, down, net.sem())
        load_down.start()

        def latents():
            for q in range(8):
                net.send(
                    lambda q=q: pairs_ref.at[2 * q + 1 - p.d],
                    lambda q=q: core_in.at[q],
                    pair_sems.at[0, q],
                    p.core,
                )
            for q in range(8):
                yield 1.5 + 0.2 * q
                net.recv(lambda q=q: core_in.at[q], pair_sems.at[0, q])
                for half in (0, 1):
                    near = core_in.at[q, half]
                    add_into(near, [near, pairs_ref.at[2 * q + p.d, half]], rows)
                net.send(
                    lambda q=q: core_in.at[q, 1 - p.t],
                    lambda q=q: tp_in.at[q],
                    pair_sems.at[1, q],
                    p.other,
                )
            for q in range(8):
                yield 4.0 + 1.1 * (q + 1)
                net.recv(lambda q=q: tp_in.at[q], pair_sems.at[1, q])
                add_into(tp_in.at[q], [tp_in.at[q], core_in.at[q, p.t]], rows)
            yield from reduce_steps(net, tp_in, pair_sum, None, *rest[:3], rows, 8, 14, 1.1, True)

        def trades():
            loads = {
                i: [
                    pltpu.make_async_copy(ref.at[i], hold.at[k], load_sems.at[n, k])
                    for n, (ref, hold) in enumerate(((own_ref, own_hold), (got_ref, ff_sum)))
                ]
                for k, i in enumerate(TRADED_BACK)
            }
            for load in loads.values():
                for part in load:
                    part.start()

            def block(i):
                return ff_sum.at[TRADED_BACK.index(i)]

            def joined(i):
                for part in loads[i]:
                    part.wait()
                k = TRADED_BACK.index(i)
                add_into(block(i), [block(i), own_hold.at[k]], unit_rows)
                return block(i)

            out = lambda i: ff_out.at[TRADED_BACK.index(i)]
            timed = ((8, 1), (2, 2), (3, 6), (9, 10), (12, 19), (6, 22), (1, 23), (7, 26))
            for i, when_to in timed + ((10, 28), (11, 37)):
                if i not in traded:
                    continue
                yield when_to
                joined(i)
                yield from trade_sends(net, block, out, ff_sems, ((i, when_to),))
            keep = pltpu.make_async_copy(joined(0), out(0), net.sem())
            keep.start()
            yield 95.0
            trade_receives(net, out, ff_sems, traded)
            keep.wait()

        def gain_sums():
            sem = net.sem()
            net.send(lambda: gain_blocks, lambda: gain_tp, sem, p.other)
            yield 45.0
            net.recv(lambda: gain_tp, sem)
            pl.loop(0, 16)(lambda g: add_into(gain_tp.at[g], [gain_tp.at[g], gain_blocks.at[g]], 16))
            yield from reduce_steps(net, gain_tp, gains_out, *rest[6:10], 16, 16, 46, 2)

        def gather_and_multiply(gather):
            yield from gather
            columns = columns_ref[...].reshape(16 * rows, columns_ref.shape[2])
            down_part[...] = matmul_tn(columns, both_all[...]).astype(BF)
            swap = swap_steps(net, down_part, down_other)
            yield next(swap)
            yield from swap
            down_sum[...] = down_part[...].astype(F32) + down_other[...].astype(F32)

        def chain():
            yield from together(
                latents(),
                reduce_steps(net, queries_ref, query_sum, None, *rest[3:6], rows, 8, 0, 2.2),
            )
            query_back, query_share = norm_back_rows(
                both_ref[:, :qr], gq_ref[...], query_sum[...]
            )
            grad_both[:, :qr] = query_back.astype(BF)
            latent_back, latent_share = norm_back_rows(
                both_ref[:, qr : qr + KVR], gl_ref[...], pair_sum[:, :KVR]
            )
            grad_both[:, qr : qr + KVR] = latent_back.astype(BF)
            grad_both[:, qr + KVR :] = turn(
                pair_sum[:, KVR:], cos_ref[...], sin_ref[...], True
            ).astype(BF)

            gather = gather_steps(net, grad_both, RowBlocks(both_all, rows), 16, 31, 3.3)
            next(gather)
            load_down.wait()
            input_back, input_share = norm_back_rows(
                x_ref[...], g1_ref[...], matmul_nt(grad_both[...], down[...])
            )
            input_half[...] = (middle_ref[...] + input_back).astype(BF)
            swap = swap_steps(net, input_half, input_other)
            next(swap)
            shares = [
                jnp.sum(share, axis=0, keepdims=True)
                for share in (input_share, query_share, latent_share, second_ref[...])
            ]
            for n in range(16):
                parts = []
                for m in range(members):
                    for share, w in zip(shares, widths):
                        at_lane = (n * members + m) * w
                        parts.append(share[:, at_lane : at_lane + w])
                row = jnp.concatenate(parts, axis=1)
                gain_blocks[n] = jnp.broadcast_to(row, gain_blocks.shape[1:]).astype(BF)
            yield from together(gather_and_multiply(gather), gain_sums(), swap)

        run_together(
            chain(),
            after(
                3.5,
                head_grads_steps(
                    net, at_ref, at_out, at_x, at_tp, x_sems, tp_sems, at.shape[1], 12
                ),
            ),
            trades(),
        )
        net.finish()

    lanes = pairs.shape[3]
    gain_lanes = members * sum(widths)
    scratch = [
        pltpu.VMEM((len(TRADED_BACK),) + ff_own.shape[1:], BF),
        pltpu.VMEM((len(TRADED_BACK),) + ff_own.shape[1:], BF),
        pltpu.VMEM((8,) + at.shape[1:], BF),
        pltpu.VMEM((2, 8) + at.shape[1:], BF),
        pltpu.VMEM((8, 2, rows, lanes), BF),
        pltpu.VMEM((8, rows, lanes), BF),
        pltpu.VMEM((rows, lanes), F32),
        pltpu.VMEM((rows, qr), F32),
        pltpu.VMEM((rows, wide), BF),
        pltpu.VMEM((16, 16, gain_lanes), BF),
        pltpu.VMEM((16, 16, gain_lanes), BF),
        pltpu.VMEM(down_shape, BF),
        pltpu.VMEM((16 * rows, wide), BF),
        pltpu.VMEM((dim // 16, wide), BF),
        pltpu.VMEM((dim // 16, wide), BF),
    ]
    scratch += reduce_scratch(rows, lanes, 8) + reduce_scratch(rows, qr, 8)
    scratch += reduce_scratch(16, gain_lanes, 16)
    scratch += [
        pltpu.SemaphoreType.DMA((2, 8)),
        pltpu.SemaphoreType.DMA((16,)),
        pltpu.SemaphoreType.DMA((2, 8)),
        pltpu.SemaphoreType.DMA((2, 8)),
        pltpu.SemaphoreType.DMA((2, len(TRADED_BACK))),
    ]
    return comm_call(
        "wind_up",
        number,
        body,
        [pairs, queries, at, both, x, grad_middle, down, *gains, second, cosine, sine_table]
        + [columns, ff_own, ff_got],
        [VMEM] * 6 + [ANY] + [VMEM] * 7 + [ANY] * 2,
        [
            shape((4,) + at.shape[1:]),
            shape((len(TRADED_BACK),) + ff_own.shape[1:]),
            shape((dim // 16, wide), F32),
            shape((rows, dim)),
            shape((rows, dim)),
            shape((16, gain_lanes), F32),
        ],
        [ANY, ANY, VMEM, VMEM, ANY, VMEM],
        scratch,
        260,
    )


def norm_factor(values):
    return lax.rsqrt(jnp.mean(values * values, axis=-1, keepdims=True) + eps_norm)


def branch_and_norm(number, parts, x, gain, gf, n_ctx):
    rows, dim = x.shape
    parts = parts.reshape(8, rows, dim)

    def body(
        parts_ref, x_ref, gain_ref, gf_ref,
        middle, norms, gfs,
        branch, normed, near, line_in, line_out, sems,
    ):
        place = Place(n_ctx)
        greet(place, line=True, across=True, core=True)
        net = Net(place, sems)

        def second():
            yield from reduce_steps(
                net, parts_ref, branch, None, near, line_in, line_out, rows, 8, 0, 7
            )

            def norm(r):
                values = x_ref[r] + residual_scale * branch[r]
                middle[r] = values
                normed[r] = (values * norm_factor(values) * gain_ref[...]).astype(BF)

            by_rows(rows, 16, norm)
            yield from gather_steps(net, normed, norms, 16, 32, 7)

        run_together(second(), after(0.5, gather_steps(net, gf_ref, gfs, 16, 0, 11)))
        net.finish()

    return comm_call(
        "branch_and_norm",
        number,
        body,
        [parts, x, gain, gf],
        [VMEM] * 3 + [ANY],
        [shape((rows, dim), F32), shape((16, rows, dim)), shape((16, rows, dim))],
        [VMEM, ANY, ANY],
        [pltpu.VMEM((rows, dim), F32), pltpu.VMEM((rows, dim), BF)]
        + reduce_scratch(rows, dim, 8),
        220,
    )


def norm_and_branch_back(number, parts, ffn_parts, middle, out_grad, gain, n_ctx):
    rows, dim = middle.shape
    parts, ffn_parts = parts.reshape(16, rows, dim), ffn_parts.reshape(16, rows, dim)

    def body(
        parts_ref, ffn_ref, middle_ref, out_grad_ref, gain_ref,
        grad_middle, gain_part, branches, output,
        upstream, branch, ffn_sum, *rest,
    ):
        place = Place(n_ctx)
        greet(place, line=True, across=True, core=True)
        net = Net(place, rest[-1])

        def chain():
            yield from reduce_steps(net, parts_ref, upstream, *rest[:4], rows, 16, 0, 7)
            gain_part[...] = jnp.zeros((8, dim), F32)

            def back(r):
                grads, share = norm_back_rows(middle_ref[r], gain_ref[...], upstream[r])
                total = out_grad_ref[r] + grads
                grad_middle[r] = total
                branch[r] = (residual_scale * total).astype(BF)
                gain_part[...] += share

            by_rows(rows, 16, back)
            yield from gather_steps(net, branch, branches, 8, 38, 7)

        run_together(
            chain(), after(0.5, reduce_steps(net, ffn_ref, ffn_sum, *rest[4:8], rows, 16, 28, 7))
        )
        output[...] = (middle_ref[...] + residual_scale * ffn_sum[...]).astype(BF)
        net.finish()

    return comm_call(
        "norm_and_branch_back",
        number,
        body,
        [parts, ffn_parts, middle, out_grad, gain],
        [VMEM] * 5,
        [
            shape((rows, dim), F32),
            shape((8, dim), F32),
            shape((8, rows, dim)),
            shape((rows, dim)),
        ],
        [VMEM, VMEM, ANY, VMEM],
        [
            pltpu.VMEM((rows, dim), F32),
            pltpu.VMEM((rows, dim), BF),
            pltpu.VMEM((rows, dim), F32),
        ]
        + reduce_scratch(rows, dim, 16) * 2,
        240,
    )


def unit_weights(g, sides, order, units, rows, lanes, wgu_ref, wd_ref):
    pad = jnp.zeros((rows, lanes - units), BF)
    for place, i in enumerate(order):
        cut = pl.ds(pl.multiple_of((g ^ i) * rows, rows), rows)
        for half, side in enumerate(sides):
            block = side(place)
            for k in range(3):
                part = jnp.concatenate([block[:, k * units : (k + 1) * units], pad], axis=1)
                into = wgu_ref if k < 2 else wd_ref
                at = (2 * lanes * k if k < 2 else 0) + half * lanes
                into[cut, at : at + lanes] = part


def forward(number, parts, x, gain, gf, own, oth, own_last, order, units, n_ctx):
    rows, dim = x.shape
    tokens, shard, wide = 16 * rows, own_last.shape[1], own_last.shape[2]
    lanes = 256
    both = 2 * lanes
    parts = parts.reshape(8, rows, dim)
    n_own, n_oth, n_last = len(own), len(oth), own_last.shape[0]
    own_places, oth_places = [
        [(a, k) for a, w in enumerate(side) for k in range(w.shape[0])] for side in (own, oth)
    ]
    n_early = len(own_places)

    def body(parts_ref, x_ref, gain_ref, gf_ref, *refs):
        own_refs, oth_refs, last_ref = refs[:n_own], refs[n_own : n_own + n_oth], refs[n_own + n_oth]
        middle, ns_out, gf_out, acts_out, gs_out, ffn_out = refs[n_own + n_oth + 1 :][:6]
        (
            branch, normed, ns_ref, gf_all, acts_ref, gs_ref, ffn_ref, wgu_ref, wd_ref, other_last,
            near, line_in, line_out, last_sems, out_sems, sems,
        ) = refs[n_own + n_oth + 7 :]
        p = Place(n_ctx)
        greet(p, line=True, across=True, core=True, other=True)
        net = Net(p, sems)

        def weights():
            for k in range(n_last):
                net.send(
                    lambda k=k: last_ref.at[k],
                    lambda k=k: other_last.at[k],
                    last_sems.at[k],
                    p.other,
                )
            yield 3.0
            own_block = lambda n: own_refs[own_places[n][0]][own_places[n][1]]
            oth_block = lambda n: oth_refs[oth_places[n][0]][oth_places[n][1]]
            unit_weights(
                p.g, (own_block, oth_block), order[:n_early], units, shard, lanes, wgu_ref, wd_ref
            )
            yield 30.5
            for k in range(n_last):
                net.recv(lambda k=k: other_last.at[k], last_sems.at[k])
            unit_weights(
                p.g,
                (lambda k: last_ref[k], lambda k: other_last[k]),
                order[n_early:],
                units,
                shard,
                lanes,
                wgu_ref,
                wd_ref,
            )

        a = p.a
        nth = (
            a,
            jnp.where(a == 0, 1, a - 1),
            jnp.where(a < 2, 2, jnp.where(a == 2, 3, 1)),
            jnp.where(a < 2, 3, 0),
        )
        stores = []

        def compute(n):
            r = pl.ds(pl.multiple_of(nth[n] * 4 * rows, 4 * rows), 4 * rows)
            gate_up = matmul(ns_ref[r], wgu_ref[...])
            gate, up = gate_up[:, :both], gate_up[:, both:]
            grad_hidden = matmul(gf_all[r], wd_ref[...])
            sigmoid_gate = 1.0 / (1.0 + jnp.exp(-gate))
            silu = gate * sigmoid_gate
            acts_ref[r, 2 * both :] = (silu * up).astype(BF)
            acts_ref[r, :both] = (
                grad_hidden * up * sigmoid_gate * (1.0 + gate * (1.0 - sigmoid_gate))
            ).astype(BF)
            acts_ref[r, both : 2 * both] = (grad_hidden * silu).astype(BF)
            gs_ref[r] = matmul_nt(acts_ref[r, : 2 * both], wgu_ref[...]).astype(BF)
            ffn_ref[r] = matmul_nt(acts_ref[r, 2 * both :], wd_ref[...]).astype(BF)
            pairs = (
                (ns_ref, ns_out), (gf_all, gf_out), (acts_ref, acts_out), (gs_ref, gs_out),
                (ffn_ref, ffn_out),
            )
            for k, (src, dst) in enumerate(pairs):
                stores.append(pltpu.make_async_copy(src.at[r], dst.at[r], out_sems.at[n, k]))
                stores[-1].start()

        def second():
            yield from reduce_steps(
                net, parts_ref, branch, None, near, line_in, line_out, rows, 8, 0, 7
            )

            def norm(r):
                values = x_ref[r] + residual_scale * branch[r]
                middle[r] = values
                normed[r] = (values * norm_factor(values) * gain_ref[...]).astype(BF)

            by_rows(rows, 16, norm)
            yield from gather_steps(net, normed, RowBlocks(ns_ref, rows), 16, 32, 7, compute)

        run_together(
            second(),
            after(0.5, gather_steps(net, gf_ref, RowBlocks(gf_all, rows), 16, 0, 8, lambda n: None)),
            after(0.7, weights()),
        )
        for store in stores:
            store.wait()
        net.finish()

    ins = [parts, x, gain, gf, *own, *oth, own_last]
    return comm_call(
        "forward",
        number,
        body,
        ins,
        [VMEM] * len(ins),
        [
            shape((rows, dim), F32),
            shape((tokens, dim)),
            shape((tokens, dim)),
            shape((tokens, 3 * both)),
            shape((tokens, dim)),
            shape((tokens, dim)),
        ],
        [VMEM] + [ANY] * 5,
        [
            pltpu.VMEM((rows, dim), F32),
            pltpu.VMEM((rows, dim), BF),
            pltpu.VMEM((tokens, dim), BF),
            pltpu.VMEM((tokens, dim), BF),
            pltpu.VMEM((tokens, 3 * both), BF),
            pltpu.VMEM((tokens, dim), BF),
            pltpu.VMEM((tokens, dim), BF),
            pltpu.VMEM((dim, 2 * both), BF),
            pltpu.VMEM((dim, both), BF),
            pltpu.VMEM(own_last.shape, BF),
        ]
        + reduce_scratch(rows, dim, 8)
        + [pltpu.SemaphoreType.DMA((n_last,)), pltpu.SemaphoreType.DMA((4, 5))],
        240,
    )


def backward(number, gs, ffn, ns, gf, acts, middle, out_grad, gain, units, wide, n_ctx):
    rows, dim = middle.shape
    tokens, shard = 16 * rows, dim // 16
    lanes = 256
    both = 2 * lanes

    def body(
        gs_hbm, ffn_hbm, ns_hbm, gf_hbm, acts_hbm, middle_ref, out_grad_ref, gain_ref,
        grad_middle, gain_part, branches, output, own_out, got_out,
        upstream, branch, ffn_sum, gs_ref, ffn_ref, ns_ref, gf_ref, acts_ref, own, oth,
        *rest,
    ):
        rest = list(rest)
        sems, other_sems, own_sems, load_sems = [rest.pop() for _ in range(4)]
        pairs = (
            (gs_hbm, gs_ref), (ffn_hbm, ffn_ref), (ns_hbm, ns_ref), (acts_hbm, acts_ref),
            (gf_hbm, gf_ref),
        )
        loads = [
            pltpu.make_async_copy(src, dst, load_sems.at[k]) for k, (src, dst) in enumerate(pairs)
        ]
        for load in loads:
            load.start()
        p = Place(n_ctx)
        greet(p, line=True, across=True, core=True, other=True)
        net = Net(p, sems)
        stores = []

        def chain():
            loads[0].wait()
            yield from reduce_steps(
                net, RowBlocks(gs_ref, rows), upstream, *rest[:4], rows, 16, 0, 7
            )
            gain_part[...] = jnp.zeros((8, dim), F32)

            def back(r):
                grads, share = norm_back_rows(middle_ref[r], gain_ref[...], upstream[r])
                total = out_grad_ref[r] + grads
                grad_middle[r] = total
                branch[r] = (residual_scale * total).astype(BF)
                gain_part[...] += share

            by_rows(rows, 16, back)
            yield from gather_steps(net, branch, branches, 8, 38, 7)

        def output_sum():
            loads[1].wait()
            yield from reduce_steps(
                net, RowBlocks(ffn_ref, rows), ffn_sum, *rest[4:8], rows, 16, 28, 7
            )

        def give(q, k, grads):
            for jj in range(4):
                for half, out in enumerate((own, oth)):
                    out[p.g ^ (4 * q + jj), :, k * units : (k + 1) * units] = grads[
                        jj * shard : (jj + 1) * shard, half * lanes : half * lanes + units
                    ].astype(BF)

        def weight_grads():
            for out in (own, oth):
                out[:, :, 3 * units :] = jnp.zeros((16, shard, wide - 3 * units), BF)
            for load in loads[2:]:
                load.wait()
            span = dim // 4
            for q in range(4):
                yield 5.0 + 7.5 * q
                cut = slice(q * span, (q + 1) * span)
                grads = matmul_tn(ns_ref[:, cut], acts_ref[:, : 2 * both])
                give(q, 0, grads[:, :both])
                give(q, 1, grads[:, both:])
                give(q, 2, matmul_tn(gf_ref[:, cut], acts_ref[:, 2 * both :]))
                for n in range(4 * q, 4 * q + 4):
                    net.send(
                        lambda n=n: oth.at[p.g ^ n],
                        lambda n=n: got_out.at[p.g ^ n],
                        other_sems.at[n],
                        p.other,
                    )
                    stores.append(
                        pltpu.make_async_copy(own.at[p.g ^ n], own_out.at[p.g ^ n], own_sems.at[n])
                    )
                    stores[-1].start()
            yield 80.0
            for n in range(16):
                net.recv(lambda n=n: got_out.at[p.g ^ n], other_sems.at[n])

        run_together(chain(), after(0.5, output_sum()), after(3.5, weight_grads()))
        output[...] = (middle_ref[...] + residual_scale * ffn_sum[...]).astype(BF)
        for store in stores:
            store.wait()
        net.finish()

    block_shape = (16, shard, wide)
    return comm_call(
        "backward",
        number,
        body,
        [gs, ffn, ns, gf, acts, middle, out_grad, gain],
        [ANY] * 5 + [VMEM] * 3,
        [
            shape((rows, dim), F32),
            shape((8, dim), F32),
            shape((8, rows, dim)),
            shape((rows, dim)),
            shape(block_shape),
            shape(block_shape),
        ],
        [VMEM, VMEM, ANY, VMEM, ANY, ANY],
        [
            pltpu.VMEM((rows, dim), F32),
            pltpu.VMEM((rows, dim), BF),
            pltpu.VMEM((rows, dim), F32),
            pltpu.VMEM((tokens, dim), BF),
            pltpu.VMEM((tokens, dim), BF),
            pltpu.VMEM((tokens, dim), BF),
            pltpu.VMEM((tokens, dim), BF),
            pltpu.VMEM((tokens, 3 * both), BF),
            pltpu.VMEM(block_shape, BF),
            pltpu.VMEM(block_shape, BF),
        ]
        + reduce_scratch(rows, dim, 16) * 2
        + [
            pltpu.SemaphoreType.DMA((5,)),
            pltpu.SemaphoreType.DMA((16,)),
            pltpu.SemaphoreType.DMA((16,)),
        ],
        240,
    )


def turn(values, cosine, sine_table, back=False):
    lane = lax.broadcasted_iota(jnp.int32, values.shape, 1)
    near = jnp.where((lane >= 80) & (lane < 96), pltpu.roll(values, 16, 1), 0.0)
    far = jnp.where((lane >= 64) & (lane < 80), pltpu.roll(values, 112, 1), 0.0)
    turned = (near - far) * sine_table
    kept = values * jnp.where(lane < 64, 1.0, jnp.where(lane < 96, cosine, 0.0))
    return kept - turned if back else kept + turned


def unpack_heads(at_ref, q_up_ref, l_up_ref, w_ref, q_rows, l_rows):
    o_rows, width = w_ref.shape[0] // 32, w_ref.shape[1]
    first = q_rows + l_rows
    for n in range(16):
        q_up_ref[n * q_rows : (n + 1) * q_rows] = at_ref[n, :q_rows]
        l_up_ref[n * l_rows : (n + 1) * l_rows] = at_ref[n, q_rows:first]
        for half in (0, 1):
            row = (2 * n + half) * o_rows
            w_ref[row : row + o_rows] = at_ref[n, first:, half * width : (half + 1) * width]


def by_rows(rows, step, body):
    pl.loop(0, rows // step)(lambda i: body(pl.ds(pl.multiple_of(i * step, step), step)))


def lanes_of(h):
    return pl.ds(pl.multiple_of(h * 128, 128), 128)


def key_tile(expanded, ropes):
    lane = lax.broadcasted_iota(jnp.int32, expanded.shape, 1)
    return jnp.where(lane < NOPE, expanded, ropes)


def attend(number, qn, at, pairs, cosine, sine_table, q_pos, ff, width, n_ctx):
    rows, keys, heads = qn.shape[0], pairs.shape[0], at.shape[2] // 128
    span, block = keys // 4, rows // 4
    q_rows, l_rows = qn.shape[1] // 16, KVR // 16
    dim = (at.shape[1] - q_rows - l_rows) * 32

    def body(
        qn_ref, at_ref, pairs_ref, cos_ref, sin_ref, pos_ref, ff_ref,
        branch_ref, q_ref, o_ref, lse_ref, att_ref, q_up_ref, l_up_ref, w_ref, far_ref,
        e_ref, top_ref, sum_ref, acc_ref, sems,
    ):
        copies = trade_away(Place(n_ctx), ff_ref, far_ref, sems)
        unpack_heads(at_ref, q_up_ref, l_up_ref, w_ref, q_rows, l_rows)
        by_rows(
            keys,
            256,
            lambda r: e_ref.__setitem__(
                r, matmul(pairs_ref[r, :KVR], l_up_ref[...]).astype(BF)
            ),
        )

        def head(h):
            lanes = lanes_of(h)
            raw = matmul(qn_ref[...], q_up_ref[:, lanes])
            q_ref[:, lanes] = turn(raw, cos_ref[...], sin_ref[...]).astype(BF)
            top_ref[...] = jnp.full(top_ref.shape, -1e30, F32)
            sum_ref[...] = jnp.zeros(sum_ref.shape, F32)
            acc_ref[...] = jnp.zeros(acc_ref.shape, F32)
            for kb in range(4):
                part, cols = slice(kb * block, rows), slice(kb * span, (kb + 1) * span)
                values = e_ref[cols, lanes]
                key = key_tile(values, pairs_ref[cols, KVR:])
                scores = matmul_nt(q_ref[part, lanes], key) * score_scale
                index = lax.broadcasted_iota(jnp.int32, scores.shape, 1) + kb * span
                scores = jnp.where(index <= pos_ref[part, :1], scores, -1e30)
                old = top_ref[part, :1]
                top = jnp.maximum(old, jnp.max(scores, axis=1, keepdims=True))
                weights = jnp.exp(scores - top)
                decay = jnp.exp(old - top)
                total = sum_ref[part, :1] * decay + jnp.sum(weights, axis=1, keepdims=True)
                acc_ref[part] = acc_ref[part] * decay + matmul(weights.astype(BF), values)
                top_ref[part] = jnp.broadcast_to(top, acc_ref[part].shape)
                sum_ref[part] = jnp.broadcast_to(total, acc_ref[part].shape)
            lane = lax.broadcasted_iota(jnp.int32, acc_ref.shape, 1)
            o_ref[:, lanes] = jnp.where(lane < NOPE, 0.0, acc_ref[...] / sum_ref[...])
            lse_ref[:, lanes] = top_ref[...] + jnp.log(sum_ref[...])

        pl.loop(0, heads)(head)
        for h in range(heads):
            att_ref[:, h * VH : (h + 1) * VH] = o_ref[
                :, h * 128 + NOPE : (h + 1) * 128
            ].astype(BF)
        for i in range(dim // 512):
            cut = slice(i * 512, (i + 1) * 512)
            branch_ref[:, cut] = matmul_nt(att_ref[...], w_ref[cut]).astype(BF)
        for copy in copies:
            copy.wait()

    wide = heads * 128
    return pl.pallas_call(
        body,
        out_shape=[
            shape((rows, dim)),
            shape((rows, wide)),
            shape((rows, wide), F32),
            shape((rows, wide), F32),
            shape((rows, heads * VH)),
            shape((qn.shape[1], wide)),
            shape((KVR, wide)),
            shape((dim, width)),
            shape(ff.shape),
        ],
        in_specs=[VMEM] * 6 + [ANY],
        out_specs=[VMEM] * 8 + [ANY],
        scratch_shapes=[pltpu.VMEM((keys, wide), BF)]
        + [pltpu.VMEM((rows, 128), F32)] * 3
        + [pltpu.SemaphoreType.DMA((2, len(TRADED_LAST)))],
        compiler_params=pltpu.CompilerParams(
            collective_id=number, has_side_effects=True, vmem_limit_bytes=60 << 20
        ),
        cost_estimate=pl.CostEstimate(
            flops=20_000_000_000, bytes_accessed=20 << 20, transcendentals=0
        ),
        name="attend",
    )(qn, at, pairs, cosine, sine_table, q_pos, ff)


def attend_back(
    number, gb, qn, q_up, pairs, l_up, w_out_t, cosine, sine_table, q_pos, q, o, lse, att,
    ff_own, ff_got, half, n_ctx,
):
    rows, keys, heads = qn.shape[0], pairs.shape[0], q_up.shape[1] // 128
    span, block = keys // 4, rows // 4
    dim, wide = gb.shape[1], heads * 128
    q_rows, l_rows, o_rows, width = qn.shape[1] // 16, KVR // 16, dim // 32, att.shape[1]
    first = q_rows + l_rows
    unit_rows = ff_own.shape[1]

    def body(
        gb_ref, qn_ref, q_up_ref, pairs_ref, l_up_ref, w_ref, cos_ref, sin_ref, pos_ref,
        q_ref, o_ref, lse_ref, att_ref, own_ref, got_ref, half_ref,
        gp_ref, gqn_ref, at_ref, far_ref, other_ref,
        e_ref, rope_ref, go_ref, gq_ref, dq_ref, inner_ref, mine_ref, theirs_ref, sems, load_sems,
    ):
        loads = [
            pltpu.make_async_copy(part.at[i], hold.at[k], load_sems.at[n, k])
            for n, (part, hold) in enumerate(((own_ref, mine_ref), (got_ref, theirs_ref)))
            for k, i in enumerate(TRADED_LAST)
        ]
        for load in loads:
            load.start()
        for load in loads:
            load.wait()
        for k in range(len(TRADED_LAST)):
            add_into(mine_ref.at[k], [mine_ref.at[k], theirs_ref.at[k]], unit_rows)
        copies = trade_away(Place(n_ctx), mine_ref, far_ref, sems, (half_ref, other_ref))

        def expand(r):
            e_ref[r] = matmul(pairs_ref[r, :KVR], l_up_ref[...]).astype(BF)
            rope_ref[r] = jnp.zeros((256, 128), F32)

        by_rows(keys, 256, expand)
        ga = matmul(gb_ref[...], w_ref[...]).astype(BF)
        for h in range(heads):
            go_ref[:, h * 128 : h * 128 + NOPE] = jnp.zeros((rows, NOPE), BF)
            go_ref[:, h * 128 + NOPE : (h + 1) * 128] = ga[:, h * VH : (h + 1) * VH]
        for i in range(4):
            part = matmul_tn(gb_ref[:, i * dim // 4 : (i + 1) * dim // 4], att_ref[...]).astype(BF)
            for k in range(8):
                half = k % 2
                at_ref[4 * i + k // 2, first:, half * width : (half + 1) * width] = part[
                    k * o_rows : (k + 1) * o_rows
                ]

        def head(h):
            lanes = lanes_of(h)
            dq_ref[...] = jnp.zeros(dq_ref.shape, F32)
            inner = jnp.sum(
                go_ref[:, lanes].astype(F32) * o_ref[:, lanes], axis=1, keepdims=True
            )
            inner_ref[...] = jnp.broadcast_to(inner, inner_ref.shape)
            for kb in range(4):
                part, cols = slice(kb * block, rows), slice(kb * span, (kb + 1) * span)
                values = e_ref[cols, lanes]
                key = key_tile(values, pairs_ref[cols, KVR:])
                queries, grads = q_ref[part, lanes], go_ref[part, lanes]
                scores = matmul_nt(queries, key) * score_scale
                index = lax.broadcasted_iota(jnp.int32, scores.shape, 1) + kb * span
                probs = jnp.where(
                    index <= pos_ref[part, :1],
                    jnp.exp(scores - lse_ref[part, lanes][:, :1]),
                    0.0,
                )
                grad_probs = matmul_nt(grads, values)
                grad_scores = (probs * (grad_probs - inner_ref[part, :1])).astype(BF)
                dq_ref[part] += matmul(grad_scores, key)
                grad_key = matmul_tn(grad_scores, queries) * score_scale
                grad_value = matmul_tn(probs.astype(BF), grads)
                lane = lax.broadcasted_iota(jnp.int32, grad_key.shape, 1)
                e_ref[cols, lanes] = jnp.where(lane < NOPE, grad_key, grad_value).astype(BF)
                rope_ref[cols] += jnp.where(lane < NOPE, 0.0, grad_key)
            gq_ref[:, lanes] = turn(
                dq_ref[...] * score_scale, cos_ref[...], sin_ref[...], True
            ).astype(BF)

        pl.loop(0, heads)(head)

        def latents(r):
            gp_ref[r, :KVR] = matmul_nt(e_ref[r], l_up_ref[...]).astype(BF)
            gp_ref[r, KVR:] = rope_ref[r].astype(BF)

        by_rows(keys, 256, latents)
        gl_up = matmul_tn(pairs_ref[:, :KVR], e_ref[...]).astype(BF)
        gq_up = matmul_tn(qn_ref[...], gq_ref[...]).astype(BF)
        for n in range(16):
            at_ref[n, :q_rows] = gq_up[n * q_rows : (n + 1) * q_rows]
            at_ref[n, q_rows:first] = gl_up[n * l_rows : (n + 1) * l_rows]
        gqn_ref[...] = matmul_nt(gq_ref[...], q_up_ref[...]).astype(BF)
        for copy in copies:
            copy.wait()

    return pl.pallas_call(
        body,
        out_shape=[
            shape(pairs.shape),
            shape(qn.shape),
            shape((16, first + o_rows, wide)),
            shape((len(TRADED_LAST),) + ff_own.shape[1:]),
            shape(half.shape),
        ],
        in_specs=[VMEM] * 13 + [ANY] * 3,
        out_specs=[VMEM] * 3 + [ANY] * 2,
        scratch_shapes=[
            pltpu.VMEM((keys, wide), BF),
            pltpu.VMEM((keys, 128), F32),
            pltpu.VMEM((rows, wide), BF),
            pltpu.VMEM((rows, wide), BF),
            pltpu.VMEM((rows, 128), F32),
            pltpu.VMEM((rows, 128), F32),
            pltpu.VMEM((len(TRADED_LAST),) + ff_own.shape[1:], BF),
            pltpu.VMEM((len(TRADED_LAST),) + ff_own.shape[1:], BF),
            pltpu.SemaphoreType.DMA((2, len(TRADED_LAST) + 1)),
            pltpu.SemaphoreType.DMA((2, len(TRADED_LAST))),
        ],
        compiler_params=pltpu.CompilerParams(
            collective_id=number, has_side_effects=True, vmem_limit_bytes=60 << 20
        ),
        cost_estimate=pl.CostEstimate(
            flops=40_000_000_000, bytes_accessed=30 << 20, transcendentals=0
        ),
        name="attend_back",
    )(gb, qn, q_up, pairs, l_up, w_out_t, cosine, sine_table, q_pos, q, o, lse, att, ff_own, ff_got, half)


def shards(
    layer_input,
    first_gain,
    query_down,
    query_gain,
    query_up,
    latent_down,
    latent_gain,
    latent_up,
    out_weight,
    second_gain,
    gate_weight,
    up_weight,
    down_weight,
    out_grad,
):
    n_ctx = lax.axis_size("ctx")
    n_tp = lax.axis_size("tp")
    members = n_ctx // 16
    c = lax.axis_index("ctx")
    t = lax.axis_index("tp")
    g = c // members
    b = lax.rem(g // 2, 2)
    d = lax.rem(g, 2)
    member = lax.rem(c, members)
    ctx_rows, dim = layer_input.shape
    rows = ctx_rows // n_tp
    shard_rows = query_down.shape[0]
    qr = query_down.shape[1]
    heads = H // 8
    units = gate_weight.shape[1] // 16
    member_lists = [[k * members + m for m in range(members)] for k in range(16)]

    def widen(blocks):
        if members == 1:
            return blocks[:, None]
        return lax.all_gather(blocks, "ctx", axis=1, axis_index_groups=member_lists)

    def narrow(blocks):
        if members == 1:
            return blocks[:, 0]
        return lax.psum_scatter(
            blocks.astype(F32), "ctx", scatter_dimension=1, axis_index_groups=member_lists
        ).astype(BF)

    widths = [first_gain.shape[0], query_gain.shape[0], latent_gain.shape[0], second_gain.shape[0]]
    starts = [0, widths[0], widths[0] + widths[1], widths[0] + widths[1] + widths[2]]
    gains = jnp.concatenate([first_gain, query_gain, latent_gain, second_gain]).astype(F32)
    gains = jnp.broadcast_to(gains[None], (8, gains.shape[0]))

    def swap_tp(block):
        return lax.ppermute(block, "tp", [(0, 1), (1, 0)])

    wide = 640
    q_rows_w, l_rows_w, o_rows_w = query_up.shape[0], latent_up.shape[0], shard_rows // 2
    q_width, o_width = heads * (NOPE + ROPE), heads * VH
    x = lax.dynamic_slice_in_dim(layer_input, t * rows, rows, 0).astype(F32)
    out_grad_rows = lax.dynamic_slice_in_dim(out_grad, t * rows, rows, 0).astype(F32)
    grad_ffn = (residual_scale * out_grad_rows).astype(BF)

    def rope_tiles(positions):
        lane = jnp.arange(128, dtype=jnp.int32) % (ROPE // 2)
        frequency = rope_base ** (-lane.astype(F32) / (ROPE // 2))
        angles = positions.astype(F32)[:, None] * frequency[None, :]
        return jnp.cos(angles), jnp.sin(angles)

    row = jnp.arange(rows, dtype=jnp.int32)
    cosine, sine_table = rope_tiles(c * ctx_rows + t * rows + row)
    block = jnp.arange(8, dtype=jnp.int32)
    block_ctx = ((block // 2 * 2 + b) * 2 + block % 2) * members + member
    q_positions = (block_ctx[:, None] * ctx_rows + t * rows + row[None, :]).reshape(-1)
    q_cos, q_sin = rope_tiles(q_positions)
    q_pos = jnp.broadcast_to(q_positions[:, None], (q_positions.shape[0], 128))

    if members == 1:
        (
            both, down_full, *all_gains, pairs, qn_all, token_columns,
            own_near, own_mid, own_last, oth_near, at_all,
        ) = front(
            1, x, query_down, latent_down, gains, gate_weight, up_weight, down_weight.T,
            query_up, latent_up, out_weight.T, cosine, sine_table, widths, n_ctx,
        )
        gain_first, gain_query, gain_latent, gain_second = all_gains
        first_gains = (gain_first, gain_query, gain_latent)
    else:
        down_shard = jnp.concatenate(
            [
                query_down,
                latent_down[:, :KVR],
                jnp.zeros((shard_rows, NOPE), BF),
                latent_down[:, KVR:],
                jnp.zeros((shard_rows, 128 - NOPE - ROPE), BF),
            ],
            axis=1,
        )

        ff = pack(gate_weight, up_weight, down_weight.T, wide, members)
        q_tiles = jnp.pad(
            query_up.reshape(q_rows_w, 4, heads, NOPE + ROPE),
            ((0, 0), (0, 0), (0, 0), (0, 128 - NOPE - ROPE)),
        ).reshape(q_rows_w, 4, wide)
        out_tiles = jnp.transpose(
            out_weight.reshape(4, o_width, 2, o_rows_w), (0, 3, 2, 1)
        ).reshape(4, o_rows_w, wide)
        at = jnp.concatenate(
            [
                jnp.transpose(q_tiles, (1, 0, 2)),
                jnp.transpose(latent_up.reshape(l_rows_w, 4, wide), (1, 0, 2)),
                out_tiles,
            ],
            axis=1,
        )

        down_full, gains, at_mine, own_near = weights_in(1, down_shard, gains, at, ff, n_ctx)
        own_near, ff = lax.optimization_barrier((own_near, ff))
        down_full = widen(down_full).reshape(dim, -1)
        gains = widen(gains[:, 0]).reshape(n_ctx, -1)
        gain_first, gain_query, gain_latent, gain_second = [
            gains[:, s : s + w].reshape(1, -1) for s, w in zip(starts, widths)
        ]
        first_gains = (gain_first, gain_query, gain_latent)
        both, _, pairs, qn_all, token_columns, own_mid, at_all = project(
            3, x, down_full, first_gains, cosine, sine_table, ff, at_mine, n_ctx
        )
        own_last = jnp.stack([ff[i] for i in TRADED_LAST])
        own_near, own_mid = lax.optimization_barrier((own_near, own_mid))
        oth_near = swap_tp(own_near[:4])
    oth_next, oth_mid = swap_tp(own_near[4:]), swap_tp(own_mid)
    lat_rope = widen(pairs).reshape(-1, KVR + 128)
    if members > 1:
        at_all = widen(at_all).reshape(n_ctx, -1, wide)
        out_tiles = at_all[:, q_rows_w + l_rows_w :].reshape(n_ctx, o_rows_w, 2, o_width)
        out_tiles = jnp.transpose(out_tiles, (0, 2, 1, 3)).reshape(16, 2, dim // 32, o_width)
        at_all = jnp.concatenate(
            [
                at_all[:, :q_rows_w].reshape(16, -1, wide),
                at_all[:, q_rows_w : q_rows_w + l_rows_w].reshape(16, -1, wide),
                jnp.transpose(out_tiles, (0, 2, 1, 3)).reshape(16, -1, wide),
            ],
            axis=1,
        )
    branch_part, queries, attended_wide, log_total, attended, q_up, l_up, w_out_t, own_far = attend(
        5, qn_all.reshape(-1, qr), at_all, lat_rope, q_cos, q_sin, q_pos, own_last, o_width, n_ctx
    )
    qn_all = qn_all.reshape(-1, qr)

    order = (0,) + TRADED_FIRST + TRADED_NEXT + TRADED_LAST
    if members == 1:
        middle, ns_all, gf_all, acts, second_part, ffn_part = forward(
            4, branch_part, x, gain_second, grad_ffn, [own_near, own_mid], [oth_near, oth_next, oth_mid],
            own_far, order, units, n_ctx,
        )
        grad_middle, second_gain_part, gb_all, out_half, grads_own, grads_got = backward(
            6, second_part, ffn_part, ns_all, gf_all, acts, middle, out_grad_rows, gain_second,
            units, wide, n_ctx,
        )
    else:
        middle, ns_all, gf_all = branch_and_norm(
            4, branch_part, x, gain_second, grad_ffn, n_ctx
        )
        ns_all, gf_all = ns_all.reshape(-1, dim), gf_all.reshape(-1, dim)
        oth_far = swap_tp(own_far)
        own = [own_near, own_mid, own_far]
        oth = [oth_near, oth_next, oth_mid, oth_far]
        ns_all, oth = lax.optimization_barrier((ns_all, oth))
        own, oth = [[widen(jnp.concatenate(w)).reshape(16, dim // 16, wide)] for w in (own, oth)]
        ffn_part, second_part, grads_own, grads_oth = feed_forward(
            ns_all, gf_all, own, oth, order, units, members
        )
        grads_own = narrow(grads_own.reshape(16, members, shard_rows, wide))
        grads_oth = narrow(grads_oth.reshape(16, members, shard_rows, wide))
        grads_got = swap_tp(grads_oth)
        grad_middle, second_gain_part, gb_all, out_half = norm_and_branch_back(
            6, second_part, ffn_part, middle, out_grad_rows, gain_second, n_ctx
        )
    gb_all, grads_got = lax.optimization_barrier((gb_all, grads_got))
    grad_pairs, gqn_part, at_part, sums_far, out_other = attend_back(
        7, gb_all.reshape(-1, dim), qn_all, q_up, lat_rope, l_up, w_out_t, q_cos, q_sin, q_pos,
        queries, attended_wide, log_total, attended, grads_own, grads_got, out_half, n_ctx,
    )
    if members > 1:
        q_part = at_part[:, : qr // 16].reshape(n_ctx, q_rows_w, wide)
        l_part = at_part[:, qr // 16 : (qr + KVR) // 16].reshape(n_ctx, l_rows_w, wide)
        o_part = at_part[:, (qr + KVR) // 16 :].reshape(16, dim // 32, 2, o_width)
        o_part = jnp.transpose(o_part, (0, 2, 1, 3)).reshape(n_ctx, 2, o_rows_w, o_width)
        o_part = jnp.transpose(o_part, (0, 2, 1, 3)).reshape(n_ctx, o_rows_w, wide)
        at_part = narrow(
            jnp.concatenate([q_part, l_part, o_part], axis=1).reshape(16, members, -1, wide)
        )
    at_sums, sums, down_sum, input_half, input_other, gain_sums = wind_up(
        8,
        narrow(grad_pairs.reshape(16, members, 2, rows, KVR + 128)),
        gqn_part.reshape(8, rows, qr),
        at_part,
        both,
        x,
        grad_middle,
        down_full,
        first_gains,
        second_gain_part,
        cosine,
        sine_table,
        grads_own,
        grads_got,
        token_columns,
        widths,
        n_ctx,
    )
    if members > 1:
        down_sum = lax.psum_scatter(down_sum, "ctx", axis_index_groups=member_lists, tiled=True)
    gain_grads = gain_sums[0]
    if members > 1:
        gain_grads = lax.psum_scatter(
            gain_grads.reshape(members, -1), "ctx", axis_index_groups=member_lists
        )
    first_gain_grad, query_gain_grad, latent_gain_grad, second_gain_grad = [
        gain_grads[s : s + w] for s, w in zip(starts, widths)
    ]

    layer_output, input_grad, *spread_out = spread(
        [sums, sums_far],
        TRADED_BACK + TRADED_LAST,
        at_sums,
        down_sum,
        [out_half, out_other, input_half, input_other],
        units,
        members,
    )
    gate_weight_grad, up_weight_grad, down_grad_t = spread_out[:3]
    if members == 1:
        query_up_grad, latent_up_grad, out_grad_t, query_down_grad, latent_down_grad = spread_out[3:]
        out_weight_grad = out_grad_t.T
    else:
        query_up_grad = jnp.transpose(
            at_sums[:, :q_rows_w].reshape(4, q_rows_w, heads, 128)[..., : NOPE + ROPE], (1, 0, 2, 3)
        ).reshape(q_rows_w, 4 * q_width)
        latent_up_grad = jnp.transpose(at_sums[:, q_rows_w : q_rows_w + l_rows_w], (1, 0, 2)).reshape(
            l_rows_w, 4 * wide
        )
        out_weight_grad = jnp.transpose(
            at_sums[:, q_rows_w + l_rows_w :].reshape(4, o_rows_w, 2, o_width), (0, 3, 2, 1)
        ).reshape(4 * o_width, shard_rows)
        query_down_grad = down_sum[:, :qr]
        latent_down_grad = jnp.concatenate(
            [
                down_sum[:, qr : qr + KVR],
                down_sum[:, qr + KVR + NOPE : qr + KVR + NOPE + ROPE],
            ],
            axis=1,
        )
    return (
        layer_output,
        input_grad,
        first_gain_grad,
        query_down_grad,
        query_gain_grad,
        query_up_grad.astype(F32),
        latent_down_grad,
        latent_gain_grad,
        latent_up_grad.astype(F32),
        out_weight_grad.astype(F32),
        second_gain_grad,
        gate_weight_grad,
        up_weight_grad,
        down_grad_t.T,
    )


def solution(mesh):
    return jax.shard_map(
        shards,
        mesh=mesh,
        in_specs=(
            P("ctx", None),
            P("ctx"),
            P("ctx", None),
            P("ctx"),
            P("ctx", "tp"),
            P("ctx", None),
            P("ctx"),
            P("ctx", "tp"),
            P("tp", "ctx"),
            P("ctx"),
            P("ctx", "tp"),
            P("ctx", "tp"),
            P("tp", "ctx"),
            P("ctx", None),
        ),
        out_specs=(
            P("ctx", None),
            P("ctx", None),
            P("ctx"),
            P("ctx", None),
            P("ctx"),
            P("ctx", "tp"),
            P("ctx", None),
            P("ctx"),
            P("ctx", "tp"),
            P("tp", "ctx"),
            P("ctx"),
            P("ctx", "tp"),
            P("ctx", "tp"),
            P("tp", "ctx"),
        ),
        check_vma=False,
    )
```

```python
import math

import jax
import jax.numpy as jnp
from jax import lax
from jax.experimental import pallas as pl
from jax.experimental.pallas import tpu as pltpu
from jax.sharding import PartitionSpec as P

BF = jnp.bfloat16
F32 = jnp.float32

H = 40
KVR = 256
NOPE = 64
ROPE = 32
VH = 64

eps_norm = 1e-06
residual_scale = 1.4 / math.sqrt(62.0)
score_scale = (NOPE + ROPE) ** (-0.5)
rope_base = 10000.0


def matmul(left_side, right_side):
    return jnp.dot(left_side, right_side, preferred_element_type=F32)


def matmul_nt(left_side, right_side):
    return lax.dot_general(
        left_side, right_side, (((1,), (1,)), ((), ())), preferred_element_type=F32
    )


def matmul_tn(left_side, right_side):
    return lax.dot_general(
        left_side, right_side, (((0,), (0,)), ((), ())), preferred_element_type=F32
    )


def rms_norm(values, scale_gain):
    factor = lax.rsqrt(jnp.mean(values * values, axis=-1, keepdims=True) + eps_norm)
    return values * factor * scale_gain


def norm_back(values, scale_gain, upstream):
    factor = lax.rsqrt(jnp.mean(values * values, axis=-1, keepdims=True) + eps_norm)
    scaled = upstream * scale_gain
    inner_sum = jnp.mean(scaled * values, axis=-1, keepdims=True)
    grad_values = factor * scaled - values * factor * factor * factor * inner_sum
    grad_gain = jnp.sum(upstream * values * factor, axis=0)
    return (grad_values, grad_gain)


def rotate(values, cosine, sine_table):
    half_width = values.shape[-1] // 2
    first_half = values[..., :half_width]
    second_half = values[..., half_width:]
    return jnp.concatenate(
        [
            first_half * cosine - second_half * sine_table,
            second_half * cosine + first_half * sine_table,
        ],
        axis=-1,
    )


def rope_tables(positions):
    frequency = rope_base ** (-jnp.arange(ROPE // 2, dtype=F32) / (ROPE // 2))
    angles = positions.astype(F32)[:, None] * frequency[None, :]
    return (jnp.cos(angles), jnp.sin(angles))


MESH = pl.DeviceIdType.MESH
OFFSETS = (0, -1, 1, -2, 2, -3, 3)


TRADED_FIRST, TRADED_NEXT, TRADED_LAST = (1, 8, 9, 12, 13), (11, 5, 6, 7), (14, 15, 10, 2, 3, 4)
TRADED_BACK = (0,) + TRADED_FIRST + TRADED_NEXT


class Place:
    def __init__(self, n_ctx):
        c = lax.axis_index("ctx")
        self.members = n_ctx // 16
        self.c = c
        self.t = lax.axis_index("tp")
        self.m = lax.rem(c, self.members)
        g = c // self.members
        self.g = g
        self.a, self.b, self.d = g // 4, lax.rem(g // 2, 2), lax.rem(g, 2)

    def at(self, a=None, b=None, d=None):
        a = self.a if a is None else a
        b = self.b if b is None else b
        d = self.d if d is None else d
        return (((a * 2 + b) * 2 + d) * self.members + self.m, self.t)

    def up(self):
        return self.at(a=self.a + 1)

    def down(self):
        return self.at(a=self.a - 1)

    def across(self):
        return self.at(b=1 - self.b)

    def core(self):
        return self.at(d=1 - self.d)

    def other(self):
        return (self.c, 1 - self.t)

    def valid(self, o):
        return None if o == 0 else (self.a + o >= 0 if o < 0 else self.a + o <= 3)


def both_of(p, q):
    if p is None:
        return q
    return p if q is None else p & q


def when(p, body):
    if p is None:
        body()
    else:
        pl.when(p)(body)


class Net:
    def __init__(self, place, sems):
        self.place, self.sems, self.count, self.pending = place, sems, 0, []

    def sem(self):
        self.count += 1
        return self.sems.at[self.count - 1]

    def send(self, src, dst, recv, to, cond=None):
        mine = self.sem()

        def copy():
            return pltpu.make_async_remote_copy(
                src(), dst(), mine, recv, device_id=to(), device_id_type=MESH
            )

        when(cond, lambda: copy().start())
        self.pending.append((cond, lambda: copy().wait_send()))
        return self.pending[-1]

    def sent(self, one):
        self.pending.remove(one)
        when(one[0], one[1])

    def recv(self, dst, sem, cond=None):
        def wait():
            ref = dst()
            pltpu.make_async_remote_copy(
                ref, ref, sem, sem, device_id=self.place.other(), device_id_type=MESH
            ).wait_recv()

        when(cond, wait)

    def finish(self):
        for cond, wait in self.pending:
            when(cond, wait)


def greet(place, line=False, across=False, core=False, other=False, everyone=0):
    barrier = pltpu.get_barrier_semaphore()

    def tell(device):
        pl.semaphore_signal(barrier, inc=1, device_id=device, device_id_type=MESH)

    count = 0
    if everyone:
        for k in range(1, everyone):
            tell((lax.rem(place.c + k * place.members, everyone * place.members), place.t))
        count = count + everyone - 1
    else:
        if line:
            pl.when(place.a < 3)(lambda: tell(place.up()))
            pl.when(place.a > 0)(lambda: tell(place.down()))
            count = count + (place.a < 3).astype(jnp.int32) + (place.a > 0).astype(jnp.int32)
        if across:
            tell(place.across())
            count = count + 1
        if core:
            tell(place.core())
            count = count + 1
    if other:
        tell(place.other())
        count = count + 1
    pl.semaphore_wait(barrier, count)


def trade_away(place, src, out, sems, swaps):
    barrier = pltpu.get_barrier_semaphore()
    count = len(TRADED_LAST)
    devices = [((place.g ^ i) * place.members + place.m, place.t) for i in TRADED_LAST]
    pairs = [(src.at[k], out.at[k]) for k in range(count)]
    devices.append(place.other())
    pairs += swaps
    for device in devices:
        pl.semaphore_signal(barrier, inc=1, device_id=device, device_id_type=MESH)
    pl.semaphore_wait(barrier, count + 1)
    devices += [place.other()] * (len(swaps) - 1)
    copies = [
        pltpu.make_async_remote_copy(
            *pairs[k],
            sems.at[0, k],
            sems.at[1, k],
            device_id=devices[k],
            device_id_type=MESH,
        )
        for k in range(len(pairs))
    ]
    for copy in copies:
        copy.start()
    return copies


def gather_steps(net, src, out, width, start, pace, ready=None):
    p = net.place
    cores = width == 16

    def slot(o, b, d):
        return out.at[((p.a + o) * 2 + b) * 2 + d] if cores else out.at[(p.a + o) * 2 + d]

    z_sem = {o: net.sem() for o in OFFSETS if o}
    x_sem = {o: net.sem() for o in OFFSETS} if cores else {}
    c_sem = {(s, o): net.sem() for s in ((0, 1) if cores else (0,)) for o in OFFSETS}
    own_sem = net.sem()
    keep = pltpu.make_async_copy(src, slot(0, p.b, p.d), own_sem)
    keep.start()

    def forward(o):
        ok = p.valid(o)
        here = lambda: slot(o, p.b, p.d)
        origin = (lambda: src) if o == 0 else here
        if o <= 0 and o > -3:
            net.send(origin, here, z_sem[o - 1], p.up, both_of(ok, p.a < 3))
        if o >= 0 and o < 3:
            net.send(origin, here, z_sem[o + 1], p.down, both_of(ok, p.a > 0))
        if cores:
            net.send(origin, here, x_sem[o], p.across, ok)
        net.send(origin, here, c_sem[0, o], p.core, ok)

    def from_line(o):
        net.recv(lambda: slot(o, p.b, p.d), z_sem[o], p.valid(o))
        forward(o)

    def from_across(o):
        if cores:
            there = lambda: slot(o, 1 - p.b, p.d)
            net.recv(there, x_sem[o], p.valid(o))
            net.send(there, there, c_sem[1, o], p.core, p.valid(o))

    def from_core(o):
        net.recv(lambda: slot(o, p.b, 1 - p.d), c_sem[0, o], p.valid(o))
        if cores:
            net.recv(lambda: slot(o, 1 - p.b, 1 - p.d), c_sem[1, o], p.valid(o))

    forward(0)
    step = pace + 2
    for near in (1, 2, 3, 4):
        yield start + near * step
        if near < 4:
            from_line(-near)
            from_line(near)
            yield start + near * step + 0.5
        around = (0,) if near == 1 else (1 - near, near - 1)
        for o in around:
            from_across(o)
        yield start + near * step + 2
        for o in around:
            from_core(o)
        if near == 1:
            keep.wait()
        if ready is not None:
            ready(near - 1)


def add_into(out, terms, rows):
    step = 16 if rows % 16 == 0 else rows

    def body(i):
        part = pl.ds(pl.multiple_of(i * step, step), step)
        total = terms[0][part].astype(F32)
        for term in terms[1:]:
            total = total + term[part].astype(F32)
        out[part] = total.astype(out.dtype)

    pl.loop(0, rows // step)(body)


def reduce_steps(
    net, parts, out, near_core, near_x, line_in, line_out, rows, width, start, pace, across=False
):
    p = net.place
    cores = width == 16
    order = (-3, 3, -2, 2, -1, 1, 0)
    if cores:
        c_sem = {(b, o): net.sem() for b in (0, 1) for o in order}
        for o in order:
            for side in (1, 0):
                def src(o=o, side=side):
                    b = 1 - p.b if side else p.b
                    return parts.at[((p.a + o) * 2 + b) * 2 + 1 - p.d]

                def dst(o=o, side=side):
                    b = 1 - p.b if side else p.b
                    return near_core.at[(p.a + o) * 2 + b]

                net.send(src, dst, c_sem[side, o], p.core, p.valid(o))
        yield min(start, 1.0)
    x_sem = {o: net.sem() for o in order}
    up_sem = {o: net.sem() for o in (0, 1, 2)}
    down_sem = {o: net.sem() for o in (0, 1, 2)}

    across = across or cores
    pair = p.b if across else p.d

    def mine(o, b):
        g = (p.a + o) * 2 + b
        return near_core.at[g] if cores else parts.at[g]

    for o in order:
        if cores:
            def join(o=o):
                g = (p.a + o) * 2 + 1 - p.b
                add_into(near_core.at[g], [near_core.at[g], parts.at[g * 2 + p.d]], rows)

            net.recv(lambda: near_core.at[(p.a + o) * 2 + 1 - p.b], c_sem[1, o], p.valid(o))
            when(p.valid(o), join)
        net.send(
            lambda o=o: mine(o, 1 - pair),
            lambda o=o: near_x.at[p.a + o],
            x_sem[o],
            p.across if across else p.core,
            p.valid(o),
        )
    for number, o in enumerate(order):
        yield start + 3 + (number // 2 + 1) * (pace + 0.5)
        ok = p.valid(o)
        if cores:
            net.recv(lambda: near_core.at[(p.a + o) * 2 + p.b], c_sem[0, o], ok)

        def terms(o=o):
            g = (p.a + o) * 2 + pair
            own = [near_core.at[g], parts.at[g * 2 + p.d]] if cores else [parts.at[g]]
            return own + [near_x.at[p.a + o]]

        net.recv(lambda: near_x.at[p.a + o], x_sem[o], ok)
        if o == 0:
            below, above = line_in.at[0, 0], line_in.at[1, 0]
            net.recv(lambda: below, up_sem[0], p.a > 0)
            net.recv(lambda: above, down_sem[0], p.a < 3)
            inner = (p.a > 0) & (p.a < 3)
            pl.when(inner)(lambda: add_into(out, terms() + [below, above], rows))
            pl.when(p.a == 0)(lambda: add_into(out, terms() + [above], rows))
            pl.when(p.a == 3)(lambda: add_into(out, terms() + [below], rows))
            continue
        far = abs(o)
        way = 0 if o > 0 else 1
        stage = line_out.at[way, far - 1]
        sems = up_sem if o > 0 else down_sem
        first = p.a == 0 if o > 0 else p.a == 3
        if far < 3:
            came = line_in.at[way, far]
            later = ok & ~first
            net.recv(lambda: came, sems[far], later)
            pl.when(later)(lambda: add_into(stage, terms() + [came], rows))
            pl.when(ok & first)(lambda: add_into(stage, terms(), rows))
        else:
            pl.when(ok)(lambda: add_into(stage, terms(), rows))
        net.send(
            lambda stage=stage: stage,
            lambda far=far, way=way: line_in.at[way, far - 1],
            sems[far - 1],
            p.up if o > 0 else p.down,
            ok,
        )


def swap_steps(net, src, dst):
    sem = net.sem()
    net.send(lambda: src, lambda: dst, sem, net.place.other)
    yield 90.0
    net.recv(lambda: dst, sem)


def together(*tasks):
    tasks = [[0.0, number, task] for number, task in enumerate(tasks)]
    while tasks:
        first = min(tasks)
        try:
            first[0] = next(first[2])
        except StopIteration:
            tasks.remove(first)
        if tasks:
            yield min(tasks)[0]


def run_together(*tasks):
    for _ in together(*tasks):
        pass


def after(start, task):
    yield start
    yield from task


ANY = pl.BlockSpec(memory_space=pl.ANY)
VMEM = pl.BlockSpec(memory_space=pltpu.VMEM)


def comm_call(name, number, body, ins, in_specs, outs, out_specs, scratch, sems):
    return pl.pallas_call(
        body,
        out_shape=outs,
        in_specs=in_specs,
        out_specs=out_specs,
        scratch_shapes=list(scratch) + [pltpu.SemaphoreType.DMA((sems,))],
        compiler_params=pltpu.CompilerParams(
            collective_id=number, has_side_effects=True, vmem_limit_bytes=62 << 20
        ),
        name=name,
    )(*ins)


def shape(dims, dtype=BF):
    return jax.ShapeDtypeStruct(tuple(dims), dtype)


def reduce_scratch(rows, cols, width):
    near_core = [pltpu.VMEM((8, rows, cols), BF)] if width == 16 else []
    return near_core + [
        pltpu.VMEM((4, rows, cols), BF),
        pltpu.VMEM((2, 3, rows, cols), BF),
        pltpu.VMEM((2, 3, rows, cols), BF),
    ]


def trade_sends(net, block, out, sems, timed, ahead=2):
    p = net.place
    going = []
    for i, when_to in timed:
        yield when_to
        if len(going) == ahead:
            net.sent(going.pop(0))
        going.append(
            net.send(
                lambda i=i: block(i),
                lambda i=i: out(i),
                sems.at[i],
                lambda i=i: ((p.g ^ i) * p.members + p.m, p.t),
            )
        )


def trade_receives(net, out, sems, which):
    for i in which:
        net.recv(lambda i=i: out(i), sems.at[i])


def weights_in(number, down, gains, at, ff, n_ctx):
    def body(
        down_ref, gains_ref, at_ref, ff_ref,
        downs, gain_blocks, heads, near,
        at_sems, ff_sems, sems,
    ):
        p = Place(n_ctx)
        greet(p, everyone=16)
        net = Net(p, sems)
        owner = p.d == p.t
        f = p.a * 2 + p.d

        def attention():
            keep = pltpu.make_async_copy(at_ref.at[p.a], heads.at[f], net.sem())
            pl.when(owner)(lambda: keep.start())
            for s in range(4):
                net.send(
                    lambda s=s: at_ref.at[s],
                    lambda: heads.at[f],
                    at_sems.at[f],
                    lambda s=s: p.at(a=s, d=p.t),
                    ~(owner & (p.a == s)),
                )
            yield 50.0
            pl.when(owner)(lambda: keep.wait())
            for q in range(8):
                net.recv(lambda q=q: heads.at[q], at_sems.at[q], owner & (f != q))

        def trades():
            keep = pltpu.make_async_copy(ff_ref.at[0], near.at[0], net.sem())
            keep.start()
            out = lambda i: near.at[1 + TRADED_FIRST.index(i)]
            timed = [(i, 3 * n) for n, i in enumerate(TRADED_FIRST)]
            yield from trade_sends(net, lambda i: ff_ref.at[i], out, ff_sems, timed)
            yield 60.0
            trade_receives(net, out, ff_sems, TRADED_FIRST)
            keep.wait()

        run_together(
            gather_steps(net, gains_ref, gain_blocks, 16, 0, 3),
            gather_steps(net, down_ref, downs, 16, 0, 8),
            after(1.5, attention()),
            trades(),
        )
        net.finish()

    outs = [
        shape((16,) + down.shape),
        shape((16,) + gains.shape, gains.dtype),
        shape((8,) + at.shape[1:]),
        shape((1 + len(TRADED_FIRST),) + ff.shape[1:]),
    ]
    return comm_call(
        "weights_in",
        number,
        body,
        [down, gains, at, ff],
        [ANY] * 4,
        outs,
        [ANY] * 4,
        [pltpu.SemaphoreType.DMA((8,)), pltpu.SemaphoreType.DMA((16,))],
        200,
    )


class RowBlocks:
    def __init__(self, ref, rows):
        self.ref, self.rows, self.at = ref, rows, self

    def __getitem__(self, i):
        return self.ref.at[pl.ds(pl.multiple_of(i * self.rows, self.rows), self.rows)]


def front(
    number, layer_input, query_down, latent_down, gains, gate, up, down_t, query_up, latent_up, out_t,
    cosine, sine_table, widths, n_ctx,
):
    rows, dim = layer_input.shape[0] // 2, layer_input.shape[1]
    shard, qr = query_down.shape
    wide = qr + KVR + 128
    units = gate.shape[1] // 16
    q_rows, l_rows, o_rows = query_up.shape[0], latent_up.shape[0], shard // 2
    heads, width = H // 8, H // 8 * VH
    lanes = heads * 128
    at_rows = q_rows + l_rows + o_rows

    def body(
        x_ref, qd_ref, ld_ref, gains_ref, gate_ref, up_ref, down_ref, qu_ref, lu_ref, ow_ref,
        cos_ref, sin_ref,
        both, x_out, down_out, g1, gq, gl, g2, pairs, queries, columns, first, mid, last,
        other_first, heads_out,
        down_block, downs, gain_blocks, ff, at, normed, pair, query_block,
        heads_mine,
        at_sems, x_sems, tp_sems, keep_sems, ff_sems, other_sems, sems,
    ):
        p = Place(n_ctx)
        x_out[...] = x_ref[pl.ds(pl.multiple_of(p.t * rows, rows), rows)].astype(F32)
        down_block[:, :qr] = qd_ref[...]
        down_block[:, qr : qr + KVR] = ld_ref[:, :KVR]
        none = jnp.zeros((shard, NOPE), BF)
        down_block[:, qr + KVR :] = jnp.concatenate(
            [none, ld_ref[:, KVR:], none[:, :ROPE]], axis=1
        )
        greet(p, everyone=16, other=True)
        net = Net(p, sems)
        owner = p.d == p.t
        f = p.a * 2 + p.d
        place = lambda q, side: (q // 2 * 2 + (1 - p.b if side else p.b)) * 2 + q % 2
        first_out = lambda i: first.at[1 + TRADED_FIRST.index(i)]
        mid_out = lambda i: mid.at[TRADED_NEXT.index(i)]

        def pack_heads():
            for s in range(4):
                for h in range(heads):
                    cut = (s * heads + h) * (NOPE + ROPE)
                    at[s, :q_rows, h * 128 : h * 128 + NOPE + ROPE] = qu_ref[
                        :, cut : cut + NOPE + ROPE
                    ]
                    at[s, :q_rows, h * 128 + NOPE + ROPE : (h + 1) * 128] = jnp.zeros(
                        (q_rows, 128 - NOPE - ROPE), BF
                    )
                at[s, q_rows : q_rows + l_rows] = lu_ref[:, s * lanes : (s + 1) * lanes]
                for half in (0, 1):
                    at[s, q_rows + l_rows :, half * width : (half + 1) * width] = ow_ref[
                        half * o_rows : (half + 1) * o_rows, s * width : (s + 1) * width
                    ]

        def pack_units():
            for n in range(16):
                cut = slice(n * units, (n + 1) * units)
                i = p.g ^ n
                for k, part in enumerate((gate_ref, up_ref, down_ref)):
                    ff[i, :, k * units : (k + 1) * units] = part[:, cut]
                ff[i, :, 3 * units :] = jnp.zeros((shard, lanes - 3 * units), BF)

        def trades():
            yield 1.0
            pack_units()
            keeps = [pltpu.make_async_copy(ff.at[0], first.at[0], net.sem())]
            keeps += [
                pltpu.make_async_copy(ff.at[i], last.at[k], net.sem())
                for k, i in enumerate(TRADED_LAST)
            ]
            for keep in keeps:
                keep.start()
            block = lambda i: ff.at[i]

            def onward(k, src):
                net.send(src, lambda: other_first.at[k], other_sems.at[k], p.other)

            onward(0, lambda: ff.at[0])
            timed = ((1, 3), (8, 5), (9, 12), (12, 30), (13, 38))
            yield from trade_sends(net, block, first_out, ff_sems, timed)
            timed = ((5, 44), (11, 49), (6, 57), (7, 62))
            for k, i in enumerate(TRADED_FIRST[:3]):
                yield 42.0 + 3 * k
                trade_receives(net, first_out, ff_sems, (i,))
                onward(1 + k, lambda i=i: first_out(i))
            yield from trade_sends(net, block, mid_out, ff_sems, timed)
            yield 90.0
            trade_receives(net, first_out, ff_sems, TRADED_FIRST[3:])
            trade_receives(net, mid_out, ff_sems, TRADED_NEXT)
            for k in range(4):
                net.recv(lambda k=k: other_first.at[k], other_sems.at[k])
            for keep in keeps:
                keep.wait()

        def attention():
            pack_heads()
            yield 1.0
            keep = pltpu.make_async_copy(at.at[p.a], heads_mine.at[f], net.sem())
            pl.when(owner)(lambda: keep.start())
            for s in range(4):
                net.send(
                    lambda s=s: at.at[s],
                    lambda: heads_mine.at[f],
                    at_sems.at[f],
                    lambda s=s: p.at(a=s, d=p.t),
                    ~(owner & (p.a == s)),
                )

            def keep_head(q):
                return pltpu.make_async_copy(
                    heads_mine.at[q], heads_out.at[place(q, 0)], keep_sems.at[q]
                )

            yield 24.0
            pl.when(owner)(lambda: keep.wait())
            for q in range(8):
                yield 24.0 + q
                net.recv(lambda q=q: heads_mine.at[q], at_sems.at[q], owner & (f != q))
                pl.when(owner)(lambda: keep_head(q).start())
                for sems_of, to in ((x_sems, p.across), (tp_sems.at[0], p.other)):
                    net.send(
                        lambda q=q: heads_mine.at[q],
                        lambda q=q: heads_out.at[place(q, 0)],
                        sems_of.at[q],
                        to,
                        owner,
                    )
            for q in range(8):
                yield 38.0 + 2 * q
                theirs = lambda q=q: heads_out.at[place(q, 1)]
                net.recv(theirs, x_sems.at[q], owner)
                net.send(theirs, theirs, tp_sems.at[1, q], p.other, owner)
            yield 85.0
            for q in range(8):
                for side in (0, 1):
                    net.recv(lambda: heads_out.at[place(q, side)], tp_sems.at[side, q], ~owner)
                pl.when(owner)(lambda: keep_head(q).wait())

        def latents():
            sem = net.sem()
            net.send(lambda: pair.at[p.t], lambda: pair.at[p.t], sem, p.other)
            yield 54.0
            net.recv(lambda: pair.at[1 - p.t], sem)
            yield from gather_steps(net, pair, pairs, 16, 55, 2.2)

        def chain():
            yield from gather_steps(net, down_block, RowBlocks(downs, shard), 16, 0, 8)
            keep = pltpu.make_async_copy(downs, down_out, net.sem())
            keep.start()
            at_lane = 0
            for out, w in zip((g1, gq, gl, g2), widths):
                for n in range(16):
                    out[:, n * w : (n + 1) * w] = gain_blocks[n, :1, at_lane : at_lane + w]
                at_lane += w
            values = x_out[...]
            normed[...] = (values * norm_factor(values) * g1[...]).astype(BF)
            both[...] = matmul(normed[...], downs[...])
            query, latent = both[:, :qr], both[:, qr : qr + KVR]
            query_block[...] = (query * norm_factor(query) * gq[...]).astype(BF)
            pair[p.t, :, :KVR] = (latent * norm_factor(latent) * gl[...]).astype(BF)
            pair[p.t, :, KVR:] = turn(both[:, qr + KVR :], cos_ref[...], sin_ref[...]).astype(BF)
            tasks = together(latents(), gather_steps(net, query_block, queries, 8, 51, 2.2))
            yield next(tasks)
            for n in range(16):
                columns[n] = normed[:, n * shard : (n + 1) * shard]
            yield from tasks
            keep.wait()

        run_together(
            chain(),
            after(0.5, gather_steps(net, gains_ref, gain_blocks, 16, 0.5, 1)),
            trades(),
            attention(),
        )
        net.finish()

    ff_shape = (shard, lanes)
    return comm_call(
        "front",
        number,
        body,
        [layer_input, query_down, latent_down, gains, gate, up, down_t, query_up, latent_up, out_t]
        + [cosine, sine_table],
        [VMEM] * 12,
        [
            shape((rows, wide), F32),
            shape((rows, dim), F32),
            shape((dim, wide)),
            *[shape((1, 16 * w), F32) for w in widths],
            shape((16, 2, rows, KVR + 128)),
            shape((8, rows, qr)),
            shape((16, rows, shard)),
            shape((1 + len(TRADED_FIRST),) + ff_shape),
            shape((len(TRADED_NEXT),) + ff_shape),
            shape((len(TRADED_LAST),) + ff_shape),
            shape((4,) + ff_shape),
            shape((16, at_rows, lanes)),
        ],
        [VMEM, VMEM, ANY] + [VMEM] * 4 + [ANY] * 2 + [VMEM] + [ANY] * 5,
        [
            pltpu.VMEM((shard, wide), BF),
            pltpu.VMEM((dim, wide), BF),
            pltpu.VMEM((16,) + gains.shape, F32),
            pltpu.VMEM((16,) + ff_shape, BF),
            pltpu.VMEM((4, at_rows, lanes), BF),
            pltpu.VMEM((rows, dim), BF),
            pltpu.VMEM((2, rows, KVR + 128), BF),
            pltpu.VMEM((rows, qr), BF),
            pltpu.VMEM((8, at_rows, lanes), BF),
            pltpu.SemaphoreType.DMA((8,)),
            pltpu.SemaphoreType.DMA((8,)),
            pltpu.SemaphoreType.DMA((2, 8)),
            pltpu.SemaphoreType.DMA((8,)),
            pltpu.SemaphoreType.DMA((16,)),
            pltpu.SemaphoreType.DMA((16,)),
        ],
        300,
    )


def head_grads_steps(net, at_ref, o_ref, o_got, at_out, at_x, at_tp, x_sems, tp_sems, start):
    p = net.place
    owner = p.d == p.t
    f = p.a * 2 + p.d
    rows, o_rows = at_ref.shape[1], o_ref.shape[1]
    place = lambda q, side: (q // 2 * 2 + (1 - p.b if side else p.b)) * 2 + q % 2
    for side in (1, 0):
        for q in range(8):
            net.send(
                lambda q=q, side=side: at_ref.at[place(q, side)],
                lambda q=q, side=side: at_tp.at[side, q, pl.ds(0, rows)],
                tp_sems.at[side, q],
                p.other,
                ~owner,
            )

    def join(side, q):
        here = at_tp.at[side, q, pl.ds(0, rows)]
        net.recv(lambda: here, tp_sems.at[side, q], owner)

        def add():
            n = place(q, side)
            add_into(here, [here, at_ref.at[n]], rows)
            add_into(at_tp.at[side, q, pl.ds(rows, o_rows)], [o_ref.at[n], o_got.at[n]], o_rows)

        pl.when(owner)(add)

    for q in range(8):
        yield start + 2 + q
        join(1, q)
        net.send(
            lambda q=q: at_tp.at[1, q], lambda q=q: at_x.at[q], x_sems.at[0, q], p.across, owner
        )
    keep = pltpu.make_async_copy(at_tp.at[0, f], at_out.at[p.a], net.sem())
    for q in range(8):
        yield start + 11 + 2 * q
        join(0, q)
        here, near = at_tp.at[0, q], at_x.at[q]
        net.recv(lambda: near, x_sems.at[0, q], owner)
        pl.when(owner)(lambda: add_into(here, [here, near], rows + o_rows))
        net.send(
            lambda here=here: here,
            lambda: at_out.at[p.a],
            x_sems.at[1, p.a],
            lambda q=q: p.at(a=q // 2, d=q % 2),
            owner & (f != q),
        )
        pl.when(owner & (f == q))(lambda: keep.start())
    yield start + 55
    for s in range(4):
        net.recv(lambda s=s: at_out.at[s], x_sems.at[1, s], ~(owner & (p.a == s)))
    pl.when(owner)(lambda: keep.wait())


def plain_call(name, body, ins, outs, scratch, members):
    def whole(array):
        return pl.BlockSpec(array.shape, lambda i, g: (0,) * len(array.shape))

    g = (lax.axis_index("ctx") // members).astype(jnp.int32).reshape(1)
    return pl.pallas_call(
        body,
        out_shape=outs,
        grid_spec=pltpu.PrefetchScalarGridSpec(
            num_scalar_prefetch=1,
            grid=(1,),
            in_specs=[whole(i) for i in ins],
            out_specs=[whole(o) for o in outs],
            scratch_shapes=scratch,
        ),
        compiler_params=pltpu.CompilerParams(vmem_limit_bytes=62 << 20),
        cost_estimate=pl.CostEstimate(
            flops=1_000_000_000, bytes_accessed=20 << 20, transcendentals=0
        ),
        name=name,
    )(g, *ins)


def pack(gate, up, down_t, wide, members):
    rows = gate.shape[0]
    units = gate.shape[1] // 16

    def body(g_ref, gate_ref, up_ref, down_ref, out):
        for n in range(16):
            cut = slice(n * units, (n + 1) * units)
            i = g_ref[0] ^ n
            for k, part in enumerate((gate_ref, up_ref, down_ref)):
                out[i, :, k * units : (k + 1) * units] = part[:, cut]
            out[i, :, 3 * units :] = jnp.zeros((rows, wide - 3 * units), BF)

    return plain_call(
        "pack", body, [gate, up, down_t], [shape((16, rows, wide))], [], members
    )[0]


def feed_forward(ns, gf, own, oth, order, units, members):
    tokens, dim = ns.shape
    rows, wide = own[0].shape[1:]
    lanes = 256
    both = 2 * lanes
    places = [[(a, k) for a, w in enumerate(side) for k in range(w.shape[0])] for side in (own, oth)]

    def body(g_ref, ns_ref, gf_ref, *refs):
        own_refs, oth_refs = refs[: len(own)], refs[len(own) : len(own) + len(oth)]
        out_ref, gs_ref, gown_ref, goth_ref = refs[len(own) + len(oth) :][:4]
        wgu_ref, wd_ref, hidden_ref, ggu_ref = refs[-4:]
        g = g_ref[0]
        for place, i in enumerate(order):
            cut = pl.ds(pl.multiple_of((g ^ i) * rows, rows), rows)
            for half, side in enumerate((own_refs, oth_refs)):
                a, k = places[half][place]
                block = side[a][k]
                pad = jnp.zeros((rows, lanes - units), BF)
                for k in range(3):
                    part = jnp.concatenate([block[:, k * units : (k + 1) * units], pad], axis=1)
                    into = wgu_ref if k < 2 else wd_ref
                    at = (both * k if k < 2 else 0) + half * lanes
                    into[cut, at : at + lanes] = part

        def forth(i):
            r = pl.ds(pl.multiple_of(i * 256, 256), 256)
            gate_up = matmul(ns_ref[r], wgu_ref[...])
            gate, up = gate_up[:, :both], gate_up[:, both:]
            grad_hidden = matmul(gf_ref[r], wd_ref[...])
            sigmoid_gate = 1.0 / (1.0 + jnp.exp(-gate))
            silu = gate * sigmoid_gate
            hidden_ref[r] = (silu * up).astype(BF)
            ggu_ref[r, :both] = (
                grad_hidden * up * sigmoid_gate * (1.0 + gate * (1.0 - sigmoid_gate))
            ).astype(BF)
            ggu_ref[r, both:] = (grad_hidden * silu).astype(BF)
            gs_ref[r] = matmul_nt(ggu_ref[r], wgu_ref[...]).astype(BF)
            out_ref[r] = matmul_nt(hidden_ref[r], wd_ref[...]).astype(BF)

        pl.loop(0, tokens // 256)(forth)

        span = dim // 4

        def give(q, k, grads):
            for jj in range(4):
                for half, out in enumerate((gown_ref, goth_ref)):
                    out[g ^ (4 * q + jj), :, k * units : (k + 1) * units] = grads[
                        jj * rows : (jj + 1) * rows, half * lanes : half * lanes + units
                    ].astype(BF)

        for q in range(4):
            cut = slice(q * span, (q + 1) * span)
            grads = matmul_tn(ns_ref[:, cut], ggu_ref[...])
            give(q, 0, grads[:, :both])
            give(q, 1, grads[:, both:])
            give(q, 2, matmul_tn(gf_ref[:, cut], hidden_ref[...]))
        for out in (gown_ref, goth_ref):
            out[:, :, 3 * units :] = jnp.zeros((16, rows, wide - 3 * units), BF)

    return plain_call(
        "feed_forward",
        body,
        [ns, gf, *own, *oth],
        [shape((tokens, dim))] * 2 + [shape((16, rows, wide))] * 2,
        [
            pltpu.VMEM((dim, 2 * both), BF),
            pltpu.VMEM((dim, both), BF),
            pltpu.VMEM((tokens, both), BF),
            pltpu.VMEM((tokens, 2 * both), BF),
        ],
        members,
    )


def spread(parts, order, at, down, halves, units, members):
    rows, cols = parts[0].shape[1:]
    places = [(a, k) for a, w in enumerate(parts) for k in range(w.shape[0])]
    n_parts = len(parts)
    heads, width = H // 8, H // 8 * VH
    o_rows = rows // 2
    q_rows, l_rows = 3 * KVR // 16, KVR // 16
    outs = [shape((rows, 16 * units), F32)] * 3
    if members == 1:
        outs += [
            shape((q_rows, 4 * heads * (NOPE + ROPE)), F32),
            shape((l_rows, 4 * cols), F32),
            shape((rows, 4 * width), F32),
            shape((rows, down.shape[1] - KVR - 128), F32),
            shape((rows, KVR + ROPE), F32),
        ]
    own_rows, dim = halves[0].shape
    outs = [shape((2 * own_rows, dim)), shape((2 * own_rows, dim), F32)] + outs
    ins = list(halves) + ([at, down] if members == 1 else []) + list(parts)
    first = len(ins) - n_parts

    def body(g_ref, *refs):
        out_refs = refs[len(ins) : -1]
        t = lax.axis_index("tp")
        for k in range(4):
            start = pl.multiple_of((t if k % 2 == 0 else 1 - t) * own_rows, own_rows)
            out = out_refs[k // 2]
            out[pl.ds(start, own_rows)] = refs[k][...].astype(out.dtype)
        hold = refs[-1]
        for i, (a, k) in zip(order, places):
            hold[g_ref[0] ^ i] = refs[first + a][k].astype(F32)
        rest = out_refs[2:]
        for n in range(16):
            for k, out in enumerate(rest[:3]):
                out[:, n * units : (n + 1) * units] = hold[n, :, k * units : (k + 1) * units]
        if members == 1:
            at_ref, down_ref = refs[4], refs[5]
            qr = down_ref.shape[1] - KVR - 128
            rest[6][...] = down_ref[:, :qr]
            rest[7][:, :KVR] = down_ref[:, qr : qr + KVR]
            rest[7][:, KVR:] = down_ref[:, qr + KVR + NOPE : qr + KVR + NOPE + ROPE]
            for s in range(4):
                part = at_ref[s].astype(F32)
                for h in range(heads):
                    cut = (s * heads + h) * (NOPE + ROPE)
                    rest[3][:, cut : cut + NOPE + ROPE] = part[
                        :q_rows, h * 128 : h * 128 + NOPE + ROPE
                    ]
                rest[4][:, s * cols : (s + 1) * cols] = part[q_rows : q_rows + l_rows]
                for half in (0, 1):
                    rest[5][half * o_rows : (half + 1) * o_rows, s * width : (s + 1) * width] = (
                        part[q_rows + l_rows :, half * width : (half + 1) * width]
                    )

    return plain_call(
        "spread",
        body,
        ins,
        outs,
        [pltpu.VMEM((16, rows, cols), F32)],
        members,
    )


def project(number, x, down, gains, cosine, sine_table, ff, heads_in, n_ctx):
    rows, dim = x.shape
    wide = down.shape[1]
    qr = wide - KVR - 128
    cols = dim // 16

    def body(
        x_ref, down_ref, g1_ref, gq_ref, gl_ref, cos_ref, sin_ref, ff_ref, heads_ref,
        both, pair, pairs, queries, columns, mid, heads,
        normed, column_blocks, pair_block, query_block,
        col_sems, ff_sems, x_sems, tp_sems, sems,
    ):
        p = Place(n_ctx)
        greet(p, everyone=16, other=True)
        net = Net(p, sems)
        owner = p.d == p.t
        place = lambda q, side: (q // 2 * 2 + (1 - p.b if side else p.b)) * 2 + q % 2
        keep_heads = [net.sem() for _ in range(8)]

        def keep_head(q):
            return pltpu.make_async_copy(heads_ref.at[q], heads.at[place(q, 0)], keep_heads[q])

        def send_head(q, sems_of, to):
            net.send(
                lambda: heads_ref.at[q], lambda: heads.at[place(q, 0)], sems_of.at[q], to, owner
            )

        for q in range(8):
            send_head(q, x_sems, p.across)

        def spread_heads():
            yield 9.5
            for q in range(8):
                pl.when(owner)(lambda: keep_head(q).start())
                send_head(q, tp_sems.at[0], p.other)
            for q in range(8):
                yield 16.0 + 2 * q
                theirs = lambda q=q: heads.at[place(q, 1)]
                net.recv(theirs, x_sems.at[q], owner)
                net.send(theirs, theirs, tp_sems.at[1, q], p.other, owner)
            yield 60.0
            for q in range(8):
                for side in (0, 1):
                    net.recv(lambda: heads.at[place(q, side)], tp_sems.at[side, q], ~owner)
                pl.when(owner)(lambda: keep_head(q).wait())

        out = lambda i: mid.at[TRADED_NEXT.index(i)]
        run_together(trade_sends(net, lambda i: ff_ref.at[i], out, ff_sems, [(i, 0) for i in TRADED_NEXT]))
        values = x_ref[...]
        normed[...] = (values * norm_factor(values) * g1_ref[...]).astype(BF)
        both[...] = matmul(normed[...], down_ref[...])
        query, latent = both[:, :qr], both[:, qr : qr + KVR]
        query_block[...] = (query * norm_factor(query) * gq_ref[...]).astype(BF)
        pair_block[:, :KVR] = (latent * norm_factor(latent) * gl_ref[...]).astype(BF)
        pair_block[:, KVR:] = turn(both[:, qr + KVR :], cos_ref[...], sin_ref[...]).astype(BF)

        def send_columns():
            for n in range(16):
                column_blocks[n] = normed[:, n * cols : (n + 1) * cols]
            keep = pltpu.make_async_copy(column_blocks.at[p.g], columns.at[p.g], net.sem())
            keep.start()
            for k in range(1, 16):
                if k % 4 == 1:
                    yield 13.0 + k
                net.send(
                    lambda k=k: column_blocks.at[p.g ^ k],
                    lambda: columns.at[p.g],
                    col_sems.at[k],
                    lambda k=k: ((p.g ^ k) * p.members + p.m, p.t),
                )
            yield 50.0
            for k in range(1, 16):
                net.recv(lambda k=k: columns.at[p.g ^ k], col_sems.at[k])
            keep.wait()

        def latents():
            sem = net.sem()
            keep = pltpu.make_async_copy(pair_block, pair.at[p.t], net.sem())
            keep.start()
            net.send(lambda: pair_block, lambda: pair.at[p.t], sem, p.other)
            yield 11.0
            net.recv(lambda: pair.at[1 - p.t], sem)
            keep.wait()
            yield from gather_steps(net, pair, pairs, 16, 12, 2.2)

        run_together(
            latents(),
            gather_steps(net, query_block, queries, 8, 9, 2.2),
            after(9.0, send_columns()),
            spread_heads(),
        )
        trade_receives(net, out, ff_sems, TRADED_NEXT)
        net.finish()

    return comm_call(
        "project",
        number,
        body,
        [x, down, *gains, cosine, sine_table, ff, heads_in],
        [VMEM] * 7 + [ANY] * 2,
        [
            shape((rows, wide), F32),
            shape((2, rows, KVR + 128)),
            shape((16, 2, rows, KVR + 128)),
            shape((8, rows, qr)),
            shape((16, rows, cols)),
            shape((len(TRADED_NEXT),) + ff.shape[1:]),
            shape((16,) + heads_in.shape[1:]),
        ],
        [VMEM] + [ANY] * 6,
        [
            pltpu.VMEM((rows, dim), BF),
            pltpu.VMEM((16, rows, cols), BF),
            pltpu.VMEM((rows, KVR + 128), BF),
            pltpu.VMEM((rows, qr), BF),
            pltpu.SemaphoreType.DMA((16,)),
            pltpu.SemaphoreType.DMA((16,)),
            pltpu.SemaphoreType.DMA((8,)),
            pltpu.SemaphoreType.DMA((2, 8)),
        ],
        240,
    )


def norm_back_rows(values, gain, upstream):
    factor = norm_factor(values)
    scaled = upstream * gain
    inner = jnp.mean(scaled * values, axis=-1, keepdims=True)
    share = upstream * values * factor
    total = share[:8]
    for i in range(1, share.shape[0] // 8):
        total = total + share[8 * i : 8 * i + 8]
    return factor * scaled - values * factor * factor * factor * inner, total


def wind_up(
    number, pairs, queries, at, at_o, at_o_got, both, x, grad_middle, down, gains, second, cosine,
    sine_table, ff_own, ff_got, columns, widths, n_ctx,
):
    rows, dim = x.shape
    wide = down.shape[1]
    qr = wide - KVR - 128
    members = n_ctx // 16
    down_shape = down.shape
    unit_rows = ff_own.shape[1]
    traded = TRADED_FIRST + TRADED_NEXT

    def body(
        pairs_ref, queries_ref, at_ref, o_ref, o_got, both_ref, x_ref, middle_ref, down_hbm,
        g1_ref, gq_ref, gl_ref, second_ref, cos_ref, sin_ref, columns_ref, own_ref, got_ref,
        at_out, ff_out, down_sum, input_half, input_other, gains_out,
        own_hold, ff_sum, at_x, at_tp, core_in, tp_in, pair_sum, query_sum, grad_both, gain_blocks, gain_tp,
        down, both_all, down_part, down_other, *rest,
    ):
        p = Place(n_ctx)
        greet(p, everyone=16, other=True)
        rest = list(rest)
        net = Net(p, rest.pop())
        load_sems, tp_sems, x_sems, ff_sems, pair_sems = [rest.pop() for _ in range(5)]
        load_down = pltpu.make_async_copy(down_hbm, down, net.sem())
        load_down.start()

        def latents():
            for q in range(8):
                net.send(
                    lambda q=q: pairs_ref.at[2 * q + 1 - p.d],
                    lambda q=q: core_in.at[q],
                    pair_sems.at[0, q],
                    p.core,
                )
            for q in range(8):
                yield 1.5 + 0.2 * q
                net.recv(lambda q=q: core_in.at[q], pair_sems.at[0, q])
                for half in (0, 1):
                    near = core_in.at[q, half]
                    add_into(near, [near, pairs_ref.at[2 * q + p.d, half]], rows)
                net.send(
                    lambda q=q: core_in.at[q, 1 - p.t],
                    lambda q=q: tp_in.at[q],
                    pair_sems.at[1, q],
                    p.other,
                )
            for q in range(8):
                yield 4.0 + 1.1 * (q + 1)
                net.recv(lambda q=q: tp_in.at[q], pair_sems.at[1, q])
                add_into(tp_in.at[q], [tp_in.at[q], core_in.at[q, p.t]], rows)
            yield from reduce_steps(net, tp_in, pair_sum, None, *rest[:3], rows, 8, 14, 1.1, True)

        def trades():
            loads = {
                i: [
                    pltpu.make_async_copy(ref.at[i], hold.at[k], load_sems.at[n, k])
                    for n, (ref, hold) in enumerate(((own_ref, own_hold), (got_ref, ff_sum)))
                ]
                for k, i in enumerate(TRADED_BACK)
            }
            for load in loads.values():
                for part in load:
                    part.start()

            def block(i):
                return ff_sum.at[TRADED_BACK.index(i)]

            def joined(i):
                for part in loads[i]:
                    part.wait()
                k = TRADED_BACK.index(i)
                add_into(block(i), [block(i), own_hold.at[k]], unit_rows)
                return block(i)

            out = lambda i: ff_out.at[TRADED_BACK.index(i)]
            timed = ((8, 1), (5, 2), (9, 10), (6, 12), (12, 19), (7, 22), (1, 23), (13, 28), (11, 37))
            for i, when_to in timed:
                yield when_to
                joined(i)
                yield from trade_sends(net, block, out, ff_sems, ((i, when_to),))
            keep = pltpu.make_async_copy(joined(0), out(0), net.sem())
            keep.start()
            yield 95.0
            trade_receives(net, out, ff_sems, traded)
            keep.wait()

        def gain_sums():
            sem = net.sem()
            net.send(lambda: gain_blocks, lambda: gain_tp, sem, p.other)
            yield 45.0
            net.recv(lambda: gain_tp, sem)
            pl.loop(0, 16)(lambda g: add_into(gain_tp.at[g], [gain_tp.at[g], gain_blocks.at[g]], 16))
            yield from reduce_steps(net, gain_tp, gains_out, *rest[6:10], 16, 16, 46, 2)

        def gather_and_multiply(gather):
            yield from gather
            columns = columns_ref[...].reshape(16 * rows, columns_ref.shape[2])
            down_part[...] = matmul_tn(columns, both_all[...]).astype(BF)
            swap = swap_steps(net, down_part, down_other)
            yield next(swap)
            yield from swap
            down_sum[...] = down_part[...].astype(F32) + down_other[...].astype(F32)

        def chain():
            yield from together(
                latents(),
                reduce_steps(net, queries_ref, query_sum, None, *rest[3:6], rows, 8, 0, 2.2),
            )
            query_back, query_share = norm_back_rows(
                both_ref[:, :qr], gq_ref[...], query_sum[...]
            )
            grad_both[:, :qr] = query_back.astype(BF)
            latent_back, latent_share = norm_back_rows(
                both_ref[:, qr : qr + KVR], gl_ref[...], pair_sum[:, :KVR]
            )
            grad_both[:, qr : qr + KVR] = latent_back.astype(BF)
            grad_both[:, qr + KVR :] = turn(
                pair_sum[:, KVR:], cos_ref[...], sin_ref[...], True
            ).astype(BF)

            gather = gather_steps(net, grad_both, RowBlocks(both_all, rows), 16, 31, 3.3)
            next(gather)
            load_down.wait()
            input_back, input_share = norm_back_rows(
                x_ref[...], g1_ref[...], matmul_nt(grad_both[...], down[...])
            )
            input_half[...] = (middle_ref[...] + input_back).astype(BF)
            swap = swap_steps(net, input_half, input_other)
            next(swap)
            shares = [
                jnp.sum(share, axis=0, keepdims=True)
                for share in (input_share, query_share, latent_share, second_ref[...])
            ]
            for n in range(16):
                parts = []
                for m in range(members):
                    for share, w in zip(shares, widths):
                        at_lane = (n * members + m) * w
                        parts.append(share[:, at_lane : at_lane + w])
                row = jnp.concatenate(parts, axis=1)
                gain_blocks[n] = jnp.broadcast_to(row, gain_blocks.shape[1:]).astype(BF)
            yield from together(gather_and_multiply(gather), gain_sums(), swap)

        run_together(
            chain(),
            after(
                3.5,
                head_grads_steps(
                    net, at_ref, o_ref, o_got, at_out, at_x, at_tp, x_sems, tp_sems, 12
                ),
            ),
            trades(),
        )
        net.finish()

    lanes = pairs.shape[3]
    gain_lanes = members * sum(widths)
    at_rows = at.shape[1] + at_o.shape[1]
    scratch = [
        pltpu.VMEM((len(TRADED_BACK),) + ff_own.shape[1:], BF),
        pltpu.VMEM((len(TRADED_BACK),) + ff_own.shape[1:], BF),
        pltpu.VMEM((8, at_rows) + at.shape[2:], BF),
        pltpu.VMEM((2, 8, at_rows) + at.shape[2:], BF),
        pltpu.VMEM((8, 2, rows, lanes), BF),
        pltpu.VMEM((8, rows, lanes), BF),
        pltpu.VMEM((rows, lanes), F32),
        pltpu.VMEM((rows, qr), F32),
        pltpu.VMEM((rows, wide), BF),
        pltpu.VMEM((16, 16, gain_lanes), BF),
        pltpu.VMEM((16, 16, gain_lanes), BF),
        pltpu.VMEM(down_shape, BF),
        pltpu.VMEM((16 * rows, wide), BF),
        pltpu.VMEM((dim // 16, wide), BF),
        pltpu.VMEM((dim // 16, wide), BF),
    ]
    scratch += reduce_scratch(rows, lanes, 8) + reduce_scratch(rows, qr, 8)
    scratch += reduce_scratch(16, gain_lanes, 16)
    scratch += [
        pltpu.SemaphoreType.DMA((2, 8)),
        pltpu.SemaphoreType.DMA((16,)),
        pltpu.SemaphoreType.DMA((2, 8)),
        pltpu.SemaphoreType.DMA((2, 8)),
        pltpu.SemaphoreType.DMA((2, len(TRADED_BACK))),
    ]
    return comm_call(
        "wind_up",
        number,
        body,
        [pairs, queries, at, at_o, at_o_got, both, x, grad_middle, down, *gains, second, cosine]
        + [sine_table, columns, ff_own, ff_got],
        [VMEM] * 8 + [ANY] + [VMEM] * 7 + [ANY] * 2,
        [
            shape((4, at_rows) + at.shape[2:]),
            shape((len(TRADED_BACK),) + ff_own.shape[1:]),
            shape((dim // 16, wide), F32),
            shape((rows, dim)),
            shape((rows, dim)),
            shape((16, gain_lanes), F32),
        ],
        [ANY, ANY, VMEM, VMEM, ANY, VMEM],
        scratch,
        260,
    )


def norm_factor(values):
    return lax.rsqrt(jnp.mean(values * values, axis=-1, keepdims=True) + eps_norm)


def branch_and_norm(number, parts, x, gain, gf, n_ctx):
    rows, dim = x.shape
    parts = parts.reshape(8, rows, dim)

    def body(
        parts_ref, x_ref, gain_ref, gf_ref,
        middle, norms, gfs,
        branch, normed, near, line_in, line_out, sems,
    ):
        place = Place(n_ctx)
        greet(place, line=True, across=True, core=True)
        net = Net(place, sems)

        def second():
            yield from reduce_steps(
                net, parts_ref, branch, None, near, line_in, line_out, rows, 8, 0, 7
            )

            def norm(r):
                values = x_ref[r] + residual_scale * branch[r]
                middle[r] = values
                normed[r] = (values * norm_factor(values) * gain_ref[...]).astype(BF)

            by_rows(rows, 16, norm)
            yield from gather_steps(net, normed, norms, 16, 32, 7)

        run_together(second(), after(0.5, gather_steps(net, gf_ref, gfs, 16, 0, 11)))
        net.finish()

    return comm_call(
        "branch_and_norm",
        number,
        body,
        [parts, x, gain, gf],
        [VMEM] * 3 + [ANY],
        [shape((rows, dim), F32), shape((16, rows, dim)), shape((16, rows, dim))],
        [VMEM, ANY, ANY],
        [pltpu.VMEM((rows, dim), F32), pltpu.VMEM((rows, dim), BF)]
        + reduce_scratch(rows, dim, 8),
        220,
    )


def norm_and_branch_back(number, parts, ffn_parts, middle, out_grad, gain, n_ctx):
    rows, dim = middle.shape
    parts, ffn_parts = parts.reshape(16, rows, dim), ffn_parts.reshape(16, rows, dim)

    def body(
        parts_ref, ffn_ref, middle_ref, out_grad_ref, gain_ref,
        grad_middle, gain_part, branches, output,
        upstream, branch, ffn_sum, *rest,
    ):
        place = Place(n_ctx)
        greet(place, line=True, across=True, core=True)
        net = Net(place, rest[-1])

        def chain():
            yield from reduce_steps(net, parts_ref, upstream, *rest[:4], rows, 16, 0, 7)
            gain_part[...] = jnp.zeros((8, dim), F32)

            def back(r):
                grads, share = norm_back_rows(middle_ref[r], gain_ref[...], upstream[r])
                total = out_grad_ref[r] + grads
                grad_middle[r] = total
                branch[r] = (residual_scale * total).astype(BF)
                gain_part[...] += share

            by_rows(rows, 16, back)
            yield from gather_steps(net, branch, branches, 8, 38, 7)

        run_together(
            chain(), after(0.5, reduce_steps(net, ffn_ref, ffn_sum, *rest[4:8], rows, 16, 28, 7))
        )
        output[...] = (middle_ref[...] + residual_scale * ffn_sum[...]).astype(BF)
        net.finish()

    return comm_call(
        "norm_and_branch_back",
        number,
        body,
        [parts, ffn_parts, middle, out_grad, gain],
        [VMEM] * 5,
        [
            shape((rows, dim), F32),
            shape((8, dim), F32),
            shape((8, rows, dim)),
            shape((rows, dim)),
        ],
        [VMEM, VMEM, ANY, VMEM],
        [
            pltpu.VMEM((rows, dim), F32),
            pltpu.VMEM((rows, dim), BF),
            pltpu.VMEM((rows, dim), F32),
        ]
        + reduce_scratch(rows, dim, 16) * 2,
        240,
    )


def unit_weights(g, sides, order, units, rows, lanes, wgu_ref, wd_ref):
    pad = jnp.zeros((rows, lanes - units), BF)
    for place, i in enumerate(order):
        cut = pl.ds(pl.multiple_of((g ^ i) * rows, rows), rows)
        for half, side in enumerate(sides):
            block = side(place)
            for k in range(3):
                part = jnp.concatenate([block[:, k * units : (k + 1) * units], pad], axis=1)
                into = wgu_ref if k < 2 else wd_ref
                at = (2 * lanes * k if k < 2 else 0) + half * lanes
                into[cut, at : at + lanes] = part


def forward(number, parts, x, gain, gf, own, oth, late, order, units, n_ctx):
    rows, dim = x.shape
    tokens, shard = 16 * rows, late[0].shape[1]
    lanes = 256
    both = 2 * lanes
    parts = parts.reshape(8, rows, dim)
    n_own, n_oth, n_late = len(own), len(oth), len(late)
    late_places = [(a, k) for a, w in enumerate(late) for k in range(w.shape[0])]
    n_last = len(late_places)
    own_places, oth_places = [
        [(a, k) for a, w in enumerate(side) for k in range(w.shape[0])] for side in (own, oth)
    ]
    n_early = len(own_places)

    def body(parts_ref, x_ref, gain_ref, gf_ref, *refs):
        own_refs, oth_refs = refs[:n_own], refs[n_own : n_own + n_oth]
        late_refs, refs = refs[n_own + n_oth :][:n_late], refs[n_own + n_oth + n_late :]
        middle, ns_out, gf_out, acts_out, gs_out, ffn_out = refs[:6]
        last_block = lambda k: late_refs[late_places[k][0]].at[late_places[k][1]]
        (
            branch, normed, ns_ref, gf_all, acts_ref, gs_ref, ffn_ref, wgu_ref, wd_ref, other_last,
            near, line_in, line_out, last_sems, out_sems, sems,
        ) = refs[6:]
        p = Place(n_ctx)
        greet(p, line=True, across=True, core=True, other=True)
        net = Net(p, sems)

        def weights():
            for k in range(n_last):
                net.send(
                    lambda k=k: last_block(k),
                    lambda k=k: other_last.at[k],
                    last_sems.at[k],
                    p.other,
                )
            yield 3.0
            own_block = lambda n: own_refs[own_places[n][0]][own_places[n][1]]
            oth_block = lambda n: oth_refs[oth_places[n][0]][oth_places[n][1]]
            unit_weights(
                p.g, (own_block, oth_block), order[:n_early], units, shard, lanes, wgu_ref, wd_ref
            )
            yield 38.0
            for k in range(n_last):
                net.recv(lambda k=k: other_last.at[k], last_sems.at[k])
            unit_weights(
                p.g,
                (lambda k: last_block(k)[...], lambda k: other_last[k]),
                order[n_early:],
                units,
                shard,
                lanes,
                wgu_ref,
                wd_ref,
            )

        a = p.a
        nth = (
            a,
            jnp.where(a == 0, 1, a - 1),
            jnp.where(a < 2, 2, jnp.where(a == 2, 3, 1)),
            jnp.where(a < 2, 3, 0),
        )
        stores = []

        def compute(n):
            r = pl.ds(pl.multiple_of(nth[n] * 4 * rows, 4 * rows), 4 * rows)
            gate_up = matmul(ns_ref[r], wgu_ref[...])
            gate, up = gate_up[:, :both], gate_up[:, both:]
            grad_hidden = matmul(gf_all[r], wd_ref[...])
            sigmoid_gate = 1.0 / (1.0 + jnp.exp(-gate))
            silu = gate * sigmoid_gate
            acts_ref[r, 2 * both :] = (silu * up).astype(BF)
            acts_ref[r, :both] = (
                grad_hidden * up * sigmoid_gate * (1.0 + gate * (1.0 - sigmoid_gate))
            ).astype(BF)
            acts_ref[r, both : 2 * both] = (grad_hidden * silu).astype(BF)
            gs_ref[r] = matmul_nt(acts_ref[r, : 2 * both], wgu_ref[...]).astype(BF)
            ffn_ref[r] = matmul_nt(acts_ref[r, 2 * both :], wd_ref[...]).astype(BF)
            pairs = (
                (ns_ref, ns_out), (gf_all, gf_out), (acts_ref, acts_out), (gs_ref, gs_out),
                (ffn_ref, ffn_out),
            )
            for k, (src, dst) in enumerate(pairs):
                stores.append(pltpu.make_async_copy(src.at[r], dst.at[r], out_sems.at[n, k]))
                stores[-1].start()

        def second():
            yield from reduce_steps(
                net, parts_ref, branch, None, near, line_in, line_out, rows, 8, 0, 7
            )

            def norm(r):
                values = x_ref[r] + residual_scale * branch[r]
                middle[r] = values
                normed[r] = (values * norm_factor(values) * gain_ref[...]).astype(BF)

            by_rows(rows, 16, norm)
            yield from gather_steps(net, normed, RowBlocks(ns_ref, rows), 16, 32, 7, compute)

        run_together(
            second(),
            after(0.5, gather_steps(net, gf_ref, RowBlocks(gf_all, rows), 16, 0, 8, lambda n: None)),
            after(0.7, weights()),
        )
        for store in stores:
            store.wait()
        net.finish()

    ins = [parts, x, gain, gf, *own, *oth, *late]
    return comm_call(
        "forward",
        number,
        body,
        ins,
        [VMEM] * len(ins),
        [
            shape((rows, dim), F32),
            shape((tokens, dim)),
            shape((tokens, dim)),
            shape((tokens, 3 * both)),
            shape((tokens, dim)),
            shape((tokens, dim)),
        ],
        [VMEM] + [ANY] * 5,
        [
            pltpu.VMEM((rows, dim), F32),
            pltpu.VMEM((rows, dim), BF),
            pltpu.VMEM((tokens, dim), BF),
            pltpu.VMEM((tokens, dim), BF),
            pltpu.VMEM((tokens, 3 * both), BF),
            pltpu.VMEM((tokens, dim), BF),
            pltpu.VMEM((tokens, dim), BF),
            pltpu.VMEM((dim, 2 * both), BF),
            pltpu.VMEM((dim, both), BF),
            pltpu.VMEM((n_last,) + late[0].shape[1:], BF),
        ]
        + reduce_scratch(rows, dim, 8)
        + [pltpu.SemaphoreType.DMA((n_last,)), pltpu.SemaphoreType.DMA((4, 5))],
        240,
    )


def backward(number, gs, ffn, ns, gf, acts, middle, out_grad, gain, columns, units, wide, n_ctx):
    rows, dim = middle.shape
    tokens, shard = 16 * rows, dim // 16
    lanes = 256
    both = 2 * lanes

    def body(
        gs_hbm, ffn_hbm, ns_hbm, gf_hbm, acts_hbm, middle_ref, out_grad_ref, gain_ref, col_ref,
        grad_middle, gain_part, branches, output, own_out, got_out, col_out,
        upstream, branch, ffn_sum, gs_ref, ffn_ref, ns_ref, gf_ref, acts_ref, own, oth,
        *rest,
    ):
        rest = list(rest)
        sems, col_sems, other_sems, own_sems, load_sems = [rest.pop() for _ in range(5)]
        pairs = (
            (gs_hbm, gs_ref), (ffn_hbm, ffn_ref), (ns_hbm, ns_ref), (acts_hbm, acts_ref),
            (gf_hbm, gf_ref),
        )
        loads = [
            pltpu.make_async_copy(src, dst, load_sems.at[k]) for k, (src, dst) in enumerate(pairs)
        ]
        for load in loads:
            load.start()
        p = Place(n_ctx)
        greet(p, everyone=16, other=True)
        net = Net(p, sems)
        stores = []

        def chain():
            loads[0].wait()
            yield from reduce_steps(
                net, RowBlocks(gs_ref, rows), upstream, *rest[:4], rows, 16, 0, 7
            )
            gain_part[...] = jnp.zeros((8, dim), F32)

            def back(r):
                grads, share = norm_back_rows(middle_ref[r], gain_ref[...], upstream[r])
                total = out_grad_ref[r] + grads
                grad_middle[r] = total
                branch[r] = (residual_scale * total).astype(BF)
                gain_part[...] += share

            by_rows(rows, 16, back)
            yield from gather_steps(net, branch, branches, 8, 38, 7)

        def output_sum():
            loads[1].wait()
            yield from reduce_steps(
                net, RowBlocks(ffn_ref, rows), ffn_sum, *rest[4:8], rows, 16, 28, 7
            )

        def give(q, k, grads):
            for jj in range(4):
                for half, out in enumerate((own, oth)):
                    out[p.g ^ (4 * q + jj), :, k * units : (k + 1) * units] = grads[
                        jj * shard : (jj + 1) * shard, half * lanes : half * lanes + units
                    ].astype(BF)

        def weight_grads():
            for out in (own, oth):
                out[:, :, 3 * units :] = jnp.zeros((16, shard, wide - 3 * units), BF)
            for load in loads[2:]:
                load.wait()
            span = dim // 4
            for q in range(4):
                yield 5.0 + 7.5 * q
                cut = slice(q * span, (q + 1) * span)
                grads = matmul_tn(ns_ref[:, cut], acts_ref[:, : 2 * both])
                give(q, 0, grads[:, :both])
                give(q, 1, grads[:, both:])
                give(q, 2, matmul_tn(gf_ref[:, cut], acts_ref[:, 2 * both :]))
                for n in range(4 * q, 4 * q + 4):
                    net.send(
                        lambda n=n: oth.at[p.g ^ n],
                        lambda n=n: got_out.at[p.g ^ n],
                        other_sems.at[n],
                        p.other,
                    )
                    stores.append(
                        pltpu.make_async_copy(own.at[p.g ^ n], own_out.at[p.g ^ n], own_sems.at[n])
                    )
                    stores[-1].start()
            yield 80.0
            for n in range(16):
                net.recv(lambda n=n: got_out.at[p.g ^ n], other_sems.at[n])

        def send_columns():
            keep = pltpu.make_async_copy(col_ref.at[p.g], col_out.at[p.g], net.sem())
            keep.start()
            for k in range(1, 16):
                yield 44.0 + 1.5 * k
                net.send(
                    lambda k=k: col_ref.at[p.g ^ k],
                    lambda: col_out.at[p.g],
                    col_sems.at[k],
                    lambda k=k: ((p.g ^ k) * p.members + p.m, p.t),
                )
            yield 82.0
            for k in range(1, 16):
                net.recv(lambda k=k: col_out.at[p.g ^ k], col_sems.at[k])
            keep.wait()

        run_together(
            chain(), after(0.5, output_sum()), after(3.5, weight_grads()), after(4.0, send_columns())
        )
        output[...] = (middle_ref[...] + residual_scale * ffn_sum[...]).astype(BF)
        for store in stores:
            store.wait()
        net.finish()

    block_shape = (16, shard, wide)
    return comm_call(
        "backward",
        number,
        body,
        [gs, ffn, ns, gf, acts, middle, out_grad, gain, columns],
        [ANY] * 5 + [VMEM] * 4,
        [
            shape((rows, dim), F32),
            shape((8, dim), F32),
            shape((8, rows, dim)),
            shape((rows, dim)),
            shape(block_shape),
            shape(block_shape),
            shape(columns.shape),
        ],
        [VMEM, VMEM, ANY, VMEM] + [ANY] * 3,
        [
            pltpu.VMEM((rows, dim), F32),
            pltpu.VMEM((rows, dim), BF),
            pltpu.VMEM((rows, dim), F32),
            pltpu.VMEM((tokens, dim), BF),
            pltpu.VMEM((tokens, dim), BF),
            pltpu.VMEM((tokens, dim), BF),
            pltpu.VMEM((tokens, dim), BF),
            pltpu.VMEM((tokens, 3 * both), BF),
            pltpu.VMEM(block_shape, BF),
            pltpu.VMEM(block_shape, BF),
        ]
        + reduce_scratch(rows, dim, 16) * 2
        + [
            pltpu.SemaphoreType.DMA((5,)),
            pltpu.SemaphoreType.DMA((16,)),
            pltpu.SemaphoreType.DMA((16,)),
            pltpu.SemaphoreType.DMA((16,)),
        ],
        240,
    )


def turn(values, cosine, sine_table, back=False):
    lane = lax.broadcasted_iota(jnp.int32, values.shape, 1)
    near = jnp.where((lane >= 80) & (lane < 96), pltpu.roll(values, 16, 1), 0.0)
    far = jnp.where((lane >= 64) & (lane < 80), pltpu.roll(values, 112, 1), 0.0)
    turned = (near - far) * sine_table
    kept = values * jnp.where(lane < 64, 1.0, jnp.where(lane < 96, cosine, 0.0))
    return kept - turned if back else kept + turned


def unpack_heads(at_ref, q_up_ref, l_up_ref, w_ref, q_rows, l_rows):
    o_rows, width = w_ref.shape[0] // 32, w_ref.shape[1]
    first = q_rows + l_rows
    for n in range(16):
        q_up_ref[n * q_rows : (n + 1) * q_rows] = at_ref[n, :q_rows]
        l_up_ref[n * l_rows : (n + 1) * l_rows] = at_ref[n, q_rows:first]
        for half in (0, 1):
            row = (2 * n + half) * o_rows
            w_ref[row : row + o_rows] = at_ref[n, first:, half * width : (half + 1) * width]


def by_rows(rows, step, body):
    pl.loop(0, rows // step)(lambda i: body(pl.ds(pl.multiple_of(i * step, step), step)))


def lanes_of(h):
    return pl.ds(pl.multiple_of(h * 128, 128), 128)


def key_tile(expanded, ropes):
    lane = lax.broadcasted_iota(jnp.int32, expanded.shape, 1)
    return jnp.where(lane < NOPE, expanded, ropes)


def attend(number, qn, at, pairs, cosine, sine_table, q_pos, ff, near, width, n_ctx):
    rows, keys, heads = qn.shape[0], pairs.shape[0], at.shape[2] // 128
    span, block = keys // 4, rows // 4
    q_rows, l_rows = qn.shape[1] // 16, KVR // 16
    dim = (at.shape[1] - q_rows - l_rows) * 32

    def body(
        qn_ref, at_ref, pairs_ref, cos_ref, sin_ref, pos_ref, ff_ref, near_ref,
        branch_ref, q_ref, o_ref, lse_ref, att_ref, q_up_ref, l_up_ref, w_ref, far_ref,
        next_out,
        e_ref, top_ref, sum_ref, acc_ref, sems,
    ):
        swaps = [(near_ref.at[pl.ds(4, near.shape[0] - 4)], next_out)]
        copies = trade_away(Place(n_ctx), ff_ref, far_ref, sems, swaps)
        unpack_heads(at_ref, q_up_ref, l_up_ref, w_ref, q_rows, l_rows)
        by_rows(
            keys,
            256,
            lambda r: e_ref.__setitem__(
                r, matmul(pairs_ref[r, :KVR], l_up_ref[...]).astype(BF)
            ),
        )

        def head(h):
            lanes = lanes_of(h)
            raw = matmul(qn_ref[...], q_up_ref[:, lanes])
            q_ref[:, lanes] = turn(raw, cos_ref[...], sin_ref[...]).astype(BF)
            top_ref[...] = jnp.full(top_ref.shape, -1e30, F32)
            sum_ref[...] = jnp.zeros(sum_ref.shape, F32)
            acc_ref[...] = jnp.zeros(acc_ref.shape, F32)
            for kb in range(4):
                part, cols = slice(kb * block, rows), slice(kb * span, (kb + 1) * span)
                values = e_ref[cols, lanes]
                key = key_tile(values, pairs_ref[cols, KVR:])
                scores = matmul_nt(q_ref[part, lanes], key) * score_scale
                index = lax.broadcasted_iota(jnp.int32, scores.shape, 1) + kb * span
                scores = jnp.where(index <= pos_ref[part, :1], scores, -1e30)
                old = top_ref[part, :1]
                top = jnp.maximum(old, jnp.max(scores, axis=1, keepdims=True))
                weights = jnp.exp(scores - top)
                decay = jnp.exp(old - top)
                total = sum_ref[part, :1] * decay + jnp.sum(weights, axis=1, keepdims=True)
                acc_ref[part] = acc_ref[part] * decay + matmul(weights.astype(BF), values)
                top_ref[part] = jnp.broadcast_to(top, acc_ref[part].shape)
                sum_ref[part] = jnp.broadcast_to(total, acc_ref[part].shape)
            lane = lax.broadcasted_iota(jnp.int32, acc_ref.shape, 1)
            o_ref[:, lanes] = jnp.where(lane < NOPE, 0.0, acc_ref[...] / sum_ref[...])
            lse_ref[:, lanes] = top_ref[...] + jnp.log(sum_ref[...])

        pl.loop(0, heads)(head)
        for h in range(heads):
            att_ref[:, h * VH : (h + 1) * VH] = o_ref[
                :, h * 128 + NOPE : (h + 1) * 128
            ].astype(BF)
        for i in range(dim // 512):
            cut = slice(i * 512, (i + 1) * 512)
            branch_ref[:, cut] = matmul_nt(att_ref[...], w_ref[cut]).astype(BF)
        for copy in copies:
            copy.wait()

    wide = heads * 128
    return pl.pallas_call(
        body,
        out_shape=[
            shape((rows, dim)),
            shape((rows, wide)),
            shape((rows, wide), F32),
            shape((rows, wide), F32),
            shape((rows, heads * VH)),
            shape((qn.shape[1], wide)),
            shape((KVR, wide)),
            shape((dim, width)),
            shape(ff.shape),
            shape((near.shape[0] - 4,) + near.shape[1:]),
        ],
        in_specs=[VMEM] * 6 + [ANY] * 2,
        out_specs=[VMEM] * 8 + [ANY] * 2,
        scratch_shapes=[pltpu.VMEM((keys, wide), BF)]
        + [pltpu.VMEM((rows, 128), F32)] * 3
        + [pltpu.SemaphoreType.DMA((2, len(TRADED_LAST) + 1))],
        compiler_params=pltpu.CompilerParams(
            collective_id=number, has_side_effects=True, vmem_limit_bytes=60 << 20
        ),
        cost_estimate=pl.CostEstimate(
            flops=20_000_000_000, bytes_accessed=20 << 20, transcendentals=0
        ),
        name="attend",
    )(qn, at, pairs, cosine, sine_table, q_pos, ff, near)


def attend_back(
    number, gb, qn, q_up, pairs, l_up, w_out_t, cosine, sine_table, q_pos, q, o, lse, att,
    ff_own, ff_got, half, n_ctx,
):
    rows, keys, heads = qn.shape[0], pairs.shape[0], q_up.shape[1] // 128
    span, block = keys // 4, rows // 4
    dim, wide = gb.shape[1], heads * 128
    q_rows, l_rows, o_rows, width = qn.shape[1] // 16, KVR // 16, dim // 32, att.shape[1]
    first = q_rows + l_rows
    unit_rows = ff_own.shape[1]

    def body(
        gb_ref, qn_ref, q_up_ref, pairs_ref, l_up_ref, w_ref, cos_ref, sin_ref, pos_ref,
        q_ref, o_ref, lse_ref, att_ref, own_ref, got_ref, half_ref,
        gp_ref, gqn_ref, at_ref, at_o_ref, at_o_got, far_ref, other_ref,
        e_ref, rope_ref, go_ref, gq_ref, dq_ref, inner_ref, mine_ref, theirs_ref, sems, load_sems, at_sems,
    ):
        loads = [
            pltpu.make_async_copy(part.at[i], hold.at[k], load_sems.at[n, k])
            for n, (part, hold) in enumerate(((own_ref, mine_ref), (got_ref, theirs_ref)))
            for k, i in enumerate(TRADED_LAST)
        ]
        for load in loads:
            load.start()
        for load in loads:
            load.wait()
        for k in range(len(TRADED_LAST)):
            add_into(mine_ref.at[k], [mine_ref.at[k], theirs_ref.at[k]], unit_rows)
        place = Place(n_ctx)
        owner = place.d == place.t
        copies = trade_away(place, mine_ref, far_ref, sems, [(half_ref, other_ref)])

        def expand(r):
            e_ref[r] = matmul(pairs_ref[r, :KVR], l_up_ref[...]).astype(BF)
            rope_ref[r] = jnp.zeros((256, 128), F32)

        by_rows(keys, 256, expand)
        ga = matmul(gb_ref[...], w_ref[...]).astype(BF)
        for h in range(heads):
            go_ref[:, h * 128 : h * 128 + NOPE] = jnp.zeros((rows, NOPE), BF)
            go_ref[:, h * 128 + NOPE : (h + 1) * 128] = ga[:, h * VH : (h + 1) * VH]
        for i in range(4):
            part = matmul_tn(gb_ref[:, i * dim // 4 : (i + 1) * dim // 4], att_ref[...]).astype(BF)
            for k in range(8):
                half = k % 2
                at_o_ref[4 * i + k // 2, :, half * width : (half + 1) * width] = part[
                    k * o_rows : (k + 1) * o_rows
                ]

        outward = pltpu.make_async_remote_copy(
            at_o_ref,
            at_o_got,
            at_sems.at[0],
            at_sems.at[1],
            device_id=place.other(),
            device_id_type=MESH,
        )
        pl.when(~owner)(lambda: outward.start())

        def head(h):
            lanes = lanes_of(h)
            dq_ref[...] = jnp.zeros(dq_ref.shape, F32)
            inner = jnp.sum(
                go_ref[:, lanes].astype(F32) * o_ref[:, lanes], axis=1, keepdims=True
            )
            inner_ref[...] = jnp.broadcast_to(inner, inner_ref.shape)
            for kb in range(4):
                part, cols = slice(kb * block, rows), slice(kb * span, (kb + 1) * span)
                values = e_ref[cols, lanes]
                key = key_tile(values, pairs_ref[cols, KVR:])
                queries, grads = q_ref[part, lanes], go_ref[part, lanes]
                scores = matmul_nt(queries, key) * score_scale
                index = lax.broadcasted_iota(jnp.int32, scores.shape, 1) + kb * span
                probs = jnp.where(
                    index <= pos_ref[part, :1],
                    jnp.exp(scores - lse_ref[part, lanes][:, :1]),
                    0.0,
                )
                grad_probs = matmul_nt(grads, values)
                grad_scores = (probs * (grad_probs - inner_ref[part, :1])).astype(BF)
                dq_ref[part] += matmul(grad_scores, key)
                grad_key = matmul_tn(grad_scores, queries) * score_scale
                grad_value = matmul_tn(probs.astype(BF), grads)
                lane = lax.broadcasted_iota(jnp.int32, grad_key.shape, 1)
                e_ref[cols, lanes] = jnp.where(lane < NOPE, grad_key, grad_value).astype(BF)
                rope_ref[cols] += jnp.where(lane < NOPE, 0.0, grad_key)
            gq_ref[:, lanes] = turn(
                dq_ref[...] * score_scale, cos_ref[...], sin_ref[...], True
            ).astype(BF)

        pl.loop(0, heads)(head)

        def latents(r):
            gp_ref[r, :KVR] = matmul_nt(e_ref[r], l_up_ref[...]).astype(BF)
            gp_ref[r, KVR:] = rope_ref[r].astype(BF)

        by_rows(keys, 256, latents)
        gl_up = matmul_tn(pairs_ref[:, :KVR], e_ref[...]).astype(BF)
        gq_up = matmul_tn(qn_ref[...], gq_ref[...]).astype(BF)
        for n in range(16):
            at_ref[n, :q_rows] = gq_up[n * q_rows : (n + 1) * q_rows]
            at_ref[n, q_rows:] = gl_up[n * l_rows : (n + 1) * l_rows]
        gqn_ref[...] = matmul_nt(gq_ref[...], q_up_ref[...]).astype(BF)
        for copy in copies:
            copy.wait()
        pl.when(~owner)(lambda: outward.wait_send())
        pl.when(owner)(lambda: outward.wait_recv())

    return pl.pallas_call(
        body,
        out_shape=[
            shape(pairs.shape),
            shape(qn.shape),
            shape((16, first, wide)),
            shape((16, o_rows, wide)),
            shape((16, o_rows, wide)),
            shape((len(TRADED_LAST),) + ff_own.shape[1:]),
            shape(half.shape),
        ],
        in_specs=[VMEM] * 13 + [ANY] * 3,
        out_specs=[VMEM] * 4 + [ANY] * 3,
        scratch_shapes=[
            pltpu.VMEM((keys, wide), BF),
            pltpu.VMEM((keys, 128), F32),
            pltpu.VMEM((rows, wide), BF),
            pltpu.VMEM((rows, wide), BF),
            pltpu.VMEM((rows, 128), F32),
            pltpu.VMEM((rows, 128), F32),
            pltpu.VMEM((len(TRADED_LAST),) + ff_own.shape[1:], BF),
            pltpu.VMEM((len(TRADED_LAST),) + ff_own.shape[1:], BF),
            pltpu.SemaphoreType.DMA((2, len(TRADED_LAST) + 1)),
            pltpu.SemaphoreType.DMA((2, len(TRADED_LAST))),
            pltpu.SemaphoreType.DMA((2,)),
        ],
        compiler_params=pltpu.CompilerParams(
            collective_id=number, has_side_effects=True, vmem_limit_bytes=60 << 20
        ),
        cost_estimate=pl.CostEstimate(
            flops=40_000_000_000, bytes_accessed=30 << 20, transcendentals=0
        ),
        name="attend_back",
    )(gb, qn, q_up, pairs, l_up, w_out_t, cosine, sine_table, q_pos, q, o, lse, att, ff_own, ff_got, half)


def shards(
    layer_input,
    first_gain,
    query_down,
    query_gain,
    query_up,
    latent_down,
    latent_gain,
    latent_up,
    out_weight,
    second_gain,
    gate_weight,
    up_weight,
    down_weight,
    out_grad,
):
    n_ctx = lax.axis_size("ctx")
    n_tp = lax.axis_size("tp")
    members = n_ctx // 16
    c = lax.axis_index("ctx")
    t = lax.axis_index("tp")
    g = c // members
    b = lax.rem(g // 2, 2)
    d = lax.rem(g, 2)
    member = lax.rem(c, members)
    ctx_rows, dim = layer_input.shape
    rows = ctx_rows // n_tp
    shard_rows = query_down.shape[0]
    qr = query_down.shape[1]
    heads = H // 8
    units = gate_weight.shape[1] // 16
    member_lists = [[k * members + m for m in range(members)] for k in range(16)]

    def widen(blocks):
        if members == 1:
            return blocks[:, None]
        return lax.all_gather(blocks, "ctx", axis=1, axis_index_groups=member_lists)

    def narrow(blocks):
        if members == 1:
            return blocks[:, 0]
        return lax.psum_scatter(
            blocks.astype(F32), "ctx", scatter_dimension=1, axis_index_groups=member_lists
        ).astype(BF)

    widths = [first_gain.shape[0], query_gain.shape[0], latent_gain.shape[0], second_gain.shape[0]]
    starts = [0, widths[0], widths[0] + widths[1], widths[0] + widths[1] + widths[2]]
    gains = jnp.concatenate([first_gain, query_gain, latent_gain, second_gain]).astype(F32)
    gains = jnp.broadcast_to(gains[None], (8, gains.shape[0]))

    def swap_tp(block):
        return lax.ppermute(block, "tp", [(0, 1), (1, 0)])

    wide = 640
    q_rows_w, l_rows_w, o_rows_w = query_up.shape[0], latent_up.shape[0], shard_rows // 2
    q_width, o_width = heads * (NOPE + ROPE), heads * VH
    out_grad_rows = lax.dynamic_slice_in_dim(out_grad, t * rows, rows, 0).astype(F32)
    grad_ffn = (residual_scale * out_grad_rows).astype(BF)

    def rope_tiles(positions):
        lane = jnp.arange(128, dtype=jnp.int32) % (ROPE // 2)
        frequency = rope_base ** (-lane.astype(F32) / (ROPE // 2))
        angles = positions.astype(F32)[:, None] * frequency[None, :]
        return jnp.cos(angles), jnp.sin(angles)

    row = jnp.arange(rows, dtype=jnp.int32)
    cosine, sine_table = rope_tiles(c * ctx_rows + t * rows + row)
    block = jnp.arange(8, dtype=jnp.int32)
    block_ctx = ((block // 2 * 2 + b) * 2 + block % 2) * members + member
    q_positions = (block_ctx[:, None] * ctx_rows + t * rows + row[None, :]).reshape(-1)
    q_cos, q_sin = rope_tiles(q_positions)
    q_pos = jnp.broadcast_to(q_positions[:, None], (q_positions.shape[0], 128))

    if members == 1:
        (
            both, x, down_full, *all_gains, pairs, qn_all, token_columns,
            own_near, own_mid, own_last, oth_near, at_all,
        ) = front(
            1, layer_input, query_down, latent_down, gains, gate_weight, up_weight, down_weight.T,
            query_up, latent_up, out_weight.T, cosine, sine_table, widths, n_ctx,
        )
        gain_first, gain_query, gain_latent, gain_second = all_gains
        first_gains = (gain_first, gain_query, gain_latent)
    else:
        x = lax.dynamic_slice_in_dim(layer_input, t * rows, rows, 0).astype(F32)
        down_shard = jnp.concatenate(
            [
                query_down,
                latent_down[:, :KVR],
                jnp.zeros((shard_rows, NOPE), BF),
                latent_down[:, KVR:],
                jnp.zeros((shard_rows, 128 - NOPE - ROPE), BF),
            ],
            axis=1,
        )

        ff = pack(gate_weight, up_weight, down_weight.T, wide, members)
        q_tiles = jnp.pad(
            query_up.reshape(q_rows_w, 4, heads, NOPE + ROPE),
            ((0, 0), (0, 0), (0, 0), (0, 128 - NOPE - ROPE)),
        ).reshape(q_rows_w, 4, wide)
        out_tiles = jnp.transpose(
            out_weight.reshape(4, o_width, 2, o_rows_w), (0, 3, 2, 1)
        ).reshape(4, o_rows_w, wide)
        at = jnp.concatenate(
            [
                jnp.transpose(q_tiles, (1, 0, 2)),
                jnp.transpose(latent_up.reshape(l_rows_w, 4, wide), (1, 0, 2)),
                out_tiles,
            ],
            axis=1,
        )

        down_full, gains, at_mine, own_near = weights_in(1, down_shard, gains, at, ff, n_ctx)
        own_near, ff = lax.optimization_barrier((own_near, ff))
        down_full = widen(down_full).reshape(dim, -1)
        gains = widen(gains[:, 0]).reshape(n_ctx, -1)
        gain_first, gain_query, gain_latent, gain_second = [
            gains[:, s : s + w].reshape(1, -1) for s, w in zip(starts, widths)
        ]
        first_gains = (gain_first, gain_query, gain_latent)
        both, _, pairs, qn_all, token_columns, own_mid, at_all = project(
            3, x, down_full, first_gains, cosine, sine_table, ff, at_mine, n_ctx
        )
        own_last = jnp.stack([ff[i] for i in TRADED_LAST])
        own_near, own_mid = lax.optimization_barrier((own_near, own_mid))
        oth_near = swap_tp(own_near[:4])
    lat_rope = widen(pairs).reshape(-1, KVR + 128)
    if members > 1:
        at_all = widen(at_all).reshape(n_ctx, -1, wide)
        out_tiles = at_all[:, q_rows_w + l_rows_w :].reshape(n_ctx, o_rows_w, 2, o_width)
        out_tiles = jnp.transpose(out_tiles, (0, 2, 1, 3)).reshape(16, 2, dim // 32, o_width)
        at_all = jnp.concatenate(
            [
                at_all[:, :q_rows_w].reshape(16, -1, wide),
                at_all[:, q_rows_w : q_rows_w + l_rows_w].reshape(16, -1, wide),
                jnp.transpose(out_tiles, (0, 2, 1, 3)).reshape(16, -1, wide),
            ],
            axis=1,
        )
    (
        branch_part, queries, attended_wide, log_total, attended, q_up, l_up, w_out_t,
        own_far, oth_next,
    ) = attend(
        5, qn_all.reshape(-1, qr), at_all, lat_rope, q_cos, q_sin, q_pos, own_last, own_near,
        o_width, n_ctx,
    )
    qn_all = qn_all.reshape(-1, qr)

    order = (0,) + TRADED_FIRST + TRADED_NEXT + TRADED_LAST
    if members == 1:
        middle, ns_all, gf_all, acts, second_part, ffn_part = forward(
            4, branch_part, x, gain_second, grad_ffn, [own_near], [oth_near, oth_next],
            [own_mid, own_far], order, units, n_ctx,
        )
        grad_middle, second_gain_part, gb_all, out_half, grads_own, grads_got, token_columns = backward(
            6, second_part, ffn_part, ns_all, gf_all, acts, middle, out_grad_rows, gain_second,
            token_columns, units, wide, n_ctx,
        )
    else:
        middle, ns_all, gf_all = branch_and_norm(
            4, branch_part, x, gain_second, grad_ffn, n_ctx
        )
        ns_all, gf_all = ns_all.reshape(-1, dim), gf_all.reshape(-1, dim)
        oth_mid, oth_far = swap_tp(own_mid), swap_tp(own_far)
        own = [own_near, own_mid, own_far]
        oth = [oth_near, oth_next, oth_mid, oth_far]
        ns_all, oth = lax.optimization_barrier((ns_all, oth))
        own, oth = [[widen(jnp.concatenate(w)).reshape(16, dim // 16, wide)] for w in (own, oth)]
        ffn_part, second_part, grads_own, grads_oth = feed_forward(
            ns_all, gf_all, own, oth, order, units, members
        )
        grads_own = narrow(grads_own.reshape(16, members, shard_rows, wide))
        grads_oth = narrow(grads_oth.reshape(16, members, shard_rows, wide))
        grads_got = swap_tp(grads_oth)
        grad_middle, second_gain_part, gb_all, out_half = norm_and_branch_back(
            6, second_part, ffn_part, middle, out_grad_rows, gain_second, n_ctx
        )
    gb_all, grads_got = lax.optimization_barrier((gb_all, grads_got))
    grad_pairs, gqn_part, at_part, at_o, at_o_got, sums_far, out_other = attend_back(
        7, gb_all.reshape(-1, dim), qn_all, q_up, lat_rope, l_up, w_out_t, q_cos, q_sin, q_pos,
        queries, attended_wide, log_total, attended, grads_own, grads_got, out_half, n_ctx,
    )
    if members > 1:
        q_part = at_part[:, : qr // 16].reshape(n_ctx, q_rows_w, wide)
        l_part = at_part[:, qr // 16 : (qr + KVR) // 16].reshape(n_ctx, l_rows_w, wide)
        at_part = narrow(
            jnp.concatenate([q_part, l_part], axis=1).reshape(16, members, -1, wide)
        )

        def by_ctx(o_part):
            o_part = o_part.reshape(16, dim // 32, 2, o_width)
            o_part = jnp.transpose(o_part, (0, 2, 1, 3)).reshape(n_ctx, 2, o_rows_w, o_width)
            o_part = jnp.transpose(o_part, (0, 2, 1, 3)).reshape(16, members, o_rows_w, wide)
            return narrow(o_part)

        at_o, at_o_got = by_ctx(at_o), by_ctx(at_o_got)
    at_sums, sums, down_sum, input_half, input_other, gain_sums = wind_up(
        8,
        narrow(grad_pairs.reshape(16, members, 2, rows, KVR + 128)),
        gqn_part.reshape(8, rows, qr),
        at_part,
        at_o,
        at_o_got,
        both,
        x,
        grad_middle,
        down_full,
        first_gains,
        second_gain_part,
        cosine,
        sine_table,
        grads_own,
        grads_got,
        token_columns,
        widths,
        n_ctx,
    )
    if members > 1:
        down_sum = lax.psum_scatter(down_sum, "ctx", axis_index_groups=member_lists, tiled=True)
    gain_grads = gain_sums[0]
    if members > 1:
        gain_grads = lax.psum_scatter(
            gain_grads.reshape(members, -1), "ctx", axis_index_groups=member_lists
        )
    first_gain_grad, query_gain_grad, latent_gain_grad, second_gain_grad = [
        gain_grads[s : s + w] for s, w in zip(starts, widths)
    ]

    layer_output, input_grad, *spread_out = spread(
        [sums, sums_far],
        TRADED_BACK + TRADED_LAST,
        at_sums,
        down_sum,
        [out_half, out_other, input_half, input_other],
        units,
        members,
    )
    gate_weight_grad, up_weight_grad, down_grad_t = spread_out[:3]
    if members == 1:
        query_up_grad, latent_up_grad, out_grad_t, query_down_grad, latent_down_grad = spread_out[3:]
        out_weight_grad = out_grad_t.T
    else:
        query_up_grad = jnp.transpose(
            at_sums[:, :q_rows_w].reshape(4, q_rows_w, heads, 128)[..., : NOPE + ROPE], (1, 0, 2, 3)
        ).reshape(q_rows_w, 4 * q_width)
        latent_up_grad = jnp.transpose(at_sums[:, q_rows_w : q_rows_w + l_rows_w], (1, 0, 2)).reshape(
            l_rows_w, 4 * wide
        )
        out_weight_grad = jnp.transpose(
            at_sums[:, q_rows_w + l_rows_w :].reshape(4, o_rows_w, 2, o_width), (0, 3, 2, 1)
        ).reshape(4 * o_width, shard_rows)
        query_down_grad = down_sum[:, :qr]
        latent_down_grad = jnp.concatenate(
            [
                down_sum[:, qr : qr + KVR],
                down_sum[:, qr + KVR + NOPE : qr + KVR + NOPE + ROPE],
            ],
            axis=1,
        )
    return (
        layer_output,
        input_grad,
        first_gain_grad,
        query_down_grad,
        query_gain_grad,
        query_up_grad.astype(F32),
        latent_down_grad,
        latent_gain_grad,
        latent_up_grad.astype(F32),
        out_weight_grad.astype(F32),
        second_gain_grad,
        gate_weight_grad,
        up_weight_grad,
        down_grad_t.T,
    )


def solution(mesh):
    return jax.shard_map(
        shards,
        mesh=mesh,
        in_specs=(
            P("ctx", None),
            P("ctx"),
            P("ctx", None),
            P("ctx"),
            P("ctx", "tp"),
            P("ctx", None),
            P("ctx"),
            P("ctx", "tp"),
            P("tp", "ctx"),
            P("ctx"),
            P("ctx", "tp"),
            P("ctx", "tp"),
            P("tp", "ctx"),
            P("ctx", None),
        ),
        out_specs=(
            P("ctx", None),
            P("ctx", None),
            P("ctx"),
            P("ctx", None),
            P("ctx"),
            P("ctx", "tp"),
            P("ctx", None),
            P("ctx"),
            P("ctx", "tp"),
            P("tp", "ctx"),
            P("ctx"),
            P("ctx", "tp"),
            P("ctx", "tp"),
            P("tp", "ctx"),
        ),
        check_vma=False,
    )
```

```python
import math

import jax
import jax.numpy as jnp
from jax import lax
from jax.experimental import pallas as pl
from jax.experimental.pallas import tpu as pltpu
from jax.sharding import PartitionSpec as P

BF = jnp.bfloat16
F32 = jnp.float32

H = 40
KVR = 256
NOPE = 64
ROPE = 32
VH = 64

eps_norm = 1e-06
residual_scale = 1.4 / math.sqrt(62.0)
score_scale = (NOPE + ROPE) ** (-0.5)
rope_base = 10000.0


def matmul(left_side, right_side):
    return jnp.dot(left_side, right_side, preferred_element_type=F32)


def matmul_nt(left_side, right_side):
    return lax.dot_general(
        left_side, right_side, (((1,), (1,)), ((), ())), preferred_element_type=F32
    )


def matmul_tn(left_side, right_side):
    return lax.dot_general(
        left_side, right_side, (((0,), (0,)), ((), ())), preferred_element_type=F32
    )


def rms_norm(values, scale_gain):
    factor = lax.rsqrt(jnp.mean(values * values, axis=-1, keepdims=True) + eps_norm)
    return values * factor * scale_gain


def norm_back(values, scale_gain, upstream):
    factor = lax.rsqrt(jnp.mean(values * values, axis=-1, keepdims=True) + eps_norm)
    scaled = upstream * scale_gain
    inner_sum = jnp.mean(scaled * values, axis=-1, keepdims=True)
    grad_values = factor * scaled - values * factor * factor * factor * inner_sum
    grad_gain = jnp.sum(upstream * values * factor, axis=0)
    return (grad_values, grad_gain)


def rotate(values, cosine, sine_table):
    half_width = values.shape[-1] // 2
    first_half = values[..., :half_width]
    second_half = values[..., half_width:]
    return jnp.concatenate(
        [
            first_half * cosine - second_half * sine_table,
            second_half * cosine + first_half * sine_table,
        ],
        axis=-1,
    )


def rope_tables(positions):
    frequency = rope_base ** (-jnp.arange(ROPE // 2, dtype=F32) / (ROPE // 2))
    angles = positions.astype(F32)[:, None] * frequency[None, :]
    return (jnp.cos(angles), jnp.sin(angles))


MESH = pl.DeviceIdType.MESH
OFFSETS = (0, -1, 1, -2, 2, -3, 3)


TRADED_FIRST, TRADED_NEXT, TRADED_LAST = (1, 8, 9, 12, 13), (11, 5, 6, 7), (14, 15, 10, 2, 3, 4)
TRADED_BACK = (0,) + TRADED_FIRST + TRADED_NEXT


class Place:
    def __init__(self, n_ctx):
        c = lax.axis_index("ctx")
        self.members = n_ctx // 16
        self.c = c
        self.t = lax.axis_index("tp")
        self.m = lax.rem(c, self.members)
        g = c // self.members
        self.g = g
        self.a, self.b, self.d = g // 4, lax.rem(g // 2, 2), lax.rem(g, 2)

    def at(self, a=None, b=None, d=None):
        a = self.a if a is None else a
        b = self.b if b is None else b
        d = self.d if d is None else d
        return (((a * 2 + b) * 2 + d) * self.members + self.m, self.t)

    def up(self):
        return self.at(a=self.a + 1)

    def down(self):
        return self.at(a=self.a - 1)

    def across(self):
        return self.at(b=1 - self.b)

    def core(self):
        return self.at(d=1 - self.d)

    def other(self):
        return (self.c, 1 - self.t)

    def valid(self, o):
        return None if o == 0 else (self.a + o >= 0 if o < 0 else self.a + o <= 3)


def both_of(p, q):
    if p is None:
        return q
    return p if q is None else p & q


def when(p, body):
    if p is None:
        body()
    else:
        pl.when(p)(body)


class Net:
    def __init__(self, place, sems):
        self.place, self.sems, self.count, self.pending = place, sems, 0, []

    def sem(self):
        self.count += 1
        return self.sems.at[self.count - 1]

    def send(self, src, dst, recv, to, cond=None):
        mine = self.sem()

        def copy():
            return pltpu.make_async_remote_copy(
                src(), dst(), mine, recv, device_id=to(), device_id_type=MESH
            )

        when(cond, lambda: copy().start())
        self.pending.append((cond, lambda: copy().wait_send()))
        return self.pending[-1]

    def sent(self, one):
        self.pending.remove(one)
        when(one[0], one[1])

    def recv(self, dst, sem, cond=None):
        def wait():
            ref = dst()
            pltpu.make_async_remote_copy(
                ref, ref, sem, sem, device_id=self.place.other(), device_id_type=MESH
            ).wait_recv()

        when(cond, wait)

    def finish(self):
        for cond, wait in self.pending:
            when(cond, wait)


def greet(place, line=False, across=False, core=False, other=False, everyone=0):
    barrier = pltpu.get_barrier_semaphore()

    def tell(device):
        pl.semaphore_signal(barrier, inc=1, device_id=device, device_id_type=MESH)

    count = 0
    if everyone:
        for k in range(1, everyone):
            tell((lax.rem(place.c + k * place.members, everyone * place.members), place.t))
        count = count + everyone - 1
    else:
        if line:
            pl.when(place.a < 3)(lambda: tell(place.up()))
            pl.when(place.a > 0)(lambda: tell(place.down()))
            count = count + (place.a < 3).astype(jnp.int32) + (place.a > 0).astype(jnp.int32)
        if across:
            tell(place.across())
            count = count + 1
        if core:
            tell(place.core())
            count = count + 1
    if other:
        tell(place.other())
        count = count + 1
    pl.semaphore_wait(barrier, count)


def trade_away(place, src, out, sems, swaps):
    barrier = pltpu.get_barrier_semaphore()
    count = len(TRADED_LAST)
    devices = [((place.g ^ i) * place.members + place.m, place.t) for i in TRADED_LAST]
    pairs = [(src.at[k], out.at[k]) for k in range(count)]
    devices.append(place.other())
    pairs += swaps
    for device in devices:
        pl.semaphore_signal(barrier, inc=1, device_id=device, device_id_type=MESH)
    pl.semaphore_wait(barrier, count + 1)
    devices += [place.other()] * (len(swaps) - 1)
    copies = [
        pltpu.make_async_remote_copy(
            *pairs[k],
            sems.at[0, k],
            sems.at[1, k],
            device_id=devices[k],
            device_id_type=MESH,
        )
        for k in range(len(pairs))
    ]
    for copy in copies:
        copy.start()
    return copies


def gather_steps(net, src, out, width, start, pace, ready=None):
    p = net.place
    cores = width == 16

    def slot(o, b, d):
        return out.at[((p.a + o) * 2 + b) * 2 + d] if cores else out.at[(p.a + o) * 2 + d]

    z_sem = {o: net.sem() for o in OFFSETS if o}
    x_sem = {o: net.sem() for o in OFFSETS} if cores else {}
    c_sem = {(s, o): net.sem() for s in ((0, 1) if cores else (0,)) for o in OFFSETS}
    own_sem = net.sem()
    keep = pltpu.make_async_copy(src, slot(0, p.b, p.d), own_sem)
    keep.start()

    def forward(o):
        ok = p.valid(o)
        here = lambda: slot(o, p.b, p.d)
        origin = (lambda: src) if o == 0 else here
        if o <= 0 and o > -3:
            net.send(origin, here, z_sem[o - 1], p.up, both_of(ok, p.a < 3))
        if o >= 0 and o < 3:
            net.send(origin, here, z_sem[o + 1], p.down, both_of(ok, p.a > 0))
        if cores:
            net.send(origin, here, x_sem[o], p.across, ok)
        net.send(origin, here, c_sem[0, o], p.core, ok)

    def from_line(o):
        net.recv(lambda: slot(o, p.b, p.d), z_sem[o], p.valid(o))
        forward(o)

    def from_across(o):
        if cores:
            there = lambda: slot(o, 1 - p.b, p.d)
            net.recv(there, x_sem[o], p.valid(o))
            net.send(there, there, c_sem[1, o], p.core, p.valid(o))

    def from_core(o):
        net.recv(lambda: slot(o, p.b, 1 - p.d), c_sem[0, o], p.valid(o))
        if cores:
            net.recv(lambda: slot(o, 1 - p.b, 1 - p.d), c_sem[1, o], p.valid(o))

    forward(0)
    step = pace + 2
    for near in (1, 2, 3, 4):
        yield start + near * step
        if near < 4:
            from_line(-near)
            from_line(near)
            yield start + near * step + 0.5
        around = (0,) if near == 1 else (1 - near, near - 1)
        for o in around:
            from_across(o)
        yield start + near * step + 2
        for o in around:
            from_core(o)
        if near == 1:
            keep.wait()
        if ready is not None:
            ready(near - 1)


def add_into(out, terms, rows):
    step = 16 if rows % 16 == 0 else rows

    def body(i):
        part = pl.ds(pl.multiple_of(i * step, step), step)
        total = terms[0][part].astype(F32)
        for term in terms[1:]:
            total = total + term[part].astype(F32)
        out[part] = total.astype(out.dtype)

    pl.loop(0, rows // step)(body)


def reduce_steps(
    net, parts, out, near_core, near_x, line_in, line_out, rows, width, start, pace, across=False
):
    p = net.place
    cores = width == 16
    order = (-3, 3, -2, 2, -1, 1, 0)
    if cores:
        c_sem = {(b, o): net.sem() for b in (0, 1) for o in order}
        for o in order:
            for side in (1, 0):
                def src(o=o, side=side):
                    b = 1 - p.b if side else p.b
                    return parts.at[((p.a + o) * 2 + b) * 2 + 1 - p.d]

                def dst(o=o, side=side):
                    b = 1 - p.b if side else p.b
                    return near_core.at[(p.a + o) * 2 + b]

                net.send(src, dst, c_sem[side, o], p.core, p.valid(o))
        yield min(start, 1.0)
    x_sem = {o: net.sem() for o in order}
    up_sem = {o: net.sem() for o in (0, 1, 2)}
    down_sem = {o: net.sem() for o in (0, 1, 2)}

    across = across or cores
    pair = p.b if across else p.d

    def mine(o, b):
        g = (p.a + o) * 2 + b
        return near_core.at[g] if cores else parts.at[g]

    for o in order:
        if cores:
            def join(o=o):
                g = (p.a + o) * 2 + 1 - p.b
                add_into(near_core.at[g], [near_core.at[g], parts.at[g * 2 + p.d]], rows)

            net.recv(lambda: near_core.at[(p.a + o) * 2 + 1 - p.b], c_sem[1, o], p.valid(o))
            when(p.valid(o), join)
        net.send(
            lambda o=o: mine(o, 1 - pair),
            lambda o=o: near_x.at[p.a + o],
            x_sem[o],
            p.across if across else p.core,
            p.valid(o),
        )
    for number, o in enumerate(order):
        yield start + 3 + (number // 2 + 1) * (pace + 0.5)
        ok = p.valid(o)
        if cores:
            net.recv(lambda: near_core.at[(p.a + o) * 2 + p.b], c_sem[0, o], ok)

        def terms(o=o):
            g = (p.a + o) * 2 + pair
            own = [near_core.at[g], parts.at[g * 2 + p.d]] if cores else [parts.at[g]]
            return own + [near_x.at[p.a + o]]

        net.recv(lambda: near_x.at[p.a + o], x_sem[o], ok)
        if o == 0:
            below, above = line_in.at[0, 0], line_in.at[1, 0]
            net.recv(lambda: below, up_sem[0], p.a > 0)
            net.recv(lambda: above, down_sem[0], p.a < 3)
            inner = (p.a > 0) & (p.a < 3)
            pl.when(inner)(lambda: add_into(out, terms() + [below, above], rows))
            pl.when(p.a == 0)(lambda: add_into(out, terms() + [above], rows))
            pl.when(p.a == 3)(lambda: add_into(out, terms() + [below], rows))
            continue
        far = abs(o)
        way = 0 if o > 0 else 1
        stage = line_out.at[way, far - 1]
        sems = up_sem if o > 0 else down_sem
        first = p.a == 0 if o > 0 else p.a == 3
        if far < 3:
            came = line_in.at[way, far]
            later = ok & ~first
            net.recv(lambda: came, sems[far], later)
            pl.when(later)(lambda: add_into(stage, terms() + [came], rows))
            pl.when(ok & first)(lambda: add_into(stage, terms(), rows))
        else:
            pl.when(ok)(lambda: add_into(stage, terms(), rows))
        net.send(
            lambda stage=stage: stage,
            lambda far=far, way=way: line_in.at[way, far - 1],
            sems[far - 1],
            p.up if o > 0 else p.down,
            ok,
        )


def swap_steps(net, src, dst):
    sem = net.sem()
    net.send(lambda: src, lambda: dst, sem, net.place.other)
    yield 90.0
    net.recv(lambda: dst, sem)


def together(*tasks):
    tasks = [[0.0, number, task] for number, task in enumerate(tasks)]
    while tasks:
        first = min(tasks)
        try:
            first[0] = next(first[2])
        except StopIteration:
            tasks.remove(first)
        if tasks:
            yield min(tasks)[0]


def run_together(*tasks):
    for _ in together(*tasks):
        pass


def after(start, task):
    yield start
    yield from task


ANY = pl.BlockSpec(memory_space=pl.ANY)
VMEM = pl.BlockSpec(memory_space=pltpu.VMEM)


def comm_call(name, number, body, ins, in_specs, outs, out_specs, scratch, sems):
    return pl.pallas_call(
        body,
        out_shape=outs,
        in_specs=in_specs,
        out_specs=out_specs,
        scratch_shapes=list(scratch) + [pltpu.SemaphoreType.DMA((sems,))],
        compiler_params=pltpu.CompilerParams(
            collective_id=number, has_side_effects=True, vmem_limit_bytes=62 << 20
        ),
        name=name,
    )(*ins)


def shape(dims, dtype=BF):
    return jax.ShapeDtypeStruct(tuple(dims), dtype)


def reduce_scratch(rows, cols, width):
    near_core = [pltpu.VMEM((8, rows, cols), BF)] if width == 16 else []
    return near_core + [
        pltpu.VMEM((4, rows, cols), BF),
        pltpu.VMEM((2, 3, rows, cols), BF),
        pltpu.VMEM((2, 3, rows, cols), BF),
    ]


def trade_sends(net, block, out, sems, timed, ahead=2):
    p = net.place
    going = []
    for i, when_to in timed:
        yield when_to
        if len(going) == ahead:
            net.sent(going.pop(0))
        going.append(
            net.send(
                lambda i=i: block(i),
                lambda i=i: out(i),
                sems.at[i],
                lambda i=i: ((p.g ^ i) * p.members + p.m, p.t),
            )
        )


def trade_receives(net, out, sems, which):
    for i in which:
        net.recv(lambda i=i: out(i), sems.at[i])


def weights_in(number, down, gains, at, ff, n_ctx):
    def body(
        down_ref, gains_ref, at_ref, ff_ref,
        downs, gain_blocks, heads, near,
        at_sems, ff_sems, sems,
    ):
        p = Place(n_ctx)
        greet(p, everyone=16)
        net = Net(p, sems)
        owner = p.d == p.t
        f = p.a * 2 + p.d

        def attention():
            keep = pltpu.make_async_copy(at_ref.at[p.a], heads.at[f], net.sem())
            pl.when(owner)(lambda: keep.start())
            for s in range(4):
                net.send(
                    lambda s=s: at_ref.at[s],
                    lambda: heads.at[f],
                    at_sems.at[f],
                    lambda s=s: p.at(a=s, d=p.t),
                    ~(owner & (p.a == s)),
                )
            yield 50.0
            pl.when(owner)(lambda: keep.wait())
            for q in range(8):
                net.recv(lambda q=q: heads.at[q], at_sems.at[q], owner & (f != q))

        def trades():
            keep = pltpu.make_async_copy(ff_ref.at[0], near.at[0], net.sem())
            keep.start()
            out = lambda i: near.at[1 + TRADED_FIRST.index(i)]
            timed = [(i, 3 * n) for n, i in enumerate(TRADED_FIRST)]
            yield from trade_sends(net, lambda i: ff_ref.at[i], out, ff_sems, timed)
            yield 60.0
            trade_receives(net, out, ff_sems, TRADED_FIRST)
            keep.wait()

        run_together(
            gather_steps(net, gains_ref, gain_blocks, 16, 0, 3),
            gather_steps(net, down_ref, downs, 16, 0, 8),
            after(1.5, attention()),
            trades(),
        )
        net.finish()

    outs = [
        shape((16,) + down.shape),
        shape((16,) + gains.shape, gains.dtype),
        shape((8,) + at.shape[1:]),
        shape((1 + len(TRADED_FIRST),) + ff.shape[1:]),
    ]
    return comm_call(
        "weights_in",
        number,
        body,
        [down, gains, at, ff],
        [ANY] * 4,
        outs,
        [ANY] * 4,
        [pltpu.SemaphoreType.DMA((8,)), pltpu.SemaphoreType.DMA((16,))],
        200,
    )


class RowBlocks:
    def __init__(self, ref, rows):
        self.ref, self.rows, self.at = ref, rows, self

    def __getitem__(self, i):
        return self.ref.at[pl.ds(pl.multiple_of(i * self.rows, self.rows), self.rows)]


def front(
    number, layer_input, query_down, latent_down, gains, gate, up, down_t, query_up, latent_up, out_t,
    cosine, sine_table, widths, n_ctx,
):
    rows, dim = layer_input.shape[0] // 2, layer_input.shape[1]
    shard, qr = query_down.shape
    wide = qr + KVR + 128
    units = gate.shape[1] // 16
    q_rows, l_rows, o_rows = query_up.shape[0], latent_up.shape[0], shard // 2
    heads, width = H // 8, H // 8 * VH
    lanes = heads * 128
    at_rows = q_rows + l_rows + o_rows

    def body(
        x_ref, qd_ref, ld_ref, gains_ref, gate_ref, up_ref, down_ref, qu_ref, lu_ref, ow_ref,
        cos_ref, sin_ref,
        both, x_out, down_out, g1, gq, gl, g2, pairs, queries, columns, first, mid, last,
        other_first, heads_out,
        down_block, downs, gain_blocks, ff, at, normed, pair, query_block,
        heads_mine,
        at_sems, x_sems, tp_sems, keep_sems, ff_sems, other_sems, sems,
    ):
        p = Place(n_ctx)
        x_out[...] = x_ref[pl.ds(pl.multiple_of(p.t * rows, rows), rows)].astype(F32)
        down_block[:, :qr] = qd_ref[...]
        down_block[:, qr : qr + KVR] = ld_ref[:, :KVR]
        none = jnp.zeros((shard, NOPE), BF)
        down_block[:, qr + KVR :] = jnp.concatenate(
            [none, ld_ref[:, KVR:], none[:, :ROPE]], axis=1
        )
        greet(p, everyone=16, other=True)
        net = Net(p, sems)
        owner = p.d == p.t
        f = p.a * 2 + p.d
        place = lambda q, side: (q // 2 * 2 + (1 - p.b if side else p.b)) * 2 + q % 2
        first_out = lambda i: first.at[1 + TRADED_FIRST.index(i)]
        mid_out = lambda i: mid.at[TRADED_NEXT.index(i)]

        def pack_heads():
            for s in range(4):
                for h in range(heads):
                    cut = (s * heads + h) * (NOPE + ROPE)
                    at[s, :q_rows, h * 128 : h * 128 + NOPE + ROPE] = qu_ref[
                        :, cut : cut + NOPE + ROPE
                    ]
                    at[s, :q_rows, h * 128 + NOPE + ROPE : (h + 1) * 128] = jnp.zeros(
                        (q_rows, 128 - NOPE - ROPE), BF
                    )
                at[s, q_rows : q_rows + l_rows] = lu_ref[:, s * lanes : (s + 1) * lanes]
                for half in (0, 1):
                    at[s, q_rows + l_rows :, half * width : (half + 1) * width] = ow_ref[
                        half * o_rows : (half + 1) * o_rows, s * width : (s + 1) * width
                    ]

        def pack_units():
            for n in range(16):
                cut = slice(n * units, (n + 1) * units)
                i = p.g ^ n
                for k, part in enumerate((gate_ref, up_ref, down_ref)):
                    ff[i, :, k * units : (k + 1) * units] = part[:, cut]
                ff[i, :, 3 * units :] = jnp.zeros((shard, lanes - 3 * units), BF)

        def trades():
            yield 1.0
            pack_units()
            keeps = [pltpu.make_async_copy(ff.at[0], first.at[0], net.sem())]
            keeps += [
                pltpu.make_async_copy(ff.at[i], last.at[k], net.sem())
                for k, i in enumerate(TRADED_LAST)
            ]
            for keep in keeps:
                keep.start()
            block = lambda i: ff.at[i]

            def onward(k, src):
                net.send(src, lambda: other_first.at[k], other_sems.at[k], p.other)

            onward(0, lambda: ff.at[0])
            timed = ((1, 3), (8, 5), (9, 12), (12, 30), (13, 38))
            yield from trade_sends(net, block, first_out, ff_sems, timed)
            timed = ((5, 44), (11, 49), (6, 57), (7, 62))
            for k, i in enumerate(TRADED_FIRST[:3]):
                yield 42.0 + 3 * k
                trade_receives(net, first_out, ff_sems, (i,))
                onward(1 + k, lambda i=i: first_out(i))
            yield from trade_sends(net, block, mid_out, ff_sems, timed)
            yield 90.0
            trade_receives(net, first_out, ff_sems, TRADED_FIRST[3:])
            trade_receives(net, mid_out, ff_sems, TRADED_NEXT)
            for k in range(4):
                net.recv(lambda k=k: other_first.at[k], other_sems.at[k])
            for keep in keeps:
                keep.wait()

        def attention():
            pack_heads()
            yield 1.0
            keep = pltpu.make_async_copy(at.at[p.a], heads_mine.at[f], net.sem())
            pl.when(owner)(lambda: keep.start())
            for s in range(4):
                net.send(
                    lambda s=s: at.at[s],
                    lambda: heads_mine.at[f],
                    at_sems.at[f],
                    lambda s=s: p.at(a=s, d=p.t),
                    ~(owner & (p.a == s)),
                )

            def keep_head(q):
                return pltpu.make_async_copy(
                    heads_mine.at[q], heads_out.at[place(q, 0)], keep_sems.at[q]
                )

            yield 24.0
            pl.when(owner)(lambda: keep.wait())
            for q in range(8):
                yield 24.0 + q
                net.recv(lambda q=q: heads_mine.at[q], at_sems.at[q], owner & (f != q))
                pl.when(owner)(lambda: keep_head(q).start())
                for sems_of, to in ((x_sems, p.across), (tp_sems.at[0], p.other)):
                    net.send(
                        lambda q=q: heads_mine.at[q],
                        lambda q=q: heads_out.at[place(q, 0)],
                        sems_of.at[q],
                        to,
                        owner,
                    )
            for q in range(8):
                yield 38.0 + 2 * q
                theirs = lambda q=q: heads_out.at[place(q, 1)]
                net.recv(theirs, x_sems.at[q], owner)
                net.send(theirs, theirs, tp_sems.at[1, q], p.other, owner)
            yield 85.0
            for q in range(8):
                for side in (0, 1):
                    net.recv(lambda: heads_out.at[place(q, side)], tp_sems.at[side, q], ~owner)
                pl.when(owner)(lambda: keep_head(q).wait())

        def latents():
            sem = net.sem()
            net.send(lambda: pair.at[p.t], lambda: pair.at[p.t], sem, p.other)
            yield 54.0
            net.recv(lambda: pair.at[1 - p.t], sem)
            yield from gather_steps(net, pair, pairs, 16, 55, 2.2)

        def chain():
            yield from gather_steps(net, down_block, RowBlocks(downs, shard), 16, 0, 8)
            keep = pltpu.make_async_copy(downs, down_out, net.sem())
            keep.start()
            at_lane = 0
            for out, w in zip((g1, gq, gl, g2), widths):
                for n in range(16):
                    out[:, n * w : (n + 1) * w] = gain_blocks[n, :1, at_lane : at_lane + w]
                at_lane += w
            values = x_out[...]
            normed[...] = (values * norm_factor(values) * g1[...]).astype(BF)
            both[...] = matmul(normed[...], downs[...])
            query, latent = both[:, :qr], both[:, qr : qr + KVR]
            query_block[...] = (query * norm_factor(query) * gq[...]).astype(BF)
            pair[p.t, :, :KVR] = (latent * norm_factor(latent) * gl[...]).astype(BF)
            pair[p.t, :, KVR:] = turn(both[:, qr + KVR :], cos_ref[...], sin_ref[...]).astype(BF)
            tasks = together(latents(), gather_steps(net, query_block, queries, 8, 51, 2.2))
            yield next(tasks)
            for n in range(16):
                columns[n] = normed[:, n * shard : (n + 1) * shard]
            yield from tasks
            keep.wait()

        run_together(
            chain(),
            after(0.5, gather_steps(net, gains_ref, gain_blocks, 16, 0.5, 1)),
            trades(),
            attention(),
        )
        net.finish()

    ff_shape = (shard, lanes)
    return comm_call(
        "front",
        number,
        body,
        [layer_input, query_down, latent_down, gains, gate, up, down_t, query_up, latent_up, out_t]
        + [cosine, sine_table],
        [VMEM] * 12,
        [
            shape((rows, wide), F32),
            shape((rows, dim), F32),
            shape((dim, wide)),
            *[shape((1, 16 * w), F32) for w in widths],
            shape((16, 2, rows, KVR + 128)),
            shape((8, rows, qr)),
            shape((16, rows, shard)),
            shape((1 + len(TRADED_FIRST),) + ff_shape),
            shape((len(TRADED_NEXT),) + ff_shape),
            shape((len(TRADED_LAST),) + ff_shape),
            shape((4,) + ff_shape),
            shape((16, at_rows, lanes)),
        ],
        [VMEM, VMEM, ANY] + [VMEM] * 4 + [ANY] * 2 + [VMEM] + [ANY] * 5,
        [
            pltpu.VMEM((shard, wide), BF),
            pltpu.VMEM((dim, wide), BF),
            pltpu.VMEM((16,) + gains.shape, F32),
            pltpu.VMEM((16,) + ff_shape, BF),
            pltpu.VMEM((4, at_rows, lanes), BF),
            pltpu.VMEM((rows, dim), BF),
            pltpu.VMEM((2, rows, KVR + 128), BF),
            pltpu.VMEM((rows, qr), BF),
            pltpu.VMEM((8, at_rows, lanes), BF),
            pltpu.SemaphoreType.DMA((8,)),
            pltpu.SemaphoreType.DMA((8,)),
            pltpu.SemaphoreType.DMA((2, 8)),
            pltpu.SemaphoreType.DMA((8,)),
            pltpu.SemaphoreType.DMA((16,)),
            pltpu.SemaphoreType.DMA((16,)),
        ],
        300,
    )


def head_grads_steps(net, at_ref, o_ref, o_got, at_out, at_x, at_tp, x_sems, tp_sems, start):
    p = net.place
    owner = p.d == p.t
    f = p.a * 2 + p.d
    rows, o_rows = at_ref.shape[1], o_ref.shape[1]
    place = lambda q, side: (q // 2 * 2 + (1 - p.b if side else p.b)) * 2 + q % 2
    for side in (1, 0):
        for q in range(8):
            net.send(
                lambda q=q, side=side: at_ref.at[place(q, side)],
                lambda q=q, side=side: at_tp.at[side, q, pl.ds(0, rows)],
                tp_sems.at[side, q],
                p.other,
                ~owner,
            )

    def join(side, q):
        here = at_tp.at[side, q, pl.ds(0, rows)]
        net.recv(lambda: here, tp_sems.at[side, q], owner)

        def add():
            n = place(q, side)
            add_into(here, [here, at_ref.at[n]], rows)
            add_into(at_tp.at[side, q, pl.ds(rows, o_rows)], [o_ref.at[n], o_got.at[n]], o_rows)

        pl.when(owner)(add)

    for q in range(8):
        yield start + 2 + q
        join(1, q)
        net.send(
            lambda q=q: at_tp.at[1, q], lambda q=q: at_x.at[q], x_sems.at[0, q], p.across, owner
        )
    keep = pltpu.make_async_copy(at_tp.at[0, f], at_out.at[p.a], net.sem())
    for q in range(8):
        yield start + 11 + 2 * q
        join(0, q)
        here, near = at_tp.at[0, q], at_x.at[q]
        net.recv(lambda: near, x_sems.at[0, q], owner)
        pl.when(owner)(lambda: add_into(here, [here, near], rows + o_rows))
        net.send(
            lambda here=here: here,
            lambda: at_out.at[p.a],
            x_sems.at[1, p.a],
            lambda q=q: p.at(a=q // 2, d=q % 2),
            owner & (f != q),
        )
        pl.when(owner & (f == q))(lambda: keep.start())
    yield start + 55
    for s in range(4):
        net.recv(lambda s=s: at_out.at[s], x_sems.at[1, s], ~(owner & (p.a == s)))
    pl.when(owner)(lambda: keep.wait())


def plain_call(name, body, ins, outs, scratch, members):
    def whole(array):
        return pl.BlockSpec(array.shape, lambda i, g: (0,) * len(array.shape))

    g = (lax.axis_index("ctx") // members).astype(jnp.int32).reshape(1)
    return pl.pallas_call(
        body,
        out_shape=outs,
        grid_spec=pltpu.PrefetchScalarGridSpec(
            num_scalar_prefetch=1,
            grid=(1,),
            in_specs=[whole(i) for i in ins],
            out_specs=[whole(o) for o in outs],
            scratch_shapes=scratch,
        ),
        compiler_params=pltpu.CompilerParams(vmem_limit_bytes=62 << 20),
        cost_estimate=pl.CostEstimate(
            flops=1_000_000_000, bytes_accessed=20 << 20, transcendentals=0
        ),
        name=name,
    )(g, *ins)


def pack(gate, up, down_t, wide, members):
    rows = gate.shape[0]
    units = gate.shape[1] // 16

    def body(g_ref, gate_ref, up_ref, down_ref, out):
        for n in range(16):
            cut = slice(n * units, (n + 1) * units)
            i = g_ref[0] ^ n
            for k, part in enumerate((gate_ref, up_ref, down_ref)):
                out[i, :, k * units : (k + 1) * units] = part[:, cut]
            out[i, :, 3 * units :] = jnp.zeros((rows, wide - 3 * units), BF)

    return plain_call(
        "pack", body, [gate, up, down_t], [shape((16, rows, wide))], [], members
    )[0]


def feed_forward(ns, gf, own, oth, order, units, members):
    tokens, dim = ns.shape
    rows, wide = own[0].shape[1:]
    lanes = 256
    both = 2 * lanes
    places = [[(a, k) for a, w in enumerate(side) for k in range(w.shape[0])] for side in (own, oth)]

    def body(g_ref, ns_ref, gf_ref, *refs):
        own_refs, oth_refs = refs[: len(own)], refs[len(own) : len(own) + len(oth)]
        out_ref, gs_ref, gown_ref, goth_ref = refs[len(own) + len(oth) :][:4]
        wgu_ref, wd_ref, hidden_ref, ggu_ref = refs[-4:]
        g = g_ref[0]
        for place, i in enumerate(order):
            cut = pl.ds(pl.multiple_of((g ^ i) * rows, rows), rows)
            for half, side in enumerate((own_refs, oth_refs)):
                a, k = places[half][place]
                block = side[a][k]
                pad = jnp.zeros((rows, lanes - units), BF)
                for k in range(3):
                    part = jnp.concatenate([block[:, k * units : (k + 1) * units], pad], axis=1)
                    into = wgu_ref if k < 2 else wd_ref
                    at = (both * k if k < 2 else 0) + half * lanes
                    into[cut, at : at + lanes] = part

        def forth(i):
            r = pl.ds(pl.multiple_of(i * 256, 256), 256)
            gate_up = matmul(ns_ref[r], wgu_ref[...])
            gate, up = gate_up[:, :both], gate_up[:, both:]
            grad_hidden = matmul(gf_ref[r], wd_ref[...])
            sigmoid_gate = 1.0 / (1.0 + jnp.exp(-gate))
            silu = gate * sigmoid_gate
            hidden_ref[r] = (silu * up).astype(BF)
            ggu_ref[r, :both] = (
                grad_hidden * up * sigmoid_gate * (1.0 + gate * (1.0 - sigmoid_gate))
            ).astype(BF)
            ggu_ref[r, both:] = (grad_hidden * silu).astype(BF)
            gs_ref[r] = matmul_nt(ggu_ref[r], wgu_ref[...]).astype(BF)
            out_ref[r] = matmul_nt(hidden_ref[r], wd_ref[...]).astype(BF)

        pl.loop(0, tokens // 256)(forth)

        span = dim // 4

        def give(q, k, grads):
            for jj in range(4):
                for half, out in enumerate((gown_ref, goth_ref)):
                    out[g ^ (4 * q + jj), :, k * units : (k + 1) * units] = grads[
                        jj * rows : (jj + 1) * rows, half * lanes : half * lanes + units
                    ].astype(BF)

        for q in range(4):
            cut = slice(q * span, (q + 1) * span)
            grads = matmul_tn(ns_ref[:, cut], ggu_ref[...])
            give(q, 0, grads[:, :both])
            give(q, 1, grads[:, both:])
            give(q, 2, matmul_tn(gf_ref[:, cut], hidden_ref[...]))
        for out in (gown_ref, goth_ref):
            out[:, :, 3 * units :] = jnp.zeros((16, rows, wide - 3 * units), BF)

    return plain_call(
        "feed_forward",
        body,
        [ns, gf, *own, *oth],
        [shape((tokens, dim))] * 2 + [shape((16, rows, wide))] * 2,
        [
            pltpu.VMEM((dim, 2 * both), BF),
            pltpu.VMEM((dim, both), BF),
            pltpu.VMEM((tokens, both), BF),
            pltpu.VMEM((tokens, 2 * both), BF),
        ],
        members,
    )


def spread(parts, order, at, down, halves, units, members):
    rows, cols = parts[0].shape[1:]
    places = [(a, k) for a, w in enumerate(parts) for k in range(w.shape[0])]
    n_parts = len(parts)
    heads, width = H // 8, H // 8 * VH
    o_rows = rows // 2
    q_rows, l_rows = 3 * KVR // 16, KVR // 16
    outs = [shape((rows, 16 * units), F32)] * 3
    if members == 1:
        outs += [
            shape((q_rows, 4 * heads * (NOPE + ROPE)), F32),
            shape((l_rows, 4 * cols), F32),
            shape((rows, 4 * width), F32),
            shape((rows, down.shape[1] - KVR - 128), F32),
            shape((rows, KVR + ROPE), F32),
        ]
    own_rows, dim = halves[0].shape
    outs = [shape((2 * own_rows, dim)), shape((2 * own_rows, dim), F32)] + outs
    ins = list(halves) + ([at, down] if members == 1 else []) + list(parts)
    first = len(ins) - n_parts

    def body(g_ref, *refs):
        out_refs = refs[len(ins) : -1]
        t = lax.axis_index("tp")
        for k in range(4):
            start = pl.multiple_of((t if k % 2 == 0 else 1 - t) * own_rows, own_rows)
            out = out_refs[k // 2]
            out[pl.ds(start, own_rows)] = refs[k][...].astype(out.dtype)
        hold = refs[-1]
        for i, (a, k) in zip(order, places):
            hold[g_ref[0] ^ i] = refs[first + a][k].astype(F32)
        rest = out_refs[2:]
        for n in range(16):
            for k, out in enumerate(rest[:3]):
                out[:, n * units : (n + 1) * units] = hold[n, :, k * units : (k + 1) * units]
        if members == 1:
            at_ref, down_ref = refs[4], refs[5]
            qr = down_ref.shape[1] - KVR - 128
            rest[6][...] = down_ref[:, :qr]
            rest[7][:, :KVR] = down_ref[:, qr : qr + KVR]
            rest[7][:, KVR:] = down_ref[:, qr + KVR + NOPE : qr + KVR + NOPE + ROPE]
            for s in range(4):
                part = at_ref[s].astype(F32)
                for h in range(heads):
                    cut = (s * heads + h) * (NOPE + ROPE)
                    rest[3][:, cut : cut + NOPE + ROPE] = part[
                        :q_rows, h * 128 : h * 128 + NOPE + ROPE
                    ]
                rest[4][:, s * cols : (s + 1) * cols] = part[q_rows : q_rows + l_rows]
                for half in (0, 1):
                    rest[5][half * o_rows : (half + 1) * o_rows, s * width : (s + 1) * width] = (
                        part[q_rows + l_rows :, half * width : (half + 1) * width]
                    )

    return plain_call(
        "spread",
        body,
        ins,
        outs,
        [pltpu.VMEM((16, rows, cols), F32)],
        members,
    )


def project(number, x, down, gains, cosine, sine_table, ff, heads_in, n_ctx):
    rows, dim = x.shape
    wide = down.shape[1]
    qr = wide - KVR - 128
    cols = dim // 16

    def body(
        x_ref, down_ref, g1_ref, gq_ref, gl_ref, cos_ref, sin_ref, ff_ref, heads_ref,
        both, pair, pairs, queries, columns, mid, heads,
        normed, column_blocks, pair_block, query_block,
        col_sems, ff_sems, x_sems, tp_sems, sems,
    ):
        p = Place(n_ctx)
        greet(p, everyone=16, other=True)
        net = Net(p, sems)
        owner = p.d == p.t
        place = lambda q, side: (q // 2 * 2 + (1 - p.b if side else p.b)) * 2 + q % 2
        keep_heads = [net.sem() for _ in range(8)]

        def keep_head(q):
            return pltpu.make_async_copy(heads_ref.at[q], heads.at[place(q, 0)], keep_heads[q])

        def send_head(q, sems_of, to):
            net.send(
                lambda: heads_ref.at[q], lambda: heads.at[place(q, 0)], sems_of.at[q], to, owner
            )

        for q in range(8):
            send_head(q, x_sems, p.across)

        def spread_heads():
            yield 9.5
            for q in range(8):
                pl.when(owner)(lambda: keep_head(q).start())
                send_head(q, tp_sems.at[0], p.other)
            for q in range(8):
                yield 16.0 + 2 * q
                theirs = lambda q=q: heads.at[place(q, 1)]
                net.recv(theirs, x_sems.at[q], owner)
                net.send(theirs, theirs, tp_sems.at[1, q], p.other, owner)
            yield 60.0
            for q in range(8):
                for side in (0, 1):
                    net.recv(lambda: heads.at[place(q, side)], tp_sems.at[side, q], ~owner)
                pl.when(owner)(lambda: keep_head(q).wait())

        out = lambda i: mid.at[TRADED_NEXT.index(i)]
        run_together(trade_sends(net, lambda i: ff_ref.at[i], out, ff_sems, [(i, 0) for i in TRADED_NEXT]))
        values = x_ref[...]
        normed[...] = (values * norm_factor(values) * g1_ref[...]).astype(BF)
        both[...] = matmul(normed[...], down_ref[...])
        query, latent = both[:, :qr], both[:, qr : qr + KVR]
        query_block[...] = (query * norm_factor(query) * gq_ref[...]).astype(BF)
        pair_block[:, :KVR] = (latent * norm_factor(latent) * gl_ref[...]).astype(BF)
        pair_block[:, KVR:] = turn(both[:, qr + KVR :], cos_ref[...], sin_ref[...]).astype(BF)

        def send_columns():
            for n in range(16):
                column_blocks[n] = normed[:, n * cols : (n + 1) * cols]
            keep = pltpu.make_async_copy(column_blocks.at[p.g], columns.at[p.g], net.sem())
            keep.start()
            for k in range(1, 16):
                if k % 4 == 1:
                    yield 13.0 + k
                net.send(
                    lambda k=k: column_blocks.at[p.g ^ k],
                    lambda: columns.at[p.g],
                    col_sems.at[k],
                    lambda k=k: ((p.g ^ k) * p.members + p.m, p.t),
                )
            yield 50.0
            for k in range(1, 16):
                net.recv(lambda k=k: columns.at[p.g ^ k], col_sems.at[k])
            keep.wait()

        def latents():
            sem = net.sem()
            keep = pltpu.make_async_copy(pair_block, pair.at[p.t], net.sem())
            keep.start()
            net.send(lambda: pair_block, lambda: pair.at[p.t], sem, p.other)
            yield 11.0
            net.recv(lambda: pair.at[1 - p.t], sem)
            keep.wait()
            yield from gather_steps(net, pair, pairs, 16, 12, 2.2)

        run_together(
            latents(),
            gather_steps(net, query_block, queries, 8, 9, 2.2),
            after(9.0, send_columns()),
            spread_heads(),
        )
        trade_receives(net, out, ff_sems, TRADED_NEXT)
        net.finish()

    return comm_call(
        "project",
        number,
        body,
        [x, down, *gains, cosine, sine_table, ff, heads_in],
        [VMEM] * 7 + [ANY] * 2,
        [
            shape((rows, wide), F32),
            shape((2, rows, KVR + 128)),
            shape((16, 2, rows, KVR + 128)),
            shape((8, rows, qr)),
            shape((16, rows, cols)),
            shape((len(TRADED_NEXT),) + ff.shape[1:]),
            shape((16,) + heads_in.shape[1:]),
        ],
        [VMEM] + [ANY] * 6,
        [
            pltpu.VMEM((rows, dim), BF),
            pltpu.VMEM((16, rows, cols), BF),
            pltpu.VMEM((rows, KVR + 128), BF),
            pltpu.VMEM((rows, qr), BF),
            pltpu.SemaphoreType.DMA((16,)),
            pltpu.SemaphoreType.DMA((16,)),
            pltpu.SemaphoreType.DMA((8,)),
            pltpu.SemaphoreType.DMA((2, 8)),
        ],
        240,
    )


def norm_back_rows(values, gain, upstream):
    factor = norm_factor(values)
    scaled = upstream * gain
    inner = jnp.mean(scaled * values, axis=-1, keepdims=True)
    share = upstream * values * factor
    total = share[:8]
    for i in range(1, share.shape[0] // 8):
        total = total + share[8 * i : 8 * i + 8]
    return factor * scaled - values * factor * factor * factor * inner, total


def wind_up(
    number, pairs, queries, at, at_o, at_o_got, both, x, grad_middle, down, gains, second, cosine,
    sine_table, ff_own, ff_got, columns, widths, n_ctx,
):
    rows, dim = x.shape
    wide = down.shape[1]
    qr = wide - KVR - 128
    members = n_ctx // 16
    down_shape = down.shape
    unit_rows = ff_own.shape[1]
    traded = TRADED_FIRST + TRADED_NEXT

    def body(
        pairs_ref, queries_ref, at_ref, o_ref, o_got, both_ref, x_ref, middle_ref, down_hbm,
        g1_ref, gq_ref, gl_ref, second_ref, cos_ref, sin_ref, columns_ref, own_ref, got_ref,
        at_out, ff_out, down_sum, input_half, input_other, gains_out,
        own_hold, ff_sum, at_x, at_tp, core_in, tp_in, pair_sum, query_sum, grad_both, gain_blocks, gain_tp,
        down, both_all, down_part, down_other, *rest,
    ):
        p = Place(n_ctx)
        greet(p, everyone=16, other=True)
        rest = list(rest)
        net = Net(p, rest.pop())
        load_sems, tp_sems, x_sems, ff_sems, pair_sems = [rest.pop() for _ in range(5)]
        load_down = pltpu.make_async_copy(down_hbm, down, net.sem())
        load_down.start()

        def latents():
            for q in range(8):
                net.send(
                    lambda q=q: pairs_ref.at[2 * q + 1 - p.d],
                    lambda q=q: core_in.at[q],
                    pair_sems.at[0, q],
                    p.core,
                )
            for q in range(8):
                yield 1.5 + 0.2 * q
                net.recv(lambda q=q: core_in.at[q], pair_sems.at[0, q])
                for half in (0, 1):
                    near = core_in.at[q, half]
                    add_into(near, [near, pairs_ref.at[2 * q + p.d, half]], rows)
                net.send(
                    lambda q=q: core_in.at[q, 1 - p.t],
                    lambda q=q: tp_in.at[q],
                    pair_sems.at[1, q],
                    p.other,
                )
            for q in range(8):
                yield 4.0 + 1.1 * (q + 1)
                net.recv(lambda q=q: tp_in.at[q], pair_sems.at[1, q])
                add_into(tp_in.at[q], [tp_in.at[q], core_in.at[q, p.t]], rows)
            yield from reduce_steps(net, tp_in, pair_sum, None, *rest[:3], rows, 8, 14, 1.1, True)

        def trades():
            loads = {
                i: [
                    pltpu.make_async_copy(ref.at[i], hold.at[k], load_sems.at[n, k])
                    for n, (ref, hold) in enumerate(((own_ref, own_hold), (got_ref, ff_sum)))
                ]
                for k, i in enumerate(TRADED_BACK)
            }
            for load in loads.values():
                for part in load:
                    part.start()

            def block(i):
                return ff_sum.at[TRADED_BACK.index(i)]

            def joined(i):
                for part in loads[i]:
                    part.wait()
                k = TRADED_BACK.index(i)
                add_into(block(i), [block(i), own_hold.at[k]], unit_rows)
                return block(i)

            out = lambda i: ff_out.at[TRADED_BACK.index(i)]
            timed = ((8, 1), (5, 2), (9, 6), (6, 8), (12, 12), (7, 14), (1, 15), (13, 18), (11, 24))
            for i, when_to in timed:
                yield when_to
                joined(i)
                yield from trade_sends(net, block, out, ff_sems, ((i, when_to),))
            keep = pltpu.make_async_copy(joined(0), out(0), net.sem())
            keep.start()
            yield 95.0
            trade_receives(net, out, ff_sems, traded)
            keep.wait()

        def gain_sums():
            sem = net.sem()
            net.send(lambda: gain_blocks, lambda: gain_tp, sem, p.other)
            yield 45.0
            net.recv(lambda: gain_tp, sem)
            pl.loop(0, 16)(lambda g: add_into(gain_tp.at[g], [gain_tp.at[g], gain_blocks.at[g]], 16))
            yield from reduce_steps(net, gain_tp, gains_out, *rest[6:10], 16, 16, 46, 2)

        def gather_and_multiply(gather):
            yield from gather
            columns = columns_ref[...].reshape(16 * rows, columns_ref.shape[2])
            down_part[...] = matmul_tn(columns, both_all[...]).astype(BF)
            swap = swap_steps(net, down_part, down_other)
            yield next(swap)
            yield from swap
            down_sum[...] = down_part[...].astype(F32) + down_other[...].astype(F32)

        def chain():
            yield from together(
                latents(),
                reduce_steps(net, queries_ref, query_sum, None, *rest[3:6], rows, 8, 0, 2.2),
            )
            query_back, query_share = norm_back_rows(
                both_ref[:, :qr], gq_ref[...], query_sum[...]
            )
            grad_both[:, :qr] = query_back.astype(BF)
            latent_back, latent_share = norm_back_rows(
                both_ref[:, qr : qr + KVR], gl_ref[...], pair_sum[:, :KVR]
            )
            grad_both[:, qr : qr + KVR] = latent_back.astype(BF)
            grad_both[:, qr + KVR :] = turn(
                pair_sum[:, KVR:], cos_ref[...], sin_ref[...], True
            ).astype(BF)

            gather = gather_steps(net, grad_both, RowBlocks(both_all, rows), 16, 31, 3.3)
            next(gather)
            load_down.wait()
            input_back, input_share = norm_back_rows(
                x_ref[...], g1_ref[...], matmul_nt(grad_both[...], down[...])
            )
            input_half[...] = (middle_ref[...] + input_back).astype(BF)
            swap = swap_steps(net, input_half, input_other)
            next(swap)
            shares = [
                jnp.sum(share, axis=0, keepdims=True)
                for share in (input_share, query_share, latent_share, second_ref[...])
            ]
            for n in range(16):
                parts = []
                for m in range(members):
                    for share, w in zip(shares, widths):
                        at_lane = (n * members + m) * w
                        parts.append(share[:, at_lane : at_lane + w])
                row = jnp.concatenate(parts, axis=1)
                gain_blocks[n] = jnp.broadcast_to(row, gain_blocks.shape[1:]).astype(BF)
            yield from together(gather_and_multiply(gather), gain_sums(), swap)

        run_together(
            chain(),
            after(
                3.5,
                head_grads_steps(
                    net, at_ref, o_ref, o_got, at_out, at_x, at_tp, x_sems, tp_sems, 12
                ),
            ),
            trades(),
        )
        net.finish()

    lanes = pairs.shape[3]
    gain_lanes = members * sum(widths)
    at_rows = at.shape[1] + at_o.shape[1]
    scratch = [
        pltpu.VMEM((len(TRADED_BACK),) + ff_own.shape[1:], BF),
        pltpu.VMEM((len(TRADED_BACK),) + ff_own.shape[1:], BF),
        pltpu.VMEM((8, at_rows) + at.shape[2:], BF),
        pltpu.VMEM((2, 8, at_rows) + at.shape[2:], BF),
        pltpu.VMEM((8, 2, rows, lanes), BF),
        pltpu.VMEM((8, rows, lanes), BF),
        pltpu.VMEM((rows, lanes), F32),
        pltpu.VMEM((rows, qr), F32),
        pltpu.VMEM((rows, wide), BF),
        pltpu.VMEM((16, 16, gain_lanes), BF),
        pltpu.VMEM((16, 16, gain_lanes), BF),
        pltpu.VMEM(down_shape, BF),
        pltpu.VMEM((16 * rows, wide), BF),
        pltpu.VMEM((dim // 16, wide), BF),
        pltpu.VMEM((dim // 16, wide), BF),
    ]
    scratch += reduce_scratch(rows, lanes, 8) + reduce_scratch(rows, qr, 8)
    scratch += reduce_scratch(16, gain_lanes, 16)
    scratch += [
        pltpu.SemaphoreType.DMA((2, 8)),
        pltpu.SemaphoreType.DMA((16,)),
        pltpu.SemaphoreType.DMA((2, 8)),
        pltpu.SemaphoreType.DMA((2, 8)),
        pltpu.SemaphoreType.DMA((2, len(TRADED_BACK))),
    ]
    return comm_call(
        "wind_up",
        number,
        body,
        [pairs, queries, at, at_o, at_o_got, both, x, grad_middle, down, *gains, second, cosine]
        + [sine_table, columns, ff_own, ff_got],
        [VMEM] * 8 + [ANY] + [VMEM] * 7 + [ANY] * 2,
        [
            shape((4, at_rows) + at.shape[2:]),
            shape((len(TRADED_BACK),) + ff_own.shape[1:]),
            shape((dim // 16, wide), F32),
            shape((rows, dim)),
            shape((rows, dim)),
            shape((16, gain_lanes), F32),
        ],
        [ANY, ANY, VMEM, VMEM, ANY, VMEM],
        scratch,
        260,
    )


def norm_factor(values):
    return lax.rsqrt(jnp.mean(values * values, axis=-1, keepdims=True) + eps_norm)


def branch_and_norm(number, parts, x, gain, gf, n_ctx):
    rows, dim = x.shape
    parts = parts.reshape(8, rows, dim)

    def body(
        parts_ref, x_ref, gain_ref, gf_ref,
        middle, norms, gfs,
        branch, normed, near, line_in, line_out, sems,
    ):
        place = Place(n_ctx)
        greet(place, line=True, across=True, core=True)
        net = Net(place, sems)

        def second():
            yield from reduce_steps(
                net, parts_ref, branch, None, near, line_in, line_out, rows, 8, 0, 7
            )

            def norm(r):
                values = x_ref[r] + residual_scale * branch[r]
                middle[r] = values
                normed[r] = (values * norm_factor(values) * gain_ref[...]).astype(BF)

            by_rows(rows, 16, norm)
            yield from gather_steps(net, normed, norms, 16, 32, 7)

        run_together(second(), after(0.5, gather_steps(net, gf_ref, gfs, 16, 0, 11)))
        net.finish()

    return comm_call(
        "branch_and_norm",
        number,
        body,
        [parts, x, gain, gf],
        [VMEM] * 3 + [ANY],
        [shape((rows, dim), F32), shape((16, rows, dim)), shape((16, rows, dim))],
        [VMEM, ANY, ANY],
        [pltpu.VMEM((rows, dim), F32), pltpu.VMEM((rows, dim), BF)]
        + reduce_scratch(rows, dim, 8),
        220,
    )


def norm_and_branch_back(number, parts, ffn_parts, middle, out_grad, gain, n_ctx):
    rows, dim = middle.shape
    parts, ffn_parts = parts.reshape(16, rows, dim), ffn_parts.reshape(16, rows, dim)

    def body(
        parts_ref, ffn_ref, middle_ref, out_grad_ref, gain_ref,
        grad_middle, gain_part, branches, output,
        upstream, branch, ffn_sum, *rest,
    ):
        place = Place(n_ctx)
        greet(place, line=True, across=True, core=True)
        net = Net(place, rest[-1])

        def chain():
            yield from reduce_steps(net, parts_ref, upstream, *rest[:4], rows, 16, 0, 7)
            gain_part[...] = jnp.zeros((8, dim), F32)

            def back(r):
                grads, share = norm_back_rows(middle_ref[r], gain_ref[...], upstream[r])
                total = out_grad_ref[r] + grads
                grad_middle[r] = total
                branch[r] = (residual_scale * total).astype(BF)
                gain_part[...] += share

            by_rows(rows, 16, back)
            yield from gather_steps(net, branch, branches, 8, 38, 7)

        run_together(
            chain(), after(0.5, reduce_steps(net, ffn_ref, ffn_sum, *rest[4:8], rows, 16, 28, 7))
        )
        output[...] = (middle_ref[...] + residual_scale * ffn_sum[...]).astype(BF)
        net.finish()

    return comm_call(
        "norm_and_branch_back",
        number,
        body,
        [parts, ffn_parts, middle, out_grad, gain],
        [VMEM] * 5,
        [
            shape((rows, dim), F32),
            shape((8, dim), F32),
            shape((8, rows, dim)),
            shape((rows, dim)),
        ],
        [VMEM, VMEM, ANY, VMEM],
        [
            pltpu.VMEM((rows, dim), F32),
            pltpu.VMEM((rows, dim), BF),
            pltpu.VMEM((rows, dim), F32),
        ]
        + reduce_scratch(rows, dim, 16) * 2,
        240,
    )


def unit_weights(g, sides, order, units, rows, lanes, wgu_ref, wd_ref):
    pad = jnp.zeros((rows, lanes - units), BF)
    for place, i in enumerate(order):
        cut = pl.ds(pl.multiple_of((g ^ i) * rows, rows), rows)
        for half, side in enumerate(sides):
            block = side(place)
            for k in range(3):
                part = jnp.concatenate([block[:, k * units : (k + 1) * units], pad], axis=1)
                into = wgu_ref if k < 2 else wd_ref
                at = (2 * lanes * k if k < 2 else 0) + half * lanes
                into[cut, at : at + lanes] = part


def forward(number, parts, x, gain, gf, own, oth, late, order, units, n_ctx):
    rows, dim = x.shape
    tokens, shard = 16 * rows, late[0].shape[1]
    lanes = 256
    both = 2 * lanes
    parts = parts.reshape(8, rows, dim)
    n_own, n_oth, n_late = len(own), len(oth), len(late)
    late_places = [(a, k) for a, w in enumerate(late) for k in range(w.shape[0])]
    n_last = len(late_places)
    own_places, oth_places = [
        [(a, k) for a, w in enumerate(side) for k in range(w.shape[0])] for side in (own, oth)
    ]
    n_early = len(own_places)

    def body(parts_ref, x_ref, gain_ref, gf_ref, *refs):
        own_refs, oth_refs = refs[:n_own], refs[n_own : n_own + n_oth]
        late_refs, refs = refs[n_own + n_oth :][:n_late], refs[n_own + n_oth + n_late :]
        middle, ns_out, gf_out, acts_out, gs_out, ffn_out = refs[:6]
        last_block = lambda k: late_refs[late_places[k][0]].at[late_places[k][1]]
        (
            branch, normed, ns_ref, gf_all, acts_ref, gs_ref, ffn_ref, wgu_ref, wd_ref, other_last,
            near, line_in, line_out, last_sems, out_sems, sems,
        ) = refs[6:]
        p = Place(n_ctx)
        greet(p, line=True, across=True, core=True, other=True)
        net = Net(p, sems)

        def weights():
            for k in range(n_last):
                net.send(
                    lambda k=k: last_block(k),
                    lambda k=k: other_last.at[k],
                    last_sems.at[k],
                    p.other,
                )
            yield 3.0
            own_block = lambda n: own_refs[own_places[n][0]][own_places[n][1]]
            oth_block = lambda n: oth_refs[oth_places[n][0]][oth_places[n][1]]
            unit_weights(
                p.g, (own_block, oth_block), order[:n_early], units, shard, lanes, wgu_ref, wd_ref
            )
            yield 38.0
            for k in range(n_last):
                net.recv(lambda k=k: other_last.at[k], last_sems.at[k])
            unit_weights(
                p.g,
                (lambda k: last_block(k)[...], lambda k: other_last[k]),
                order[n_early:],
                units,
                shard,
                lanes,
                wgu_ref,
                wd_ref,
            )

        a = p.a
        nth = (
            a,
            jnp.where(a == 0, 1, a - 1),
            jnp.where(a < 2, 2, jnp.where(a == 2, 3, 1)),
            jnp.where(a < 2, 3, 0),
        )
        stores = []

        def compute(n):
            r = pl.ds(pl.multiple_of(nth[n] * 4 * rows, 4 * rows), 4 * rows)
            gate_up = matmul(ns_ref[r], wgu_ref[...])
            gate, up = gate_up[:, :both], gate_up[:, both:]
            grad_hidden = matmul(gf_all[r], wd_ref[...])
            sigmoid_gate = 1.0 / (1.0 + jnp.exp(-gate))
            silu = gate * sigmoid_gate
            acts_ref[r, 2 * both :] = (silu * up).astype(BF)
            acts_ref[r, :both] = (
                grad_hidden * up * sigmoid_gate * (1.0 + gate * (1.0 - sigmoid_gate))
            ).astype(BF)
            acts_ref[r, both : 2 * both] = (grad_hidden * silu).astype(BF)
            gs_ref[r] = matmul_nt(acts_ref[r, : 2 * both], wgu_ref[...]).astype(BF)
            ffn_ref[r] = matmul_nt(acts_ref[r, 2 * both :], wd_ref[...]).astype(BF)
            pairs = (
                (ns_ref, ns_out), (gf_all, gf_out), (acts_ref, acts_out), (gs_ref, gs_out),
                (ffn_ref, ffn_out),
            )
            for k, (src, dst) in enumerate(pairs):
                stores.append(pltpu.make_async_copy(src.at[r], dst.at[r], out_sems.at[n, k]))
                stores[-1].start()

        def second():
            yield from reduce_steps(
                net, parts_ref, branch, None, near, line_in, line_out, rows, 8, 0, 7
            )

            def norm(r):
                values = x_ref[r] + residual_scale * branch[r]
                middle[r] = values
                normed[r] = (values * norm_factor(values) * gain_ref[...]).astype(BF)

            by_rows(rows, 16, norm)
            yield from gather_steps(net, normed, RowBlocks(ns_ref, rows), 16, 32, 7, compute)

        run_together(
            second(),
            after(0.5, gather_steps(net, gf_ref, RowBlocks(gf_all, rows), 16, 0, 8, lambda n: None)),
            after(0.7, weights()),
        )
        for store in stores:
            store.wait()
        net.finish()

    ins = [parts, x, gain, gf, *own, *oth, *late]
    return comm_call(
        "forward",
        number,
        body,
        ins,
        [VMEM] * len(ins),
        [
            shape((rows, dim), F32),
            shape((tokens, dim)),
            shape((tokens, dim)),
            shape((tokens, 3 * both)),
            shape((tokens, dim)),
            shape((tokens, dim)),
        ],
        [VMEM] + [ANY] * 5,
        [
            pltpu.VMEM((rows, dim), F32),
            pltpu.VMEM((rows, dim), BF),
            pltpu.VMEM((tokens, dim), BF),
            pltpu.VMEM((tokens, dim), BF),
            pltpu.VMEM((tokens, 3 * both), BF),
            pltpu.VMEM((tokens, dim), BF),
            pltpu.VMEM((tokens, dim), BF),
            pltpu.VMEM((dim, 2 * both), BF),
            pltpu.VMEM((dim, both), BF),
            pltpu.VMEM((n_last,) + late[0].shape[1:], BF),
        ]
        + reduce_scratch(rows, dim, 8)
        + [pltpu.SemaphoreType.DMA((n_last,)), pltpu.SemaphoreType.DMA((4, 5))],
        240,
    )


def backward(number, gs, ffn, ns, gf, acts, middle, out_grad, gain, columns, units, wide, n_ctx):
    rows, dim = middle.shape
    tokens, shard = 16 * rows, dim // 16
    lanes = 256
    both = 2 * lanes

    def body(
        gs_hbm, ffn_hbm, ns_hbm, gf_hbm, acts_hbm, middle_ref, out_grad_ref, gain_ref, col_ref,
        grad_middle, gain_part, branches, output, own_out, got_out, col_out,
        upstream, branch, ffn_sum, gs_ref, ffn_ref, ns_ref, gf_ref, acts_ref, own, oth,
        *rest,
    ):
        rest = list(rest)
        sems, col_sems, other_sems, own_sems, load_sems = [rest.pop() for _ in range(5)]
        pairs = (
            (gs_hbm, gs_ref), (ffn_hbm, ffn_ref), (ns_hbm, ns_ref), (acts_hbm, acts_ref),
            (gf_hbm, gf_ref),
        )
        loads = [
            pltpu.make_async_copy(src, dst, load_sems.at[k]) for k, (src, dst) in enumerate(pairs)
        ]
        for load in loads:
            load.start()
        p = Place(n_ctx)
        greet(p, everyone=16, other=True)
        net = Net(p, sems)
        stores = []

        def chain():
            loads[0].wait()
            yield from reduce_steps(
                net, RowBlocks(gs_ref, rows), upstream, *rest[:4], rows, 16, 0, 7
            )
            gain_part[...] = jnp.zeros((8, dim), F32)

            def back(r):
                grads, share = norm_back_rows(middle_ref[r], gain_ref[...], upstream[r])
                total = out_grad_ref[r] + grads
                grad_middle[r] = total
                branch[r] = (residual_scale * total).astype(BF)
                gain_part[...] += share

            by_rows(rows, 16, back)
            yield from gather_steps(net, branch, branches, 8, 38, 7)

        def output_sum():
            loads[1].wait()
            yield from reduce_steps(
                net, RowBlocks(ffn_ref, rows), ffn_sum, *rest[4:8], rows, 16, 28, 7
            )

        def give(q, k, grads):
            for jj in range(4):
                for half, out in enumerate((own, oth)):
                    out[p.g ^ (4 * q + jj), :, k * units : (k + 1) * units] = grads[
                        jj * shard : (jj + 1) * shard, half * lanes : half * lanes + units
                    ].astype(BF)

        def weight_grads():
            for out in (own, oth):
                out[:, :, 3 * units :] = jnp.zeros((16, shard, wide - 3 * units), BF)
            for load in loads[2:]:
                load.wait()
            span = dim // 4
            for q in range(4):
                yield 5.0 + 7.5 * q
                cut = slice(q * span, (q + 1) * span)
                grads = matmul_tn(ns_ref[:, cut], acts_ref[:, : 2 * both])
                give(q, 0, grads[:, :both])
                give(q, 1, grads[:, both:])
                give(q, 2, matmul_tn(gf_ref[:, cut], acts_ref[:, 2 * both :]))
                for n in range(4 * q, 4 * q + 4):
                    net.send(
                        lambda n=n: oth.at[p.g ^ n],
                        lambda n=n: got_out.at[p.g ^ n],
                        other_sems.at[n],
                        p.other,
                    )
                    stores.append(
                        pltpu.make_async_copy(own.at[p.g ^ n], own_out.at[p.g ^ n], own_sems.at[n])
                    )
                    stores[-1].start()
            yield 80.0
            for n in range(16):
                net.recv(lambda n=n: got_out.at[p.g ^ n], other_sems.at[n])

        def send_columns():
            keep = pltpu.make_async_copy(col_ref.at[p.g], col_out.at[p.g], net.sem())
            keep.start()
            for k in range(1, 16):
                yield 8.0 + 1.5 * k
                net.send(
                    lambda k=k: col_ref.at[p.g ^ k],
                    lambda: col_out.at[p.g],
                    col_sems.at[k],
                    lambda k=k: ((p.g ^ k) * p.members + p.m, p.t),
                )
            yield 82.0
            for k in range(1, 16):
                net.recv(lambda k=k: col_out.at[p.g ^ k], col_sems.at[k])
            keep.wait()

        run_together(
            chain(), after(0.5, output_sum()), after(3.5, weight_grads()), after(4.0, send_columns())
        )
        output[...] = (middle_ref[...] + residual_scale * ffn_sum[...]).astype(BF)
        for store in stores:
            store.wait()
        net.finish()

    block_shape = (16, shard, wide)
    return comm_call(
        "backward",
        number,
        body,
        [gs, ffn, ns, gf, acts, middle, out_grad, gain, columns],
        [ANY] * 5 + [VMEM] * 4,
        [
            shape((rows, dim), F32),
            shape((8, dim), F32),
            shape((8, rows, dim)),
            shape((rows, dim)),
            shape(block_shape),
            shape(block_shape),
            shape(columns.shape),
        ],
        [VMEM, VMEM, ANY, VMEM] + [ANY] * 3,
        [
            pltpu.VMEM((rows, dim), F32),
            pltpu.VMEM((rows, dim), BF),
            pltpu.VMEM((rows, dim), F32),
            pltpu.VMEM((tokens, dim), BF),
            pltpu.VMEM((tokens, dim), BF),
            pltpu.VMEM((tokens, dim), BF),
            pltpu.VMEM((tokens, dim), BF),
            pltpu.VMEM((tokens, 3 * both), BF),
            pltpu.VMEM(block_shape, BF),
            pltpu.VMEM(block_shape, BF),
        ]
        + reduce_scratch(rows, dim, 16) * 2
        + [
            pltpu.SemaphoreType.DMA((5,)),
            pltpu.SemaphoreType.DMA((16,)),
            pltpu.SemaphoreType.DMA((16,)),
            pltpu.SemaphoreType.DMA((16,)),
        ],
        240,
    )


def turn(values, cosine, sine_table, back=False):
    lane = lax.broadcasted_iota(jnp.int32, values.shape, 1)
    near = jnp.where((lane >= 80) & (lane < 96), pltpu.roll(values, 16, 1), 0.0)
    far = jnp.where((lane >= 64) & (lane < 80), pltpu.roll(values, 112, 1), 0.0)
    turned = (near - far) * sine_table
    kept = values * jnp.where(lane < 64, 1.0, jnp.where(lane < 96, cosine, 0.0))
    return kept - turned if back else kept + turned


def unpack_heads(at_ref, q_up_ref, l_up_ref, w_ref, q_rows, l_rows):
    o_rows, width = w_ref.shape[0] // 32, w_ref.shape[1]
    first = q_rows + l_rows
    for n in range(16):
        q_up_ref[n * q_rows : (n + 1) * q_rows] = at_ref[n, :q_rows]
        l_up_ref[n * l_rows : (n + 1) * l_rows] = at_ref[n, q_rows:first]
        for half in (0, 1):
            row = (2 * n + half) * o_rows
            w_ref[row : row + o_rows] = at_ref[n, first:, half * width : (half + 1) * width]


def by_rows(rows, step, body):
    pl.loop(0, rows // step)(lambda i: body(pl.ds(pl.multiple_of(i * step, step), step)))


def lanes_of(h):
    return pl.ds(pl.multiple_of(h * 128, 128), 128)


def key_tile(expanded, ropes):
    lane = lax.broadcasted_iota(jnp.int32, expanded.shape, 1)
    return jnp.where(lane < NOPE, expanded, ropes)


def attend(number, qn, at, pairs, cosine, sine_table, q_pos, ff, near, width, n_ctx):
    rows, keys, heads = qn.shape[0], pairs.shape[0], at.shape[2] // 128
    span, block = keys // 4, rows // 4
    q_rows, l_rows = qn.shape[1] // 16, KVR // 16
    dim = (at.shape[1] - q_rows - l_rows) * 32

    def body(
        qn_ref, at_ref, pairs_ref, cos_ref, sin_ref, pos_ref, ff_ref, near_ref,
        branch_ref, q_ref, o_ref, lse_ref, att_ref, q_up_ref, l_up_ref, w_ref, far_ref,
        next_out,
        e_ref, top_ref, sum_ref, acc_ref, sems,
    ):
        swaps = [(near_ref.at[pl.ds(4, near.shape[0] - 4)], next_out)]
        copies = trade_away(Place(n_ctx), ff_ref, far_ref, sems, swaps)
        unpack_heads(at_ref, q_up_ref, l_up_ref, w_ref, q_rows, l_rows)
        by_rows(
            keys,
            256,
            lambda r: e_ref.__setitem__(
                r, matmul(pairs_ref[r, :KVR], l_up_ref[...]).astype(BF)
            ),
        )

        def head(h):
            lanes = lanes_of(h)
            raw = matmul(qn_ref[...], q_up_ref[:, lanes])
            q_ref[:, lanes] = turn(raw, cos_ref[...], sin_ref[...]).astype(BF)
            top_ref[...] = jnp.full(top_ref.shape, -1e30, F32)
            sum_ref[...] = jnp.zeros(sum_ref.shape, F32)
            acc_ref[...] = jnp.zeros(acc_ref.shape, F32)
            for kb in range(4):
                part, cols = slice(kb * block, rows), slice(kb * span, (kb + 1) * span)
                values = e_ref[cols, lanes]
                key = key_tile(values, pairs_ref[cols, KVR:])
                scores = matmul_nt(q_ref[part, lanes], key) * score_scale
                index = lax.broadcasted_iota(jnp.int32, scores.shape, 1) + kb * span
                scores = jnp.where(index <= pos_ref[part, :1], scores, -1e30)
                old = top_ref[part, :1]
                top = jnp.maximum(old, jnp.max(scores, axis=1, keepdims=True))
                weights = jnp.exp(scores - top)
                decay = jnp.exp(old - top)
                total = sum_ref[part, :1] * decay + jnp.sum(weights, axis=1, keepdims=True)
                acc_ref[part] = acc_ref[part] * decay + matmul(weights.astype(BF), values)
                top_ref[part] = jnp.broadcast_to(top, acc_ref[part].shape)
                sum_ref[part] = jnp.broadcast_to(total, acc_ref[part].shape)
            lane = lax.broadcasted_iota(jnp.int32, acc_ref.shape, 1)
            o_ref[:, lanes] = jnp.where(lane < NOPE, 0.0, acc_ref[...] / sum_ref[...])
            lse_ref[:, lanes] = top_ref[...] + jnp.log(sum_ref[...])

        pl.loop(0, heads)(head)
        for h in range(heads):
            att_ref[:, h * VH : (h + 1) * VH] = o_ref[
                :, h * 128 + NOPE : (h + 1) * 128
            ].astype(BF)
        for i in range(dim // 512):
            cut = slice(i * 512, (i + 1) * 512)
            branch_ref[:, cut] = matmul_nt(att_ref[...], w_ref[cut]).astype(BF)
        for copy in copies:
            copy.wait()

    wide = heads * 128
    return pl.pallas_call(
        body,
        out_shape=[
            shape((rows, dim)),
            shape((rows, wide)),
            shape((rows, wide), F32),
            shape((rows, wide), F32),
            shape((rows, heads * VH)),
            shape((qn.shape[1], wide)),
            shape((KVR, wide)),
            shape((dim, width)),
            shape(ff.shape),
            shape((near.shape[0] - 4,) + near.shape[1:]),
        ],
        in_specs=[VMEM] * 6 + [ANY] * 2,
        out_specs=[VMEM] * 8 + [ANY] * 2,
        scratch_shapes=[pltpu.VMEM((keys, wide), BF)]
        + [pltpu.VMEM((rows, 128), F32)] * 3
        + [pltpu.SemaphoreType.DMA((2, len(TRADED_LAST) + 1))],
        compiler_params=pltpu.CompilerParams(
            collective_id=number, has_side_effects=True, vmem_limit_bytes=60 << 20
        ),
        cost_estimate=pl.CostEstimate(
            flops=20_000_000_000, bytes_accessed=20 << 20, transcendentals=0
        ),
        name="attend",
    )(qn, at, pairs, cosine, sine_table, q_pos, ff, near)


def attend_back(
    number, gb, qn, q_up, pairs, l_up, w_out_t, cosine, sine_table, q_pos, q, o, lse, att,
    ff_own, ff_got, half, n_ctx,
):
    rows, keys, heads = qn.shape[0], pairs.shape[0], q_up.shape[1] // 128
    span, block = keys // 4, rows // 4
    dim, wide = gb.shape[1], heads * 128
    q_rows, l_rows, o_rows, width = qn.shape[1] // 16, KVR // 16, dim // 32, att.shape[1]
    first = q_rows + l_rows
    unit_rows = ff_own.shape[1]

    def body(
        gb_ref, qn_ref, q_up_ref, pairs_ref, l_up_ref, w_ref, cos_ref, sin_ref, pos_ref,
        q_ref, o_ref, lse_ref, att_ref, own_ref, got_ref, half_ref,
        gp_ref, gqn_ref, at_ref, at_o_ref, at_o_got, far_ref, other_ref,
        e_ref, rope_ref, go_ref, gq_ref, dq_ref, inner_ref, mine_ref, theirs_ref, sems, load_sems, at_sems,
    ):
        loads = [
            pltpu.make_async_copy(part.at[i], hold.at[k], load_sems.at[n, k])
            for n, (part, hold) in enumerate(((own_ref, mine_ref), (got_ref, theirs_ref)))
            for k, i in enumerate(TRADED_LAST)
        ]
        for load in loads:
            load.start()
        for load in loads:
            load.wait()
        for k in range(len(TRADED_LAST)):
            add_into(mine_ref.at[k], [mine_ref.at[k], theirs_ref.at[k]], unit_rows)
        place = Place(n_ctx)
        owner = place.d == place.t
        copies = trade_away(place, mine_ref, far_ref, sems, [(half_ref, other_ref)])

        def expand(r):
            e_ref[r] = matmul(pairs_ref[r, :KVR], l_up_ref[...]).astype(BF)
            rope_ref[r] = jnp.zeros((256, 128), F32)

        by_rows(keys, 256, expand)
        ga = matmul(gb_ref[...], w_ref[...]).astype(BF)
        for h in range(heads):
            go_ref[:, h * 128 : h * 128 + NOPE] = jnp.zeros((rows, NOPE), BF)
            go_ref[:, h * 128 + NOPE : (h + 1) * 128] = ga[:, h * VH : (h + 1) * VH]
        for i in range(4):
            part = matmul_tn(gb_ref[:, i * dim // 4 : (i + 1) * dim // 4], att_ref[...]).astype(BF)
            for k in range(8):
                half = k % 2
                at_o_ref[4 * i + k // 2, :, half * width : (half + 1) * width] = part[
                    k * o_rows : (k + 1) * o_rows
                ]

        outward = pltpu.make_async_remote_copy(
            at_o_ref,
            at_o_got,
            at_sems.at[0],
            at_sems.at[1],
            device_id=place.other(),
            device_id_type=MESH,
        )
        pl.when(~owner)(lambda: outward.start())

        def head(h):
            lanes = lanes_of(h)
            dq_ref[...] = jnp.zeros(dq_ref.shape, F32)
            inner = jnp.sum(
                go_ref[:, lanes].astype(F32) * o_ref[:, lanes], axis=1, keepdims=True
            )
            inner_ref[...] = jnp.broadcast_to(inner, inner_ref.shape)
            for kb in range(4):
                part, cols = slice(kb * block, rows), slice(kb * span, (kb + 1) * span)
                values = e_ref[cols, lanes]
                key = key_tile(values, pairs_ref[cols, KVR:])
                queries, grads = q_ref[part, lanes], go_ref[part, lanes]
                scores = matmul_nt(queries, key) * score_scale
                index = lax.broadcasted_iota(jnp.int32, scores.shape, 1) + kb * span
                probs = jnp.where(
                    index <= pos_ref[part, :1],
                    jnp.exp(scores - lse_ref[part, lanes][:, :1]),
                    0.0,
                )
                grad_probs = matmul_nt(grads, values)
                grad_scores = (probs * (grad_probs - inner_ref[part, :1])).astype(BF)
                dq_ref[part] += matmul(grad_scores, key)
                grad_key = matmul_tn(grad_scores, queries) * score_scale
                grad_value = matmul_tn(probs.astype(BF), grads)
                lane = lax.broadcasted_iota(jnp.int32, grad_key.shape, 1)
                e_ref[cols, lanes] = jnp.where(lane < NOPE, grad_key, grad_value).astype(BF)
                rope_ref[cols] += jnp.where(lane < NOPE, 0.0, grad_key)
            gq_ref[:, lanes] = turn(
                dq_ref[...] * score_scale, cos_ref[...], sin_ref[...], True
            ).astype(BF)

        pl.loop(0, heads)(head)

        def latents(r):
            gp_ref[r, :KVR] = matmul_nt(e_ref[r], l_up_ref[...]).astype(BF)
            gp_ref[r, KVR:] = rope_ref[r].astype(BF)

        by_rows(keys, 256, latents)
        gl_up = matmul_tn(pairs_ref[:, :KVR], e_ref[...]).astype(BF)
        gq_up = matmul_tn(qn_ref[...], gq_ref[...]).astype(BF)
        for n in range(16):
            at_ref[n, :q_rows] = gq_up[n * q_rows : (n + 1) * q_rows]
            at_ref[n, q_rows:] = gl_up[n * l_rows : (n + 1) * l_rows]
        gqn_ref[...] = matmul_nt(gq_ref[...], q_up_ref[...]).astype(BF)
        for copy in copies:
            copy.wait()
        pl.when(~owner)(lambda: outward.wait_send())
        pl.when(owner)(lambda: outward.wait_recv())

    return pl.pallas_call(
        body,
        out_shape=[
            shape(pairs.shape),
            shape(qn.shape),
            shape((16, first, wide)),
            shape((16, o_rows, wide)),
            shape((16, o_rows, wide)),
            shape((len(TRADED_LAST),) + ff_own.shape[1:]),
            shape(half.shape),
        ],
        in_specs=[VMEM] * 13 + [ANY] * 3,
        out_specs=[VMEM] * 4 + [ANY] * 3,
        scratch_shapes=[
            pltpu.VMEM((keys, wide), BF),
            pltpu.VMEM((keys, 128), F32),
            pltpu.VMEM((rows, wide), BF),
            pltpu.VMEM((rows, wide), BF),
            pltpu.VMEM((rows, 128), F32),
            pltpu.VMEM((rows, 128), F32),
            pltpu.VMEM((len(TRADED_LAST),) + ff_own.shape[1:], BF),
            pltpu.VMEM((len(TRADED_LAST),) + ff_own.shape[1:], BF),
            pltpu.SemaphoreType.DMA((2, len(TRADED_LAST) + 1)),
            pltpu.SemaphoreType.DMA((2, len(TRADED_LAST))),
            pltpu.SemaphoreType.DMA((2,)),
        ],
        compiler_params=pltpu.CompilerParams(
            collective_id=number, has_side_effects=True, vmem_limit_bytes=60 << 20
        ),
        cost_estimate=pl.CostEstimate(
            flops=40_000_000_000, bytes_accessed=30 << 20, transcendentals=0
        ),
        name="attend_back",
    )(gb, qn, q_up, pairs, l_up, w_out_t, cosine, sine_table, q_pos, q, o, lse, att, ff_own, ff_got, half)


def shards(
    layer_input,
    first_gain,
    query_down,
    query_gain,
    query_up,
    latent_down,
    latent_gain,
    latent_up,
    out_weight,
    second_gain,
    gate_weight,
    up_weight,
    down_weight,
    out_grad,
):
    n_ctx = lax.axis_size("ctx")
    n_tp = lax.axis_size("tp")
    members = n_ctx // 16
    c = lax.axis_index("ctx")
    t = lax.axis_index("tp")
    g = c // members
    b = lax.rem(g // 2, 2)
    d = lax.rem(g, 2)
    member = lax.rem(c, members)
    ctx_rows, dim = layer_input.shape
    rows = ctx_rows // n_tp
    shard_rows = query_down.shape[0]
    qr = query_down.shape[1]
    heads = H // 8
    units = gate_weight.shape[1] // 16
    member_lists = [[k * members + m for m in range(members)] for k in range(16)]

    def widen(blocks):
        if members == 1:
            return blocks[:, None]
        return lax.all_gather(blocks, "ctx", axis=1, axis_index_groups=member_lists)

    def narrow(blocks):
        if members == 1:
            return blocks[:, 0]
        return lax.psum_scatter(
            blocks.astype(F32), "ctx", scatter_dimension=1, axis_index_groups=member_lists
        ).astype(BF)

    widths = [first_gain.shape[0], query_gain.shape[0], latent_gain.shape[0], second_gain.shape[0]]
    starts = [0, widths[0], widths[0] + widths[1], widths[0] + widths[1] + widths[2]]
    gains = jnp.concatenate([first_gain, query_gain, latent_gain, second_gain]).astype(F32)
    gains = jnp.broadcast_to(gains[None], (8, gains.shape[0]))

    def swap_tp(block):
        return lax.ppermute(block, "tp", [(0, 1), (1, 0)])

    wide = 640
    q_rows_w, l_rows_w, o_rows_w = query_up.shape[0], latent_up.shape[0], shard_rows // 2
    q_width, o_width = heads * (NOPE + ROPE), heads * VH
    out_grad_rows = lax.dynamic_slice_in_dim(out_grad, t * rows, rows, 0).astype(F32)
    grad_ffn = (residual_scale * out_grad_rows).astype(BF)

    def rope_tiles(positions):
        lane = jnp.arange(128, dtype=jnp.int32) % (ROPE // 2)
        frequency = rope_base ** (-lane.astype(F32) / (ROPE // 2))
        angles = positions.astype(F32)[:, None] * frequency[None, :]
        return jnp.cos(angles), jnp.sin(angles)

    row = jnp.arange(rows, dtype=jnp.int32)
    cosine, sine_table = rope_tiles(c * ctx_rows + t * rows + row)
    block = jnp.arange(8, dtype=jnp.int32)
    block_ctx = ((block // 2 * 2 + b) * 2 + block % 2) * members + member
    q_positions = (block_ctx[:, None] * ctx_rows + t * rows + row[None, :]).reshape(-1)
    q_cos, q_sin = rope_tiles(q_positions)
    q_pos = jnp.broadcast_to(q_positions[:, None], (q_positions.shape[0], 128))

    if members == 1:
        (
            both, x, down_full, *all_gains, pairs, qn_all, token_columns,
            own_near, own_mid, own_last, oth_near, at_all,
        ) = front(
            1, layer_input, query_down, latent_down, gains, gate_weight, up_weight, down_weight.T,
            query_up, latent_up, out_weight.T, cosine, sine_table, widths, n_ctx,
        )
        gain_first, gain_query, gain_latent, gain_second = all_gains
        first_gains = (gain_first, gain_query, gain_latent)
    else:
        x = lax.dynamic_slice_in_dim(layer_input, t * rows, rows, 0).astype(F32)
        down_shard = jnp.concatenate(
            [
                query_down,
                latent_down[:, :KVR],
                jnp.zeros((shard_rows, NOPE), BF),
                latent_down[:, KVR:],
                jnp.zeros((shard_rows, 128 - NOPE - ROPE), BF),
            ],
            axis=1,
        )

        ff = pack(gate_weight, up_weight, down_weight.T, wide, members)
        q_tiles = jnp.pad(
            query_up.reshape(q_rows_w, 4, heads, NOPE + ROPE),
            ((0, 0), (0, 0), (0, 0), (0, 128 - NOPE - ROPE)),
        ).reshape(q_rows_w, 4, wide)
        out_tiles = jnp.transpose(
            out_weight.reshape(4, o_width, 2, o_rows_w), (0, 3, 2, 1)
        ).reshape(4, o_rows_w, wide)
        at = jnp.concatenate(
            [
                jnp.transpose(q_tiles, (1, 0, 2)),
                jnp.transpose(latent_up.reshape(l_rows_w, 4, wide), (1, 0, 2)),
                out_tiles,
            ],
            axis=1,
        )

        down_full, gains, at_mine, own_near = weights_in(1, down_shard, gains, at, ff, n_ctx)
        own_near, ff = lax.optimization_barrier((own_near, ff))
        down_full = widen(down_full).reshape(dim, -1)
        gains = widen(gains[:, 0]).reshape(n_ctx, -1)
        gain_first, gain_query, gain_latent, gain_second = [
            gains[:, s : s + w].reshape(1, -1) for s, w in zip(starts, widths)
        ]
        first_gains = (gain_first, gain_query, gain_latent)
        both, _, pairs, qn_all, token_columns, own_mid, at_all = project(
            3, x, down_full, first_gains, cosine, sine_table, ff, at_mine, n_ctx
        )
        own_last = jnp.stack([ff[i] for i in TRADED_LAST])
        own_near, own_mid = lax.optimization_barrier((own_near, own_mid))
        oth_near = swap_tp(own_near[:4])
    lat_rope = widen(pairs).reshape(-1, KVR + 128)
    if members > 1:
        at_all = widen(at_all).reshape(n_ctx, -1, wide)
        out_tiles = at_all[:, q_rows_w + l_rows_w :].reshape(n_ctx, o_rows_w, 2, o_width)
        out_tiles = jnp.transpose(out_tiles, (0, 2, 1, 3)).reshape(16, 2, dim // 32, o_width)
        at_all = jnp.concatenate(
            [
                at_all[:, :q_rows_w].reshape(16, -1, wide),
                at_all[:, q_rows_w : q_rows_w + l_rows_w].reshape(16, -1, wide),
                jnp.transpose(out_tiles, (0, 2, 1, 3)).reshape(16, -1, wide),
            ],
            axis=1,
        )
    (
        branch_part, queries, attended_wide, log_total, attended, q_up, l_up, w_out_t,
        own_far, oth_next,
    ) = attend(
        5, qn_all.reshape(-1, qr), at_all, lat_rope, q_cos, q_sin, q_pos, own_last, own_near,
        o_width, n_ctx,
    )
    qn_all = qn_all.reshape(-1, qr)

    order = (0,) + TRADED_FIRST + TRADED_NEXT + TRADED_LAST
    if members == 1:
        middle, ns_all, gf_all, acts, second_part, ffn_part = forward(
            4, branch_part, x, gain_second, grad_ffn, [own_near], [oth_near, oth_next],
            [own_mid, own_far], order, units, n_ctx,
        )
        grad_middle, second_gain_part, gb_all, out_half, grads_own, grads_got, token_columns = backward(
            6, second_part, ffn_part, ns_all, gf_all, acts, middle, out_grad_rows, gain_second,
            token_columns, units, wide, n_ctx,
        )
    else:
        middle, ns_all, gf_all = branch_and_norm(
            4, branch_part, x, gain_second, grad_ffn, n_ctx
        )
        ns_all, gf_all = ns_all.reshape(-1, dim), gf_all.reshape(-1, dim)
        oth_mid, oth_far = swap_tp(own_mid), swap_tp(own_far)
        own = [own_near, own_mid, own_far]
        oth = [oth_near, oth_next, oth_mid, oth_far]
        ns_all, oth = lax.optimization_barrier((ns_all, oth))
        own, oth = [[widen(jnp.concatenate(w)).reshape(16, dim // 16, wide)] for w in (own, oth)]
        ffn_part, second_part, grads_own, grads_oth = feed_forward(
            ns_all, gf_all, own, oth, order, units, members
        )
        grads_own = narrow(grads_own.reshape(16, members, shard_rows, wide))
        grads_oth = narrow(grads_oth.reshape(16, members, shard_rows, wide))
        grads_got = swap_tp(grads_oth)
        grad_middle, second_gain_part, gb_all, out_half = norm_and_branch_back(
            6, second_part, ffn_part, middle, out_grad_rows, gain_second, n_ctx
        )
    gb_all, grads_got = lax.optimization_barrier((gb_all, grads_got))
    grad_pairs, gqn_part, at_part, at_o, at_o_got, sums_far, out_other = attend_back(
        7, gb_all.reshape(-1, dim), qn_all, q_up, lat_rope, l_up, w_out_t, q_cos, q_sin, q_pos,
        queries, attended_wide, log_total, attended, grads_own, grads_got, out_half, n_ctx,
    )
    if members > 1:
        q_part = at_part[:, : qr // 16].reshape(n_ctx, q_rows_w, wide)
        l_part = at_part[:, qr // 16 : (qr + KVR) // 16].reshape(n_ctx, l_rows_w, wide)
        at_part = narrow(
            jnp.concatenate([q_part, l_part], axis=1).reshape(16, members, -1, wide)
        )

        def by_ctx(o_part):
            o_part = o_part.reshape(16, dim // 32, 2, o_width)
            o_part = jnp.transpose(o_part, (0, 2, 1, 3)).reshape(n_ctx, 2, o_rows_w, o_width)
            o_part = jnp.transpose(o_part, (0, 2, 1, 3)).reshape(16, members, o_rows_w, wide)
            return narrow(o_part)

        at_o, at_o_got = by_ctx(at_o), by_ctx(at_o_got)
    at_sums, sums, down_sum, input_half, input_other, gain_sums = wind_up(
        8,
        narrow(grad_pairs.reshape(16, members, 2, rows, KVR + 128)),
        gqn_part.reshape(8, rows, qr),
        at_part,
        at_o,
        at_o_got,
        both,
        x,
        grad_middle,
        down_full,
        first_gains,
        second_gain_part,
        cosine,
        sine_table,
        grads_own,
        grads_got,
        token_columns,
        widths,
        n_ctx,
    )
    if members > 1:
        down_sum = lax.psum_scatter(down_sum, "ctx", axis_index_groups=member_lists, tiled=True)
    gain_grads = gain_sums[0]
    if members > 1:
        gain_grads = lax.psum_scatter(
            gain_grads.reshape(members, -1), "ctx", axis_index_groups=member_lists
        )
    first_gain_grad, query_gain_grad, latent_gain_grad, second_gain_grad = [
        gain_grads[s : s + w] for s, w in zip(starts, widths)
    ]

    layer_output, input_grad, *spread_out = spread(
        [sums, sums_far],
        TRADED_BACK + TRADED_LAST,
        at_sums,
        down_sum,
        [out_half, out_other, input_half, input_other],
        units,
        members,
    )
    gate_weight_grad, up_weight_grad, down_grad_t = spread_out[:3]
    if members == 1:
        query_up_grad, latent_up_grad, out_grad_t, query_down_grad, latent_down_grad = spread_out[3:]
        out_weight_grad = out_grad_t.T
    else:
        query_up_grad = jnp.transpose(
            at_sums[:, :q_rows_w].reshape(4, q_rows_w, heads, 128)[..., : NOPE + ROPE], (1, 0, 2, 3)
        ).reshape(q_rows_w, 4 * q_width)
        latent_up_grad = jnp.transpose(at_sums[:, q_rows_w : q_rows_w + l_rows_w], (1, 0, 2)).reshape(
            l_rows_w, 4 * wide
        )
        out_weight_grad = jnp.transpose(
            at_sums[:, q_rows_w + l_rows_w :].reshape(4, o_rows_w, 2, o_width), (0, 3, 2, 1)
        ).reshape(4 * o_width, shard_rows)
        query_down_grad = down_sum[:, :qr]
        latent_down_grad = jnp.concatenate(
            [
                down_sum[:, qr : qr + KVR],
                down_sum[:, qr + KVR + NOPE : qr + KVR + NOPE + ROPE],
            ],
            axis=1,
        )
    return (
        layer_output,
        input_grad,
        first_gain_grad,
        query_down_grad,
        query_gain_grad,
        query_up_grad.astype(F32),
        latent_down_grad,
        latent_gain_grad,
        latent_up_grad.astype(F32),
        out_weight_grad.astype(F32),
        second_gain_grad,
        gate_weight_grad,
        up_weight_grad,
        down_grad_t.T,
    )


def solution(mesh):
    return jax.shard_map(
        shards,
        mesh=mesh,
        in_specs=(
            P("ctx", None),
            P("ctx"),
            P("ctx", None),
            P("ctx"),
            P("ctx", "tp"),
            P("ctx", None),
            P("ctx"),
            P("ctx", "tp"),
            P("tp", "ctx"),
            P("ctx"),
            P("ctx", "tp"),
            P("ctx", "tp"),
            P("tp", "ctx"),
            P("ctx", None),
        ),
        out_specs=(
            P("ctx", None),
            P("ctx", None),
            P("ctx"),
            P("ctx", None),
            P("ctx"),
            P("ctx", "tp"),
            P("ctx", None),
            P("ctx"),
            P("ctx", "tp"),
            P("tp", "ctx"),
            P("ctx"),
            P("ctx", "tp"),
            P("ctx", "tp"),
            P("tp", "ctx"),
        ),
        check_vma=False,
    )
```
